32 devices in a mesh: rep: 4 (over y, x), exp: 8 (over z, core).
Axes of the slice: x: 2, y: 2, z: 4, core: 2. Of those that a mesh axis runs over, the one named last changes fastest.
Arguments:
- tokens: bfloat16 [32, 576, 768], P(('rep', 'exp')), may hold values from -6 to 6
- segments: int32 [32, 576], P(('rep', 'exp')), may hold values from 0 to 3, never falling along the last dimension, each value on 1 to 288 neighbouring positions
- valid: int32 [32, 576], P(('rep', 'exp')), may hold values 0 or 1
- routes: int32 [32, 576, 2], P(('rep', 'exp')), may hold values from 0 to 31, all different within a row
- priority: int32 [32, 576], P(('rep', 'exp')), may hold values from 0 to 575, each once within a row
- ln1_gain: bfloat16 [768], P(('rep', 'exp')), may hold values from 0.5 to 1.5
- ln1_bias: bfloat16 [768], P(('rep', 'exp')), may hold values from -1.1953125 to 1.1953125
- w_query: bfloat16 [768, 768], P(('rep', 'exp')), may hold values from -0.21875 to 0.21875
- query_bias: bfloat16 [768], P(('rep', 'exp')), may hold values from -1.1953125 to 1.1953125
- w_key: bfloat16 [768, 768], P(('rep', 'exp')), may hold values from -0.21875 to 0.21875
- w_value: bfloat16 [768, 768], P(('rep', 'exp')), may hold values from -0.21875 to 0.21875
- value_bias: bfloat16 [768], P(('rep', 'exp')), may hold values from -1.1953125 to 1.1953125
- w_attn_out: bfloat16 [768, 768], P(('rep', 'exp')), may hold values from -2 to 2
- attn_out_bias: bfloat16 [768], P(('rep', 'exp')), may hold values from -1.1953125 to 1.1953125
- ln2_gain: bfloat16 [768], P(('rep', 'exp')), may hold values from 0.5 to 1.5
- ln2_bias: bfloat16 [768], P(('rep', 'exp')), may hold values from -1.1953125 to 1.1953125
- w_router: bfloat16 [768, 32], P(('rep', 'exp')), may hold values from -0.15625 to 0.15625
- expert_in: bfloat16 [32, 768, 3072], P('exp'), may hold values from -0.21875 to 0.21875
- expert_in_bias: bfloat16 [32, 3072], P('exp'), may hold values from -1.796875 to 1.796875
- expert_out: bfloat16 [32, 3072, 768], P('exp'), may hold values from -1.75 to 1.75
- expert_out_bias: bfloat16 [32, 768], P(None, ('rep', 'exp')), may hold values from -12 to 12
- cotangent: bfloat16 [32, 576, 768], P(('rep', 'exp')), may hold values from -6 to 6
Outputs:
- block_output: bfloat16 [32, 576, 768], P(('rep', 'exp'))
- tokens_grad: float32 [32, 576, 768], P(('rep', 'exp'))
- ln1_gain_grad: float32 [768], P(('rep', 'exp'))
- ln1_bias_grad: float32 [768], P(('rep', 'exp'))
- w_query_grad: float32 [768, 768], P(('rep', 'exp'))
- query_bias_grad: float32 [768], P(('rep', 'exp'))
- w_key_grad: float32 [768, 768], P(('rep', 'exp'))
- w_value_grad: float32 [768, 768], P(('rep', 'exp'))
- value_bias_grad: float32 [768], P(('rep', 'exp'))
- w_attn_out_grad: float32 [768, 768], P(('rep', 'exp'))
- attn_out_bias_grad: float32 [768], P(('rep', 'exp'))
- ln2_gain_grad: float32 [768], P(('rep', 'exp'))
- ln2_bias_grad: float32 [768], P(('rep', 'exp'))
- w_router_grad: float32 [768, 32], P(('rep', 'exp'))
- expert_in_grad: float32 [32, 768, 3072], P('exp', None, 'rep')
- expert_in_bias_grad: float32 [32, 3072], P('exp', 'rep')
- expert_out_grad: float32 [32, 3072, 768], P('exp', 'rep')
- expert_out_bias_grad: float32 [32, 768], P(None, ('rep', 'exp'))
The draws below stay inside these ranges and needn't reach their ends.
Inputs may be any that keep to these rules, and one draw needn't show every extreme that they name: `segments`: within a row segment numbers never fall; each image holds 1 to 288 patches, one exactly that many. `routes`: the 2 experts of one patch differ from each other; different patches of a row may name the same experts; every expert is named by some patch. `priority`: each row holds every patch index once.
All inputs are finite; a program needn't handle non-finite values. No bound on the sum of `valid` on one device may be relied on, other than what follows from the above.
Results may differ from the reference program's by a relative error of at most 0.015.
Values may be sent and summed in bfloat16 or wider, within the bound.
A program may use at most 320 MiB of HBM per device.

```python
import math
import jax
import jax.numpy as jnp
import numpy as np
from jax import lax

D = 768
HEADS = 12
HD = 64
FF = 3072
EXPERTS = 32
ROW = 576
SEGS = 4
TOPK = 2
SPLIT = 1
PIECES = 32
FFS = 3072
CAP = 38
ROWS = 32


def set_ends(drawn, stream_key, least, top_value):
    index_at = [jax.random.randint(jax.random.fold_in(stream_key, axis), (), 0, length) for axis, length in enumerate(drawn.shape)]
    longest = drawn.shape.index(max(drawn.shape))
    neighbour = index_at[:longest] + [(index_at[longest] + 1) % drawn.shape[longest]] + index_at[longest + 1:]
    return drawn.at[tuple(index_at)].set(least).at[tuple(neighbour)].set(top_value)


def levels(rng, extent, shards, low, top_value):
    level, own = 1.0, jax.random.fold_in(rng, 6)
    for dim, blocks in shards:
        draws = jnp.exp(jax.random.uniform(jax.random.fold_in(own, dim), (blocks,), jnp.float32, low / len(shards), top_value / len(shards)))
        level = level * jnp.repeat(draws, extent[dim] // blocks).reshape([-1 if axis == dim else 1 for axis in range(len(extent))])
    return level


def picks_of(key, rows, count, top, lift):
    ranking = jax.random.permutation(jax.random.fold_in(key, 1), count)
    boost = ranking
    for power in range(3):
        boost = boost * boost // count
    boost = boost * lift // count
    tickets = jax.random.randint(jax.random.fold_in(key, 2), (rows, count), 0, 4096) + boost
    holders = jax.random.permutation(jax.random.fold_in(key, 3), rows)[jnp.arange(count) % rows]
    tickets = jnp.where(jnp.arange(rows)[:, None] == holders[None, :], 1 << 14, tickets)
    score = tickets * count + jnp.arange(count)
    return lax.top_k(score.astype(jnp.int32), top)[1].astype(jnp.int32)


def profile(number_of, total, reach, skew):
    weights = [(1 << 20) // math.isqrt(standing ** skew) + 1 for standing in range(2, number_of + 1)]
    rest, given = total - reach - (number_of - 1), [1] * (number_of - 1)
    while rest > 0:
        movable = [i for i in range(number_of - 1) if given[i] < reach]
        mass, budget = sum([weights[i] for i in movable]), rest
        for i in movable:
            more = min(reach - given[i], max(1, budget * weights[i] // mass), rest)
            given[i] = given[i] + more
            rest = rest - more
    return np.array([reach] + given)


def uneven_parts(key, count, total, most, lean):
    if count == 2:
        one = jax.random.randint(key, (), max(1, total - most), min(most, total - 1) + 1)
        return jnp.stack([one, total - one])
    lengths = jnp.asarray(profile(count, total, most, lean), jnp.int32)
    couples = (count - 1) // 2
    giver, taker = lengths[1:1 + 2 * couples:2], lengths[2:2 + 2 * couples:2]
    margin = jnp.minimum(giver - 1, most - taker)
    passed = jax.random.randint(jax.random.fold_in(key, 1), (couples,), 0, 1 << 20) % (margin + 1)
    lengths = lengths.at[1:1 + 2 * couples:2].set(giver - passed).at[2:2 + 2 * couples:2].set(taker + passed)
    return lengths[jax.random.permutation(jax.random.fold_in(key, 2), count)]


def bell_draw(rng, dims, scale, limit, cuts=(), held_as=jnp.bfloat16):
    entries = jax.random.normal(rng, dims, jnp.float32) * scale
    if len(cuts) > 0:
        entries = levels(rng, dims, cuts, -0.22, 0.18) * entries
    return jnp.clip(entries, min=-limit, max=limit).astype(held_as)


def setup_inputs(seed: int = 0) -> dict:
    arg_keys = jax.random.split(jax.random.key(seed), 23)
    tokens = bell_draw(arg_keys[0], (ROWS, ROW, D), 1.0, 6.0, ((0, 32),))
    segments = jax.vmap(lambda own: jnp.searchsorted(jnp.cumsum(uneven_parts(own, SEGS, ROW, ROW // 2, 0)), jnp.arange(ROW), side="right"))(jax.random.split(arg_keys[1], ROWS)).reshape((ROWS, ROW)).astype(jnp.int32)
    valid = set_ends((jax.random.randint(arg_keys[2], (ROWS, ROW), 0, 8) < 7).astype(jnp.int32), jax.random.fold_in(arg_keys[2], 1), 0, 1)
    routes = picks_of(arg_keys[3], ROWS * ROW, EXPERTS, TOPK, 512).reshape((ROWS, ROW, TOPK))
    priority = jax.vmap(lambda own: jax.random.permutation(own, ROW))(jax.random.split(arg_keys[4], ROWS)).reshape((ROWS, ROW)).astype(jnp.int32)
    ln1_gain = jnp.clip(1.0 + 0.1 * jax.random.normal(arg_keys[5], (D,), jnp.float32), 0.5, 1.5).astype(jnp.bfloat16)
    ln1_bias = bell_draw(arg_keys[6], (D,), 0.2, 1.1953125, ((0, 32),))
    w_query = bell_draw(arg_keys[7], (D, D), D ** -0.5, 0.21875, ((0, 32),))
    query_bias = bell_draw(arg_keys[8], (D,), 0.2, 1.1953125, ((0, 32),))
    w_key = bell_draw(arg_keys[9], (D, D), D ** -0.5, 0.21875, ((0, 32),))
    w_value = bell_draw(arg_keys[10], (D, D), D ** -0.5, 0.21875, ((0, 32),))
    value_bias = bell_draw(arg_keys[11], (D,), 0.2, 1.1953125, ((0, 32),))
    w_attn_out = bell_draw(arg_keys[12], (D, D), (D * 8 // ROW) ** -0.5, 2.0, ((0, 32),))
    attn_out_bias = bell_draw(arg_keys[13], (D,), 0.2, 1.1953125, ((0, 32),))
    ln2_gain = jnp.clip(1.0 + 0.1 * jax.random.normal(arg_keys[14], (D,), jnp.float32), 0.5, 1.5).astype(jnp.bfloat16)
    ln2_bias = bell_draw(arg_keys[15], (D,), 0.2, 1.1953125, ((0, 32),))
    w_router = bell_draw(arg_keys[16], (D, EXPERTS), (2 * D) ** -0.5, 0.15625, ((0, 32),))
    expert_in = bell_draw(arg_keys[17], (PIECES, D, FFS), D ** -0.5, 0.21875, ((0, 8),))
    expert_in_bias = bell_draw(arg_keys[18], (PIECES, FFS), 0.3, 1.796875, ((0, 8),))
    expert_out = bell_draw(arg_keys[19], (PIECES, FFS, D), (max(1, FF * 4 // (EXPERTS * EXPERTS))) ** -0.5, 1.75, ((0, 8),))
    expert_out_bias = bell_draw(arg_keys[20], (EXPERTS, D), (max(1, EXPERTS // 16)), 12.0, ((1, 32),))
    cotangent = bell_draw(arg_keys[21], (ROWS, ROW, D), 1.0, 6.0, ((0, 32),))
    return dict(tokens=tokens, segments=segments, valid=valid, routes=routes, priority=priority, ln1_gain=ln1_gain, ln1_bias=ln1_bias, w_query=w_query, query_bias=query_bias, w_key=w_key, w_value=w_value, value_bias=value_bias, w_attn_out=w_attn_out, attn_out_bias=attn_out_bias, ln2_gain=ln2_gain, ln2_bias=ln2_bias, w_router=w_router, expert_in=expert_in, expert_in_bias=expert_in_bias, expert_out=expert_out, expert_out_bias=expert_out_bias, cotangent=cotangent)


@jax.custom_vjp
def low(v):
    return lax.optimization_barrier(v.astype(jnp.bfloat16)).astype(jnp.float32)

@jax.custom_vjp
def low_back(v):
    return v

def low_keep(v):
    return (low(v), None)

def low_pass(kept, grad):
    return (grad,)

def back_keep(v):
    return (v, None)

def back_low(kept, grad):
    return (low(grad),)
low.defvjp(low_keep, low_pass)
low_back.defvjp(back_keep, back_low)
epsilon = 1e-06
masked_score = -1e+30
highest = lax.Precision.HIGHEST

def layer_norm(values, gain, bias):
    center = values - lax.optimization_barrier(jnp.mean(values, axis=-1, keepdims=True))
    spread = lax.optimization_barrier(jnp.mean(center * center, axis=-1, keepdims=True))
    return center * lax.rsqrt(spread + epsilon) * gain + bias

def slot_table(row_routes, row_priority, valid_mask):
    chosen = row_routes[row_priority]
    seq_expert = jnp.transpose(chosen).reshape(-1).astype(jnp.int32)
    seq_token = jnp.tile(row_priority, TOPK).astype(jnp.int32)
    seq_valid = jnp.tile(valid_mask[row_priority], TOPK).astype(jnp.int32)
    expert_ids = jnp.arange(EXPERTS, dtype=jnp.int32)
    onehot = (seq_expert[:, None] == expert_ids[None, :]).astype(jnp.int32) * seq_valid[:, None]
    before = jnp.cumsum(onehot, axis=0, dtype=jnp.int32) - onehot
    position = lax.optimization_barrier(jnp.sum(before * onehot, axis=1, dtype=jnp.int32))
    kept_mask = seq_valid * (position < CAP).astype(jnp.int32)
    slot_id = jnp.where(kept_mask > 0, seq_expert * CAP + position, EXPERTS * CAP).astype(jnp.int32)
    return (seq_token, seq_expert, slot_id, kept_mask)

def row_forward(params, row_tokens, row_segments, row_valid, row_routes, row_priority):
    ln1_gain, ln1_bias, w_query, query_bias, w_key, w_value, value_bias, w_attn_out, attn_out_bias, ln2_gain, ln2_bias, w_router, expert_in, expert_in_bias, expert_out, expert_out_bias = params
    length = row_tokens.shape[0]
    normed = low(layer_norm(row_tokens, ln1_gain, ln1_bias))
    query_rows = low(low_back(jnp.dot(normed, w_query, precision=highest) + query_bias)).reshape(length, HEADS, HD)
    key_rows = low(low_back(jnp.dot(normed, w_key, precision=highest))).reshape(length, HEADS, HD)
    value_rows = low(low_back(jnp.dot(normed, w_value, precision=highest) + value_bias)).reshape(length, HEADS, HD)
    scores = low_back(jnp.einsum('qhd,khd->hqk', query_rows, key_rows, precision=highest) * HD ** (-0.5))
    positions = jnp.arange(length, dtype=jnp.int32)
    allowed = (row_segments[:, None] == row_segments[None, :]) & ((row_valid[None, :] > 0) | (positions[:, None] == positions[None, :]))
    masked = jnp.where(allowed[None], scores, masked_score)
    top_score = lax.optimization_barrier(jnp.max(masked, axis=-1, keepdims=True))
    expo = jnp.exp(masked - top_score)
    probs = expo / lax.optimization_barrier(jnp.sum(expo, axis=-1, keepdims=True))
    mixed = jnp.einsum('hqk,khd->qhd', low(probs), value_rows, precision=highest).reshape(length, HEADS * HD)
    mixed = low(low_back(mixed))
    branch = low_back(jnp.dot(mixed, w_attn_out, precision=highest) + attn_out_bias)
    residual = row_tokens + branch
    normed_two = low(layer_norm(residual, ln2_gain, ln2_bias))
    logits = low_back(jnp.dot(normed_two, w_router, precision=highest))
    logit_top = lax.optimization_barrier(jnp.max(logits, axis=-1, keepdims=True))
    logit_exp = jnp.exp(logits - logit_top)
    router_probs = logit_exp / lax.optimization_barrier(jnp.sum(logit_exp, axis=-1, keepdims=True))
    seq_token, seq_expert, slot_id, kept_mask = slot_table(row_routes, row_priority, row_valid)
    buffer = jnp.zeros((EXPERTS * CAP + 1, D), jnp.float32).at[slot_id].add(normed_two[seq_token])
    slots = buffer[:EXPERTS * CAP].reshape(EXPERTS, CAP, D)
    in_blocks = expert_in.reshape(EXPERTS, SPLIT, D, FFS)
    in_bias_blocks = expert_in_bias.reshape(EXPERTS, SPLIT, FFS)
    out_blocks = expert_out.reshape(EXPERTS, SPLIT, FFS, D)
    total = jnp.zeros((EXPERTS, CAP, D), jnp.float32)
    for block in range(SPLIT):
        block_slots = low_back(slots)
        pre_act = low_back(jnp.einsum('ecd,edf->ecf', block_slots, in_blocks[:, block], precision=highest) + in_bias_blocks[:, block, None, :])
        active = low(jax.nn.gelu(pre_act, approximate=False))
        part = jnp.einsum('ecf,efd->ecd', active, out_blocks[:, block], precision=highest)
        total = total + low(low_back(part))
    result = total + expert_out_bias[:, None, :]
    flat_result = jnp.concatenate([result.reshape(EXPERTS * CAP, D), jnp.zeros((1, D), jnp.float32)], axis=0)
    gate_values = router_probs[seq_token, seq_expert] * kept_mask.astype(jnp.float32)
    combined = jnp.zeros((length, D), jnp.float32).at[seq_token].add(gate_values[:, None] * flat_result[slot_id])
    return residual + combined

def block_forward(params, pieces):
    block_tokens, block_segments, block_valid, block_routes, block_priority = pieces
    return jax.vmap(row_forward, in_axes=(None, 0, 0, 0, 0, 0))(params, block_tokens, block_segments, block_valid, block_routes, block_priority)

def reference(tokens, segments, valid, routes, priority, ln1_gain, ln1_bias, w_query, query_bias, w_key, w_value, value_bias, w_attn_out, attn_out_bias, ln2_gain, ln2_bias, w_router, expert_in, expert_in_bias, expert_out, expert_out_bias, cotangent):
    params = jax.tree.map(lambda leaf_array: leaf_array.astype(jnp.float32), (ln1_gain, ln1_bias, w_query, query_bias, w_key, w_value, value_bias, w_attn_out, attn_out_bias, ln2_gain, ln2_bias, w_router, expert_in, expert_in_bias, expert_out, expert_out_bias))
    blocks = ROWS // 4
    inputs = tokens.astype(jnp.float32).reshape(blocks, 4, ROW, D)
    int_blocks = (segments.reshape(blocks, 4, ROW), valid.reshape(blocks, 4, ROW), routes.reshape(blocks, 4, ROW, TOPK), priority.reshape(blocks, 4, ROW))
    remat_block = jax.checkpoint(block_forward)

    def forward(weights, block_inputs):
        return lax.map(lambda pieces: remat_block(weights, pieces), (block_inputs,) + int_blocks)
    output, pullback = jax.vjp(forward, params, inputs)
    param_grads, input_grad = pullback(cotangent.astype(jnp.float32).reshape(blocks, 4, ROW, D))
    return (output.reshape(ROWS, ROW, D).astype(jnp.bfloat16), input_grad.reshape(ROWS, ROW, D), param_grads[0], param_grads[1], param_grads[2], param_grads[3], param_grads[4], param_grads[5], param_grads[6], param_grads[7], param_grads[8], param_grads[9], param_grads[10], param_grads[11], param_grads[12], param_grads[13], param_grads[14], param_grads[15])
```

```python
import functools
import jax
import jax.numpy as jnp
from jax import lax
from jax.experimental import pallas as pl
from jax.experimental.pallas import tpu as pltpu
from jax.sharding import PartitionSpec as P

HEADS = 12
EXPERTS = 32
MESH = pl.DeviceIdType.MESH
MIB = 1 << 20

def bit_dims(reps, groups):
    rb, gb = reps.bit_length() - 1, groups.bit_length() - 1
    return [(0, 1 << k) for k in reversed(range(rb))] + [(1, 1 << k) for k in reversed(range(gb))]

def orders(dims):
    last = len(dims) - 1
    rep = [i for i, d in enumerate(dims) if d[0] == 0]
    exp = [i for i, d in enumerate(dims) if d[0] == 1 and i != last]
    exp = exp[::-1]
    return [[last] + rep + exp, [last] + rep[::-1] + exp, [last] + exp + rep]

def my_bits(dims):
    at = (lax.axis_index("rep"), lax.axis_index("exp"))
    return [(at[a] // s) % 2 for a, s in dims], at

def partner(dims, at, i):
    a, s = dims[i]
    bit = (at[a] // s) % 2
    there = at[a] + (1 - 2 * bit) * s
    return (there, at[1]) if a == 0 else (at[0], there)

def greet(dims, at):
    barrier = pltpu.get_barrier_semaphore()
    for i in range(len(dims)):
        pl.semaphore_signal(barrier, inc=1, device_id=partner(dims, at, i), device_id_type=MESH)
    pl.semaphore_wait(barrier, len(dims))

def gather_kernel(dims, widths, count, *refs):
    ins, small_in = refs[:count], refs[count]
    outs, small_out = refs[count + 1:2 * count + 1], refs[2 * count + 1]
    own_sem, send_sem, recv_sem = refs[2 * count + 2:]
    bits, at = my_bits(dims)
    n = len(dims)
    own = [pltpu.make_async_copy(a, o.at[tuple(bits)], own_sem.at[i]) for i, (a, o) in enumerate(zip(ins + (small_in,), outs + (small_out,)))]
    for c in own: c.start()
    greet(dims, at)
    for c in own: c.wait()
    plan = [o[::-1] for o in orders(dims)]
    parts = len(plan)
    def copies(p, k):
        done = plan[p][:k]
        i = plan[p][k]
        lead = tuple(slice(None) if j in done else bits[j] for j in range(n))
        out = []
        for a, o in enumerate(outs):
            where = o.at[lead + (slice(None), pl.ds(widths[p][0], widths[p][1]))]
            out.append(pltpu.make_async_remote_copy(where, where, send_sem.at[p, k, a], recv_sem.at[p, k, a], device_id=partner(dims, at, i), device_id_type=MESH))
        if p == 0:
            where = small_out.at[lead]
            out.append(pltpu.make_async_remote_copy(where, where, send_sem.at[p, k, count], recv_sem.at[p, k, count], device_id=partner(dims, at, i), device_id_type=MESH))
        return out
    live = []
    for k in range(n):
        for p in range(parts):
            if k > 0:
                for c in live[(k - 1) * parts + p]: c.wait_recv()
            cs = copies(p, k)
            for c in cs: c.start()
            live.append(cs)
    for p in range(parts):
        for c in live[(n - 1) * parts + p]: c.wait_recv()
    for cs in live:
        for c in cs: c.wait_send()

def gather_params(weights, small, reps, groups, space=pl.ANY):
    dims = bit_dims(reps, groups)
    n = len(dims)
    rows, cols = weights[0].shape
    third = cols // 3 // 128 * 128
    widths = [(0, third), (third, third), (2 * third, cols - 2 * third)]
    count = len(weights)
    lead = (2,) * n
    outs = pl.pallas_call(
        functools.partial(gather_kernel, dims, widths, count),
        out_shape=[jax.ShapeDtypeStruct(lead + w.shape, w.dtype) for w in weights] + [jax.ShapeDtypeStruct(lead + small.shape, small.dtype)],
        in_specs=[pl.BlockSpec(memory_space=space)] * (count + 1),
        out_specs=[pl.BlockSpec(memory_space=space)] * (count + 1),
        scratch_shapes=[pltpu.SemaphoreType.DMA((count + 1,)), pltpu.SemaphoreType.DMA((3, n, count + 1)), pltpu.SemaphoreType.DMA((3, n, count + 1))],
        compiler_params=pltpu.CompilerParams(collective_id=0, has_side_effects=True, vmem_limit_bytes=40 * MIB),
    )(*weights, small)
    return [o.reshape((reps * groups * o.shape[-2], o.shape[-1])) for o in outs[:count]], outs[count].reshape((reps * groups,) + small.shape)

def scatter_kernel(dims, widths, count, *refs):
    ins, small_in = refs[:count], refs[count]
    outs, small_out = refs[count + 1:2 * count + 1], refs[2 * count + 1]
    n = len(dims)
    scr = refs[2 * count + 2:]
    parts = 3
    send_sem, recv_sem = scr[:2]
    scr = scr[2:]
    take = iter(scr)
    bufs = [[(next(take), next(take), next(take) if k < n - 1 else None) for p in range(parts)] for k in range(n)]
    smalls = [(next(take), next(take) if k < n - 1 else None) for k in range(n)]
    bits, at = my_bits(dims)
    plan = orders(dims)
    left = [list(range(n)) for _ in range(parts)]
    small_left = list(range(n))
    small_cur = small_in
    def split(have, i, b):
        return tuple(b if j == i else slice(None) for j in have)
    live = []
    def begin(k, p):
        i = plan[p][k]
        sb, rb, _ = bufs[k][p]
        far = split(left[p], i, 1 - bits[i])
        cols = pl.ds(widths[p][0], widths[p][1]) if k == 0 else slice(None)
        for a in range(count):
            src = ins[a][far + (slice(None), cols)] if k == 0 else bufs[k - 1][p][2][(a,) + far]
            sb[a] = src.astype(sb.dtype)
        c = [pltpu.make_async_remote_copy(sb, rb, send_sem.at[k, p], recv_sem.at[k, p], device_id=partner(dims, at, i), device_id_type=MESH)]
        if p == 0:
            src = (small_in if k == 0 else smalls[k - 1][1]).at[far]
            c.append(pltpu.make_async_remote_copy(src, smalls[k][0], send_sem.at[k, parts], recv_sem.at[k, parts], device_id=partner(dims, at, i), device_id_type=MESH))
        for x in c: x.start()
        return c
    def finish(k, p, c):
        i = plan[p][k]
        sb, rb, acc = bufs[k][p]
        near = split(left[p], i, bits[i])
        cols = pl.ds(widths[p][0], widths[p][1]) if k == 0 else slice(None)
        for x in c: x.wait_recv()
        for a in range(count):
            src = ins[a][near + (slice(None), cols)] if k == 0 else bufs[k - 1][p][2][(a,) + near]
            tot = src + rb[a].astype(jnp.float32)
            if k < n - 1:
                acc[a] = tot
            else:
                outs[a][:, widths[p][0]:widths[p][0] + widths[p][1]] = tot
        if p == 0:
            src = (small_in if k == 0 else smalls[k - 1][1])[near]
            tot = src + smalls[k][0][...]
            if k < n - 1:
                smalls[k][1][...] = tot
            else:
                small_out[...] = tot
        left[p].remove(i)
    greet(dims, at)
    live = [begin(0, p) for p in range(parts)]
    every = list(live)
    for k in range(n):
        for p in range(parts):
            finish(k, p, live[p])
            if k < n - 1:
                live[p] = begin(k + 1, p)
                every.append(live[p])
    for cs in every:
        for c in cs: c.wait_send()

def scatter_grads(grads, small, reps, groups, link=jnp.bfloat16):
    dims = bit_dims(reps, groups)
    n = len(dims)
    full, cols = grads[0].shape
    rows = full // (reps * groups)
    third = cols // 3 // 128 * 128
    widths = [(0, third), (third, third), (2 * third, cols - 2 * third)]
    count = len(grads)
    lead = (2,) * n
    grads = [g.reshape(lead + (rows, cols)) for g in grads]
    small = small.reshape(lead + small.shape[1:])
    scratch = [pltpu.SemaphoreType.DMA((n, 4)), pltpu.SemaphoreType.DMA((n, 4))]
    for k in range(n):
        for p in range(3):
            shape = (count,) + (2,) * (n - 1 - k) + (rows, widths[p][1])
            scratch += [pltpu.VMEM(shape, link), pltpu.VMEM(shape, link)]
            if k < n - 1:
                scratch.append(pltpu.VMEM(shape, jnp.float32))
    for k in range(n):
        shape = (2,) * (n - 1 - k) + small.shape[n:]
        scratch.append(pltpu.VMEM(shape, jnp.float32))
        if k < n - 1:
            scratch.append(pltpu.VMEM(shape, jnp.float32))
    vm = pl.BlockSpec(memory_space=pltpu.VMEM)
    outs = pl.pallas_call(
        functools.partial(scatter_kernel, dims, widths, count),
        out_shape=[jax.ShapeDtypeStruct((rows, cols), jnp.float32)] * count + [jax.ShapeDtypeStruct(small.shape[n:], jnp.float32)],
        in_specs=[vm] * (count + 1),
        out_specs=[vm] * (count + 1),
        scratch_shapes=scratch,
        compiler_params=pltpu.CompilerParams(collective_id=1, has_side_effects=True, vmem_limit_bytes=56 * MIB),
    )(*grads, small)
    return outs[:count], outs[count]


def pack_small(parts, lead):
    flat = jnp.concatenate([p.reshape(lead + (-1,)) for p in parts], axis=-1)
    size = flat.shape[-1]
    room = -(-size // 2048) * 2048
    flat = jnp.pad(flat, [(0, 0)] * len(lead) + [(0, room - size)])
    return flat.reshape(lead + (room // 128, 128))


def gather_all(vectors, weights, router, shift):
    axes = ("rep", "exp")
    reps, groups = lax.axis_size("rep"), lax.axis_size("exp")
    devices = reps * groups
    per = weights[0].shape[0]
    if per % 8 or devices & (devices - 1):
        return (
            [lax.all_gather(v, axes, axis=0, tiled=True) for v in vectors],
            [lax.all_gather(w, axes, axis=0, tiled=True) for w in weights],
            lax.all_gather(router, axes, axis=0, tiled=True),
            lax.all_gather(shift, axes, axis=1, tiled=True),
        )
    small = pack_small(vectors + [router, shift], ())
    weights, small = gather_params(weights, small, reps, groups)
    small = small.reshape(devices, -1)
    count = len(vectors)
    got = [small[:, i * per : (i + 1) * per].reshape(-1) for i in range(count)]
    at = count * per
    wide = router.shape[1]
    routers = small[:, at : at + per * wide].reshape(-1, wide)
    at += per * wide
    rows = shift.shape[0]
    shifts = small[:, at : at + rows * per].reshape(devices, rows, per)
    shifts = jnp.transpose(shifts, (1, 0, 2)).reshape(rows, -1)
    return got, weights, routers, shifts


def scatter_all(vectors, weights, router, shift):
    axes = ("rep", "exp")
    reps, groups = lax.axis_size("rep"), lax.axis_size("exp")
    devices = reps * groups
    per = weights[0].shape[0] // devices
    if per % 8 or devices & (devices - 1):
        return (
            [lax.psum_scatter(v, axes, scatter_dimension=0, tiled=True) for v in vectors],
            [lax.psum_scatter(w, axes, scatter_dimension=0, tiled=True) for w in weights],
            lax.psum_scatter(router, axes, scatter_dimension=0, tiled=True),
            lax.psum_scatter(shift, axes, scatter_dimension=1, tiled=True),
        )
    rows = shift.shape[0]
    parted = jnp.transpose(shift.reshape(rows, devices, per), (1, 0, 2))
    small = pack_small(vectors + [router, parted], (devices,))
    weights, small = scatter_grads(weights, small, reps, groups)
    small = small.reshape(-1)
    count = len(vectors)
    got = [small[i * per : (i + 1) * per] for i in range(count)]
    at = count * per
    wide = router.shape[1]
    routers = small[at : at + per * wide].reshape(per, wide)
    at += per * wide
    return got, weights, routers, small[at : at + rows * per].reshape(rows, per)


epsilon = 1e-06
masked_score = -1e30


def layer_norm(values, gain, bias):
    center = values - jnp.mean(values, axis=-1, keepdims=True)
    spread = jnp.mean(center * center, axis=-1, keepdims=True)
    return center * lax.rsqrt(spread + epsilon) * gain + bias


def slot_table(row_routes, row_priority, valid_mask, experts, capacity):
    top_count = row_routes.shape[1]
    chosen = row_routes[row_priority]
    seq_expert = jnp.transpose(chosen).reshape(-1)
    seq_token = jnp.tile(row_priority, top_count)
    seq_valid = jnp.tile(valid_mask[row_priority], top_count)
    expert_ids = jnp.arange(experts, dtype=jnp.int32)
    onehot = (seq_expert[:, None] == expert_ids[None, :]).astype(jnp.int32) * seq_valid[:, None]
    before = jnp.cumsum(onehot, axis=0, dtype=jnp.int32) - onehot
    position = jnp.sum(before * onehot, axis=1, dtype=jnp.int32)
    kept_mask = seq_valid * (position < capacity).astype(jnp.int32)
    slot_id = jnp.where(kept_mask > 0, seq_expert * capacity + position, experts * capacity)
    return (seq_token, seq_expert, slot_id, kept_mask)


def attention_probs(query_heads, key_heads, allowed, score_scale, log_total):
    scores = (
        jnp.einsum("qhd,khd->hqk", query_heads, key_heads, preferred_element_type=jnp.float32)
        * score_scale
    )
    masked = jnp.where(allowed[None], scores, masked_score)
    if log_total is None:
        top_score = jnp.max(masked, axis=-1, keepdims=True)
        log_total = top_score + jnp.log(
            jnp.sum(jnp.exp(masked - top_score), axis=-1, keepdims=True)
        )
    return (jnp.exp(masked - log_total), log_total)


def gelu_exact(values):
    return jax.nn.gelu(values, approximate=False)


def body(
    tokens,
    segments,
    valid,
    routes,
    priority,
    ln1_gain,
    ln1_bias,
    w_query,
    query_bias,
    w_key,
    w_value,
    value_bias,
    w_attn_out,
    attn_out_bias,
    ln2_gain,
    ln2_bias,
    w_router,
    expert_in,
    expert_in_bias,
    expert_out,
    expert_out_bias,
    cotangent,
):
    vectors, weights, router_weight, result_shift = gather_all(
        [ln1_gain, ln1_bias, query_bias, value_bias, attn_out_bias, ln2_gain, ln2_bias],
        [w_query, w_key, w_value, w_attn_out],
        w_router,
        expert_out_bias,
    )
    gain_one, bias_one, query_shift, value_shift, proj_shift, gain_two, bias_two = vectors
    query_weight, key_weight, value_weight, proj_weight = weights
    gain_one = gain_one.astype(jnp.float32)
    bias_one = bias_one.astype(jnp.float32)
    gain_two = gain_two.astype(jnp.float32)
    bias_two = bias_two.astype(jnp.float32)
    length = tokens.shape[1]
    feature_dim = tokens.shape[2]
    head_count = HEADS
    head_dim = feature_dim // head_count
    local_blocks = expert_in.shape[0]
    groups = lax.axis_size("exp")
    experts = EXPERTS
    split = local_blocks * groups // experts
    top_count = routes.shape[2]
    capacity = (105 * top_count * length + 100 * experts - 1) // (100 * experts)
    score_scale = head_dim ** (-0.5)
    inputs = tokens[0].astype(jnp.float32)
    row_segments = segments[0]
    row_valid = valid[0]
    positions = jnp.arange(length, dtype=jnp.int32)
    allowed = (row_segments[:, None] == row_segments[None, :]) & (
        (row_valid[None, :] > 0) | (positions[:, None] == positions[None, :])
    )
    normed = layer_norm(inputs, gain_one, bias_one).astype(jnp.bfloat16)
    query_rows = (
        jnp.dot(normed, query_weight, preferred_element_type=jnp.float32)
        + query_shift.astype(jnp.float32)
    ).astype(jnp.bfloat16)
    key_rows = jnp.dot(normed, key_weight, preferred_element_type=jnp.float32).astype(jnp.bfloat16)
    value_rows = (
        jnp.dot(normed, value_weight, preferred_element_type=jnp.float32)
        + value_shift.astype(jnp.float32)
    ).astype(jnp.bfloat16)
    query_heads = query_rows.reshape(length, head_count, head_dim)
    key_heads = key_rows.reshape(length, head_count, head_dim)
    value_heads = value_rows.reshape(length, head_count, head_dim)
    attn_weights, log_total = attention_probs(query_heads, key_heads, allowed, score_scale, None)
    mixed = jnp.einsum(
        "hqk,khd->qhd",
        attn_weights.astype(jnp.bfloat16),
        value_heads,
        preferred_element_type=jnp.float32,
    )
    mixed = mixed.reshape(length, feature_dim).astype(jnp.bfloat16)
    residual = (
        inputs
        + jnp.dot(mixed, proj_weight, preferred_element_type=jnp.float32)
        + proj_shift.astype(jnp.float32)
    )
    normed_two = layer_norm(residual, gain_two, bias_two).astype(jnp.bfloat16)
    logits = jnp.dot(normed_two, router_weight, preferred_element_type=jnp.float32)
    logit_exp = jnp.exp(logits - jnp.max(logits, axis=-1, keepdims=True))
    router_probs = logit_exp / jnp.sum(logit_exp, axis=-1, keepdims=True)
    seq_token, seq_expert, slot_id, kept_mask = slot_table(
        routes[0], priority[0], row_valid, experts, capacity
    )
    kept_float = kept_mask.astype(jnp.float32)
    buffer = (
        jnp.zeros((experts * capacity + 1, feature_dim), jnp.bfloat16)
        .at[slot_id]
        .add(normed_two[seq_token])
    )
    expert_slots = buffer[: experts * capacity].reshape(experts, capacity, feature_dim)
    outgoing = jnp.repeat(expert_slots, split, axis=0).reshape(
        groups, local_blocks, capacity, feature_dim
    )
    received = lax.all_to_all(outgoing, "exp", split_axis=0, concat_axis=0, tiled=True)
    pre_act = (
        jnp.einsum("secd,edf->secf", received, expert_in, preferred_element_type=jnp.float32)
        + expert_in_bias.astype(jnp.float32)[None, :, None, :]
    )
    active = gelu_exact(pre_act).astype(jnp.bfloat16)
    result = jnp.einsum("secf,efd->secd", active, expert_out, preferred_element_type=jnp.float32)
    returned = lax.all_to_all(
        result.astype(jnp.bfloat16), "exp", split_axis=0, concat_axis=0, tiled=True
    )
    summed = jnp.sum(
        returned.reshape(experts, split, capacity, feature_dim).astype(jnp.float32), axis=1
    )
    summed = summed + result_shift.astype(jnp.float32)[:, None, :]
    flat_result = jnp.concatenate(
        [summed.reshape(experts * capacity, feature_dim), jnp.zeros((1, feature_dim), jnp.float32)],
        axis=0,
    )
    picked = flat_result[slot_id]
    gate_values = router_probs[seq_token, seq_expert] * kept_float
    combined = (
        jnp.zeros((length, feature_dim), jnp.float32)
        .at[seq_token]
        .add(gate_values[:, None] * picked)
    )
    output = residual + combined
    upstream = cotangent[0].astype(jnp.float32)
    token_grad = upstream[seq_token]
    gate_grad = jnp.sum(token_grad * picked, axis=1) * kept_float
    slot_terms = (
        jnp.zeros((experts * capacity + 1, feature_dim), jnp.float32)
        .at[slot_id]
        .add(gate_values[:, None] * token_grad)
    )
    slot_terms = slot_terms[: experts * capacity].reshape(experts, capacity, feature_dim)
    shift_grad = jnp.sum(slot_terms, axis=1)
    slot_grad = jnp.repeat(slot_terms.astype(jnp.bfloat16), split, axis=0).reshape(
        groups, local_blocks, capacity, feature_dim
    )
    back_grad = lax.all_to_all(slot_grad, "exp", split_axis=0, concat_axis=0, tiled=True)
    active_grad = jnp.einsum(
        "secd,efd->secf", back_grad, expert_out, preferred_element_type=jnp.float32
    )
    gelu_back = jax.vjp(gelu_exact, pre_act)[1]
    pre_grad = gelu_back(active_grad)[0].astype(jnp.bfloat16)
    slot_input_grad = jnp.einsum(
        "secf,edf->secd", pre_grad, expert_in, preferred_element_type=jnp.float32
    ).astype(jnp.bfloat16)
    sent_back = lax.all_to_all(slot_input_grad, "exp", split_axis=0, concat_axis=0, tiled=True)
    back_sum = jnp.sum(
        sent_back.reshape(experts, split, capacity, feature_dim).astype(jnp.float32), axis=1
    )
    flat_back = jnp.concatenate(
        [
            back_sum.reshape(experts * capacity, feature_dim),
            jnp.zeros((1, feature_dim), jnp.float32),
        ],
        axis=0,
    )
    moe_grad = jnp.zeros((length, feature_dim), jnp.float32).at[seq_token].add(flat_back[slot_id])
    out_w_grad = jnp.einsum("secf,secd->efd", active, back_grad, preferred_element_type=jnp.float32)
    in_w_grad = jnp.einsum("secd,secf->edf", received, pre_grad, preferred_element_type=jnp.float32)
    in_b_grad = jnp.sum(pre_grad, axis=(0, 2), dtype=jnp.float32)
    expert_sums = (
        lax.psum_scatter(
            in_w_grad.astype(jnp.bfloat16), "rep", scatter_dimension=2, tiled=True
        ).astype(jnp.float32),
        lax.psum_scatter(
            in_b_grad.astype(jnp.bfloat16), "rep", scatter_dimension=1, tiled=True
        ).astype(jnp.float32),
        lax.psum_scatter(
            out_w_grad.astype(jnp.bfloat16), "rep", scatter_dimension=1, tiled=True
        ).astype(jnp.float32),
    )
    prob_grad = jnp.zeros((length, experts), jnp.float32).at[seq_token, seq_expert].add(gate_grad)
    logit_grad = (
        router_probs * (prob_grad - jnp.sum(router_probs * prob_grad, axis=-1, keepdims=True))
    ).astype(jnp.bfloat16)
    router_w_grad = jnp.dot(normed_two.T, logit_grad, preferred_element_type=jnp.float32)
    normed_two_grad = moe_grad + jnp.dot(
        logit_grad, router_weight.T, preferred_element_type=jnp.float32
    )
    norm_two_back = jax.vjp(layer_norm, residual, gain_two, bias_two)[1]
    residual_ln_grad, gain_two_grad, bias_two_grad = norm_two_back(normed_two_grad)
    residual_grad = upstream + residual_ln_grad
    branch_grad = residual_grad.astype(jnp.bfloat16)
    proj_w_grad = jnp.dot(mixed.T, branch_grad, preferred_element_type=jnp.float32)
    proj_b_grad = jnp.sum(branch_grad, axis=0, dtype=jnp.float32)
    mixed_grad = jnp.dot(branch_grad, proj_weight.T, preferred_element_type=jnp.float32).astype(
        jnp.bfloat16
    )
    mixed_grad = mixed_grad.reshape(length, head_count, head_dim)
    again_probs = attention_probs(query_heads, key_heads, allowed, score_scale, log_total)[0]
    prob_grads = jnp.einsum(
        "qhd,khd->hqk", mixed_grad, value_heads, preferred_element_type=jnp.float32
    )
    value_grad = jnp.einsum(
        "hqk,qhd->khd",
        again_probs.astype(jnp.bfloat16),
        mixed_grad,
        preferred_element_type=jnp.float32,
    )
    value_grad = value_grad.astype(jnp.bfloat16).reshape(length, feature_dim)
    inner_sum = jnp.sum(again_probs * prob_grads, axis=-1, keepdims=True)
    score_grad = (again_probs * (prob_grads - inner_sum)).astype(jnp.bfloat16)
    query_grad = (
        (
            jnp.einsum("hqk,khd->qhd", score_grad, key_heads, preferred_element_type=jnp.float32)
            * score_scale
        )
        .astype(jnp.bfloat16)
        .reshape(length, feature_dim)
    )
    key_grad = (
        (
            jnp.einsum("hqk,qhd->khd", score_grad, query_heads, preferred_element_type=jnp.float32)
            * score_scale
        )
        .astype(jnp.bfloat16)
        .reshape(length, feature_dim)
    )
    query_w_grad = jnp.dot(normed.T, query_grad, preferred_element_type=jnp.float32)
    query_b_grad = jnp.sum(query_grad, axis=0, dtype=jnp.float32)
    key_w_grad = jnp.dot(normed.T, key_grad, preferred_element_type=jnp.float32)
    value_w_grad = jnp.dot(normed.T, value_grad, preferred_element_type=jnp.float32)
    value_b_grad = jnp.sum(value_grad, axis=0, dtype=jnp.float32)
    normed_grad = jnp.dot(query_grad, query_weight.T, preferred_element_type=jnp.float32)
    normed_grad = normed_grad + jnp.dot(key_grad, key_weight.T, preferred_element_type=jnp.float32)
    normed_grad = normed_grad + jnp.dot(
        value_grad, value_weight.T, preferred_element_type=jnp.float32
    )
    norm_one_back = jax.vjp(layer_norm, inputs, gain_one, bias_one)[1]
    input_ln_grad, gain_one_grad, bias_one_grad = norm_one_back(normed_grad)
    tokens_grad = residual_grad + input_ln_grad
    vector_sums, weight_sums, router_sum, shift_sum = scatter_all(
        [
            gain_one_grad,
            bias_one_grad,
            query_b_grad,
            value_b_grad,
            proj_b_grad,
            gain_two_grad,
            bias_two_grad,
        ],
        [query_w_grad, key_w_grad, value_w_grad, proj_w_grad],
        router_w_grad,
        shift_grad,
    )
    return (
        output.astype(jnp.bfloat16)[None],
        tokens_grad[None],
        vector_sums[0],
        vector_sums[1],
        weight_sums[0],
        vector_sums[2],
        weight_sums[1],
        weight_sums[2],
        vector_sums[3],
        weight_sums[3],
        vector_sums[4],
        vector_sums[5],
        vector_sums[6],
        router_sum,
        expert_sums[0],
        expert_sums[1],
        expert_sums[2],
        shift_sum,
    )


def solution(mesh):
    in_specs = (
        P(("rep", "exp"), None, None),
        P(("rep", "exp"), None),
        P(("rep", "exp"), None),
        P(("rep", "exp"), None, None),
        P(("rep", "exp"), None),
        P(("rep", "exp")),
        P(("rep", "exp")),
        P(("rep", "exp"), None),
        P(("rep", "exp")),
        P(("rep", "exp"), None),
        P(("rep", "exp"), None),
        P(("rep", "exp")),
        P(("rep", "exp"), None),
        P(("rep", "exp")),
        P(("rep", "exp")),
        P(("rep", "exp")),
        P(("rep", "exp"), None),
        P("exp", None, None),
        P("exp", None),
        P("exp", None, None),
        P(None, ("rep", "exp")),
        P(("rep", "exp"), None, None),
    )
    out_specs = (
        P(("rep", "exp"), None, None),
        P(("rep", "exp"), None, None),
        P(("rep", "exp")),
        P(("rep", "exp")),
        P(("rep", "exp"), None),
        P(("rep", "exp")),
        P(("rep", "exp"), None),
        P(("rep", "exp"), None),
        P(("rep", "exp")),
        P(("rep", "exp"), None),
        P(("rep", "exp")),
        P(("rep", "exp")),
        P(("rep", "exp")),
        P(("rep", "exp"), None),
        P("exp", None, "rep"),
        P("exp", "rep"),
        P("exp", "rep", None),
        P(None, ("rep", "exp")),
    )
    return jax.shard_map(body, mesh=mesh, in_specs=in_specs, out_specs=out_specs, check_vma=False)
```

```python
import functools
import jax
import jax.numpy as jnp
from jax import lax
from jax.experimental import pallas as pl
from jax.experimental.pallas import tpu as pltpu
from jax.sharding import PartitionSpec as P

HEADS = 12
EXPERTS = 32
MESH = pl.DeviceIdType.MESH
MIB = 1 << 20

def bit_dims(reps, groups):
    rb, gb = reps.bit_length() - 1, groups.bit_length() - 1
    return [(0, 1 << k) for k in reversed(range(rb))] + [(1, 1 << k) for k in reversed(range(gb))]

def orders(dims):
    last = len(dims) - 1
    rep = [i for i, d in enumerate(dims) if d[0] == 0]
    exp = [i for i, d in enumerate(dims) if d[0] == 1 and i != last]
    exp = exp[::-1]
    return [[last] + rep + exp, [last] + rep[::-1] + exp, [last] + exp + rep]

def my_bits(dims):
    at = (lax.axis_index("rep"), lax.axis_index("exp"))
    return [(at[a] // s) % 2 for a, s in dims], at

def partner(dims, at, i):
    a, s = dims[i]
    bit = (at[a] // s) % 2
    there = at[a] + (1 - 2 * bit) * s
    return (there, at[1]) if a == 0 else (at[0], there)

def greet(dims, at):
    barrier = pltpu.get_barrier_semaphore()
    for i in range(len(dims)):
        pl.semaphore_signal(barrier, inc=1, device_id=partner(dims, at, i), device_id_type=MESH)
    pl.semaphore_wait(barrier, len(dims))

def gather_kernel(dims, widths, count, *refs):
    ins, small_in = refs[:count], refs[count]
    outs, small_out = refs[count + 1:2 * count + 1], refs[2 * count + 1]
    own_sem, send_sem, recv_sem = refs[2 * count + 2:]
    bits, at = my_bits(dims)
    n = len(dims)
    own = [pltpu.make_async_copy(a, o.at[tuple(bits)], own_sem.at[i]) for i, (a, o) in enumerate(zip(ins + (small_in,), outs + (small_out,)))]
    for c in own: c.start()
    greet(dims, at)
    for c in own: c.wait()
    plan = [o[::-1] for o in orders(dims)]
    parts = len(plan)
    def copies(p, k):
        done = plan[p][:k]
        i = plan[p][k]
        lead = tuple(slice(None) if j in done else bits[j] for j in range(n))
        out = []
        for a, o in enumerate(outs):
            where = o.at[lead + (slice(None), pl.ds(widths[p][0], widths[p][1]))]
            out.append(pltpu.make_async_remote_copy(where, where, send_sem.at[p, k, a], recv_sem.at[p, k, a], device_id=partner(dims, at, i), device_id_type=MESH))
        if p == 0:
            where = small_out.at[lead]
            out.append(pltpu.make_async_remote_copy(where, where, send_sem.at[p, k, count], recv_sem.at[p, k, count], device_id=partner(dims, at, i), device_id_type=MESH))
        return out
    live = []
    for k in range(n):
        for p in range(parts):
            if k > 0:
                for c in live[(k - 1) * parts + p]: c.wait_recv()
            cs = copies(p, k)
            for c in cs: c.start()
            live.append(cs)
    for p in range(parts):
        for c in live[(n - 1) * parts + p]: c.wait_recv()
    for cs in live:
        for c in cs: c.wait_send()

def gather_params(weights, small, reps, groups, space=pl.ANY):
    dims = bit_dims(reps, groups)
    n = len(dims)
    rows, cols = weights[0].shape
    third = cols // 3 // 128 * 128
    widths = [(0, third), (third, third), (2 * third, cols - 2 * third)]
    count = len(weights)
    lead = (2,) * n
    outs = pl.pallas_call(
        functools.partial(gather_kernel, dims, widths, count),
        out_shape=[jax.ShapeDtypeStruct(lead + w.shape, w.dtype) for w in weights] + [jax.ShapeDtypeStruct(lead + small.shape, small.dtype)],
        in_specs=[pl.BlockSpec(memory_space=space)] * (count + 1),
        out_specs=[pl.BlockSpec(memory_space=space)] * (count + 1),
        scratch_shapes=[pltpu.SemaphoreType.DMA((count + 1,)), pltpu.SemaphoreType.DMA((3, n, count + 1)), pltpu.SemaphoreType.DMA((3, n, count + 1))],
        compiler_params=pltpu.CompilerParams(collective_id=0, has_side_effects=True, vmem_limit_bytes=40 * MIB),
    )(*weights, small)
    return [o.reshape((reps * groups * o.shape[-2], o.shape[-1])) for o in outs[:count]], outs[count].reshape((reps * groups,) + small.shape)

def scatter_kernel(dims, widths, count, *refs):
    ins, small_in = refs[:count], refs[count]
    outs, small_out = refs[count + 1:2 * count + 1], refs[2 * count + 1]
    n = len(dims)
    scr = refs[2 * count + 2:]
    parts = 3
    send_sem, recv_sem = scr[:2]
    scr = scr[2:]
    take = iter(scr)
    bufs = [[(next(take), next(take), next(take) if k < n - 1 else None) for p in range(parts)] for k in range(n)]
    smalls = [(next(take), next(take) if k < n - 1 else None) for k in range(n)]
    bits, at = my_bits(dims)
    plan = orders(dims)
    left = [list(range(n)) for _ in range(parts)]
    small_left = list(range(n))
    small_cur = small_in
    def split(have, i, b):
        return tuple(b if j == i else slice(None) for j in have)
    live = []
    def begin(k, p):
        i = plan[p][k]
        sb, rb, _ = bufs[k][p]
        far = split(left[p], i, 1 - bits[i])
        cols = pl.ds(widths[p][0], widths[p][1]) if k == 0 else slice(None)
        for a in range(count):
            src = ins[a][far + (slice(None), cols)] if k == 0 else bufs[k - 1][p][2][(a,) + far]
            sb[a] = src.astype(sb.dtype)
        c = [pltpu.make_async_remote_copy(sb, rb, send_sem.at[k, p], recv_sem.at[k, p], device_id=partner(dims, at, i), device_id_type=MESH)]
        if p == 0:
            src = (small_in if k == 0 else smalls[k - 1][1]).at[far]
            c.append(pltpu.make_async_remote_copy(src, smalls[k][0], send_sem.at[k, parts], recv_sem.at[k, parts], device_id=partner(dims, at, i), device_id_type=MESH))
        for x in c: x.start()
        return c
    def finish(k, p, c):
        i = plan[p][k]
        sb, rb, acc = bufs[k][p]
        near = split(left[p], i, bits[i])
        cols = pl.ds(widths[p][0], widths[p][1]) if k == 0 else slice(None)
        for x in c: x.wait_recv()
        for a in range(count):
            src = ins[a][near + (slice(None), cols)] if k == 0 else bufs[k - 1][p][2][(a,) + near]
            tot = src + rb[a].astype(jnp.float32)
            if k < n - 1:
                acc[a] = tot
            else:
                outs[a][:, widths[p][0]:widths[p][0] + widths[p][1]] = tot
        if p == 0:
            src = (small_in if k == 0 else smalls[k - 1][1])[near]
            tot = src + smalls[k][0][...]
            if k < n - 1:
                smalls[k][1][...] = tot
            else:
                small_out[...] = tot
        left[p].remove(i)
    greet(dims, at)
    live = [begin(0, p) for p in range(parts)]
    every = list(live)
    for k in range(n):
        for p in range(parts):
            finish(k, p, live[p])
            if k < n - 1:
                live[p] = begin(k + 1, p)
                every.append(live[p])
    for cs in every:
        for c in cs: c.wait_send()

def scatter_grads(grads, small, reps, groups, link=jnp.bfloat16):
    dims = bit_dims(reps, groups)
    n = len(dims)
    full, cols = grads[0].shape
    rows = full // (reps * groups)
    third = cols // 3 // 128 * 128
    widths = [(0, third), (third, third), (2 * third, cols - 2 * third)]
    count = len(grads)
    lead = (2,) * n
    grads = [g.reshape(lead + (rows, cols)) for g in grads]
    small = small.reshape(lead + small.shape[1:])
    scratch = [pltpu.SemaphoreType.DMA((n, 4)), pltpu.SemaphoreType.DMA((n, 4))]
    for k in range(n):
        for p in range(3):
            shape = (count,) + (2,) * (n - 1 - k) + (rows, widths[p][1])
            scratch += [pltpu.VMEM(shape, link), pltpu.VMEM(shape, link)]
            if k < n - 1:
                scratch.append(pltpu.VMEM(shape, jnp.float32))
    for k in range(n):
        shape = (2,) * (n - 1 - k) + small.shape[n:]
        scratch.append(pltpu.VMEM(shape, jnp.float32))
        if k < n - 1:
            scratch.append(pltpu.VMEM(shape, jnp.float32))
    vm = pl.BlockSpec(memory_space=pltpu.VMEM)
    outs = pl.pallas_call(
        functools.partial(scatter_kernel, dims, widths, count),
        out_shape=[jax.ShapeDtypeStruct((rows, cols), jnp.float32)] * count + [jax.ShapeDtypeStruct(small.shape[n:], jnp.float32)],
        in_specs=[vm] * (count + 1),
        out_specs=[vm] * (count + 1),
        scratch_shapes=scratch,
        compiler_params=pltpu.CompilerParams(collective_id=1, has_side_effects=True, vmem_limit_bytes=56 * MIB),
    )(*grads, small)
    return outs[:count], outs[count]


def pack_small(parts, lead):
    flat = jnp.concatenate([p.reshape(lead + (-1,)) for p in parts], axis=-1)
    size = flat.shape[-1]
    room = -(-size // 2048) * 2048
    flat = jnp.pad(flat, [(0, 0)] * len(lead) + [(0, room - size)])
    return flat.reshape(lead + (room // 128, 128))


def gather_all(vectors, weights, router, shift):
    axes = ("rep", "exp")
    reps, groups = lax.axis_size("rep"), lax.axis_size("exp")
    devices = reps * groups
    per = weights[0].shape[0]
    if per % 8 or devices & (devices - 1):
        return (
            [lax.all_gather(v, axes, axis=0, tiled=True) for v in vectors],
            [lax.all_gather(w, axes, axis=0, tiled=True) for w in weights],
            lax.all_gather(router, axes, axis=0, tiled=True),
            lax.all_gather(shift, axes, axis=1, tiled=True),
        )
    small = pack_small(vectors + [router, shift], ())
    weights, small = gather_params(weights, small, reps, groups)
    small = small.reshape(devices, -1)
    count = len(vectors)
    got = [small[:, i * per : (i + 1) * per].reshape(-1) for i in range(count)]
    at = count * per
    wide = router.shape[1]
    routers = small[:, at : at + per * wide].reshape(-1, wide)
    at += per * wide
    rows = shift.shape[0]
    shifts = small[:, at : at + rows * per].reshape(devices, rows, per)
    shifts = jnp.transpose(shifts, (1, 0, 2)).reshape(rows, -1)
    return got, weights, routers, shifts


def scatter_all(vectors, weights, router, shift):
    axes = ("rep", "exp")
    reps, groups = lax.axis_size("rep"), lax.axis_size("exp")
    devices = reps * groups
    per = weights[0].shape[0] // devices
    if per % 8 or devices & (devices - 1):
        return (
            [lax.psum_scatter(v, axes, scatter_dimension=0, tiled=True) for v in vectors],
            [lax.psum_scatter(w, axes, scatter_dimension=0, tiled=True) for w in weights],
            lax.psum_scatter(router, axes, scatter_dimension=0, tiled=True),
            lax.psum_scatter(shift, axes, scatter_dimension=1, tiled=True),
        )
    rows = shift.shape[0]
    parted = jnp.transpose(shift.reshape(rows, devices, per), (1, 0, 2))
    small = pack_small(vectors + [router, parted], (devices,))
    weights, small = scatter_grads(weights, small, reps, groups)
    small = small.reshape(-1)
    count = len(vectors)
    got = [small[i * per : (i + 1) * per] for i in range(count)]
    at = count * per
    wide = router.shape[1]
    routers = small[at : at + per * wide].reshape(per, wide)
    at += per * wide
    return got, weights, routers, small[at : at + rows * per].reshape(rows, per)

def normal_parts(v):
    e = jnp.exp(v * v * -0.5)
    t = 1.0 / (1.0 + (0.3275911 * 0.7071067811865476) * jnp.abs(v))
    poly = t * (0.127414796 + t * (-0.142248368 + t * (0.7107068705 + t * (-0.7265760135 + t * 0.5307027145))))
    q = poly * e
    return jnp.where(v < 0, q, 1.0 - q), e * 0.3989422804014327

def dot(a, b, ca, cb):
    return lax.dot_general(a, b, (((ca,), (cb,)), ((), ())), preferred_element_type=jnp.float32)

def experts_kernel(reps, groups, compute, x_ref, g_ref, win_ref, bias_ref, wout_ref,
                   res_ref, ig_ref, gin_ref, gb_ref, gout_ref,
                   x_all, g_all, res_send, ig_send, wi, wo, wis, wos, act_all, pg_all, gin_buf, gout_buf, res_acc, ig_acc,
                   own_sem, dsem, drec, rsem, rrec, bsem, brec, bown, wsem, ssem, osem):
    me, rep = lax.axis_index("exp"), lax.axis_index("rep")
    blocks = x_ref.shape[1]
    cap, wide = x_ref.shape[2:]
    rows = groups * cap
    chunks, part = wi.shape[0], wi.shape[2]
    half = groups // 2
    peers = [lax.rem(me + s, groups) for s in range(1, groups)]
    side = (rep + 1 - 2 * (rep % 2), rep + 2 - 4 * ((rep // 2) % 2))
    both = ((x_ref, x_all), (g_ref, g_all))
    back = ((res_send, res_ref), (ig_send, ig_ref))

    def load(j, f):
        return (pltpu.make_async_copy(win_ref.at[j, :, pl.ds(f * part, part)], wi.at[f], wsem.at[0, f]),
                pltpu.make_async_copy(wout_ref.at[j, pl.ds(f * part, part)], wo.at[f], wsem.at[1, f]))
    def load_slice(j):
        at = pl.ds(pl.multiple_of(rep * part, part), part)
        return (pltpu.make_async_copy(win_ref.at[j, :, at], wis, ssem.at[0]),
                pltpu.make_async_copy(wout_ref.at[j, at], wos, ssem.at[1]))
    def out_copies(j):
        return (pltpu.make_async_copy(gin_buf, gin_ref.at[j], osem.at[0]),
                pltpu.make_async_copy(gout_buf, gout_ref.at[j], osem.at[1]))
    def dispatch(j, t, s):
        src, dst = both[t]
        return pltpu.make_async_remote_copy(src.at[peers[s], j], dst.at[j, 0, me], dsem.at[t, j, s], drec.at[t, j, s],
                                            device_id=(rep, peers[s]), device_id_type=MESH)
    def own(j, t):
        src, dst = both[t]
        return pltpu.make_async_copy(src.at[me, j], dst.at[j, 0, me], own_sem.at[t, j])
    def across(j, t, n):
        dst = both[t][1]
        return pltpu.make_async_remote_copy(dst.at[j, 0], dst.at[j, 1 + n], rsem.at[t, j, n], rrec.at[t, j, n],
                                            device_id=(side[n], me), device_id_type=MESH)
    def onward(j, t, n):
        dst = both[t][1]
        at = pl.ds(n * half, half)
        return pltpu.make_async_remote_copy(dst.at[j, 1 + n, at], dst.at[j, 3, at], rsem.at[t, j, 2 + n], rrec.at[t, j, 2 + n],
                                            device_id=(side[1 - n], me), device_id_type=MESH)
    def give(j, t, s):
        src, dst = back[t]
        return pltpu.make_async_remote_copy(src.at[j, peers[s]], dst.at[me, j], bsem.at[t, j, s], brec.at[t, j, s],
                                            device_id=(rep, peers[s]), device_id_type=MESH)
    def give_own(j, t):
        src, dst = back[t]
        return pltpu.make_async_copy(src.at[j, me], dst.at[me, j], bown.at[t, j])
    def flat(v):
        return v.astype(jnp.float32).reshape(-1, wide).astype(jnp.bfloat16)

    barrier = pltpu.get_barrier_semaphore()
    for p in peers:
        pl.semaphore_signal(barrier, inc=1, device_id=(rep, p), device_id_type=MESH)
    for n in side:
        pl.semaphore_signal(barrier, inc=1, device_id=(n, me), device_id_type=MESH)
    pl.semaphore_wait(barrier, groups - 1 + 2)

    def send_all(j, _):
        for t in range(2):
            for s in range(groups - 1):
                dispatch(j, t, s).start()
            own(j, t).start()
        return 0
    lax.fori_loop(0, blocks, send_all, 0)
    if compute:
        for f in range(chunks):
            for c in load(0, f): c.start()
        for c in load_slice(0): c.start()

    def own_rows(j):
        x, g = flat(x_all[j, 0]), flat(g_all[j, 0])
        def chunk(f, _):
            for c in load(j, f): c.wait()
            pre = dot(x, wi[f], 1, 0) + bias_ref[j, f]
            cdf, pdf = normal_parts(pre)
            act = (pre * cdf).astype(jnp.bfloat16)
            ag = dot(g, wo[f], 1, 1)
            pg = (ag * (cdf + pre * pdf)).astype(jnp.bfloat16)
            more, less = dot(act, wo[f], 1, 0), dot(pg, wi[f], 1, 1)
            @pl.when(f == 0)
            def _():
                res_acc[...] = more
                ig_acc[...] = less
            @pl.when(f > 0)
            def _():
                res_acc[...] += more
                ig_acc[...] += less
            @pl.when(j + 1 < blocks)
            def _():
                for c in load(j + 1, f): c.start()
            return 0
        lax.fori_loop(0, chunks, chunk, 0)
        res_send[j] = res_acc[...].reshape(groups, cap, wide).astype(jnp.bfloat16)
        ig_send[j] = ig_acc[...].reshape(groups, cap, wide).astype(jnp.bfloat16)

    def weights(j):
        for c in load_slice(j): c.wait()
        def one(r, _):
            x, g = flat(x_all[j, r]), flat(g_all[j, r])
            pre = dot(x, wis[...], 1, 0) + bias_ref[j, rep]
            cdf, pdf = normal_parts(pre)
            act_all[r] = (pre * cdf).astype(jnp.bfloat16)
            pg_all[r] = (dot(g, wos[...], 1, 1) * (cdf + pre * pdf)).astype(jnp.bfloat16)
            return 0
        lax.fori_loop(0, reps, one, 0)
        @pl.when(j + 1 < blocks)
        def _():
            for c in load_slice(j + 1): c.start()
        @pl.when(j > 0)
        def _():
            for c in out_copies(j - 1): c.wait()
        act, pg = act_all[...].reshape(reps * rows, part), pg_all[...].reshape(reps * rows, part)
        gout_buf[...] = dot(act, flat(g_all[j]), 0, 0)
        gin_buf[...] = dot(flat(x_all[j]), pg, 0, 0)
        gb_ref[j] = jnp.sum(pg.astype(jnp.float32), axis=0, keepdims=True)
        for c in out_copies(j): c.start()

    def step(k, _):
        @pl.when(k < blocks)
        def _():
            for t in range(2):
                for s in range(groups - 1):
                    dispatch(k, t, s).wait_recv()
                own(k, t).wait()
                for n in range(2):
                    across(k, t, n).start()
            if compute:
                own_rows(k)
            else:
                res_send[k] = x_all[k, 0]
                ig_send[k] = g_all[k, 0]
            for t in range(2):
                for s in range(groups - 1):
                    give(k, t, s).start()
                give_own(k, t).start()
        @pl.when((k > 0) & (k <= blocks))
        def _():
            for t in range(2):
                for n in range(2):
                    across(k - 1, t, n).wait_recv()
                for n in range(2):
                    onward(k - 1, t, n).start()
        @pl.when(k > 1)
        def _():
            for t in range(2):
                for n in range(2):
                    onward(k - 2, t, n).wait_recv()
            if compute:
                weights(k - 2)
        return 0
    lax.fori_loop(0, blocks + 2, step, 0)

    if compute:
        for c in out_copies(blocks - 1): c.wait()
    def drain(j, _):
        for t in range(2):
            for s in range(groups - 1):
                give(j, t, s).wait_recv()
                give(j, t, s).wait_send()
                dispatch(j, t, s).wait_send()
            give_own(j, t).wait()
            for n in range(2):
                across(j, t, n).wait_send()
                onward(j, t, n).wait_send()
        return 0
    lax.fori_loop(0, blocks, drain, 0)


def experts_call(x, g, w_in, b_in, w_out, reps, groups, compute=True):
    _, blocks, cap, wide = x.shape
    hidden = w_in.shape[2]
    part = hidden // reps
    bias = b_in.astype(jnp.float32).reshape(blocks, reps, 1, part)
    anyw = pl.BlockSpec(memory_space=pl.ANY)
    vm = pl.BlockSpec(memory_space=pltpu.VMEM)
    bf, f32 = jnp.bfloat16, jnp.float32
    sem = pltpu.SemaphoreType.DMA
    n = groups - 1
    rows = groups * cap
    return pl.pallas_call(
        functools.partial(experts_kernel, reps, groups, compute),
        out_shape=[jax.ShapeDtypeStruct(x.shape, bf), jax.ShapeDtypeStruct(x.shape, bf),
                   jax.ShapeDtypeStruct((blocks, wide, part), f32), jax.ShapeDtypeStruct((blocks, 1, part), f32),
                   jax.ShapeDtypeStruct((blocks, part, wide), f32)],
        in_specs=[anyw, anyw, anyw, vm, anyw],
        out_specs=[anyw, anyw, anyw, vm, anyw],
        scratch_shapes=[
            pltpu.VMEM((blocks, reps, groups, cap, wide), bf), pltpu.VMEM((blocks, reps, groups, cap, wide), bf),
            pltpu.VMEM((blocks, groups, cap, wide), bf), pltpu.VMEM((blocks, groups, cap, wide), bf),
            pltpu.VMEM((reps, wide, part), bf), pltpu.VMEM((reps, part, wide), bf),
            pltpu.VMEM((wide, part), bf), pltpu.VMEM((part, wide), bf),
            pltpu.VMEM((reps, rows, part), bf), pltpu.VMEM((reps, rows, part), bf),
            pltpu.VMEM((wide, part), f32), pltpu.VMEM((part, wide), f32),
            pltpu.VMEM((rows, wide), f32), pltpu.VMEM((rows, wide), f32),
            sem((2, blocks)), sem((2, blocks, n)), sem((2, blocks, n)), sem((2, blocks, 4)), sem((2, blocks, 4)),
            sem((2, blocks, n)), sem((2, blocks, n)), sem((2, blocks)), sem((2, reps)), sem((2,)), sem((2,))],
        compiler_params=pltpu.CompilerParams(collective_id=2, has_side_effects=True, vmem_limit_bytes=60 * MIB),
    )(x, g, w_in, bias, w_out)

def experts_plain(x, g, w_in, b_in, w_out):
    bf, f32 = jnp.bfloat16, jnp.float32
    rx = lax.all_to_all(x, "exp", split_axis=0, concat_axis=0, tiled=True)
    rg = lax.all_to_all(g, "exp", split_axis=0, concat_axis=0, tiled=True)
    pre = jnp.einsum("secd,edf->secf", rx, w_in, preferred_element_type=f32)
    pre = pre + b_in.astype(f32)[None, :, None, :]
    cdf, pdf = normal_parts(pre)
    act = (pre * cdf).astype(bf)
    res = jnp.einsum("secf,efd->secd", act, w_out, preferred_element_type=f32).astype(bf)
    pg = jnp.einsum("secd,efd->secf", rg, w_out, preferred_element_type=f32) * (cdf + pre * pdf)
    pg = pg.astype(bf)
    ig = jnp.einsum("secf,edf->secd", pg, w_in, preferred_element_type=f32).astype(bf)
    gout = jnp.einsum("secf,secd->efd", act, rg, preferred_element_type=f32).astype(bf)
    gin = jnp.einsum("secd,secf->edf", rx, pg, preferred_element_type=f32).astype(bf)
    gb = jnp.sum(pg, axis=(0, 2), dtype=f32).astype(bf)
    return (
        lax.all_to_all(res, "exp", split_axis=0, concat_axis=0, tiled=True),
        lax.all_to_all(ig, "exp", split_axis=0, concat_axis=0, tiled=True),
        lax.psum_scatter(gin, "rep", scatter_dimension=2, tiled=True).astype(f32),
        lax.psum_scatter(gb, "rep", scatter_dimension=1, tiled=True).astype(f32)[:, None],
        lax.psum_scatter(gout, "rep", scatter_dimension=1, tiled=True).astype(f32),
    )


epsilon = 1e-06
masked_score = -1e30


def normalize(values):
    center = values - jnp.mean(values, axis=-1, keepdims=True)
    spread = jnp.mean(center * center, axis=-1, keepdims=True)
    scale = lax.rsqrt(spread + epsilon)
    return center * scale, scale


def normalize_back(grad, unit, scale):
    mean = jnp.mean(grad, axis=-1, keepdims=True)
    along = jnp.mean(grad * unit, axis=-1, keepdims=True)
    return (grad - mean - unit * along) * scale


def two_parts(v):
    high = v.astype(jnp.bfloat16)
    return high, (v - high.astype(jnp.float32)).astype(jnp.bfloat16)


def positions_of(routes, valid_col, priority_col, priority_row, experts):
    length = routes.shape[0]
    f32, bf = jnp.float32, jnp.bfloat16
    token_row = lax.broadcasted_iota(jnp.int32, (length, length), 1)
    token_col = lax.broadcasted_iota(jnp.int32, (length, length), 0)
    rank_col = jnp.sum(
        jnp.where(priority_row == token_col, token_row, 0).astype(f32), axis=1, keepdims=True
    )
    rank_row = jnp.sum(
        jnp.where(priority_col == token_row, token_col, 0).astype(f32), axis=0, keepdims=True
    )
    earlier = (rank_row < rank_col).astype(f32).astype(bf)
    expert_row = lax.broadcasted_iota(jnp.int32, (length, experts), 1)
    ones = [(routes[:, k : k + 1] == expert_row).astype(f32) for k in range(routes.shape[1])]
    before = jnp.zeros((1, experts), f32)
    places = []
    for one in ones:
        live = one * valid_col
        count = dot(earlier, live.astype(bf), 1, 0) + before
        places.append(jnp.sum(count * one, axis=1, keepdims=True))
        before = before + jnp.sum(live, axis=0, keepdims=True)
    return ones, places


def body(
    tokens,
    segments,
    valid,
    routes,
    priority,
    ln1_gain,
    ln1_bias,
    w_query,
    query_bias,
    w_key,
    w_value,
    value_bias,
    w_attn_out,
    attn_out_bias,
    ln2_gain,
    ln2_bias,
    w_router,
    expert_in,
    expert_in_bias,
    expert_out,
    expert_out_bias,
    cotangent,
):
    f32, bf = jnp.float32, jnp.bfloat16
    vectors, weights, router_weight, result_shift = gather_all(
        [ln1_gain, ln1_bias, query_bias, value_bias, attn_out_bias, ln2_gain, ln2_bias],
        [w_query, w_key, w_value, w_attn_out],
        w_router,
        expert_out_bias,
    )
    vectors = [v.astype(f32)[None] for v in vectors]
    gain_one, bias_one, query_shift, value_shift, proj_shift, gain_two, bias_two = vectors
    query_weight, key_weight, value_weight, proj_weight = weights
    length = tokens.shape[1]
    feature_dim = tokens.shape[2]
    head_dim = feature_dim // HEADS
    local_blocks = expert_in.shape[0]
    reps, groups = lax.axis_size("rep"), lax.axis_size("exp")
    experts = EXPERTS
    split = local_blocks * groups // experts
    top_count = routes.shape[2]
    capacity = (105 * top_count * length + 100 * experts - 1) // (100 * experts)
    room = -(-capacity // 8) * 8
    score_scale = head_dim ** (-0.5)
    inputs = tokens[0].astype(f32)
    row_segments = segments[0]
    row_valid = valid[0]
    places = jnp.arange(length, dtype=jnp.int32)
    allowed = (row_segments[:, None] == row_segments[None, :]) & (
        (row_valid[None, :] > 0) | (places[:, None] == places[None, :])
    )
    unit_one, scale_one = normalize(inputs)
    normed = (unit_one * gain_one + bias_one).astype(bf)
    query_rows = (dot(normed, query_weight, 1, 0) + query_shift).astype(bf)
    key_rows = dot(normed, key_weight, 1, 0).astype(bf)
    value_rows = (dot(normed, value_weight, 1, 0) + value_shift).astype(bf)
    query_heads = query_rows.reshape(length, HEADS, head_dim)
    key_heads = key_rows.reshape(length, HEADS, head_dim)
    value_heads = value_rows.reshape(length, HEADS, head_dim)

    def scores():
        return jnp.where(
            allowed[None],
            jnp.einsum("qhd,khd->hqk", query_heads, key_heads, preferred_element_type=f32)
            * score_scale,
            masked_score,
        )

    masked = scores()
    top_score = jnp.max(masked, axis=-1, keepdims=True)
    log_total = top_score + jnp.log(jnp.sum(jnp.exp(masked - top_score), axis=-1, keepdims=True))
    mixed = jnp.einsum(
        "hqk,khd->qhd",
        jnp.exp(masked - log_total).astype(bf),
        value_heads,
        preferred_element_type=f32,
    )
    mixed = mixed.reshape(length, feature_dim).astype(bf)
    residual = inputs + dot(mixed, proj_weight, 1, 0) + proj_shift
    unit_two, scale_two = normalize(residual)
    normed_two = (unit_two * gain_two + bias_two).astype(bf)
    logits = dot(normed_two, router_weight, 1, 0)
    logit_exp = jnp.exp(logits - jnp.max(logits, axis=-1, keepdims=True))
    router_probs = logit_exp / jnp.sum(logit_exp, axis=-1, keepdims=True)
    upstream = cotangent[0].astype(f32)
    ones, positions = positions_of(
        routes[0], row_valid[:, None].astype(f32), priority[0][:, None], priority[0][None], experts
    )
    expert_row = lax.broadcasted_iota(jnp.int32, (1, experts), 1).astype(f32)
    slot_row = lax.broadcasted_iota(jnp.int32, (1, experts * room), 1)
    kept, gates, slots, sent = [], [], [], jnp.zeros((experts * room, feature_dim), f32)
    for one, position in zip(ones, positions):
        keep = row_valid[:, None].astype(f32) * (position < capacity).astype(f32)
        gate = jnp.sum(router_probs * one, axis=1, keepdims=True) * keep
        place = jnp.sum(one * expert_row, axis=1, keepdims=True) * room + position
        place = jnp.where(keep > 0, place, -1.0).astype(jnp.int32)
        hot = (place == slot_row).astype(f32).astype(bf)
        kept.append(one * keep)
        gates.append(gate)
        slots.append(hot)
        sent = sent + dot(hot, (gate * upstream).astype(bf), 0, 0)
    any_slot = slots[0]
    for hot in slots[1:]:
        any_slot = any_slot + hot
    expert_slots = dot(any_slot, normed_two, 0, 0).astype(bf)
    gated = sum(one * gate for one, gate in zip(kept, gates))
    high, low = two_parts(gated)
    shift_grad = dot(high, cotangent[0], 0, 0) + dot(low, cotangent[0], 0, 0)

    def outgoing(v):
        v = v.astype(bf).reshape(experts, room, feature_dim)
        return jnp.repeat(v, split, axis=0).reshape(groups, local_blocks, room, feature_dim)

    small = reps == 4 and groups * room <= 512 and expert_in.shape[2] % (128 * reps) == 0
    if small:
        moved = experts_call(
            outgoing(expert_slots), outgoing(sent), expert_in, expert_in_bias, expert_out, reps, groups
        )
    else:
        moved = experts_plain(
            outgoing(expert_slots), outgoing(sent), expert_in, expert_in_bias, expert_out
        )
    result, slot_back, in_w_grad, in_b_grad, out_w_grad = moved
    result = result.reshape(experts, split, room, feature_dim)
    slot_back = slot_back.reshape(experts, split, room, feature_dim)
    results = [result[:, s].reshape(experts * room, feature_dim) for s in range(split)]
    backs = [slot_back[:, s].reshape(experts * room, feature_dim) for s in range(split)]
    combined, prob_grad = 0.0, 0.0
    for one, gate, hot in zip(kept, gates, slots):
        picked = dot(one.astype(bf), result_shift, 1, 0)
        for part in results:
            picked = picked + dot(hot, part, 1, 0)
        combined = combined + gate * picked
        prob_grad = prob_grad + one * jnp.sum(upstream * picked, axis=1, keepdims=True)
    output = residual + combined
    logit_grad = (
        router_probs * (prob_grad - jnp.sum(router_probs * prob_grad, axis=-1, keepdims=True))
    ).astype(bf)
    router_w_grad = dot(normed_two, logit_grad, 0, 0)
    normed_two_grad = dot(logit_grad, router_weight, 1, 1)
    for part in backs:
        normed_two_grad = normed_two_grad + dot(any_slot, part, 1, 0)
    gain_two_grad = jnp.sum(normed_two_grad * unit_two, axis=0)
    bias_two_grad = jnp.sum(normed_two_grad, axis=0)
    residual_grad = upstream + normalize_back(normed_two_grad * gain_two, unit_two, scale_two)
    branch_grad = residual_grad.astype(bf)
    proj_w_grad = dot(mixed, branch_grad, 0, 0)
    proj_b_grad = jnp.sum(branch_grad, axis=0, dtype=f32)
    mixed_grad = dot(branch_grad, proj_weight, 1, 1).astype(bf)
    mixed_grad = mixed_grad.reshape(length, HEADS, head_dim)
    again_probs = jnp.exp(scores() - log_total)
    prob_grads = jnp.einsum("qhd,khd->hqk", mixed_grad, value_heads, preferred_element_type=f32)
    value_grad = jnp.einsum(
        "hqk,qhd->khd", again_probs.astype(bf), mixed_grad, preferred_element_type=f32
    )
    value_grad = value_grad.astype(bf).reshape(length, feature_dim)
    inner_sum = jnp.sum(again_probs * prob_grads, axis=-1, keepdims=True)
    score_grad = (again_probs * (prob_grads - inner_sum)).astype(bf)
    query_grad = jnp.einsum("hqk,khd->qhd", score_grad, key_heads, preferred_element_type=f32)
    query_grad = (query_grad * score_scale).astype(bf).reshape(length, feature_dim)
    key_grad = jnp.einsum("hqk,qhd->khd", score_grad, query_heads, preferred_element_type=f32)
    key_grad = (key_grad * score_scale).astype(bf).reshape(length, feature_dim)
    query_w_grad = dot(normed, query_grad, 0, 0)
    query_b_grad = jnp.sum(query_grad, axis=0, dtype=f32)
    key_w_grad = dot(normed, key_grad, 0, 0)
    value_w_grad = dot(normed, value_grad, 0, 0)
    value_b_grad = jnp.sum(value_grad, axis=0, dtype=f32)
    normed_grad = dot(query_grad, query_weight, 1, 1)
    normed_grad = normed_grad + dot(key_grad, key_weight, 1, 1)
    normed_grad = normed_grad + dot(value_grad, value_weight, 1, 1)
    gain_one_grad = jnp.sum(normed_grad * unit_one, axis=0)
    bias_one_grad = jnp.sum(normed_grad, axis=0)
    tokens_grad = residual_grad + normalize_back(normed_grad * gain_one, unit_one, scale_one)
    vector_sums, weight_sums, router_sum, shift_sum = scatter_all(
        [
            gain_one_grad,
            bias_one_grad,
            query_b_grad,
            value_b_grad,
            proj_b_grad,
            gain_two_grad,
            bias_two_grad,
        ],
        [query_w_grad, key_w_grad, value_w_grad, proj_w_grad],
        router_w_grad,
        shift_grad,
    )
    return (
        output.astype(jnp.bfloat16)[None],
        tokens_grad[None],
        vector_sums[0],
        vector_sums[1],
        weight_sums[0],
        vector_sums[2],
        weight_sums[1],
        weight_sums[2],
        vector_sums[3],
        weight_sums[3],
        vector_sums[4],
        vector_sums[5],
        vector_sums[6],
        router_sum,
        in_w_grad,
        in_b_grad[:, 0],
        out_w_grad,
        shift_sum,
    )


def solution(mesh):
    in_specs = (
        P(("rep", "exp"), None, None),
        P(("rep", "exp"), None),
        P(("rep", "exp"), None),
        P(("rep", "exp"), None, None),
        P(("rep", "exp"), None),
        P(("rep", "exp")),
        P(("rep", "exp")),
        P(("rep", "exp"), None),
        P(("rep", "exp")),
        P(("rep", "exp"), None),
        P(("rep", "exp"), None),
        P(("rep", "exp")),
        P(("rep", "exp"), None),
        P(("rep", "exp")),
        P(("rep", "exp")),
        P(("rep", "exp")),
        P(("rep", "exp"), None),
        P("exp", None, None),
        P("exp", None),
        P("exp", None, None),
        P(None, ("rep", "exp")),
        P(("rep", "exp"), None, None),
    )
    out_specs = (
        P(("rep", "exp"), None, None),
        P(("rep", "exp"), None, None),
        P(("rep", "exp")),
        P(("rep", "exp")),
        P(("rep", "exp"), None),
        P(("rep", "exp")),
        P(("rep", "exp"), None),
        P(("rep", "exp"), None),
        P(("rep", "exp")),
        P(("rep", "exp"), None),
        P(("rep", "exp")),
        P(("rep", "exp")),
        P(("rep", "exp")),
        P(("rep", "exp"), None),
        P("exp", None, "rep"),
        P("exp", "rep"),
        P("exp", "rep", None),
        P(None, ("rep", "exp")),
    )
    return jax.shard_map(body, mesh=mesh, in_specs=in_specs, out_specs=out_specs, check_vma=False)
```

```python
import functools
import jax
import jax.numpy as jnp
from jax import lax
from jax.experimental import pallas as pl
from jax.experimental.pallas import tpu as pltpu
from jax.sharding import PartitionSpec as P

HEADS = 12
EXPERTS = 32
MESH = pl.DeviceIdType.MESH
MIB = 1 << 20

def bit_dims(reps, groups):
    rb, gb = reps.bit_length() - 1, groups.bit_length() - 1
    return [(0, 1 << k) for k in reversed(range(rb))] + [(1, 1 << k) for k in reversed(range(gb))]

def orders(dims):
    last = len(dims) - 1
    rep = [i for i, d in enumerate(dims) if d[0] == 0]
    exp = [i for i, d in enumerate(dims) if d[0] == 1 and i != last]
    exp = exp[::-1]
    return [[last] + rep + exp, [last] + rep[::-1] + exp, [last] + exp + rep]

def my_bits(dims):
    at = (lax.axis_index("rep"), lax.axis_index("exp"))
    return [(at[a] // s) % 2 for a, s in dims], at

def partner(dims, at, i):
    a, s = dims[i]
    bit = (at[a] // s) % 2
    there = at[a] + (1 - 2 * bit) * s
    return (there, at[1]) if a == 0 else (at[0], there)

def greet(dims, at):
    barrier = pltpu.get_barrier_semaphore()
    for i in range(len(dims)):
        pl.semaphore_signal(barrier, inc=1, device_id=partner(dims, at, i), device_id_type=MESH)
    pl.semaphore_wait(barrier, len(dims))

def gather_kernel(dims, widths, count, *refs):
    ins, small_in = refs[:count], refs[count]
    outs, small_out = refs[count + 1:2 * count + 1], refs[2 * count + 1]
    own_sem, send_sem, recv_sem = refs[2 * count + 2:]
    bits, at = my_bits(dims)
    n = len(dims)
    own = [pltpu.make_async_copy(a, o.at[tuple(bits)], own_sem.at[i]) for i, (a, o) in enumerate(zip(ins + (small_in,), outs + (small_out,)))]
    for c in own: c.start()
    greet(dims, at)
    for c in own: c.wait()
    plan = [o[::-1] for o in orders(dims)]
    parts = len(plan)
    def copies(p, k):
        done = plan[p][:k]
        i = plan[p][k]
        lead = tuple(slice(None) if j in done else bits[j] for j in range(n))
        out = []
        for a, o in enumerate(outs):
            where = o.at[lead + (slice(None), pl.ds(widths[p][0], widths[p][1]))]
            out.append(pltpu.make_async_remote_copy(where, where, send_sem.at[p, k, a], recv_sem.at[p, k, a], device_id=partner(dims, at, i), device_id_type=MESH))
        if p == 0:
            where = small_out.at[lead]
            out.append(pltpu.make_async_remote_copy(where, where, send_sem.at[p, k, count], recv_sem.at[p, k, count], device_id=partner(dims, at, i), device_id_type=MESH))
        return out
    live = []
    for k in range(n):
        for p in range(parts):
            if k > 0:
                for c in live[(k - 1) * parts + p]: c.wait_recv()
            cs = copies(p, k)
            for c in cs: c.start()
            live.append(cs)
    for p in range(parts):
        for c in live[(n - 1) * parts + p]: c.wait_recv()
    for cs in live:
        for c in cs: c.wait_send()

def gather_params(weights, small, reps, groups, space=pl.ANY):
    dims = bit_dims(reps, groups)
    n = len(dims)
    rows, cols = weights[0].shape
    third = cols // 3 // 128 * 128
    widths = [(0, third), (third, third), (2 * third, cols - 2 * third)]
    count = len(weights)
    lead = (2,) * n
    outs = pl.pallas_call(
        functools.partial(gather_kernel, dims, widths, count),
        out_shape=[jax.ShapeDtypeStruct(lead + w.shape, w.dtype) for w in weights] + [jax.ShapeDtypeStruct(lead + small.shape, small.dtype)],
        in_specs=[pl.BlockSpec(memory_space=space)] * (count + 1),
        out_specs=[pl.BlockSpec(memory_space=space)] * (count + 1),
        scratch_shapes=[pltpu.SemaphoreType.DMA((count + 1,)), pltpu.SemaphoreType.DMA((3, n, count + 1)), pltpu.SemaphoreType.DMA((3, n, count + 1))],
        compiler_params=pltpu.CompilerParams(collective_id=0, has_side_effects=True, vmem_limit_bytes=40 * MIB),
    )(*weights, small)
    return [o.reshape((reps * groups * o.shape[-2], o.shape[-1])) for o in outs[:count]], outs[count].reshape((reps * groups,) + small.shape)

def scatter_kernel(dims, widths, count, *refs):
    ins, small_in = refs[:count], refs[count]
    outs, small_out = refs[count + 1:2 * count + 1], refs[2 * count + 1]
    n = len(dims)
    scr = refs[2 * count + 2:]
    parts = 3
    send_sem, recv_sem = scr[:2]
    scr = scr[2:]
    take = iter(scr)
    bufs = [[(next(take), next(take), next(take) if k < n - 1 else None) for p in range(parts)] for k in range(n)]
    smalls = [(next(take), next(take) if k < n - 1 else None) for k in range(n)]
    bits, at = my_bits(dims)
    plan = orders(dims)
    left = [list(range(n)) for _ in range(parts)]
    small_left = list(range(n))
    small_cur = small_in
    def split(have, i, b):
        return tuple(b if j == i else slice(None) for j in have)
    live = []
    def begin(k, p):
        i = plan[p][k]
        sb, rb, _ = bufs[k][p]
        far = split(left[p], i, 1 - bits[i])
        cols = pl.ds(widths[p][0], widths[p][1]) if k == 0 else slice(None)
        for a in range(count):
            src = ins[a][far + (slice(None), cols)] if k == 0 else bufs[k - 1][p][2][(a,) + far]
            sb[a] = src.astype(sb.dtype)
        c = [pltpu.make_async_remote_copy(sb, rb, send_sem.at[k, p], recv_sem.at[k, p], device_id=partner(dims, at, i), device_id_type=MESH)]
        if p == 0:
            src = (small_in if k == 0 else smalls[k - 1][1]).at[far]
            c.append(pltpu.make_async_remote_copy(src, smalls[k][0], send_sem.at[k, parts], recv_sem.at[k, parts], device_id=partner(dims, at, i), device_id_type=MESH))
        for x in c: x.start()
        return c
    def finish(k, p, c):
        i = plan[p][k]
        sb, rb, acc = bufs[k][p]
        near = split(left[p], i, bits[i])
        cols = pl.ds(widths[p][0], widths[p][1]) if k == 0 else slice(None)
        for x in c: x.wait_recv()
        for a in range(count):
            src = ins[a][near + (slice(None), cols)] if k == 0 else bufs[k - 1][p][2][(a,) + near]
            tot = src + rb[a].astype(jnp.float32)
            if k < n - 1:
                acc[a] = tot
            else:
                outs[a][:, widths[p][0]:widths[p][0] + widths[p][1]] = tot
        if p == 0:
            src = (small_in if k == 0 else smalls[k - 1][1])[near]
            tot = src + smalls[k][0][...]
            if k < n - 1:
                smalls[k][1][...] = tot
            else:
                small_out[...] = tot
        left[p].remove(i)
    greet(dims, at)
    live = [begin(0, p) for p in range(parts)]
    every = list(live)
    for k in range(n):
        for p in range(parts):
            finish(k, p, live[p])
            if k < n - 1:
                live[p] = begin(k + 1, p)
                every.append(live[p])
    for cs in every:
        for c in cs: c.wait_send()

def scatter_grads(grads, small, reps, groups, link=jnp.bfloat16):
    dims = bit_dims(reps, groups)
    n = len(dims)
    full, cols = grads[0].shape
    rows = full // (reps * groups)
    third = cols // 3 // 128 * 128
    widths = [(0, third), (third, third), (2 * third, cols - 2 * third)]
    count = len(grads)
    lead = (2,) * n
    grads = [g.reshape(lead + (rows, cols)) for g in grads]
    small = small.reshape(lead + small.shape[1:])
    scratch = [pltpu.SemaphoreType.DMA((n, 4)), pltpu.SemaphoreType.DMA((n, 4))]
    for k in range(n):
        for p in range(3):
            shape = (count,) + (2,) * (n - 1 - k) + (rows, widths[p][1])
            scratch += [pltpu.VMEM(shape, link), pltpu.VMEM(shape, link)]
            if k < n - 1:
                scratch.append(pltpu.VMEM(shape, jnp.float32))
    for k in range(n):
        shape = (2,) * (n - 1 - k) + small.shape[n:]
        scratch.append(pltpu.VMEM(shape, jnp.float32))
        if k < n - 1:
            scratch.append(pltpu.VMEM(shape, jnp.float32))
    vm = pl.BlockSpec(memory_space=pltpu.VMEM)
    outs = pl.pallas_call(
        functools.partial(scatter_kernel, dims, widths, count),
        out_shape=[jax.ShapeDtypeStruct((rows, cols), jnp.float32)] * count + [jax.ShapeDtypeStruct(small.shape[n:], jnp.float32)],
        in_specs=[vm] * (count + 1),
        out_specs=[vm] * (count + 1),
        scratch_shapes=scratch,
        compiler_params=pltpu.CompilerParams(collective_id=1, has_side_effects=True, vmem_limit_bytes=56 * MIB),
    )(*grads, small)
    return outs[:count], outs[count]


def gather_all(vectors, weights, router, shift):
    axes = ("rep", "exp")
    return (
        [lax.all_gather(v, axes, axis=0, tiled=True) for v in vectors],
        [lax.all_gather(w, axes, axis=0, tiled=True) for w in weights],
        lax.all_gather(router, axes, axis=0, tiled=True),
        lax.all_gather(shift, axes, axis=1, tiled=True),
    )


def scatter_all(vectors, weights, router, shift):
    axes = ("rep", "exp")
    return (
        [lax.psum_scatter(v, axes, scatter_dimension=0, tiled=True) for v in vectors],
        [lax.psum_scatter(w, axes, scatter_dimension=0, tiled=True) for w in weights],
        lax.psum_scatter(router, axes, scatter_dimension=0, tiled=True),
        lax.psum_scatter(shift, axes, scatter_dimension=1, tiled=True),
    )


def normal_parts(v):
    e = jnp.exp(v * v * -0.5)
    t = 1.0 / (1.0 + (0.3275911 * 0.7071067811865476) * jnp.abs(v))
    poly = t * (0.127414796 + t * (-0.142248368 + t * (0.7107068705 + t * (-0.7265760135 + t * 0.5307027145))))
    q = poly * e
    return jnp.where(v < 0, q, 1.0 - q), e * 0.3989422804014327

def dot(a, b, ca, cb):
    return lax.dot_general(a, b, (((ca,), (cb,)), ((), ())), preferred_element_type=jnp.float32)

def experts_kernel(reps, groups, compute, x_ref, g_ref, win_ref, bias_ref, wout_ref,
                   res_ref, ig_ref, gin_ref, gb_ref, gout_ref,
                   x_all, g_all, res_send, ig_send, wi, wo, wis, wos, act_all, pg_all, gin_buf, gout_buf, res_acc, ig_acc,
                   own_sem, dsem, drec, rsem, rrec, bsem, brec, bown, wsem, ssem, osem):
    me, rep = lax.axis_index("exp"), lax.axis_index("rep")
    blocks = x_ref.shape[1]
    cap, wide = x_ref.shape[2:]
    rows = groups * cap
    chunks, part = wi.shape[0], wi.shape[2]
    half = groups // 2
    peers = [lax.rem(me + s, groups) for s in range(1, groups)]
    side = (rep + 1 - 2 * (rep % 2), rep + 2 - 4 * ((rep // 2) % 2))
    both = ((x_ref, x_all), (g_ref, g_all))
    back = ((res_send, res_ref), (ig_send, ig_ref))

    def load(j, f):
        return (pltpu.make_async_copy(win_ref.at[j, :, pl.ds(f * part, part)], wi.at[f], wsem.at[0, f]),
                pltpu.make_async_copy(wout_ref.at[j, pl.ds(f * part, part)], wo.at[f], wsem.at[1, f]))
    def load_slice(j):
        at = pl.ds(pl.multiple_of(rep * part, part), part)
        return (pltpu.make_async_copy(win_ref.at[j, :, at], wis, ssem.at[0]),
                pltpu.make_async_copy(wout_ref.at[j, at], wos, ssem.at[1]))
    def out_copies(j):
        return (pltpu.make_async_copy(gin_buf, gin_ref.at[j], osem.at[0]),
                pltpu.make_async_copy(gout_buf, gout_ref.at[j], osem.at[1]))
    def dispatch(j, t, s):
        src, dst = both[t]
        return pltpu.make_async_remote_copy(src.at[peers[s], j], dst.at[j, 0, me], dsem.at[t, j, s], drec.at[t, j, s],
                                            device_id=(rep, peers[s]), device_id_type=MESH)
    def own(j, t):
        src, dst = both[t]
        return pltpu.make_async_copy(src.at[me, j], dst.at[j, 0, me], own_sem.at[t, j])
    def across(j, t, n):
        dst = both[t][1]
        return pltpu.make_async_remote_copy(dst.at[j, 0], dst.at[j, 1 + n], rsem.at[t, j, n], rrec.at[t, j, n],
                                            device_id=(side[n], me), device_id_type=MESH)
    def onward(j, t, n):
        dst = both[t][1]
        at = pl.ds(n * half, half)
        return pltpu.make_async_remote_copy(dst.at[j, 1 + n, at], dst.at[j, 3, at], rsem.at[t, j, 2 + n], rrec.at[t, j, 2 + n],
                                            device_id=(side[1 - n], me), device_id_type=MESH)
    def give(j, t, s):
        src, dst = back[t]
        return pltpu.make_async_remote_copy(src.at[j, peers[s]], dst.at[me, j], bsem.at[t, j, s], brec.at[t, j, s],
                                            device_id=(rep, peers[s]), device_id_type=MESH)
    def give_own(j, t):
        src, dst = back[t]
        return pltpu.make_async_copy(src.at[j, me], dst.at[me, j], bown.at[t, j])
    def flat(v):
        return v.astype(jnp.float32).reshape(-1, wide).astype(jnp.bfloat16)

    barrier = pltpu.get_barrier_semaphore()
    for p in peers:
        pl.semaphore_signal(barrier, inc=1, device_id=(rep, p), device_id_type=MESH)
    for n in side:
        pl.semaphore_signal(barrier, inc=1, device_id=(n, me), device_id_type=MESH)
    pl.semaphore_wait(barrier, groups - 1 + 2)

    def send_all(j, _):
        for t in range(2):
            for s in range(groups - 1):
                dispatch(j, t, s).start()
            own(j, t).start()
        return 0
    lax.fori_loop(0, blocks, send_all, 0)
    if compute:
        for f in range(chunks):
            for c in load(0, f): c.start()
        for c in load_slice(0): c.start()

    def own_rows(j):
        x, g = flat(x_all[j, 0]), flat(g_all[j, 0])
        def chunk(f, _):
            for c in load(j, f): c.wait()
            pre = dot(x, wi[f], 1, 0) + bias_ref[j, f]
            cdf, pdf = normal_parts(pre)
            act = (pre * cdf).astype(jnp.bfloat16)
            ag = dot(g, wo[f], 1, 1)
            pg = (ag * (cdf + pre * pdf)).astype(jnp.bfloat16)
            more, less = dot(act, wo[f], 1, 0), dot(pg, wi[f], 1, 1)
            @pl.when(f == 0)
            def _():
                res_acc[...] = more
                ig_acc[...] = less
            @pl.when(f > 0)
            def _():
                res_acc[...] += more
                ig_acc[...] += less
            @pl.when(j + 1 < blocks)
            def _():
                for c in load(j + 1, f): c.start()
            return 0
        lax.fori_loop(0, chunks, chunk, 0)
        res_send[j] = res_acc[...].reshape(groups, cap, wide).astype(jnp.bfloat16)
        ig_send[j] = ig_acc[...].reshape(groups, cap, wide).astype(jnp.bfloat16)

    def weights(j):
        for c in load_slice(j): c.wait()
        def one(r, _):
            x, g = flat(x_all[j, r]), flat(g_all[j, r])
            pre = dot(x, wis[...], 1, 0) + bias_ref[j, rep]
            cdf, pdf = normal_parts(pre)
            act_all[r] = (pre * cdf).astype(jnp.bfloat16)
            pg_all[r] = (dot(g, wos[...], 1, 1) * (cdf + pre * pdf)).astype(jnp.bfloat16)
            return 0
        lax.fori_loop(0, reps, one, 0)
        @pl.when(j + 1 < blocks)
        def _():
            for c in load_slice(j + 1): c.start()
        @pl.when(j > 0)
        def _():
            for c in out_copies(j - 1): c.wait()
        act, pg = act_all[...].reshape(reps * rows, part), pg_all[...].reshape(reps * rows, part)
        gout_buf[...] = dot(act, flat(g_all[j]), 0, 0)
        gin_buf[...] = dot(flat(x_all[j]), pg, 0, 0)
        gb_ref[j] = jnp.sum(pg.astype(jnp.float32), axis=0, keepdims=True)
        for c in out_copies(j): c.start()

    def step(k, _):
        @pl.when(k < blocks)
        def _():
            for t in range(2):
                for s in range(groups - 1):
                    dispatch(k, t, s).wait_recv()
                own(k, t).wait()
                for n in range(2):
                    across(k, t, n).start()
            if compute:
                own_rows(k)
            else:
                res_send[k] = x_all[k, 0]
                ig_send[k] = g_all[k, 0]
            for t in range(2):
                for s in range(groups - 1):
                    give(k, t, s).start()
                give_own(k, t).start()
        @pl.when((k > 0) & (k <= blocks))
        def _():
            for t in range(2):
                for n in range(2):
                    across(k - 1, t, n).wait_recv()
                for n in range(2):
                    onward(k - 1, t, n).start()
        @pl.when(k > 1)
        def _():
            for t in range(2):
                for n in range(2):
                    onward(k - 2, t, n).wait_recv()
            if compute:
                weights(k - 2)
        return 0
    lax.fori_loop(0, blocks + 2, step, 0)

    if compute:
        for c in out_copies(blocks - 1): c.wait()
    def drain(j, _):
        for t in range(2):
            for s in range(groups - 1):
                give(j, t, s).wait_recv()
                give(j, t, s).wait_send()
                dispatch(j, t, s).wait_send()
            give_own(j, t).wait()
            for n in range(2):
                across(j, t, n).wait_send()
                onward(j, t, n).wait_send()
        return 0
    lax.fori_loop(0, blocks, drain, 0)


def experts_call(x, g, w_in, b_in, w_out, reps, groups, compute=True):
    _, blocks, cap, wide = x.shape
    hidden = w_in.shape[2]
    part = hidden // reps
    bias = b_in.astype(jnp.float32).reshape(blocks, reps, 1, part)
    anyw = pl.BlockSpec(memory_space=pl.ANY)
    vm = pl.BlockSpec(memory_space=pltpu.VMEM)
    bf, f32 = jnp.bfloat16, jnp.float32
    sem = pltpu.SemaphoreType.DMA
    n = groups - 1
    rows = groups * cap
    return pl.pallas_call(
        functools.partial(experts_kernel, reps, groups, compute),
        out_shape=[jax.ShapeDtypeStruct(x.shape, bf), jax.ShapeDtypeStruct(x.shape, bf),
                   jax.ShapeDtypeStruct((blocks, wide, part), f32), jax.ShapeDtypeStruct((blocks, 1, part), f32),
                   jax.ShapeDtypeStruct((blocks, part, wide), f32)],
        in_specs=[anyw, anyw, anyw, vm, anyw],
        out_specs=[anyw, anyw, anyw, vm, anyw],
        scratch_shapes=[
            pltpu.VMEM((blocks, reps, groups, cap, wide), bf), pltpu.VMEM((blocks, reps, groups, cap, wide), bf),
            pltpu.VMEM((blocks, groups, cap, wide), bf), pltpu.VMEM((blocks, groups, cap, wide), bf),
            pltpu.VMEM((reps, wide, part), bf), pltpu.VMEM((reps, part, wide), bf),
            pltpu.VMEM((wide, part), bf), pltpu.VMEM((part, wide), bf),
            pltpu.VMEM((reps, rows, part), bf), pltpu.VMEM((reps, rows, part), bf),
            pltpu.VMEM((wide, part), f32), pltpu.VMEM((part, wide), f32),
            pltpu.VMEM((rows, wide), f32), pltpu.VMEM((rows, wide), f32),
            sem((2, blocks)), sem((2, blocks, n)), sem((2, blocks, n)), sem((2, blocks, 4)), sem((2, blocks, 4)),
            sem((2, blocks, n)), sem((2, blocks, n)), sem((2, blocks)), sem((2, reps)), sem((2,)), sem((2,))],
        compiler_params=pltpu.CompilerParams(collective_id=2, has_side_effects=True, vmem_limit_bytes=60 * MIB),
    )(x, g, w_in, bias, w_out)

def experts_plain(x, g, w_in, b_in, w_out):
    bf, f32 = jnp.bfloat16, jnp.float32
    rx = lax.all_to_all(x, "exp", split_axis=0, concat_axis=0, tiled=True)
    rg = lax.all_to_all(g, "exp", split_axis=0, concat_axis=0, tiled=True)
    pre = jnp.einsum("secd,edf->secf", rx, w_in, preferred_element_type=f32)
    pre = pre + b_in.astype(f32)[None, :, None, :]
    cdf, pdf = normal_parts(pre)
    act = (pre * cdf).astype(bf)
    res = jnp.einsum("secf,efd->secd", act, w_out, preferred_element_type=f32).astype(bf)
    pg = jnp.einsum("secd,efd->secf", rg, w_out, preferred_element_type=f32) * (cdf + pre * pdf)
    pg = pg.astype(bf)
    ig = jnp.einsum("secf,edf->secd", pg, w_in, preferred_element_type=f32).astype(bf)
    gout = jnp.einsum("secf,secd->efd", act, rg, preferred_element_type=f32).astype(bf)
    gin = jnp.einsum("secd,secf->edf", rx, pg, preferred_element_type=f32).astype(bf)
    gb = jnp.sum(pg, axis=(0, 2), dtype=f32).astype(bf)
    return (
        lax.all_to_all(res, "exp", split_axis=0, concat_axis=0, tiled=True),
        lax.all_to_all(ig, "exp", split_axis=0, concat_axis=0, tiled=True),
        lax.psum_scatter(gin, "rep", scatter_dimension=2, tiled=True).astype(f32),
        lax.psum_scatter(gb, "rep", scatter_dimension=1, tiled=True).astype(f32)[:, None],
        lax.psum_scatter(gout, "rep", scatter_dimension=1, tiled=True).astype(f32),
    )


epsilon = 1e-06
masked_score = -1e30


def normalize(values):
    center = values - jnp.mean(values, axis=-1, keepdims=True)
    spread = jnp.mean(center * center, axis=-1, keepdims=True)
    scale = lax.rsqrt(spread + epsilon)
    return center * scale, scale


def normalize_back(grad, unit, scale):
    mean = jnp.mean(grad, axis=-1, keepdims=True)
    along = jnp.mean(grad * unit, axis=-1, keepdims=True)
    return (grad - mean - unit * along) * scale


def two_parts(v):
    high = v.astype(jnp.bfloat16)
    return high, (v - high.astype(jnp.float32)).astype(jnp.bfloat16)


def positions_of(routes, valid_col, priority_col, priority_row, experts):
    length = routes.shape[0]
    f32, bf = jnp.float32, jnp.bfloat16
    token_row = lax.broadcasted_iota(jnp.int32, (length, length), 1)
    token_col = lax.broadcasted_iota(jnp.int32, (length, length), 0)
    rank_col = jnp.sum(
        jnp.where(priority_row == token_col, token_row, 0).astype(f32), axis=1, keepdims=True
    )
    rank_row = jnp.sum(
        jnp.where(priority_col == token_row, token_col, 0).astype(f32), axis=0, keepdims=True
    )
    earlier = (rank_row < rank_col).astype(f32).astype(bf)
    expert_row = lax.broadcasted_iota(jnp.int32, (length, experts), 1)
    ones = [(routes[:, k : k + 1] == expert_row).astype(f32) for k in range(routes.shape[1])]
    before = jnp.zeros((1, experts), f32)
    places = []
    for one in ones:
        live = one * valid_col
        count = dot(earlier, live.astype(bf), 1, 0) + before
        places.append(jnp.sum(count * one, axis=1, keepdims=True))
        before = before + jnp.sum(live, axis=0, keepdims=True)
    return ones, places


def body_plain(
    tokens,
    segments,
    valid,
    routes,
    priority,
    ln1_gain,
    ln1_bias,
    w_query,
    query_bias,
    w_key,
    w_value,
    value_bias,
    w_attn_out,
    attn_out_bias,
    ln2_gain,
    ln2_bias,
    w_router,
    expert_in,
    expert_in_bias,
    expert_out,
    expert_out_bias,
    cotangent,
):
    f32, bf = jnp.float32, jnp.bfloat16
    vectors, weights, router_weight, result_shift = gather_all(
        [ln1_gain, ln1_bias, query_bias, value_bias, attn_out_bias, ln2_gain, ln2_bias],
        [w_query, w_key, w_value, w_attn_out],
        w_router,
        expert_out_bias,
    )
    vectors = [v.astype(f32)[None] for v in vectors]
    gain_one, bias_one, query_shift, value_shift, proj_shift, gain_two, bias_two = vectors
    query_weight, key_weight, value_weight, proj_weight = weights
    length = tokens.shape[1]
    feature_dim = tokens.shape[2]
    head_dim = feature_dim // HEADS
    local_blocks = expert_in.shape[0]
    reps, groups = lax.axis_size("rep"), lax.axis_size("exp")
    experts = EXPERTS
    split = local_blocks * groups // experts
    top_count = routes.shape[2]
    capacity = (105 * top_count * length + 100 * experts - 1) // (100 * experts)
    room = -(-capacity // 8) * 8
    score_scale = head_dim ** (-0.5)
    inputs = tokens[0].astype(f32)
    row_segments = segments[0]
    row_valid = valid[0]
    places = jnp.arange(length, dtype=jnp.int32)
    allowed = (row_segments[:, None] == row_segments[None, :]) & (
        (row_valid[None, :] > 0) | (places[:, None] == places[None, :])
    )
    unit_one, scale_one = normalize(inputs)
    normed = (unit_one * gain_one + bias_one).astype(bf)
    query_rows = (dot(normed, query_weight, 1, 0) + query_shift).astype(bf)
    key_rows = dot(normed, key_weight, 1, 0).astype(bf)
    value_rows = (dot(normed, value_weight, 1, 0) + value_shift).astype(bf)
    query_heads = query_rows.reshape(length, HEADS, head_dim)
    key_heads = key_rows.reshape(length, HEADS, head_dim)
    value_heads = value_rows.reshape(length, HEADS, head_dim)

    def scores():
        return jnp.where(
            allowed[None],
            jnp.einsum("qhd,khd->hqk", query_heads, key_heads, preferred_element_type=f32)
            * score_scale,
            masked_score,
        )

    masked = scores()
    top_score = jnp.max(masked, axis=-1, keepdims=True)
    log_total = top_score + jnp.log(jnp.sum(jnp.exp(masked - top_score), axis=-1, keepdims=True))
    mixed = jnp.einsum(
        "hqk,khd->qhd",
        jnp.exp(masked - log_total).astype(bf),
        value_heads,
        preferred_element_type=f32,
    )
    mixed = mixed.reshape(length, feature_dim).astype(bf)
    residual = inputs + dot(mixed, proj_weight, 1, 0) + proj_shift
    unit_two, scale_two = normalize(residual)
    normed_two = (unit_two * gain_two + bias_two).astype(bf)
    logits = dot(normed_two, router_weight, 1, 0)
    logit_exp = jnp.exp(logits - jnp.max(logits, axis=-1, keepdims=True))
    router_probs = logit_exp / jnp.sum(logit_exp, axis=-1, keepdims=True)
    upstream = cotangent[0].astype(f32)
    ones, positions = positions_of(
        routes[0], row_valid[:, None].astype(f32), priority[0][:, None], priority[0][None], experts
    )
    expert_row = lax.broadcasted_iota(jnp.int32, (1, experts), 1).astype(f32)
    slot_row = lax.broadcasted_iota(jnp.int32, (1, experts * room), 1)
    kept, gates, slots, sent = [], [], [], jnp.zeros((experts * room, feature_dim), f32)
    for one, position in zip(ones, positions):
        keep = row_valid[:, None].astype(f32) * (position < capacity).astype(f32)
        gate = jnp.sum(router_probs * one, axis=1, keepdims=True) * keep
        place = jnp.sum(one * expert_row, axis=1, keepdims=True) * room + position
        place = jnp.where(keep > 0, place, -1.0).astype(jnp.int32)
        hot = (place == slot_row).astype(f32).astype(bf)
        kept.append(one * keep)
        gates.append(gate)
        slots.append(hot)
        sent = sent + dot(hot, (gate * upstream).astype(bf), 0, 0)
    any_slot = slots[0]
    for hot in slots[1:]:
        any_slot = any_slot + hot
    expert_slots = dot(any_slot, normed_two, 0, 0).astype(bf)
    gated = sum(one * gate for one, gate in zip(kept, gates))
    high, low = two_parts(gated)
    shift_grad = dot(high, cotangent[0], 0, 0) + dot(low, cotangent[0], 0, 0)

    def outgoing(v):
        v = v.astype(bf).reshape(experts, room, feature_dim)
        return jnp.repeat(v, split, axis=0).reshape(groups, local_blocks, room, feature_dim)

    moved = experts_plain(
        outgoing(expert_slots), outgoing(sent), expert_in, expert_in_bias, expert_out
    )
    result, slot_back, in_w_grad, in_b_grad, out_w_grad = moved
    result = result.reshape(experts, split, room, feature_dim)
    slot_back = slot_back.reshape(experts, split, room, feature_dim)
    results = [result[:, s].reshape(experts * room, feature_dim) for s in range(split)]
    backs = [slot_back[:, s].reshape(experts * room, feature_dim) for s in range(split)]
    combined, prob_grad = 0.0, 0.0
    for one, gate, hot in zip(kept, gates, slots):
        picked = dot(one.astype(bf), result_shift, 1, 0)
        for part in results:
            picked = picked + dot(hot, part, 1, 0)
        combined = combined + gate * picked
        prob_grad = prob_grad + one * jnp.sum(upstream * picked, axis=1, keepdims=True)
    output = residual + combined
    logit_grad = (
        router_probs * (prob_grad - jnp.sum(router_probs * prob_grad, axis=-1, keepdims=True))
    ).astype(bf)
    router_w_grad = dot(normed_two, logit_grad, 0, 0)
    normed_two_grad = dot(logit_grad, router_weight, 1, 1)
    for part in backs:
        normed_two_grad = normed_two_grad + dot(any_slot, part, 1, 0)
    gain_two_grad = jnp.sum(normed_two_grad * unit_two, axis=0)
    bias_two_grad = jnp.sum(normed_two_grad, axis=0)
    residual_grad = upstream + normalize_back(normed_two_grad * gain_two, unit_two, scale_two)
    branch_grad = residual_grad.astype(bf)
    proj_w_grad = dot(mixed, branch_grad, 0, 0)
    proj_b_grad = jnp.sum(branch_grad, axis=0, dtype=f32)
    mixed_grad = dot(branch_grad, proj_weight, 1, 1).astype(bf)
    mixed_grad = mixed_grad.reshape(length, HEADS, head_dim)
    again_probs = jnp.exp(scores() - log_total)
    prob_grads = jnp.einsum("qhd,khd->hqk", mixed_grad, value_heads, preferred_element_type=f32)
    value_grad = jnp.einsum(
        "hqk,qhd->khd", again_probs.astype(bf), mixed_grad, preferred_element_type=f32
    )
    value_grad = value_grad.astype(bf).reshape(length, feature_dim)
    inner_sum = jnp.sum(again_probs * prob_grads, axis=-1, keepdims=True)
    score_grad = (again_probs * (prob_grads - inner_sum)).astype(bf)
    query_grad = jnp.einsum("hqk,khd->qhd", score_grad, key_heads, preferred_element_type=f32)
    query_grad = (query_grad * score_scale).astype(bf).reshape(length, feature_dim)
    key_grad = jnp.einsum("hqk,qhd->khd", score_grad, query_heads, preferred_element_type=f32)
    key_grad = (key_grad * score_scale).astype(bf).reshape(length, feature_dim)
    query_w_grad = dot(normed, query_grad, 0, 0)
    query_b_grad = jnp.sum(query_grad, axis=0, dtype=f32)
    key_w_grad = dot(normed, key_grad, 0, 0)
    value_w_grad = dot(normed, value_grad, 0, 0)
    value_b_grad = jnp.sum(value_grad, axis=0, dtype=f32)
    normed_grad = dot(query_grad, query_weight, 1, 1)
    normed_grad = normed_grad + dot(key_grad, key_weight, 1, 1)
    normed_grad = normed_grad + dot(value_grad, value_weight, 1, 1)
    gain_one_grad = jnp.sum(normed_grad * unit_one, axis=0)
    bias_one_grad = jnp.sum(normed_grad, axis=0)
    tokens_grad = residual_grad + normalize_back(normed_grad * gain_one, unit_one, scale_one)
    vector_sums, weight_sums, router_sum, shift_sum = scatter_all(
        [
            gain_one_grad,
            bias_one_grad,
            query_b_grad,
            value_b_grad,
            proj_b_grad,
            gain_two_grad,
            bias_two_grad,
        ],
        [query_w_grad, key_w_grad, value_w_grad, proj_w_grad],
        router_w_grad,
        shift_grad,
    )
    return (
        output.astype(jnp.bfloat16)[None],
        tokens_grad[None],
        vector_sums[0],
        vector_sums[1],
        weight_sums[0],
        vector_sums[2],
        weight_sums[1],
        weight_sums[2],
        vector_sums[3],
        weight_sums[3],
        vector_sums[4],
        vector_sums[5],
        vector_sums[6],
        router_sum,
        in_w_grad,
        in_b_grad[:, 0],
        out_w_grad,
        shift_sum,
    )


def eye_of(n):
    same = lax.broadcasted_iota(jnp.int32, (n, n), 0) == lax.broadcasted_iota(jnp.int32, (n, n), 1)
    return same.astype(jnp.float32).astype(jnp.bfloat16)


def lanes_of(n=1):
    return lax.broadcasted_iota(jnp.int32, (n, 128), 1)


def mask_of(ints, cols):
    n = ints.shape[1]
    same = lax.broadcasted_iota(jnp.int32, (n, n), 0) == lax.broadcasted_iota(jnp.int32, (n, n), 1)
    near = cols[:, 0:1] == ints[0:1]
    open_key = jnp.where(same, 1.0, cols[:, 1:2]) > 0
    return jnp.where(near & open_key, 0.0, masked_score)


def side_masks(head_dim):
    lane = lanes_of()
    return [
        ((lane >= s * head_dim) & (lane < (s + 1) * head_dim)).astype(jnp.float32).astype(jnp.bfloat16)
        for s in range(128 // head_dim)
    ]


def front_kernel(
    capacity,
    room,
    head_dim,
    tokens_ref,
    cot_ref,
    ints_ref,
    small_ref,
    wq_ref,
    wk_ref,
    wv_ref,
    wo_ref,
    xs_ref,
    gs_ref,
    resid_ref,
    q_ref,
    k_ref,
    v_ref,
    mixed_ref,
    lse_ref,
    info_ref,
    mask_ref,
    a2_ref,
    sent_ref,
):
    f32, bf = jnp.float32, jnp.bfloat16
    length, wide = tokens_ref.shape
    groups, blocks = xs_ref.shape[:2]
    ints = ints_ref[...]
    eye = eye_of(length)
    cols = dot(eye, ints.astype(bf), 1, 1)
    rows = jnp.transpose(small_ref[...].astype(f32))
    gain_one, bias_one, query_shift, value_shift, proj_shift, gain_two, bias_two = [
        rows[64 + i : 65 + i] for i in range(7)
    ]
    inputs = tokens_ref[...].astype(f32)
    unit_one, _ = normalize(inputs)
    normed = (unit_one * gain_one + bias_one).astype(bf)
    q_ref[...] = (dot(normed, wq_ref[...], 1, 0) + query_shift).astype(bf)
    k_ref[...] = dot(normed, wk_ref[...], 1, 0).astype(bf)
    v_ref[...] = (dot(normed, wv_ref[...], 1, 0) + value_shift).astype(bf)
    mask_ref[...] = mask_of(ints, cols)
    sides = side_masks(head_dim)
    per = len(sides)
    scale = jnp.full((1, 128), head_dim**-0.5, f32).astype(bf)

    def heads(h, _):
        at = pl.ds(pl.multiple_of(h * 128, 128), 128)
        query = q_ref[:, at] * scale
        total = jnp.zeros((128, length), f32)
        for s, side in enumerate(sides):
            score = dot(k_ref[:, at] * side, query, 1, 1) + mask_ref[...]
            top = jnp.max(score, axis=0, keepdims=True)
            expo = jnp.exp(score - top)
            norm = jnp.sum(expo, axis=0, keepdims=True)
            lse_ref[pl.ds(h * per + s, 1), :] = top + jnp.log(norm)
            probs = (expo * (1.0 / norm)).astype(bf)
            total = total + dot(v_ref[:, at] * side, probs, 0, 0)
        mixed_ref[at, :] = total.astype(bf)
        return 0

    lax.fori_loop(0, wide // 128, heads, 0)
    residual = inputs + dot(mixed_ref[...], wo_ref[...], 0, 0) + proj_shift
    resid_ref[...] = residual
    unit_two, _ = normalize(residual)
    normed_two = (unit_two * gain_two + bias_two).astype(bf)
    a2_ref[...] = normed_two
    lane = lanes_of()
    routed = (lane >= 32) & (lane < 64)
    logits = jnp.where(routed, dot(normed_two, small_ref[...], 1, 0), masked_score)
    logit_exp = jnp.exp(logits - jnp.max(logits, axis=1, keepdims=True))
    probs = logit_exp / jnp.sum(logit_exp, axis=1, keepdims=True)
    token_row = lax.broadcasted_iota(jnp.int32, (length, length), 1).astype(f32)
    token_col = lax.broadcasted_iota(jnp.int32, (length, length), 0).astype(f32)
    priority_row = ints[2:3] * 64.0 + ints[3:4]
    priority_col = cols[:, 2:3] * 64.0 + cols[:, 3:4]
    rank_col = jnp.sum(jnp.where(priority_row == token_col, token_row, 0.0), axis=1, keepdims=True)
    rank_row = jnp.sum(jnp.where(priority_col == token_row, token_col, 0.0), axis=0, keepdims=True)
    earlier = (rank_row < rank_col).astype(f32).astype(bf)
    expert_lane = (lane - 32).astype(f32)
    valid_col = cols[:, 1:2]
    before = jnp.zeros((1, 128), f32)
    info = probs
    marks = jnp.zeros((length, 128), f32)
    upstream = cot_ref[...].astype(f32)
    for k in range(2):
        expert = cols[:, 4 + k : 5 + k]
        one = (expert == expert_lane).astype(f32)
        live = one * valid_col
        count = dot(earlier, live.astype(bf), 1, 0) + before
        before = before + jnp.sum(live, axis=0, keepdims=True)
        position = jnp.sum(count * one, axis=1, keepdims=True)
        keep = valid_col * (position < capacity).astype(f32)
        gate = jnp.sum(probs * one, axis=1, keepdims=True) * keep
        place = jnp.where(keep > 0, expert * room + position, -1.0)
        high = jnp.floor(place * (1.0 / 32.0))
        low = place - high * 32.0
        marks = jnp.where(lane == 2 * k, high, jnp.where(lane == 2 * k + 1, low, marks))
        info = jnp.where(lane == k, place, jnp.where(lane == 2 + k, expert, info))
        sent_ref[k] = (gate * upstream).astype(bf)
    info_ref[...] = info
    turned = dot(marks.astype(bf), eye, 0, 0)
    place_rows = [turned[2 * k : 2 * k + 1] * 32.0 + turned[2 * k + 1 : 2 * k + 2] for k in range(2)]
    part = blocks * room
    slot = lax.broadcasted_iota(jnp.int32, (part, length), 0).astype(f32)

    def fill(d, _):
        first = (d * part).astype(f32)
        hots = [(slot == row - first).astype(f32).astype(bf) for row in place_rows]
        inside = dot(hots[0] + hots[1], a2_ref[...], 1, 0)
        xs_ref[d] = inside.reshape(blocks, room, wide).astype(bf)
        grads = dot(hots[0], sent_ref[0], 1, 0) + dot(hots[1], sent_ref[1], 1, 0)
        gs_ref[d] = grads.reshape(blocks, room, wide).astype(bf)
        return 0

    lax.fori_loop(0, groups, fill, 0)


def back_kernel(
    head_dim,
    tokens_ref,
    cot_ref,
    ints_ref,
    small_ref,
    wq_ref,
    wk_ref,
    wv_ref,
    wo_ref,
    res_ref,
    ig_ref,
    resid_ref,
    q_ref,
    k_ref,
    v_ref,
    mixed_ref,
    lse_ref,
    info_ref,
    gin_ref,
    gout_ref,
    out_ref,
    tokens_grad_ref,
    wq_grad_ref,
    wk_grad_ref,
    wv_grad_ref,
    wo_grad_ref,
    small_grad_ref,
    gin_out_ref,
    gout_out_ref,
    mask_ref,
    mixed_grad_ref,
    query_grad_ref,
    key_grad_ref,
    value_grad_ref,
    gin_buf,
    gout_buf,
    sem,
):
    f32, bf = jnp.float32, jnp.bfloat16
    length, wide = tokens_ref.shape
    slots = res_ref.shape[0]
    pieces = gin_ref.shape[0]
    carried = ((gin_ref, gin_buf, gin_out_ref), (gout_ref, gout_buf, gout_out_ref))

    def loads(j):
        return [
            pltpu.make_async_copy(src.at[j], buf, sem.at[0, i])
            for i, (src, buf, _) in enumerate(carried)
        ]

    def stores(j):
        return [
            pltpu.make_async_copy(buf, dst.at[j], sem.at[1, i])
            for i, (_, buf, dst) in enumerate(carried)
        ]

    for c in loads(0):
        c.start()
    ints = ints_ref[...]
    cols = dot(eye_of(length), ints.astype(bf), 1, 1)
    mask_ref[...] = mask_of(ints, cols)
    small = small_ref[...]
    rows = jnp.transpose(small.astype(f32))
    gain_one, bias_one, _, _, _, gain_two, bias_two = [rows[64 + i : 65 + i] for i in range(7)]
    lane = lanes_of()
    routed = ((lane >= 32) & (lane < 64)).astype(f32)
    info = info_ref[...]
    probs = info * routed
    upstream = cot_ref[...].astype(f32)
    slot_row = lax.broadcasted_iota(jnp.int32, (1, slots), 1).astype(f32)
    expert_lane = (lane - 32).astype(f32)
    residual = resid_ref[...]
    combined = residual
    prob_grad = jnp.zeros((length, 128), f32)
    gated = jnp.zeros((length, 128), f32)
    hots = []
    for k in range(2):
        place, expert = info[:, k : k + 1], info[:, 2 + k : 3 + k]
        kept = (expert == expert_lane).astype(f32) * (place >= 0).astype(f32)
        gate = jnp.sum(probs * kept, axis=1, keepdims=True)
        hot = (place == slot_row).astype(f32).astype(bf)
        hots.append(hot)
        picked = dot(hot, res_ref[...], 1, 0)
        picked = picked + dot(pltpu.roll(kept, 96, 1).astype(bf), small, 1, 1)
        combined = combined + gate * picked
        prob_grad = prob_grad + kept * jnp.sum(upstream * picked, axis=1, keepdims=True)
        gated = gated + kept * gate
    out_ref[...] = combined.astype(bf)
    inner = jnp.sum(probs * prob_grad, axis=1, keepdims=True)
    logit_grad = (probs * (prob_grad - inner)).astype(bf)
    unit_two, scale_two = normalize(residual)
    normed_two = (unit_two * gain_two + bias_two).astype(bf)
    high, low = two_parts(pltpu.roll(gated, 96, 1))
    small_grad = dot(normed_two, logit_grad, 0, 0)
    small_grad = small_grad + dot(cot_ref[...], high, 0, 0) + dot(cot_ref[...], low, 0, 0)
    normed_two_grad = dot(hots[0] + hots[1], ig_ref[...], 1, 0) + dot(logit_grad, small, 1, 1)
    vector_grads = {}
    vector_grads[5] = jnp.sum(normed_two_grad * unit_two, axis=0, keepdims=True)
    vector_grads[6] = jnp.sum(normed_two_grad, axis=0, keepdims=True)
    residual_grad = upstream + normalize_back(normed_two_grad * gain_two, unit_two, scale_two)
    tokens_grad_ref[...] = residual_grad
    branch_grad = residual_grad.astype(bf)
    wo_grad_ref[...] = dot(mixed_ref[...], branch_grad, 1, 0)
    vector_grads[4] = jnp.sum(branch_grad.astype(f32), axis=0, keepdims=True)
    mixed_grad_ref[...] = dot(branch_grad, wo_ref[...], 1, 1).astype(bf)
    sides = side_masks(head_dim)
    per = len(sides)
    scale = jnp.full((1, 128), head_dim**-0.5, f32).astype(bf)

    def heads(h, _):
        at = pl.ds(pl.multiple_of(h * 128, 128), 128)
        query = q_ref[:, at] * scale
        mixed_grad = mixed_grad_ref[:, at]

        @pl.when(h < pieces)
        def _():
            for c in loads(h):
                c.wait()
            for c in stores(h):
                c.start()

        query_total = jnp.zeros((128, length), f32)
        key_total = jnp.zeros((length, 128), f32)
        value_total = jnp.zeros((length, 128), f32)
        for s, side in enumerate(sides):
            key = k_ref[:, at] * side
            score = dot(key, query, 1, 1) + mask_ref[...]
            probs = jnp.exp(score - lse_ref[pl.ds(h * per + s, 1), :])
            prob_grads = dot(v_ref[:, at] * side, mixed_grad, 1, 1)
            inner = jnp.sum(probs * prob_grads, axis=0, keepdims=True)
            score_grad = (probs * (prob_grads - inner)).astype(bf)
            value_total = value_total + dot(probs.astype(bf), mixed_grad * side, 1, 0)
            key_total = key_total + dot(score_grad, query * side, 1, 0)
            query_total = query_total + dot(key * scale, score_grad, 0, 0)
        @pl.when(h < pieces)
        def _():
            for c in stores(h):
                c.wait()

        @pl.when(h + 1 < pieces)
        def _():
            for c in loads(h + 1):
                c.start()

        query_grad_ref[:, at] = jnp.transpose(query_total).astype(bf)
        key_grad_ref[:, at] = key_total.astype(bf)
        value_grad_ref[:, at] = value_total.astype(bf)
        return 0

    lax.fori_loop(0, wide // 128, heads, 0)
    inputs = tokens_ref[...].astype(f32)
    unit_one, scale_one = normalize(inputs)
    normed = (unit_one * gain_one + bias_one).astype(bf)
    wq_grad_ref[...] = dot(normed, query_grad_ref[...], 0, 0)
    wk_grad_ref[...] = dot(normed, key_grad_ref[...], 0, 0)
    wv_grad_ref[...] = dot(normed, value_grad_ref[...], 0, 0)
    vector_grads[2] = jnp.sum(query_grad_ref[...].astype(f32), axis=0, keepdims=True)
    vector_grads[3] = jnp.sum(value_grad_ref[...].astype(f32), axis=0, keepdims=True)
    normed_grad = dot(query_grad_ref[...], wq_ref[...], 1, 1)
    normed_grad = normed_grad + dot(key_grad_ref[...], wk_ref[...], 1, 1)
    normed_grad = normed_grad + dot(value_grad_ref[...], wv_ref[...], 1, 1)
    vector_grads[0] = jnp.sum(normed_grad * unit_one, axis=0, keepdims=True)
    vector_grads[1] = jnp.sum(normed_grad, axis=0, keepdims=True)
    tokens_grad_ref[...] += normalize_back(normed_grad * gain_one, unit_one, scale_one)
    line = lax.broadcasted_iota(jnp.int32, (128, wide), 0)
    stacked = jnp.zeros((128, wide), f32)
    for i in range(7):
        stacked = jnp.where(line == 64 + i, vector_grads[i], stacked)
    small_grad_ref[...] = small_grad + jnp.transpose(stacked)


def front_call(capacity, room, groups, blocks, tokens, cot, ints, small, weights):
    f32, bf = jnp.float32, jnp.bfloat16
    length, wide = tokens.shape
    shape = jax.ShapeDtypeStruct
    vm = pl.BlockSpec(memory_space=pltpu.VMEM)
    slots = shape((groups, blocks, room, wide), bf)
    line = shape((length, wide), bf)
    outs = [slots, slots, shape((length, wide), f32), line, line, line]
    outs += [shape((wide, length), bf), shape((16, length), f32), shape((length, 128), f32)]
    return pl.pallas_call(
        functools.partial(front_kernel, capacity, room, wide // HEADS),
        out_shape=outs,
        in_specs=[vm] * 8,
        out_specs=[vm] * len(outs),
        scratch_shapes=[
            pltpu.VMEM((length, length), f32),
            pltpu.VMEM((length, wide), bf),
            pltpu.VMEM((2, length, wide), bf),
        ],
        compiler_params=pltpu.CompilerParams(vmem_limit_bytes=60 * MIB),
    )(tokens, cot, ints, small, *weights)


def back_call(tokens, cot, ints, small, weights, res, ig, kept, gin, gout):
    f32, bf = jnp.float32, jnp.bfloat16
    length, wide = tokens.shape
    shape = jax.ShapeDtypeStruct
    vm = pl.BlockSpec(memory_space=pltpu.VMEM)
    hbm = pl.BlockSpec(memory_space=pl.ANY)
    square = shape((wide, wide), f32)
    outs = [shape((length, wide), bf), shape((length, wide), f32)] + [square] * 4
    outs += [shape((wide, 128), f32), shape(gin.shape, f32), shape(gout.shape, f32)]
    line = pltpu.VMEM((length, wide), bf)
    return pl.pallas_call(
        functools.partial(back_kernel, wide // HEADS),
        out_shape=outs,
        in_specs=[vm] * 17 + [hbm] * 2,
        out_specs=[vm] * 7 + [hbm] * 2,
        scratch_shapes=[
            pltpu.VMEM((length, length), f32),
            line,
            line,
            line,
            line,
            pltpu.VMEM(gin.shape[1:], f32),
            pltpu.VMEM(gout.shape[1:], f32),
            pltpu.SemaphoreType.DMA((2, 2)),
        ],
        compiler_params=pltpu.CompilerParams(vmem_limit_bytes=60 * MIB),
    )(tokens, cot, ints, small, *weights, res, ig, *kept, gin, gout)


def body_fast(
    tokens,
    segments,
    valid,
    routes,
    priority,
    ln1_gain,
    ln1_bias,
    w_query,
    query_bias,
    w_key,
    w_value,
    value_bias,
    w_attn_out,
    attn_out_bias,
    ln2_gain,
    ln2_bias,
    w_router,
    expert_in,
    expert_in_bias,
    expert_out,
    expert_out_bias,
    cotangent,
):
    f32 = jnp.float32
    reps, groups = lax.axis_size("rep"), lax.axis_size("exp")
    devices = reps * groups
    length, wide = tokens.shape[1:]
    per = w_query.shape[0]
    blocks = expert_in.shape[0]
    capacity, room = capacity_of(routes.shape[2], length)
    vectors = [ln1_gain, ln1_bias, query_bias, value_bias, attn_out_bias, ln2_gain, ln2_bias]
    small = jnp.concatenate([expert_out_bias.T, w_router, jnp.stack(vectors, axis=1)], axis=1)
    small = jnp.pad(small, ((0, 0), (0, 128 - small.shape[1])))
    weights, small = gather_params([w_query, w_key, w_value, w_attn_out], small, reps, groups)
    small = small.reshape(wide, 128)
    first = priority[0]
    ints = [segments[0], valid[0], first // 64, first % 64, routes[0, :, 0], routes[0, :, 1]]
    ints = jnp.stack(ints + [first * 0] * 2).astype(f32)
    xs, gs, *kept = front_call(
        capacity, room, groups, blocks, tokens[0], cotangent[0], ints, small, weights
    )
    res, ig, gin, gb, gout = experts_call(
        xs, gs, expert_in, expert_in_bias, expert_out, reps, groups
    )
    slots = groups * blocks * room
    output, tokens_grad, *grads, small_grad, gin, gout = back_call(
        tokens[0],
        cotangent[0],
        ints,
        small,
        weights,
        res.reshape(slots, wide),
        ig.reshape(slots, wide),
        kept,
        gin,
        gout,
    )
    sums, last = scatter_grads(grads, small_grad.reshape(devices, per, 128), reps, groups)
    columns = [last[:, 64 + i] for i in range(7)]
    return (
        output[None],
        tokens_grad[None],
        columns[0],
        columns[1],
        sums[0],
        columns[2],
        sums[1],
        sums[2],
        columns[3],
        sums[3],
        columns[4],
        columns[5],
        columns[6],
        last[:, 32:64],
        gin,
        gb[:, 0],
        gout,
        last[:, :32].T,
    )


def capacity_of(top_count, length):
    capacity = (105 * top_count * length + 100 * EXPERTS - 1) // (100 * EXPERTS)
    return capacity, -(-capacity // 8) * 8


def body(*args):
    routes, w_query, expert_in = args[3], args[7], args[17]
    reps, groups = lax.axis_size("rep"), lax.axis_size("exp")
    _, room = capacity_of(routes.shape[2], routes.shape[1])
    wide = w_query.shape[1]
    suits = (
        reps == 4
        and groups & (groups - 1) == 0
        and w_query.shape[0] % 8 == 0
        and groups * room <= 512
        and groups * expert_in.shape[0] == EXPERTS == 32
        and expert_in.shape[2] % (128 * reps) == 0
        and routes.shape[2] == 2
        and routes.shape[1] <= 64 * 256
        and 128 % (wide // HEADS) == 0
        and HEADS <= 16
        and expert_in.shape[0] < wide // 128
    )
    return body_fast(*args) if suits else body_plain(*args)


def solution(mesh):
    in_specs = (
        P(("rep", "exp"), None, None),
        P(("rep", "exp"), None),
        P(("rep", "exp"), None),
        P(("rep", "exp"), None, None),
        P(("rep", "exp"), None),
        P(("rep", "exp")),
        P(("rep", "exp")),
        P(("rep", "exp"), None),
        P(("rep", "exp")),
        P(("rep", "exp"), None),
        P(("rep", "exp"), None),
        P(("rep", "exp")),
        P(("rep", "exp"), None),
        P(("rep", "exp")),
        P(("rep", "exp")),
        P(("rep", "exp")),
        P(("rep", "exp"), None),
        P("exp", None, None),
        P("exp", None),
        P("exp", None, None),
        P(None, ("rep", "exp")),
        P(("rep", "exp"), None, None),
    )
    out_specs = (
        P(("rep", "exp"), None, None),
        P(("rep", "exp"), None, None),
        P(("rep", "exp")),
        P(("rep", "exp")),
        P(("rep", "exp"), None),
        P(("rep", "exp")),
        P(("rep", "exp"), None),
        P(("rep", "exp"), None),
        P(("rep", "exp")),
        P(("rep", "exp"), None),
        P(("rep", "exp")),
        P(("rep", "exp")),
        P(("rep", "exp")),
        P(("rep", "exp"), None),
        P("exp", None, "rep"),
        P("exp", "rep"),
        P("exp", "rep", None),
        P(None, ("rep", "exp")),
    )
    return jax.shard_map(body, mesh=mesh, in_specs=in_specs, out_specs=out_specs, check_vma=False)
```

```python
import functools
import jax
import jax.numpy as jnp
from jax import lax
from jax.experimental import pallas as pl
from jax.experimental.pallas import tpu as pltpu
from jax.sharding import PartitionSpec as P

HEADS = 12
EXPERTS = 32
MESH = pl.DeviceIdType.MESH
MIB = 1 << 20

def bit_dims(reps, groups):
    rb, gb = reps.bit_length() - 1, groups.bit_length() - 1
    return [(0, 1 << k) for k in reversed(range(rb))] + [(1, 1 << k) for k in reversed(range(gb))]

def orders(dims):
    last = len(dims) - 1
    rep = [i for i, d in enumerate(dims) if d[0] == 0]
    exp = [i for i, d in enumerate(dims) if d[0] == 1 and i != last]
    exp = exp[::-1]
    return [[last] + rep + exp, [last] + rep[::-1] + exp, [last] + exp + rep]

def my_bits(dims):
    at = (lax.axis_index("rep"), lax.axis_index("exp"))
    return [(at[a] // s) % 2 for a, s in dims], at

def partner(dims, at, i):
    a, s = dims[i]
    bit = (at[a] // s) % 2
    there = at[a] + (1 - 2 * bit) * s
    return (there, at[1]) if a == 0 else (at[0], there)

def greet(dims, at):
    barrier = pltpu.get_barrier_semaphore()
    for i in range(len(dims)):
        pl.semaphore_signal(barrier, inc=1, device_id=partner(dims, at, i), device_id_type=MESH)
    pl.semaphore_wait(barrier, len(dims))

def scatter_kernel(dims, widths, count, *refs):
    ins, small_in = refs[:count], refs[count]
    outs, small_out = refs[count + 1], refs[count + 2]
    n = len(dims)
    scr = refs[count + 3:]
    parts = 3
    send_sem, recv_sem = scr[:2]
    scr = scr[2:]
    take = iter(scr)
    bufs = [[(next(take), next(take), next(take) if k < n - 1 else None) for p in range(parts)] for k in range(n)]
    smalls = [(next(take), next(take) if k < n - 1 else None) for k in range(n)]
    bits, at = my_bits(dims)
    plan = orders(dims)
    left = [list(range(n)) for _ in range(parts)]
    small_left = list(range(n))
    small_cur = small_in
    def split(have, i, b):
        return tuple(b if j == i else slice(None) for j in have)
    live = []
    def begin(k, p):
        i = plan[p][k]
        sb, rb, _ = bufs[k][p]
        far = split(left[p], i, 1 - bits[i])
        cols = pl.ds(widths[p][0], widths[p][1]) if k == 0 else slice(None)
        for a in range(count):
            src = ins[a][far + (slice(None), cols)] if k == 0 else bufs[k - 1][p][2][(a,) + far]
            sb[a] = src.astype(sb.dtype)
        c = [pltpu.make_async_remote_copy(sb, rb, send_sem.at[k, p], recv_sem.at[k, p], device_id=partner(dims, at, i), device_id_type=MESH)]
        if p == 0:
            src = (small_in if k == 0 else smalls[k - 1][1]).at[far]
            c.append(pltpu.make_async_remote_copy(src, smalls[k][0], send_sem.at[k, parts], recv_sem.at[k, parts], device_id=partner(dims, at, i), device_id_type=MESH))
        for x in c: x.start()
        return c
    def finish(k, p, c):
        i = plan[p][k]
        sb, rb, acc = bufs[k][p]
        near = split(left[p], i, bits[i])
        cols = pl.ds(widths[p][0], widths[p][1]) if k == 0 else slice(None)
        for x in c: x.wait_recv()
        for a in range(count):
            src = ins[a][near + (slice(None), cols)] if k == 0 else bufs[k - 1][p][2][(a,) + near]
            tot = src + rb[a].astype(jnp.float32)
            if k < n - 1:
                acc[a] = tot
            else:
                outs[a, :, widths[p][0]:widths[p][0] + widths[p][1]] = tot
        if p == 0:
            src = (small_in if k == 0 else smalls[k - 1][1])[near]
            tot = src + smalls[k][0][...]
            if k < n - 1:
                smalls[k][1][...] = tot
            else:
                small_out[...] = tot
        left[p].remove(i)
    greet(dims, at)
    live = [begin(0, p) for p in range(parts)]
    every = list(live)
    for k in range(n):
        for p in range(parts):
            finish(k, p, live[p])
            if k < n - 1:
                live[p] = begin(k + 1, p)
                every.append(live[p])
    for cs in every:
        for c in cs: c.wait_send()

def scatter_grads(grads, small, reps, groups, link=jnp.bfloat16):
    dims = bit_dims(reps, groups)
    n = len(dims)
    full, cols = grads[0].shape
    rows = full // (reps * groups)
    third = cols // 3 // 128 * 128
    widths = [(0, third), (third, third), (2 * third, cols - 2 * third)]
    count = len(grads)
    lead = (2,) * n
    grads = [g.reshape(lead + (rows, cols)) for g in grads]
    small = small.reshape(lead + small.shape[1:])
    scratch = [pltpu.SemaphoreType.DMA((n, 4)), pltpu.SemaphoreType.DMA((n, 4))]
    for k in range(n):
        for p in range(3):
            shape = (count,) + (2,) * (n - 1 - k) + (rows, widths[p][1])
            scratch += [pltpu.VMEM(shape, link), pltpu.VMEM(shape, link)]
            if k < n - 1:
                scratch.append(pltpu.VMEM(shape, jnp.float32))
    for k in range(n):
        shape = (2,) * (n - 1 - k) + small.shape[n:]
        scratch.append(pltpu.VMEM(shape, jnp.float32))
        if k < n - 1:
            scratch.append(pltpu.VMEM(shape, jnp.float32))
    vm = pl.BlockSpec(memory_space=pltpu.VMEM)
    outs = pl.pallas_call(
        functools.partial(scatter_kernel, dims, widths, count),
        out_shape=[jax.ShapeDtypeStruct((count, rows, cols), jnp.float32), jax.ShapeDtypeStruct(small.shape[n:], jnp.float32)],
        in_specs=[vm] * (count + 1),
        out_specs=[vm] * 2,
        scratch_shapes=scratch,
        compiler_params=pltpu.CompilerParams(collective_id=1, has_side_effects=True, vmem_limit_bytes=56 * MIB),
    )(*grads, small)
    return outs[0], outs[1]


def gather_all(vectors, weights, router, shift):
    axes = ("rep", "exp")
    return (
        [lax.all_gather(v, axes, axis=0, tiled=True) for v in vectors],
        [lax.all_gather(w, axes, axis=0, tiled=True) for w in weights],
        lax.all_gather(router, axes, axis=0, tiled=True),
        lax.all_gather(shift, axes, axis=1, tiled=True),
    )


def scatter_all(vectors, weights, router, shift):
    axes = ("rep", "exp")
    return (
        [lax.psum_scatter(v, axes, scatter_dimension=0, tiled=True) for v in vectors],
        [lax.psum_scatter(w, axes, scatter_dimension=0, tiled=True) for w in weights],
        lax.psum_scatter(router, axes, scatter_dimension=0, tiled=True),
        lax.psum_scatter(shift, axes, scatter_dimension=1, tiled=True),
    )


def normal_parts(v):
    e = jnp.exp(v * v * -0.5)
    t = 1.0 / (1.0 + (0.3275911 * 0.7071067811865476) * jnp.abs(v))
    poly = t * (0.127414796 + t * (-0.142248368 + t * (0.7107068705 + t * (-0.7265760135 + t * 0.5307027145))))
    q = poly * e
    return jnp.where(v < 0, q, 1.0 - q), e * 0.3989422804014327

def dot(a, b, ca, cb):
    return lax.dot_general(a, b, (((ca,), (cb,)), ((), ())), preferred_element_type=jnp.float32)

def experts_kernel(reps, groups, compute, x_ref, g_ref, win_ref, bias_in, wout_ref,
                   res_ref, ig_ref, gin_ref, gb_ref, gout_ref,
                   x_all, g_all, res_send, ig_send, wi, wo, wis, wos, act_all, pg_all, gin_buf, gout_buf, res_acc, ig_acc, bias_ref,
                   own_sem, dsem, drec, rsem, rrec, bsem, brec, bown, wsem, ssem, osem):
    me, rep = lax.axis_index("exp"), lax.axis_index("rep")
    blocks = x_ref.shape[1]
    cap, wide = x_ref.shape[2:]
    rows = groups * cap
    chunks, part = wi.shape[0], wi.shape[2]
    half = groups // 2
    peers = [lax.rem(me + s, groups) for s in range(1, groups)]
    side = (rep + 1 - 2 * (rep % 2), rep + 2 - 4 * ((rep // 2) % 2))
    both = ((x_ref, x_all), (g_ref, g_all))
    back = ((res_send, res_ref), (ig_send, ig_ref))

    def load(j, f):
        return (pltpu.make_async_copy(win_ref.at[j, :, pl.ds(f * part, part)], wi.at[f], wsem.at[0, f]),
                pltpu.make_async_copy(wout_ref.at[j, pl.ds(f * part, part)], wo.at[f], wsem.at[1, f]))
    def load_slice(j):
        at = pl.ds(pl.multiple_of(rep * part, part), part)
        return (pltpu.make_async_copy(win_ref.at[j, :, at], wis, ssem.at[0]),
                pltpu.make_async_copy(wout_ref.at[j, at], wos, ssem.at[1]))
    def out_copies(j):
        return (pltpu.make_async_copy(gin_buf, gin_ref.at[j], osem.at[0]),
                pltpu.make_async_copy(gout_buf, gout_ref.at[j], osem.at[1]))
    def dispatch(j, t, s):
        src, dst = both[t]
        return pltpu.make_async_remote_copy(src.at[peers[s], j], dst.at[j, 0, me], dsem.at[t, j, s], drec.at[t, j, s],
                                            device_id=(rep, peers[s]), device_id_type=MESH)
    def own(j, t):
        src, dst = both[t]
        return pltpu.make_async_copy(src.at[me, j], dst.at[j, 0, me], own_sem.at[t, j])
    def across(j, t, n):
        dst = both[t][1]
        return pltpu.make_async_remote_copy(dst.at[j, 0], dst.at[j, 1 + n], rsem.at[t, j, n], rrec.at[t, j, n],
                                            device_id=(side[n], me), device_id_type=MESH)
    def onward(j, t, n):
        dst = both[t][1]
        at = pl.ds(n * half, half)
        return pltpu.make_async_remote_copy(dst.at[j, 1 + n, at], dst.at[j, 3, at], rsem.at[t, j, 2 + n], rrec.at[t, j, 2 + n],
                                            device_id=(side[1 - n], me), device_id_type=MESH)
    def give(j, t, s):
        src, dst = back[t]
        return pltpu.make_async_remote_copy(src.at[j, peers[s]], dst.at[me, j], bsem.at[t, j, s], brec.at[t, j, s],
                                            device_id=(rep, peers[s]), device_id_type=MESH)
    def give_own(j, t):
        src, dst = back[t]
        return pltpu.make_async_copy(src.at[j, me], dst.at[me, j], bown.at[t, j])
    def flat(v):
        return v.astype(jnp.float32).reshape(-1, wide).astype(jnp.bfloat16)

    barrier = pltpu.get_barrier_semaphore()
    for p in peers:
        pl.semaphore_signal(barrier, inc=1, device_id=(rep, p), device_id_type=MESH)
    for n in side:
        pl.semaphore_signal(barrier, inc=1, device_id=(n, me), device_id_type=MESH)
    pl.semaphore_wait(barrier, groups - 1 + 2)

    def send_all(j, _):
        for t in range(2):
            for s in range(groups - 1):
                dispatch(j, t, s).start()
            own(j, t).start()
        return 0
    lax.fori_loop(0, blocks, send_all, 0)
    for j in range(blocks):
        for f in range(chunks):
            bias_ref[j, f] = bias_in[j : j + 1, f * part : (f + 1) * part].astype(jnp.float32)
    if compute:
        for f in range(chunks):
            for c in load(0, f): c.start()
        for c in load_slice(0): c.start()

    def own_rows(j):
        x, g = flat(x_all[j, 0]), flat(g_all[j, 0])
        def chunk(f, _):
            for c in load(j, f): c.wait()
            pre = dot(x, wi[f], 1, 0) + bias_ref[j, f]
            cdf, pdf = normal_parts(pre)
            act = (pre * cdf).astype(jnp.bfloat16)
            ag = dot(g, wo[f], 1, 1)
            pg = (ag * (cdf + pre * pdf)).astype(jnp.bfloat16)
            more, less = dot(act, wo[f], 1, 0), dot(pg, wi[f], 1, 1)
            @pl.when(f == 0)
            def _():
                res_acc[...] = more
                ig_acc[...] = less
            @pl.when(f > 0)
            def _():
                res_acc[...] += more
                ig_acc[...] += less
            @pl.when(j + 1 < blocks)
            def _():
                for c in load(j + 1, f): c.start()
            return 0
        lax.fori_loop(0, chunks, chunk, 0)
        res_send[j] = res_acc[...].reshape(groups, cap, wide).astype(jnp.bfloat16)
        ig_send[j] = ig_acc[...].reshape(groups, cap, wide).astype(jnp.bfloat16)

    def weights(j):
        for c in load_slice(j): c.wait()
        def one(r, _):
            x, g = flat(x_all[j, r]), flat(g_all[j, r])
            pre = dot(x, wis[...], 1, 0) + bias_ref[j, rep]
            cdf, pdf = normal_parts(pre)
            act_all[r] = (pre * cdf).astype(jnp.bfloat16)
            pg_all[r] = (dot(g, wos[...], 1, 1) * (cdf + pre * pdf)).astype(jnp.bfloat16)
            return 0
        lax.fori_loop(0, reps, one, 0)
        @pl.when(j + 1 < blocks)
        def _():
            for c in load_slice(j + 1): c.start()
        @pl.when(j > 0)
        def _():
            for c in out_copies(j - 1): c.wait()
        act, pg = act_all[...].reshape(reps * rows, part), pg_all[...].reshape(reps * rows, part)
        gout_buf[...] = dot(act, flat(g_all[j]), 0, 0)
        gin_buf[...] = dot(flat(x_all[j]), pg, 0, 0)
        gb_ref[j] = jnp.sum(pg.astype(jnp.float32), axis=0, keepdims=True)
        for c in out_copies(j): c.start()

    def step(k, _):
        @pl.when(k < blocks)
        def _():
            for t in range(2):
                for s in range(groups - 1):
                    dispatch(k, t, s).wait_recv()
                own(k, t).wait()
                for n in range(2):
                    across(k, t, n).start()
            if compute:
                own_rows(k)
            else:
                res_send[k] = x_all[k, 0]
                ig_send[k] = g_all[k, 0]
            for t in range(2):
                for s in range(groups - 1):
                    give(k, t, s).start()
                give_own(k, t).start()
        @pl.when((k > 0) & (k <= blocks))
        def _():
            for t in range(2):
                for n in range(2):
                    across(k - 1, t, n).wait_recv()
                for n in range(2):
                    onward(k - 1, t, n).start()
        @pl.when(k > 1)
        def _():
            for t in range(2):
                for n in range(2):
                    onward(k - 2, t, n).wait_recv()
            if compute:
                weights(k - 2)
        return 0
    lax.fori_loop(0, blocks + 2, step, 0)

    if compute:
        for c in out_copies(blocks - 1): c.wait()
    def drain(j, _):
        for t in range(2):
            for s in range(groups - 1):
                give(j, t, s).wait_recv()
                give(j, t, s).wait_send()
                dispatch(j, t, s).wait_send()
            give_own(j, t).wait()
            for n in range(2):
                across(j, t, n).wait_send()
                onward(j, t, n).wait_send()
        return 0
    lax.fori_loop(0, blocks, drain, 0)


def experts_call(x, g, w_in, b_in, w_out, reps, groups, compute=True):
    _, blocks, cap, wide = x.shape
    hidden = w_in.shape[2]
    part = hidden // reps
    anyw = pl.BlockSpec(memory_space=pl.ANY)
    vm = pl.BlockSpec(memory_space=pltpu.VMEM)
    bf, f32 = jnp.bfloat16, jnp.float32
    sem = pltpu.SemaphoreType.DMA
    n = groups - 1
    rows = groups * cap
    return pl.pallas_call(
        functools.partial(experts_kernel, reps, groups, compute),
        out_shape=[jax.ShapeDtypeStruct(x.shape, bf), jax.ShapeDtypeStruct(x.shape, bf),
                   jax.ShapeDtypeStruct((blocks, wide, part), f32), jax.ShapeDtypeStruct((blocks, 1, part), f32),
                   jax.ShapeDtypeStruct((blocks, part, wide), f32)],
        in_specs=[anyw, anyw, anyw, vm, anyw],
        out_specs=[anyw, anyw, anyw, vm, anyw],
        scratch_shapes=[
            pltpu.VMEM((blocks, reps, groups, cap, wide), bf), pltpu.VMEM((blocks, reps, groups, cap, wide), bf),
            pltpu.VMEM((blocks, groups, cap, wide), bf), pltpu.VMEM((blocks, groups, cap, wide), bf),
            pltpu.VMEM((reps, wide, part), bf), pltpu.VMEM((reps, part, wide), bf),
            pltpu.VMEM((wide, part), bf), pltpu.VMEM((part, wide), bf),
            pltpu.VMEM((reps, rows, part), bf), pltpu.VMEM((reps, rows, part), bf),
            pltpu.VMEM((wide, part), f32), pltpu.VMEM((part, wide), f32),
            pltpu.VMEM((rows, wide), f32), pltpu.VMEM((rows, wide), f32), pltpu.VMEM((blocks, reps, 1, part), f32),
            sem((2, blocks)), sem((2, blocks, n)), sem((2, blocks, n)), sem((2, blocks, 4)), sem((2, blocks, 4)),
            sem((2, blocks, n)), sem((2, blocks, n)), sem((2, blocks)), sem((2, reps)), sem((2,)), sem((2,))],
        compiler_params=pltpu.CompilerParams(collective_id=2, has_side_effects=True, vmem_limit_bytes=60 * MIB),
    )(x, g, w_in, b_in, w_out)

def experts_plain(x, g, w_in, b_in, w_out):
    bf, f32 = jnp.bfloat16, jnp.float32
    rx = lax.all_to_all(x, "exp", split_axis=0, concat_axis=0, tiled=True)
    rg = lax.all_to_all(g, "exp", split_axis=0, concat_axis=0, tiled=True)
    pre = jnp.einsum("secd,edf->secf", rx, w_in, preferred_element_type=f32)
    pre = pre + b_in.astype(f32)[None, :, None, :]
    cdf, pdf = normal_parts(pre)
    act = (pre * cdf).astype(bf)
    res = jnp.einsum("secf,efd->secd", act, w_out, preferred_element_type=f32).astype(bf)
    pg = jnp.einsum("secd,efd->secf", rg, w_out, preferred_element_type=f32) * (cdf + pre * pdf)
    pg = pg.astype(bf)
    ig = jnp.einsum("secf,edf->secd", pg, w_in, preferred_element_type=f32).astype(bf)
    gout = jnp.einsum("secf,secd->efd", act, rg, preferred_element_type=f32).astype(bf)
    gin = jnp.einsum("secd,secf->edf", rx, pg, preferred_element_type=f32).astype(bf)
    gb = jnp.sum(pg, axis=(0, 2), dtype=f32).astype(bf)
    return (
        lax.all_to_all(res, "exp", split_axis=0, concat_axis=0, tiled=True),
        lax.all_to_all(ig, "exp", split_axis=0, concat_axis=0, tiled=True),
        lax.psum_scatter(gin, "rep", scatter_dimension=2, tiled=True).astype(f32),
        lax.psum_scatter(gb, "rep", scatter_dimension=1, tiled=True).astype(f32)[:, None],
        lax.psum_scatter(gout, "rep", scatter_dimension=1, tiled=True).astype(f32),
    )


epsilon = 1e-06
masked_score = -1e30


def normalize(values):
    center = values - jnp.mean(values, axis=-1, keepdims=True)
    spread = jnp.mean(center * center, axis=-1, keepdims=True)
    scale = lax.rsqrt(spread + epsilon)
    return center * scale, scale


def normalize_back(grad, unit, scale):
    mean = jnp.mean(grad, axis=-1, keepdims=True)
    along = jnp.mean(grad * unit, axis=-1, keepdims=True)
    return (grad - mean - unit * along) * scale


def two_parts(v):
    high = v.astype(jnp.bfloat16)
    return high, (v - high.astype(jnp.float32)).astype(jnp.bfloat16)


def positions_of(routes, valid_col, priority_col, priority_row, experts):
    length = routes.shape[0]
    f32, bf = jnp.float32, jnp.bfloat16
    token_row = lax.broadcasted_iota(jnp.int32, (length, length), 1)
    token_col = lax.broadcasted_iota(jnp.int32, (length, length), 0)
    rank_col = jnp.sum(
        jnp.where(priority_row == token_col, token_row, 0).astype(f32), axis=1, keepdims=True
    )
    rank_row = jnp.sum(
        jnp.where(priority_col == token_row, token_col, 0).astype(f32), axis=0, keepdims=True
    )
    earlier = (rank_row < rank_col).astype(f32).astype(bf)
    expert_row = lax.broadcasted_iota(jnp.int32, (length, experts), 1)
    ones = [(routes[:, k : k + 1] == expert_row).astype(f32) for k in range(routes.shape[1])]
    before = jnp.zeros((1, experts), f32)
    places = []
    for one in ones:
        live = one * valid_col
        count = dot(earlier, live.astype(bf), 1, 0) + before
        places.append(jnp.sum(count * one, axis=1, keepdims=True))
        before = before + jnp.sum(live, axis=0, keepdims=True)
    return ones, places


def body_plain(
    tokens,
    segments,
    valid,
    routes,
    priority,
    ln1_gain,
    ln1_bias,
    w_query,
    query_bias,
    w_key,
    w_value,
    value_bias,
    w_attn_out,
    attn_out_bias,
    ln2_gain,
    ln2_bias,
    w_router,
    expert_in,
    expert_in_bias,
    expert_out,
    expert_out_bias,
    cotangent,
):
    f32, bf = jnp.float32, jnp.bfloat16
    vectors, weights, router_weight, result_shift = gather_all(
        [ln1_gain, ln1_bias, query_bias, value_bias, attn_out_bias, ln2_gain, ln2_bias],
        [w_query, w_key, w_value, w_attn_out],
        w_router,
        expert_out_bias,
    )
    vectors = [v.astype(f32)[None] for v in vectors]
    gain_one, bias_one, query_shift, value_shift, proj_shift, gain_two, bias_two = vectors
    query_weight, key_weight, value_weight, proj_weight = weights
    length = tokens.shape[1]
    feature_dim = tokens.shape[2]
    head_dim = feature_dim // HEADS
    local_blocks = expert_in.shape[0]
    reps, groups = lax.axis_size("rep"), lax.axis_size("exp")
    experts = EXPERTS
    split = local_blocks * groups // experts
    top_count = routes.shape[2]
    capacity = (105 * top_count * length + 100 * experts - 1) // (100 * experts)
    room = -(-capacity // 8) * 8
    score_scale = head_dim ** (-0.5)
    inputs = tokens[0].astype(f32)
    row_segments = segments[0]
    row_valid = valid[0]
    places = jnp.arange(length, dtype=jnp.int32)
    allowed = (row_segments[:, None] == row_segments[None, :]) & (
        (row_valid[None, :] > 0) | (places[:, None] == places[None, :])
    )
    unit_one, scale_one = normalize(inputs)
    normed = (unit_one * gain_one + bias_one).astype(bf)
    query_rows = (dot(normed, query_weight, 1, 0) + query_shift).astype(bf)
    key_rows = dot(normed, key_weight, 1, 0).astype(bf)
    value_rows = (dot(normed, value_weight, 1, 0) + value_shift).astype(bf)
    query_heads = query_rows.reshape(length, HEADS, head_dim)
    key_heads = key_rows.reshape(length, HEADS, head_dim)
    value_heads = value_rows.reshape(length, HEADS, head_dim)

    def scores():
        return jnp.where(
            allowed[None],
            jnp.einsum("qhd,khd->hqk", query_heads, key_heads, preferred_element_type=f32)
            * score_scale,
            masked_score,
        )

    masked = scores()
    top_score = jnp.max(masked, axis=-1, keepdims=True)
    log_total = top_score + jnp.log(jnp.sum(jnp.exp(masked - top_score), axis=-1, keepdims=True))
    mixed = jnp.einsum(
        "hqk,khd->qhd",
        jnp.exp(masked - log_total).astype(bf),
        value_heads,
        preferred_element_type=f32,
    )
    mixed = mixed.reshape(length, feature_dim).astype(bf)
    residual = inputs + dot(mixed, proj_weight, 1, 0) + proj_shift
    unit_two, scale_two = normalize(residual)
    normed_two = (unit_two * gain_two + bias_two).astype(bf)
    logits = dot(normed_two, router_weight, 1, 0)
    logit_exp = jnp.exp(logits - jnp.max(logits, axis=-1, keepdims=True))
    router_probs = logit_exp / jnp.sum(logit_exp, axis=-1, keepdims=True)
    upstream = cotangent[0].astype(f32)
    ones, positions = positions_of(
        routes[0], row_valid[:, None].astype(f32), priority[0][:, None], priority[0][None], experts
    )
    expert_row = lax.broadcasted_iota(jnp.int32, (1, experts), 1).astype(f32)
    slot_row = lax.broadcasted_iota(jnp.int32, (1, experts * room), 1)
    kept, gates, slots, sent = [], [], [], jnp.zeros((experts * room, feature_dim), f32)
    for one, position in zip(ones, positions):
        keep = row_valid[:, None].astype(f32) * (position < capacity).astype(f32)
        gate = jnp.sum(router_probs * one, axis=1, keepdims=True) * keep
        place = jnp.sum(one * expert_row, axis=1, keepdims=True) * room + position
        place = jnp.where(keep > 0, place, -1.0).astype(jnp.int32)
        hot = (place == slot_row).astype(f32).astype(bf)
        kept.append(one * keep)
        gates.append(gate)
        slots.append(hot)
        sent = sent + dot(hot, (gate * upstream).astype(bf), 0, 0)
    any_slot = slots[0]
    for hot in slots[1:]:
        any_slot = any_slot + hot
    expert_slots = dot(any_slot, normed_two, 0, 0).astype(bf)
    gated = sum(one * gate for one, gate in zip(kept, gates))
    high, low = two_parts(gated)
    shift_grad = dot(high, cotangent[0], 0, 0) + dot(low, cotangent[0], 0, 0)

    def outgoing(v):
        v = v.astype(bf).reshape(experts, room, feature_dim)
        return jnp.repeat(v, split, axis=0).reshape(groups, local_blocks, room, feature_dim)

    moved = experts_plain(
        outgoing(expert_slots), outgoing(sent), expert_in, expert_in_bias, expert_out
    )
    result, slot_back, in_w_grad, in_b_grad, out_w_grad = moved
    result = result.reshape(experts, split, room, feature_dim)
    slot_back = slot_back.reshape(experts, split, room, feature_dim)
    results = [result[:, s].reshape(experts * room, feature_dim) for s in range(split)]
    backs = [slot_back[:, s].reshape(experts * room, feature_dim) for s in range(split)]
    combined, prob_grad = 0.0, 0.0
    for one, gate, hot in zip(kept, gates, slots):
        picked = dot(one.astype(bf), result_shift, 1, 0)
        for part in results:
            picked = picked + dot(hot, part, 1, 0)
        combined = combined + gate * picked
        prob_grad = prob_grad + one * jnp.sum(upstream * picked, axis=1, keepdims=True)
    output = residual + combined
    logit_grad = (
        router_probs * (prob_grad - jnp.sum(router_probs * prob_grad, axis=-1, keepdims=True))
    ).astype(bf)
    router_w_grad = dot(normed_two, logit_grad, 0, 0)
    normed_two_grad = dot(logit_grad, router_weight, 1, 1)
    for part in backs:
        normed_two_grad = normed_two_grad + dot(any_slot, part, 1, 0)
    gain_two_grad = jnp.sum(normed_two_grad * unit_two, axis=0)
    bias_two_grad = jnp.sum(normed_two_grad, axis=0)
    residual_grad = upstream + normalize_back(normed_two_grad * gain_two, unit_two, scale_two)
    branch_grad = residual_grad.astype(bf)
    proj_w_grad = dot(mixed, branch_grad, 0, 0)
    proj_b_grad = jnp.sum(branch_grad, axis=0, dtype=f32)
    mixed_grad = dot(branch_grad, proj_weight, 1, 1).astype(bf)
    mixed_grad = mixed_grad.reshape(length, HEADS, head_dim)
    again_probs = jnp.exp(scores() - log_total)
    prob_grads = jnp.einsum("qhd,khd->hqk", mixed_grad, value_heads, preferred_element_type=f32)
    value_grad = jnp.einsum(
        "hqk,qhd->khd", again_probs.astype(bf), mixed_grad, preferred_element_type=f32
    )
    value_grad = value_grad.astype(bf).reshape(length, feature_dim)
    inner_sum = jnp.sum(again_probs * prob_grads, axis=-1, keepdims=True)
    score_grad = (again_probs * (prob_grads - inner_sum)).astype(bf)
    query_grad = jnp.einsum("hqk,khd->qhd", score_grad, key_heads, preferred_element_type=f32)
    query_grad = (query_grad * score_scale).astype(bf).reshape(length, feature_dim)
    key_grad = jnp.einsum("hqk,qhd->khd", score_grad, query_heads, preferred_element_type=f32)
    key_grad = (key_grad * score_scale).astype(bf).reshape(length, feature_dim)
    query_w_grad = dot(normed, query_grad, 0, 0)
    query_b_grad = jnp.sum(query_grad, axis=0, dtype=f32)
    key_w_grad = dot(normed, key_grad, 0, 0)
    value_w_grad = dot(normed, value_grad, 0, 0)
    value_b_grad = jnp.sum(value_grad, axis=0, dtype=f32)
    normed_grad = dot(query_grad, query_weight, 1, 1)
    normed_grad = normed_grad + dot(key_grad, key_weight, 1, 1)
    normed_grad = normed_grad + dot(value_grad, value_weight, 1, 1)
    gain_one_grad = jnp.sum(normed_grad * unit_one, axis=0)
    bias_one_grad = jnp.sum(normed_grad, axis=0)
    tokens_grad = residual_grad + normalize_back(normed_grad * gain_one, unit_one, scale_one)
    vector_sums, weight_sums, router_sum, shift_sum = scatter_all(
        [
            gain_one_grad,
            bias_one_grad,
            query_b_grad,
            value_b_grad,
            proj_b_grad,
            gain_two_grad,
            bias_two_grad,
        ],
        [query_w_grad, key_w_grad, value_w_grad, proj_w_grad],
        router_w_grad,
        shift_grad,
    )
    return (
        output.astype(jnp.bfloat16)[None],
        tokens_grad[None],
        vector_sums[0],
        vector_sums[1],
        weight_sums[0],
        vector_sums[2],
        weight_sums[1],
        weight_sums[2],
        vector_sums[3],
        weight_sums[3],
        vector_sums[4],
        vector_sums[5],
        vector_sums[6],
        router_sum,
        in_w_grad,
        in_b_grad[:, 0],
        out_w_grad,
        shift_sum,
    )


def eye_of(n):
    same = lax.broadcasted_iota(jnp.int32, (n, n), 0) == lax.broadcasted_iota(jnp.int32, (n, n), 1)
    return same.astype(jnp.float32).astype(jnp.bfloat16)


def lanes_of(n=1):
    return lax.broadcasted_iota(jnp.int32, (n, 128), 1)


def mask_of(ints, cols):
    n = ints.shape[1]
    same = lax.broadcasted_iota(jnp.int32, (n, n), 0) == lax.broadcasted_iota(jnp.int32, (n, n), 1)
    near = cols[:, 0:1] == ints[0:1]
    open_key = jnp.where(same, 1.0, cols[:, 1:2]) > 0
    return jnp.where(near & open_key, 0.0, masked_score)


def side_masks(head_dim):
    lane = lanes_of()
    return [
        ((lane >= s * head_dim) & (lane < (s + 1) * head_dim)).astype(jnp.float32).astype(jnp.bfloat16)
        for s in range(128 // head_dim)
    ]


def vectors_of(small_ref):
    f32, bf = jnp.float32, jnp.bfloat16
    reps, groups, lines, _ = small_ref.shape
    count = reps * groups
    per = lines - 8
    tail = small_ref[...].astype(f32)[:, :, per:].reshape(count * 8, 128).astype(bf)
    wide = count * per
    spread = lax.broadcasted_iota(jnp.int32, (128, wide), 1) % per
    spread = (spread == lax.broadcasted_iota(jnp.int32, (128, wide), 0)).astype(f32).astype(bf)
    laid = dot(tail, spread, 1, 0)
    owner = lax.broadcasted_iota(jnp.int32, (count * 8, wide), 1) // per
    mine = owner == lax.broadcasted_iota(jnp.int32, (count * 8, wide), 0) // 8
    pick = lax.broadcasted_iota(jnp.int32, (8, count * 8), 1) % 8
    pick = (pick == lax.broadcasted_iota(jnp.int32, (8, count * 8), 0)).astype(f32).astype(bf)
    rows = dot(pick, jnp.where(mine, laid, 0.0).astype(bf), 1, 0)
    return [rows[i : i + 1] for i in range(7)]


def matrix_of(small_ref):
    reps, groups, lines, _ = small_ref.shape
    per = lines - 8
    part = small_ref[...].astype(jnp.float32)[:, :, :per]
    return part.reshape(reps * groups * per, 128).astype(jnp.bfloat16)


def weight_of(ref):
    wide = ref.shape[-1]
    return ref.astype(jnp.float32).reshape(-1, wide).astype(jnp.bfloat16)


def integer_rows(raw):
    raw = raw.astype(jnp.float32)
    line = lax.broadcasted_iota(jnp.int32, raw.shape, 0)
    order = raw[2:3]
    high = jnp.floor(order * (1.0 / 64.0))
    low = order - high * 64.0
    return jnp.where(line == 2, high, jnp.where(line == 5, low, raw)), order


def front_kernel(
    capacity,
    room,
    head_dim,
    tokens_ref,
    cot_ref,
    ints_ref,
    small_in,
    wq_in,
    wk_in,
    wv_in,
    wo_in,
    xs_ref,
    gs_ref,
    resid_ref,
    q_ref,
    k_ref,
    v_ref,
    mixed_ref,
    lse_ref,
    info_ref,
    wa_ref,
    wo_ref,
    small_ref,
    mask_ref,
    a2_ref,
    sent_ref,
    own_sem,
    send_sem,
    recv_sem,
):
    f32, bf = jnp.float32, jnp.bfloat16
    length, wide = tokens_ref.shape
    groups, blocks = xs_ref.shape[:2]
    me, rep = lax.axis_index("exp"), lax.axis_index("rep")
    level, core = me // 2, me % 2
    levels = groups // 2
    beside = (rep + 1 - 2 * (rep % 2), rep + 2 - 4 * ((rep // 2) % 2))
    bufs = (wa_ref, small_ref, wo_ref)
    mine = [
        pltpu.make_async_copy(wq_in, wa_ref.at[rep, me, 0], own_sem.at[0]),
        pltpu.make_async_copy(wk_in, wa_ref.at[rep, me, 1], own_sem.at[1]),
        pltpu.make_async_copy(wv_in, wa_ref.at[rep, me, 2], own_sem.at[2]),
        pltpu.make_async_copy(small_in, small_ref.at[rep, me], own_sem.at[3]),
        pltpu.make_async_copy(wo_in, wo_ref.at[rep, me], own_sem.at[4]),
    ]
    for c in mine:
        c.start()

    def block(r):
        return lax.rem(level - r + levels, levels) * 2 + core

    def send(src, a, r, n, device):
        return pltpu.make_async_remote_copy(
            src, src, send_sem.at[a, r, n], recv_sem.at[a, r, n], device_id=device, device_id_type=MESH
        )

    def up(a, r):
        return send(bufs[a].at[rep, me], a, r, 0, (rep, lax.rem(level + r, levels) * 2 + core))

    def aside(a, r, n):
        return send(bufs[a].at[rep, block(r)], a, r, 1 + n, (beside[n], me))

    def onward(a, r, n):
        ref = bufs[a].at[beside[n], block(r)]
        if a == 1:
            half = ref.shape[0] // 2
            ref = ref.at[pl.ds(n * half, half)]
        else:
            half = wide // 2
            ref = ref.at[(slice(None),) * (len(ref.shape) - 1) + (pl.ds(n * half, half),)]
        return send(ref, a, r, 3 + n, (beside[1 - n], me))

    def over(a, r):
        return send(bufs[a].at[:, block(r)], a, r, 5, (rep, me + 1 - 2 * core))

    barrier = pltpu.get_barrier_semaphore()
    for r in range(1, levels):
        there = (rep, lax.rem(level + r, levels) * 2 + core)
        pl.semaphore_signal(barrier, inc=1, device_id=there, device_id_type=MESH)
    for n in beside:
        pl.semaphore_signal(barrier, inc=1, device_id=(n, me), device_id_type=MESH)
    pl.semaphore_signal(barrier, inc=1, device_id=(rep, me + 1 - 2 * core), device_id_type=MESH)
    pl.semaphore_wait(barrier, levels + 2)
    for c in mine:
        c.wait()

    def step(sets, r):
        for a in sets:
            if 0 < r < levels:
                up(a, r).wait_recv()
            if r < levels:
                for n in range(2):
                    aside(a, r, n).start()
            if 0 < r <= levels:
                for n in range(2):
                    aside(a, r - 1, n).wait_recv()
                for n in range(2):
                    onward(a, r - 1, n).start()
            if 1 < r <= levels + 1:
                for n in range(2):
                    onward(a, r - 2, n).wait_recv()
                over(a, r - 2).start()

    early, late = (0, 1), (2,)
    for a in early + late:
        for r in range(1, levels):
            up(a, r).start()
    step(early, 0)
    ints, priority_row = integer_rows(ints_ref[...])
    eye = eye_of(length)
    cols = dot(eye, ints.astype(bf), 1, 1)
    mask_ref[...] = mask_of(ints, cols)
    inputs = tokens_ref[...].astype(f32)
    unit_one, _ = normalize(inputs)
    step(early, 1)
    token_row = lax.broadcasted_iota(jnp.int32, (length, length), 1).astype(f32)
    token_col = lax.broadcasted_iota(jnp.int32, (length, length), 0).astype(f32)
    priority_col = cols[:, 2:3] * 64.0 + cols[:, 5:6]
    rank_col = jnp.sum(jnp.where(priority_row == token_col, token_row, 0.0), axis=1, keepdims=True)
    rank_row = jnp.sum(jnp.where(priority_col == token_row, token_col, 0.0), axis=0, keepdims=True)
    step(early, 2)
    earlier = (rank_row < rank_col).astype(f32).astype(bf)
    lane = lanes_of()
    expert_lane = (lane - 32).astype(f32)
    valid_col = cols[:, 1:2]
    before = jnp.zeros((1, 128), f32)
    places = []
    for k in range(2):
        one = (cols[:, 3 + k : 4 + k] == expert_lane).astype(f32)
        live = one * valid_col
        count = dot(earlier, live.astype(bf), 1, 0) + before
        before = before + jnp.sum(live, axis=0, keepdims=True)
        places.append(jnp.sum(count * one, axis=1, keepdims=True))
    for r in range(3, levels + 2):
        step(early, r)
    for r in range(levels):
        step(late, r)
    for a in early:
        for r in range(levels):
            over(a, r).wait_recv()
    small_matrix = matrix_of(small_ref)
    gain_one, bias_one, query_shift, value_shift, proj_shift, gain_two, bias_two = vectors_of(small_ref)
    normed = (unit_one * gain_one + bias_one).astype(bf)
    q_ref[...] = (dot(normed, weight_of(wa_ref[:, :, 0]), 1, 0) + query_shift).astype(bf)
    k_ref[...] = dot(normed, weight_of(wa_ref[:, :, 1]), 1, 0).astype(bf)
    v_ref[...] = (dot(normed, weight_of(wa_ref[:, :, 2]), 1, 0) + value_shift).astype(bf)
    step(late, levels)
    sides = side_masks(head_dim)
    per = len(sides)
    scale = jnp.full((1, 128), head_dim**-0.5, f32).astype(bf)

    def heads(h, _):
        at = pl.ds(pl.multiple_of(h * 128, 128), 128)
        query = q_ref[:, at] * scale
        total = jnp.zeros((128, length), f32)
        for s, side in enumerate(sides):
            score = dot(k_ref[:, at] * side, query, 1, 1) + mask_ref[...]
            top = jnp.max(score, axis=0, keepdims=True)
            expo = jnp.exp(score - top)
            norm = jnp.sum(expo, axis=0, keepdims=True)
            lse_ref[pl.ds(h * per + s, 1), :] = top + jnp.log(norm)
            probs = (expo * (1.0 / norm)).astype(bf)
            total = total + dot(v_ref[:, at] * side, probs, 0, 0)
        mixed_ref[at, :] = total.astype(bf)
        return 0

    half = wide // 256
    lax.fori_loop(0, half, heads, 0)
    step(late, levels + 1)
    lax.fori_loop(half, wide // 128, heads, 0)
    for r in range(levels):
        over(2, r).wait_recv()
    residual = inputs + dot(mixed_ref[...], weight_of(wo_ref[...]), 0, 0) + proj_shift
    resid_ref[...] = residual
    unit_two, _ = normalize(residual)
    normed_two = (unit_two * gain_two + bias_two).astype(bf)
    a2_ref[...] = normed_two
    routed = (lane >= 32) & (lane < 64)
    logits = jnp.where(routed, dot(normed_two, small_matrix, 1, 0), masked_score)
    logit_exp = jnp.exp(logits - jnp.max(logits, axis=1, keepdims=True))
    probs = logit_exp / jnp.sum(logit_exp, axis=1, keepdims=True)
    info = probs
    marks = jnp.zeros((length, 128), f32)
    upstream = cot_ref[...].astype(f32)
    for k in range(2):
        expert, position = cols[:, 3 + k : 4 + k], places[k]
        one = (expert == expert_lane).astype(f32)
        keep = valid_col * (position < capacity).astype(f32)
        gate = jnp.sum(probs * one, axis=1, keepdims=True) * keep
        place = jnp.where(keep > 0, expert * room + position, -1.0)
        high = jnp.floor(place * (1.0 / 32.0))
        low = place - high * 32.0
        marks = jnp.where(lane == 2 * k, high, jnp.where(lane == 2 * k + 1, low, marks))
        info = jnp.where(lane == k, place, jnp.where(lane == 2 + k, expert, info))
        sent_ref[k] = (gate * upstream).astype(bf)
    info_ref[...] = info
    turned = dot(marks.astype(bf), eye, 0, 0)
    place_rows = [turned[2 * k : 2 * k + 1] * 32.0 + turned[2 * k + 1 : 2 * k + 2] for k in range(2)]
    part = blocks * room
    slot = lax.broadcasted_iota(jnp.int32, (part, length), 0).astype(f32)

    def fill(d, _):
        first = (d * part).astype(f32)
        hots = [(slot == row - first).astype(f32).astype(bf) for row in place_rows]
        inside = dot(hots[0] + hots[1], a2_ref[...], 1, 0)
        xs_ref[d] = inside.reshape(blocks, room, wide).astype(bf)
        grads = dot(hots[0], sent_ref[0], 1, 0) + dot(hots[1], sent_ref[1], 1, 0)
        gs_ref[d] = grads.reshape(blocks, room, wide).astype(bf)
        return 0

    lax.fori_loop(0, groups, fill, 0)
    for a in early + late:
        for r in range(levels):
            if r > 0:
                up(a, r).wait_send()
            for n in range(2):
                aside(a, r, n).wait_send()
                onward(a, r, n).wait_send()
            over(a, r).wait_send()


def back_kernel(
    head_dim,
    tokens_ref,
    cot_ref,
    ints_ref,
    small_ref,
    wa_ref,
    wo_ref,
    res_ref,
    ig_ref,
    resid_ref,
    q_ref,
    k_ref,
    v_ref,
    mixed_ref,
    lse_ref,
    info_ref,
    gin_ref,
    gout_ref,
    out_ref,
    tokens_grad_ref,
    wq_grad_ref,
    wk_grad_ref,
    wv_grad_ref,
    wo_grad_ref,
    small_grad_ref,
    gin_out_ref,
    gout_out_ref,
    mask_ref,
    mixed_grad_ref,
    query_grad_ref,
    key_grad_ref,
    value_grad_ref,
    gin_buf,
    gout_buf,
    sem,
):
    f32, bf = jnp.float32, jnp.bfloat16
    length, wide = tokens_ref.shape
    slots = res_ref.shape[0]
    pieces = gin_ref.shape[0]
    carried = ((gin_ref, gin_buf, gin_out_ref), (gout_ref, gout_buf, gout_out_ref))

    def loads(j):
        return [
            pltpu.make_async_copy(src.at[j], buf, sem.at[0, i])
            for i, (src, buf, _) in enumerate(carried)
        ]

    def stores(j):
        return [
            pltpu.make_async_copy(buf, dst.at[j], sem.at[1, i])
            for i, (_, buf, dst) in enumerate(carried)
        ]

    for c in loads(0):
        c.start()
    ints, _ = integer_rows(ints_ref[...])
    cols = dot(eye_of(length), ints.astype(bf), 1, 1)
    mask_ref[...] = mask_of(ints, cols)
    small = matrix_of(small_ref)
    gain_one, bias_one, _, _, _, gain_two, bias_two = vectors_of(small_ref)
    lane = lanes_of()
    routed = ((lane >= 32) & (lane < 64)).astype(f32)
    info = info_ref[...]
    probs = info * routed
    upstream = cot_ref[...].astype(f32)
    slot_row = lax.broadcasted_iota(jnp.int32, (1, slots), 1).astype(f32)
    expert_lane = (lane - 32).astype(f32)
    residual = resid_ref[...]
    combined = residual
    prob_grad = jnp.zeros((length, 128), f32)
    gated = jnp.zeros((length, 128), f32)
    hots = []
    for k in range(2):
        place, expert = info[:, k : k + 1], info[:, 2 + k : 3 + k]
        kept = (expert == expert_lane).astype(f32) * (place >= 0).astype(f32)
        gate = jnp.sum(probs * kept, axis=1, keepdims=True)
        hot = (place == slot_row).astype(f32).astype(bf)
        hots.append(hot)
        picked = dot(hot, res_ref[...], 1, 0)
        picked = picked + dot(pltpu.roll(kept, 96, 1).astype(bf), small, 1, 1)
        combined = combined + gate * picked
        prob_grad = prob_grad + kept * jnp.sum(upstream * picked, axis=1, keepdims=True)
        gated = gated + kept * gate
    out_ref[...] = combined.astype(bf)
    inner = jnp.sum(probs * prob_grad, axis=1, keepdims=True)
    logit_grad = (probs * (prob_grad - inner)).astype(bf)
    unit_two, scale_two = normalize(residual)
    normed_two = (unit_two * gain_two + bias_two).astype(bf)
    high, low = two_parts(pltpu.roll(gated, 96, 1))
    small_grad = dot(normed_two, logit_grad, 0, 0)
    small_grad = small_grad + dot(cot_ref[...], high, 0, 0) + dot(cot_ref[...], low, 0, 0)
    normed_two_grad = dot(hots[0] + hots[1], ig_ref[...], 1, 0) + dot(logit_grad, small, 1, 1)
    vector_grads = {}
    vector_grads[5] = jnp.sum(normed_two_grad * unit_two, axis=0, keepdims=True)
    vector_grads[6] = jnp.sum(normed_two_grad, axis=0, keepdims=True)
    residual_grad = upstream + normalize_back(normed_two_grad * gain_two, unit_two, scale_two)
    tokens_grad_ref[...] = residual_grad
    branch_grad = residual_grad.astype(bf)
    wo_grad_ref[...] = dot(mixed_ref[...], branch_grad, 1, 0)
    vector_grads[4] = jnp.sum(branch_grad.astype(f32), axis=0, keepdims=True)
    mixed_grad_ref[...] = dot(branch_grad, weight_of(wo_ref[...]), 1, 1).astype(bf)
    sides = side_masks(head_dim)
    per = len(sides)
    scale = jnp.full((1, 128), head_dim**-0.5, f32).astype(bf)

    def heads(h, _):
        at = pl.ds(pl.multiple_of(h * 128, 128), 128)
        query = q_ref[:, at] * scale
        mixed_grad = mixed_grad_ref[:, at]

        @pl.when(h < pieces)
        def _():
            for c in loads(h):
                c.wait()
            for c in stores(h):
                c.start()

        query_total = jnp.zeros((128, length), f32)
        key_total = jnp.zeros((length, 128), f32)
        value_total = jnp.zeros((length, 128), f32)
        for s, side in enumerate(sides):
            key = k_ref[:, at] * side
            score = dot(key, query, 1, 1) + mask_ref[...]
            probs = jnp.exp(score - lse_ref[pl.ds(h * per + s, 1), :])
            prob_grads = dot(v_ref[:, at] * side, mixed_grad, 1, 1)
            inner = jnp.sum(probs * prob_grads, axis=0, keepdims=True)
            score_grad = (probs * (prob_grads - inner)).astype(bf)
            value_total = value_total + dot(probs.astype(bf), mixed_grad * side, 1, 0)
            key_total = key_total + dot(score_grad, query * side, 1, 0)
            query_total = query_total + dot(key * scale, score_grad, 0, 0)
        @pl.when(h < pieces)
        def _():
            for c in stores(h):
                c.wait()

        @pl.when(h + 1 < pieces)
        def _():
            for c in loads(h + 1):
                c.start()

        query_grad_ref[:, at] = jnp.transpose(query_total).astype(bf)
        key_grad_ref[:, at] = key_total.astype(bf)
        value_grad_ref[:, at] = value_total.astype(bf)
        return 0

    lax.fori_loop(0, wide // 128, heads, 0)
    inputs = tokens_ref[...].astype(f32)
    unit_one, scale_one = normalize(inputs)
    normed = (unit_one * gain_one + bias_one).astype(bf)
    wq_grad_ref[...] = dot(normed, query_grad_ref[...], 0, 0)
    wk_grad_ref[...] = dot(normed, key_grad_ref[...], 0, 0)
    wv_grad_ref[...] = dot(normed, value_grad_ref[...], 0, 0)
    vector_grads[2] = jnp.sum(query_grad_ref[...].astype(f32), axis=0, keepdims=True)
    vector_grads[3] = jnp.sum(value_grad_ref[...].astype(f32), axis=0, keepdims=True)
    normed_grad = dot(query_grad_ref[...], weight_of(wa_ref[:, :, 0]), 1, 1)
    normed_grad = normed_grad + dot(key_grad_ref[...], weight_of(wa_ref[:, :, 1]), 1, 1)
    normed_grad = normed_grad + dot(value_grad_ref[...], weight_of(wa_ref[:, :, 2]), 1, 1)
    vector_grads[0] = jnp.sum(normed_grad * unit_one, axis=0, keepdims=True)
    vector_grads[1] = jnp.sum(normed_grad, axis=0, keepdims=True)
    tokens_grad_ref[...] += normalize_back(normed_grad * gain_one, unit_one, scale_one)
    line = lax.broadcasted_iota(jnp.int32, (128, wide), 0)
    stacked = jnp.zeros((128, wide), f32)
    for i in range(7):
        stacked = jnp.where(line == 64 + i, vector_grads[i], stacked)
    small_grad_ref[...] = small_grad + jnp.transpose(stacked)


def front_call(capacity, room, groups, blocks, tokens, cot, ints, small, weights, reps):
    f32, bf = jnp.float32, jnp.bfloat16
    length, wide = tokens.shape
    shape = jax.ShapeDtypeStruct
    vm = pl.BlockSpec(memory_space=pltpu.VMEM)
    slots = shape((groups, blocks, room, wide), bf)
    line = shape((length, wide), bf)
    outs = [slots, slots, shape((length, wide), f32), line, line, line]
    outs += [shape((wide, length), bf), shape((16, length), f32), shape((length, 128), f32)]
    per = weights[0].shape[0]
    outs += [shape((reps, groups, 3, per, wide), bf), shape((reps, groups, per, wide), bf)]
    outs += [shape((reps, groups) + small.shape, bf)]
    sems = pltpu.SemaphoreType.DMA((3, groups // 2, 6))
    return pl.pallas_call(
        functools.partial(front_kernel, capacity, room, wide // HEADS),
        out_shape=outs,
        in_specs=[vm] * 8,
        out_specs=[vm] * len(outs),
        scratch_shapes=[
            pltpu.VMEM((length, length), f32),
            pltpu.VMEM((length, wide), bf),
            pltpu.VMEM((2, length, wide), bf),
            pltpu.SemaphoreType.DMA((5,)),
            sems,
            sems,
        ],
        compiler_params=pltpu.CompilerParams(
            collective_id=0, has_side_effects=True, vmem_limit_bytes=60 * MIB
        ),
    )(tokens, cot, ints, small, *weights)


def back_call(tokens, cot, ints, small, weights, res, ig, kept, gin, gout):
    f32, bf = jnp.float32, jnp.bfloat16
    length, wide = tokens.shape
    shape = jax.ShapeDtypeStruct
    vm = pl.BlockSpec(memory_space=pltpu.VMEM)
    hbm = pl.BlockSpec(memory_space=pl.ANY)
    square = shape((wide, wide), f32)
    outs = [shape((length, wide), bf), shape((length, wide), f32)] + [square] * 4
    outs += [shape((wide, 128), f32), shape(gin.shape, f32), shape(gout.shape, f32)]
    line = pltpu.VMEM((length, wide), bf)
    return pl.pallas_call(
        functools.partial(back_kernel, wide // HEADS),
        out_shape=outs,
        in_specs=[vm] * 15 + [hbm] * 2,
        out_specs=[vm] * 7 + [hbm] * 2,
        scratch_shapes=[
            pltpu.VMEM((length, length), f32),
            line,
            line,
            line,
            line,
            pltpu.VMEM(gin.shape[1:], f32),
            pltpu.VMEM(gout.shape[1:], f32),
            pltpu.SemaphoreType.DMA((2, 2)),
        ],
        compiler_params=pltpu.CompilerParams(vmem_limit_bytes=60 * MIB),
    )(tokens, cot, ints, small, *weights, res, ig, *kept, gin, gout)


def body_fast(
    tokens,
    segments,
    valid,
    routes,
    priority,
    ln1_gain,
    ln1_bias,
    w_query,
    query_bias,
    w_key,
    w_value,
    value_bias,
    w_attn_out,
    attn_out_bias,
    ln2_gain,
    ln2_bias,
    w_router,
    expert_in,
    expert_in_bias,
    expert_out,
    expert_out_bias,
    cotangent,
):
    reps, groups = lax.axis_size("rep"), lax.axis_size("exp")
    devices = reps * groups
    length, wide = tokens.shape[1:]
    per = w_query.shape[0]
    blocks = expert_in.shape[0]
    capacity, room = capacity_of(routes.shape[2], length)
    vectors = [ln1_gain, ln1_bias, query_bias, value_bias, attn_out_bias, ln2_gain, ln2_bias]
    small = jnp.concatenate([expert_out_bias.T, w_router], axis=1)
    small = jnp.pad(small, ((0, 0), (0, 128 - small.shape[1])))
    vectors = jnp.pad(jnp.stack(vectors), ((0, 1), (0, 128 - per)))
    small = jnp.concatenate([small, vectors], axis=0)
    ints = jnp.concatenate([segments, valid, priority, routes[0].T], axis=0)
    ints = jnp.pad(ints, ((0, 3), (0, 0)))
    weights = [w_query, w_key, w_value, w_attn_out]
    xs, gs, *kept, wa, wo, small = front_call(
        capacity, room, groups, blocks, tokens[0], cotangent[0], ints, small, weights, reps
    )
    weights = [wa, wo]
    res, ig, gin, gb, gout = experts_call(
        xs, gs, expert_in, expert_in_bias, expert_out, reps, groups
    )
    slots = groups * blocks * room
    output, tokens_grad, *grads, small_grad, gin, gout = back_call(
        tokens[0],
        cotangent[0],
        ints,
        small,
        weights,
        res.reshape(slots, wide),
        ig.reshape(slots, wide),
        kept,
        gin,
        gout,
    )
    sums, last = scatter_grads(grads, small_grad.reshape(devices, per, 128), reps, groups)
    columns = [last[:, 64 + i] for i in range(7)]
    return (
        output[None],
        tokens_grad[None],
        columns[0],
        columns[1],
        sums[0],
        columns[2],
        sums[1],
        sums[2],
        columns[3],
        sums[3],
        columns[4],
        columns[5],
        columns[6],
        last[:, 32:64],
        gin,
        gb[:, 0],
        gout,
        last[:, :32].T,
    )


def capacity_of(top_count, length):
    capacity = (105 * top_count * length + 100 * EXPERTS - 1) // (100 * EXPERTS)
    return capacity, -(-capacity // 8) * 8


def body(*args):
    routes, w_query, expert_in = args[3], args[7], args[17]
    reps, groups = lax.axis_size("rep"), lax.axis_size("exp")
    _, room = capacity_of(routes.shape[2], routes.shape[1])
    wide = w_query.shape[1]
    suits = (
        reps == 4
        and groups & (groups - 1) == 0
        and groups > 2
        and w_query.shape[0] % 8 == 0
        and w_query.shape[0] <= 128
        and groups * room <= 512
        and groups * expert_in.shape[0] == EXPERTS == 32
        and expert_in.shape[2] % (128 * reps) == 0
        and routes.shape[2] == 2
        and routes.shape[1] <= 64 * 256
        and 128 % (wide // HEADS) == 0
        and HEADS <= 16
        and expert_in.shape[0] < wide // 128
    )
    return body_fast(*args) if suits else body_plain(*args)


def solution(mesh):
    in_specs = (
        P(("rep", "exp"), None, None),
        P(("rep", "exp"), None),
        P(("rep", "exp"), None),
        P(("rep", "exp"), None, None),
        P(("rep", "exp"), None),
        P(("rep", "exp")),
        P(("rep", "exp")),
        P(("rep", "exp"), None),
        P(("rep", "exp")),
        P(("rep", "exp"), None),
        P(("rep", "exp"), None),
        P(("rep", "exp")),
        P(("rep", "exp"), None),
        P(("rep", "exp")),
        P(("rep", "exp")),
        P(("rep", "exp")),
        P(("rep", "exp"), None),
        P("exp", None, None),
        P("exp", None),
        P("exp", None, None),
        P(None, ("rep", "exp")),
        P(("rep", "exp"), None, None),
    )
    out_specs = (
        P(("rep", "exp"), None, None),
        P(("rep", "exp"), None, None),
        P(("rep", "exp")),
        P(("rep", "exp")),
        P(("rep", "exp"), None),
        P(("rep", "exp")),
        P(("rep", "exp"), None),
        P(("rep", "exp"), None),
        P(("rep", "exp")),
        P(("rep", "exp"), None),
        P(("rep", "exp")),
        P(("rep", "exp")),
        P(("rep", "exp")),
        P(("rep", "exp"), None),
        P("exp", None, "rep"),
        P("exp", "rep"),
        P("exp", "rep", None),
        P(None, ("rep", "exp")),
    )
    return jax.shard_map(body, mesh=mesh, in_specs=in_specs, out_specs=out_specs, check_vma=False)
```

```python
import functools
import jax
import jax.numpy as jnp
from jax import lax
from jax.experimental import pallas as pl
from jax.experimental.pallas import tpu as pltpu
from jax.sharding import PartitionSpec as P

HEADS = 12
EXPERTS = 32
MESH = pl.DeviceIdType.MESH
MIB = 1 << 20

def bit_dims(reps, groups):
    rb, gb = reps.bit_length() - 1, groups.bit_length() - 1
    return [(0, 1 << k) for k in reversed(range(rb))] + [(1, 1 << k) for k in reversed(range(gb))]

def orders(dims):
    last = len(dims) - 1
    rep = [i for i, d in enumerate(dims) if d[0] == 0]
    exp = [i for i, d in enumerate(dims) if d[0] == 1 and i != last]
    exp = exp[::-1]
    return [[last] + rep + exp, [last] + rep[::-1] + exp, [last] + exp + rep]

def my_bits(dims):
    at = (lax.axis_index("rep"), lax.axis_index("exp"))
    return [(at[a] // s) % 2 for a, s in dims], at

def partner(dims, at, i):
    a, s = dims[i]
    bit = (at[a] // s) % 2
    there = at[a] + (1 - 2 * bit) * s
    return (there, at[1]) if a == 0 else (at[0], there)

def greet(dims, at):
    barrier = pltpu.get_barrier_semaphore()
    for i in range(len(dims)):
        pl.semaphore_signal(barrier, inc=1, device_id=partner(dims, at, i), device_id_type=MESH)
    pl.semaphore_wait(barrier, len(dims))

def scatter_kernel(dims, widths, count, *refs):
    ins, small_in = refs[:count], refs[count]
    outs, small_out = refs[count + 1], refs[count + 2]
    n = len(dims)
    scr = refs[count + 3:]
    parts = 3
    send_sem, recv_sem = scr[:2]
    scr = scr[2:]
    take = iter(scr)
    bufs = [[(next(take), next(take), next(take) if k < n - 1 else None) for p in range(parts)] for k in range(n)]
    smalls = [(next(take), next(take) if k < n - 1 else None) for k in range(n)]
    bits, at = my_bits(dims)
    plan = orders(dims)
    left = [list(range(n)) for _ in range(parts)]
    small_left = list(range(n))
    small_cur = small_in
    def split(have, i, b):
        return tuple(b if j == i else slice(None) for j in have)
    live = []
    def begin(k, p):
        i = plan[p][k]
        sb, rb, _ = bufs[k][p]
        far = split(left[p], i, 1 - bits[i])
        cols = pl.ds(widths[p][0], widths[p][1]) if k == 0 else slice(None)
        for a in range(count):
            src = ins[a][far + (slice(None), cols)] if k == 0 else bufs[k - 1][p][2][(a,) + far]
            sb[a] = src.astype(sb.dtype)
        c = [pltpu.make_async_remote_copy(sb, rb, send_sem.at[k, p], recv_sem.at[k, p], device_id=partner(dims, at, i), device_id_type=MESH)]
        if p == 0:
            src = (small_in if k == 0 else smalls[k - 1][1]).at[far]
            c.append(pltpu.make_async_remote_copy(src, smalls[k][0], send_sem.at[k, parts], recv_sem.at[k, parts], device_id=partner(dims, at, i), device_id_type=MESH))
        for x in c: x.start()
        return c
    def finish(k, p, c):
        i = plan[p][k]
        sb, rb, acc = bufs[k][p]
        near = split(left[p], i, bits[i])
        cols = pl.ds(widths[p][0], widths[p][1]) if k == 0 else slice(None)
        for x in c: x.wait_recv()
        for a in range(count):
            src = ins[a][near + (slice(None), cols)] if k == 0 else bufs[k - 1][p][2][(a,) + near]
            tot = src + rb[a].astype(jnp.float32)
            if k < n - 1:
                acc[a] = tot
            else:
                outs[a, :, widths[p][0]:widths[p][0] + widths[p][1]] = tot
        if p == 0:
            src = (small_in if k == 0 else smalls[k - 1][1])[near]
            tot = src + smalls[k][0][...]
            if k < n - 1:
                smalls[k][1][...] = tot
            else:
                small_out[...] = tot
        left[p].remove(i)
    greet(dims, at)
    live = [begin(0, p) for p in range(parts)]
    every = list(live)
    for k in range(n):
        for p in range(parts):
            finish(k, p, live[p])
            if k < n - 1:
                live[p] = begin(k + 1, p)
                every.append(live[p])
    for cs in every:
        for c in cs: c.wait_send()

def scatter_grads(grads, small, reps, groups, link=jnp.bfloat16):
    dims = bit_dims(reps, groups)
    n = len(dims)
    full, cols = grads[0].shape
    rows = full // (reps * groups)
    third = cols // 3 // 128 * 128
    widths = [(0, third), (third, third), (2 * third, cols - 2 * third)]
    count = len(grads)
    lead = (2,) * n
    grads = [g.reshape(lead + (rows, cols)) for g in grads]
    small = small.reshape(lead + small.shape[1:])
    scratch = [pltpu.SemaphoreType.DMA((n, 4)), pltpu.SemaphoreType.DMA((n, 4))]
    for k in range(n):
        for p in range(3):
            shape = (count,) + (2,) * (n - 1 - k) + (rows, widths[p][1])
            scratch += [pltpu.VMEM(shape, link), pltpu.VMEM(shape, link)]
            if k < n - 1:
                scratch.append(pltpu.VMEM(shape, jnp.float32))
    for k in range(n):
        shape = (2,) * (n - 1 - k) + small.shape[n:]
        scratch.append(pltpu.VMEM(shape, jnp.float32))
        if k < n - 1:
            scratch.append(pltpu.VMEM(shape, jnp.float32))
    vm = pl.BlockSpec(memory_space=pltpu.VMEM)
    outs = pl.pallas_call(
        functools.partial(scatter_kernel, dims, widths, count),
        out_shape=[jax.ShapeDtypeStruct((count, rows, cols), jnp.float32), jax.ShapeDtypeStruct(small.shape[n:], jnp.float32)],
        in_specs=[vm] * (count + 1),
        out_specs=[vm] * 2,
        scratch_shapes=scratch,
        compiler_params=pltpu.CompilerParams(collective_id=1, has_side_effects=True, vmem_limit_bytes=56 * MIB),
    )(*grads, small)
    return outs[0], outs[1]


def gather_all(vectors, weights, router, shift):
    axes = ("rep", "exp")
    return (
        [lax.all_gather(v, axes, axis=0, tiled=True) for v in vectors],
        [lax.all_gather(w, axes, axis=0, tiled=True) for w in weights],
        lax.all_gather(router, axes, axis=0, tiled=True),
        lax.all_gather(shift, axes, axis=1, tiled=True),
    )


def scatter_all(vectors, weights, router, shift):
    axes = ("rep", "exp")
    return (
        [lax.psum_scatter(v, axes, scatter_dimension=0, tiled=True) for v in vectors],
        [lax.psum_scatter(w, axes, scatter_dimension=0, tiled=True) for w in weights],
        lax.psum_scatter(router, axes, scatter_dimension=0, tiled=True),
        lax.psum_scatter(shift, axes, scatter_dimension=1, tiled=True),
    )


def normal_parts(v):
    e = jnp.exp(v * v * -0.5)
    t = 1.0 / (1.0 + (0.3275911 * 0.7071067811865476) * jnp.abs(v))
    poly = t * (0.127414796 + t * (-0.142248368 + t * (0.7107068705 + t * (-0.7265760135 + t * 0.5307027145))))
    q = poly * e
    return jnp.where(v < 0, q, 1.0 - q), e * 0.3989422804014327

def dot(a, b, ca, cb):
    return lax.dot_general(a, b, (((ca,), (cb,)), ((), ())), preferred_element_type=jnp.float32)

def experts_kernel(reps, groups, x_ref, g_ref, p_ref, win_ref, bias_in, wout_ref,
                   res_ref, ig_ref, gin_ref, gb_ref, gout_ref,
                   x_all, g_all, res_send, ig_send, wi, wo, wis, wos, act_all, pg_all, gin_buf, gout_buf, res_acc, ig_acc, bias_ref, p_all, p_turned, rg_all, p_rows,
                   own_sem, psem, prec, dsem, drec, rsem, rrec, bsem, brec, bown, wsem, ssem, osem):
    me, rep = lax.axis_index("exp"), lax.axis_index("rep")
    blocks = x_ref.shape[1]
    cap, wide = x_ref.shape[2:]
    rows = groups * cap
    chunks, part = wi.shape[0], wi.shape[2]
    half = groups // 2
    peers = [lax.rem(me + s, groups) for s in range(1, groups)]
    side = (rep + 1 - 2 * (rep % 2), rep + 2 - 4 * ((rep // 2) % 2))
    both = (x_all, g_all, p_all)
    back = ((res_send, res_ref), (ig_send, ig_ref))

    def load(j, f):
        return (pltpu.make_async_copy(win_ref.at[j, :, pl.ds(f * part, part)], wi.at[f], wsem.at[0, f]),
                pltpu.make_async_copy(wout_ref.at[j, pl.ds(f * part, part)], wo.at[f], wsem.at[1, f]))
    def load_slice(j):
        at = pl.ds(pl.multiple_of(rep * part, part), part)
        return (pltpu.make_async_copy(win_ref.at[j, :, at], wis, ssem.at[0]),
                pltpu.make_async_copy(wout_ref.at[j, at], wos, ssem.at[1]))
    def out_copies(j):
        return (pltpu.make_async_copy(gin_buf, gin_ref.at[j], osem.at[0]),
                pltpu.make_async_copy(gout_buf, gout_ref.at[j], osem.at[1]))
    ahead = AHEAD
    def dispatch(j, s):
        return pltpu.make_async_remote_copy(x_ref.at[peers[s], j], x_all.at[j, 0, me], dsem.at[j, s], drec.at[j, s],
                                            device_id=(rep, peers[s]), device_id_type=MESH)
    def dispatch_gates(s):
        return pltpu.make_async_remote_copy(p_ref.at[peers[s]], p_all.at[0, 0, me], psem.at[s], prec.at[s],
                                            device_id=(rep, peers[s]), device_id_type=MESH)
    def own(j, t):
        if t == 0:
            return pltpu.make_async_copy(x_ref.at[me, j], x_all.at[j, 0, me], own_sem.at[t, j])
        if t == 1:
            if isinstance(j, int) and j < ahead:
                return pltpu.make_async_copy(g_ref.at[j], g_all.at[j], own_sem.at[t, j])
            return pltpu.make_async_copy(g_ref.at[j, 0], g_all.at[j, 0], own_sem.at[t, j])
        return pltpu.make_async_copy(p_ref.at[me], p_all.at[0, 0, me], own_sem.at[t, 0])
    def across(j, t, n):
        dst = both[t]
        return pltpu.make_async_remote_copy(dst.at[j, 0], dst.at[j, 1 + n], rsem.at[t, j, n], rrec.at[t, j, n],
                                            device_id=(side[n], me), device_id_type=MESH)
    def onward(j, t, n):
        dst = both[t]
        at = pl.ds(n * half, half)
        return pltpu.make_async_remote_copy(dst.at[j, 1 + n, at], dst.at[j, 3, at], rsem.at[t, j, 2 + n], rrec.at[t, j, 2 + n],
                                            device_id=(side[1 - n], me), device_id_type=MESH)
    def give(j, t, s):
        src, dst = back[t]
        return pltpu.make_async_remote_copy(src.at[j, peers[s]], dst.at[me, j], bsem.at[t, j, s], brec.at[t, j, s],
                                            device_id=(rep, peers[s]), device_id_type=MESH)
    def give_own(j, t):
        src, dst = back[t]
        return pltpu.make_async_copy(src.at[j, me], dst.at[me, j], bown.at[t, j])
    def flat(v):
        return v.astype(jnp.float32).reshape(-1, wide).astype(jnp.bfloat16)

    barrier = pltpu.get_barrier_semaphore()
    for p in peers:
        pl.semaphore_signal(barrier, inc=1, device_id=(rep, p), device_id_type=MESH)
    for n in side:
        pl.semaphore_signal(barrier, inc=1, device_id=(n, me), device_id_type=MESH)
    pl.semaphore_wait(barrier, groups - 1 + 2)

    for s in range(groups - 1):
        dispatch_gates(s).start()
    own(0, 2).start()

    def send_inputs(j):
        for s in range(groups - 1):
            dispatch(j, s).start()
        own(j, 0).start()
    for j in range(min(2, blocks)):
        send_inputs(j)
    for j in range(blocks):
        own(j, 1).start()
    for j in range(blocks):
        for f in range(chunks):
            bias_ref[j, f] = bias_in[j : j + 1, f * part : (f + 1) * part].astype(jnp.float32)
    for f in range(chunks):
        for c in load(0, f): c.start()
    for c in load_slice(0): c.start()

    def turn_gates(r):
        for s in range(groups):
            p_rows[s : s + 1] = p_all[0, r, s, 0:1]
        p_turned[r] = jnp.transpose(p_rows[...])

    def gated(j, r):
        gates = p_turned[r, pl.ds(pl.multiple_of(j * cap, 8), cap)]
        parts = [g_all[j, r, s].astype(jnp.float32) * gates[:, s : s + 1] for s in range(groups)]
        return jnp.concatenate(parts, axis=0).astype(jnp.bfloat16)

    p_rows[...] = jnp.zeros(p_rows.shape, jnp.float32)
    for j in range(blocks):
        own(j, 1).wait()
        if j >= ahead:
            for n in range(2):
                across(j, 1, n).start()
    for s in range(groups - 1):
        dispatch_gates(s).wait_recv()
    own(0, 2).wait()
    for n in range(2):
        across(0, 2, n).start()
    turn_gates(0)

    def own_rows(j):
        x, g = flat(x_all[j, 0]), gated(j, 0)
        def chunk(f, _):
            for c in load(j, f): c.wait()
            pre = dot(x, wi[f], 1, 0) + bias_ref[j, f]
            cdf, pdf = normal_parts(pre)
            act = (pre * cdf).astype(jnp.bfloat16)
            ag = dot(g, wo[f], 1, 1)
            pg = (ag * (cdf + pre * pdf)).astype(jnp.bfloat16)
            more, less = dot(act, wo[f], 1, 0), dot(pg, wi[f], 1, 1)
            @pl.when(f == 0)
            def _():
                res_acc[...] = more
                ig_acc[...] = less
            @pl.when(f > 0)
            def _():
                res_acc[...] += more
                ig_acc[...] += less
            @pl.when(j + 1 < blocks)
            def _():
                for c in load(j + 1, f): c.start()
            return 0
        lax.fori_loop(0, chunks, chunk, 0)
        res_send[j] = res_acc[...].reshape(groups, cap, wide).astype(jnp.bfloat16)
        ig_send[j] = ig_acc[...].reshape(groups, cap, wide).astype(jnp.bfloat16)

    def weights(j):
        for c in load_slice(j): c.wait()
        def one(r, _):
            x, g = flat(x_all[j, r]), gated(j, r)
            rg_all[r] = g
            pre = dot(x, wis[...], 1, 0) + bias_ref[j, rep]
            cdf, pdf = normal_parts(pre)
            act_all[r] = (pre * cdf).astype(jnp.bfloat16)
            pg_all[r] = (dot(g, wos[...], 1, 1) * (cdf + pre * pdf)).astype(jnp.bfloat16)
            return 0
        lax.fori_loop(0, reps, one, 0)
        @pl.when(j + 1 < blocks)
        def _():
            for c in load_slice(j + 1): c.start()
        @pl.when(j > 0)
        def _():
            for c in out_copies(j - 1): c.wait()
        act, pg = act_all[...].reshape(reps * rows, part), pg_all[...].reshape(reps * rows, part)
        gout_buf[...] = dot(act, rg_all[...].reshape(reps * rows, wide), 0, 0)
        gin_buf[...] = dot(flat(x_all[j]), pg, 0, 0)
        gb_ref[j] = jnp.sum(pg.astype(jnp.float32), axis=0, keepdims=True)
        for c in out_copies(j): c.start()

    def step(k, _):
        @pl.when(k < blocks)
        def _():
            for s in range(groups - 1):
                dispatch(k, s).wait_recv()
            own(k, 0).wait()
            @pl.when(k + 2 < blocks)
            def _():
                send_inputs(k + 2)
            for n in range(2):
                across(k, 0, n).start()
            own_rows(k)
            for t in range(2):
                for s in range(groups - 1):
                    give(k, t, s).start()
                give_own(k, t).start()
        @pl.when((k > 0) & (k <= blocks))
        def _():
            for n in range(2):
                across(k - 1, 0, n).wait_recv()
            for n in range(2):
                onward(k - 1, 0, n).start()
        @pl.when((k > 0) & (k <= blocks - ahead))
        def _():
            for n in range(2):
                across(k - 1 + ahead, 1, n).wait_recv()
            for n in range(2):
                onward(k - 1 + ahead, 1, n).start()
        @pl.when(k == 1)
        def _():
            for n in range(2):
                across(0, 2, n).wait_recv()
            for n in range(2):
                onward(0, 2, n).start()
        @pl.when(k == 2)
        def _():
            for n in range(2):
                onward(0, 2, n).wait_recv()
            for r in range(1, reps):
                turn_gates(r)
        @pl.when(k > 1)
        def _():
            for n in range(2):
                onward(k - 2, 0, n).wait_recv()
            @pl.when(k - 2 >= ahead)
            def _():
                for n in range(2):
                    onward(k - 2, 1, n).wait_recv()
            weights(k - 2)
        return 0
    lax.fori_loop(0, blocks + 2, step, 0)

    for c in out_copies(blocks - 1): c.wait()
    def drain(j, _):
        for s in range(groups - 1):
            dispatch(j, s).wait_send()
        for t in range(2):
            for s in range(groups - 1):
                give(j, t, s).wait_recv()
                give(j, t, s).wait_send()
            give_own(j, t).wait()
        for n in range(2):
            across(j, 0, n).wait_send()
            onward(j, 0, n).wait_send()
        @pl.when(j >= ahead)
        def _():
            for n in range(2):
                across(j, 1, n).wait_send()
                onward(j, 1, n).wait_send()
        return 0
    lax.fori_loop(0, blocks, drain, 0)
    for s in range(groups - 1):
        dispatch_gates(s).wait_send()
    for n in range(2):
        across(0, 2, n).wait_send()
        onward(0, 2, n).wait_send()


def experts_call(x, g, gate, w_in, b_in, w_out, reps, groups):
    _, blocks, cap, wide = x.shape
    hidden = w_in.shape[2]
    part = hidden // reps
    anyw = pl.BlockSpec(memory_space=pl.ANY)
    vm = pl.BlockSpec(memory_space=pltpu.VMEM)
    bf, f32 = jnp.bfloat16, jnp.float32
    sem = pltpu.SemaphoreType.DMA
    n = groups - 1
    rows = groups * cap
    lanes = gate.shape[-1]
    return pl.pallas_call(
        functools.partial(experts_kernel, reps, groups),
        out_shape=[jax.ShapeDtypeStruct(x.shape, bf), jax.ShapeDtypeStruct(x.shape, bf),
                   jax.ShapeDtypeStruct((blocks, wide, part), f32), jax.ShapeDtypeStruct((blocks, 1, part), f32),
                   jax.ShapeDtypeStruct((blocks, part, wide), f32)],
        in_specs=[anyw, anyw, vm, anyw, vm, anyw],
        out_specs=[anyw, anyw, anyw, vm, anyw],
        scratch_shapes=[
            pltpu.VMEM((blocks, reps, groups, cap, wide), bf), pltpu.VMEM((blocks, reps, groups, cap, wide), bf),
            pltpu.VMEM((blocks, groups, cap, wide), bf), pltpu.VMEM((blocks, groups, cap, wide), bf),
            pltpu.VMEM((reps, wide, part), bf), pltpu.VMEM((reps, part, wide), bf),
            pltpu.VMEM((wide, part), bf), pltpu.VMEM((part, wide), bf),
            pltpu.VMEM((reps, rows, part), bf), pltpu.VMEM((reps, rows, part), bf),
            pltpu.VMEM((wide, part), f32), pltpu.VMEM((part, wide), f32),
            pltpu.VMEM((rows, wide), f32), pltpu.VMEM((rows, wide), f32), pltpu.VMEM((blocks, reps, 1, part), f32),
            pltpu.VMEM((1, reps) + gate.shape, f32), pltpu.VMEM((reps, lanes, 128), f32), pltpu.VMEM((reps, rows, wide), bf), pltpu.VMEM((128, lanes), f32),
            sem((3, blocks)), sem((n,)), sem((n,)), sem((blocks, n)), sem((blocks, n)), sem((3, blocks, 4)), sem((3, blocks, 4)),
            sem((2, blocks, n)), sem((2, blocks, n)), sem((2, blocks)), sem((2, reps)), sem((2,)), sem((2,))],
        compiler_params=pltpu.CompilerParams(collective_id=2, has_side_effects=True, vmem_limit_bytes=60 * MIB),
    )(x, g, gate, w_in, b_in, w_out)

def experts_plain(x, g, w_in, b_in, w_out):
    bf, f32 = jnp.bfloat16, jnp.float32
    rx = lax.all_to_all(x, "exp", split_axis=0, concat_axis=0, tiled=True)
    rg = lax.all_to_all(g, "exp", split_axis=0, concat_axis=0, tiled=True)
    pre = jnp.einsum("secd,edf->secf", rx, w_in, preferred_element_type=f32)
    pre = pre + b_in.astype(f32)[None, :, None, :]
    cdf, pdf = normal_parts(pre)
    act = (pre * cdf).astype(bf)
    res = jnp.einsum("secf,efd->secd", act, w_out, preferred_element_type=f32).astype(bf)
    pg = jnp.einsum("secd,efd->secf", rg, w_out, preferred_element_type=f32) * (cdf + pre * pdf)
    pg = pg.astype(bf)
    ig = jnp.einsum("secf,edf->secd", pg, w_in, preferred_element_type=f32).astype(bf)
    gout = jnp.einsum("secf,secd->efd", act, rg, preferred_element_type=f32).astype(bf)
    gin = jnp.einsum("secd,secf->edf", rx, pg, preferred_element_type=f32).astype(bf)
    gb = jnp.sum(pg, axis=(0, 2), dtype=f32).astype(bf)
    return (
        lax.all_to_all(res, "exp", split_axis=0, concat_axis=0, tiled=True),
        lax.all_to_all(ig, "exp", split_axis=0, concat_axis=0, tiled=True),
        lax.psum_scatter(gin, "rep", scatter_dimension=2, tiled=True).astype(f32),
        lax.psum_scatter(gb, "rep", scatter_dimension=1, tiled=True).astype(f32)[:, None],
        lax.psum_scatter(gout, "rep", scatter_dimension=1, tiled=True).astype(f32),
    )


epsilon = 1e-06
masked_score = -1e30


def normalize(values):
    center = values - jnp.mean(values, axis=-1, keepdims=True)
    spread = jnp.mean(center * center, axis=-1, keepdims=True)
    scale = lax.rsqrt(spread + epsilon)
    return center * scale, scale


def normalize_back(grad, unit, scale):
    mean = jnp.mean(grad, axis=-1, keepdims=True)
    along = jnp.mean(grad * unit, axis=-1, keepdims=True)
    return (grad - mean - unit * along) * scale


def two_parts(v):
    high = v.astype(jnp.bfloat16)
    return high, (v - high.astype(jnp.float32)).astype(jnp.bfloat16)


def positions_of(routes, valid_col, priority_col, priority_row, experts):
    length = routes.shape[0]
    f32, bf = jnp.float32, jnp.bfloat16
    token_row = lax.broadcasted_iota(jnp.int32, (length, length), 1)
    token_col = lax.broadcasted_iota(jnp.int32, (length, length), 0)
    rank_col = jnp.sum(
        jnp.where(priority_row == token_col, token_row, 0).astype(f32), axis=1, keepdims=True
    )
    rank_row = jnp.sum(
        jnp.where(priority_col == token_row, token_col, 0).astype(f32), axis=0, keepdims=True
    )
    earlier = (rank_row < rank_col).astype(f32).astype(bf)
    expert_row = lax.broadcasted_iota(jnp.int32, (length, experts), 1)
    ones = [(routes[:, k : k + 1] == expert_row).astype(f32) for k in range(routes.shape[1])]
    before = jnp.zeros((1, experts), f32)
    places = []
    for one in ones:
        live = one * valid_col
        count = dot(earlier, live.astype(bf), 1, 0) + before
        places.append(jnp.sum(count * one, axis=1, keepdims=True))
        before = before + jnp.sum(live, axis=0, keepdims=True)
    return ones, places


def body_plain(
    tokens,
    segments,
    valid,
    routes,
    priority,
    ln1_gain,
    ln1_bias,
    w_query,
    query_bias,
    w_key,
    w_value,
    value_bias,
    w_attn_out,
    attn_out_bias,
    ln2_gain,
    ln2_bias,
    w_router,
    expert_in,
    expert_in_bias,
    expert_out,
    expert_out_bias,
    cotangent,
):
    f32, bf = jnp.float32, jnp.bfloat16
    vectors, weights, router_weight, result_shift = gather_all(
        [ln1_gain, ln1_bias, query_bias, value_bias, attn_out_bias, ln2_gain, ln2_bias],
        [w_query, w_key, w_value, w_attn_out],
        w_router,
        expert_out_bias,
    )
    vectors = [v.astype(f32)[None] for v in vectors]
    gain_one, bias_one, query_shift, value_shift, proj_shift, gain_two, bias_two = vectors
    query_weight, key_weight, value_weight, proj_weight = weights
    length = tokens.shape[1]
    feature_dim = tokens.shape[2]
    head_dim = feature_dim // HEADS
    local_blocks = expert_in.shape[0]
    reps, groups = lax.axis_size("rep"), lax.axis_size("exp")
    experts = EXPERTS
    split = local_blocks * groups // experts
    top_count = routes.shape[2]
    capacity = (105 * top_count * length + 100 * experts - 1) // (100 * experts)
    room = -(-capacity // 8) * 8
    score_scale = head_dim ** (-0.5)
    inputs = tokens[0].astype(f32)
    row_segments = segments[0]
    row_valid = valid[0]
    places = jnp.arange(length, dtype=jnp.int32)
    allowed = (row_segments[:, None] == row_segments[None, :]) & (
        (row_valid[None, :] > 0) | (places[:, None] == places[None, :])
    )
    unit_one, scale_one = normalize(inputs)
    normed = (unit_one * gain_one + bias_one).astype(bf)
    query_rows = (dot(normed, query_weight, 1, 0) + query_shift).astype(bf)
    key_rows = dot(normed, key_weight, 1, 0).astype(bf)
    value_rows = (dot(normed, value_weight, 1, 0) + value_shift).astype(bf)
    query_heads = query_rows.reshape(length, HEADS, head_dim)
    key_heads = key_rows.reshape(length, HEADS, head_dim)
    value_heads = value_rows.reshape(length, HEADS, head_dim)

    def scores():
        return jnp.where(
            allowed[None],
            jnp.einsum("qhd,khd->hqk", query_heads, key_heads, preferred_element_type=f32)
            * score_scale,
            masked_score,
        )

    masked = scores()
    top_score = jnp.max(masked, axis=-1, keepdims=True)
    log_total = top_score + jnp.log(jnp.sum(jnp.exp(masked - top_score), axis=-1, keepdims=True))
    mixed = jnp.einsum(
        "hqk,khd->qhd",
        jnp.exp(masked - log_total).astype(bf),
        value_heads,
        preferred_element_type=f32,
    )
    mixed = mixed.reshape(length, feature_dim).astype(bf)
    residual = inputs + dot(mixed, proj_weight, 1, 0) + proj_shift
    unit_two, scale_two = normalize(residual)
    normed_two = (unit_two * gain_two + bias_two).astype(bf)
    logits = dot(normed_two, router_weight, 1, 0)
    logit_exp = jnp.exp(logits - jnp.max(logits, axis=-1, keepdims=True))
    router_probs = logit_exp / jnp.sum(logit_exp, axis=-1, keepdims=True)
    upstream = cotangent[0].astype(f32)
    ones, positions = positions_of(
        routes[0], row_valid[:, None].astype(f32), priority[0][:, None], priority[0][None], experts
    )
    expert_row = lax.broadcasted_iota(jnp.int32, (1, experts), 1).astype(f32)
    slot_row = lax.broadcasted_iota(jnp.int32, (1, experts * room), 1)
    kept, gates, slots, sent = [], [], [], jnp.zeros((experts * room, feature_dim), f32)
    for one, position in zip(ones, positions):
        keep = row_valid[:, None].astype(f32) * (position < capacity).astype(f32)
        gate = jnp.sum(router_probs * one, axis=1, keepdims=True) * keep
        place = jnp.sum(one * expert_row, axis=1, keepdims=True) * room + position
        place = jnp.where(keep > 0, place, -1.0).astype(jnp.int32)
        hot = (place == slot_row).astype(f32).astype(bf)
        kept.append(one * keep)
        gates.append(gate)
        slots.append(hot)
        sent = sent + dot(hot, (gate * upstream).astype(bf), 0, 0)
    any_slot = slots[0]
    for hot in slots[1:]:
        any_slot = any_slot + hot
    expert_slots = dot(any_slot, normed_two, 0, 0).astype(bf)
    gated = sum(one * gate for one, gate in zip(kept, gates))
    high, low = two_parts(gated)
    shift_grad = dot(high, cotangent[0], 0, 0) + dot(low, cotangent[0], 0, 0)

    def outgoing(v):
        v = v.astype(bf).reshape(experts, room, feature_dim)
        return jnp.repeat(v, split, axis=0).reshape(groups, local_blocks, room, feature_dim)

    moved = experts_plain(
        outgoing(expert_slots), outgoing(sent), expert_in, expert_in_bias, expert_out
    )
    result, slot_back, in_w_grad, in_b_grad, out_w_grad = moved
    result = result.reshape(experts, split, room, feature_dim)
    slot_back = slot_back.reshape(experts, split, room, feature_dim)
    results = [result[:, s].reshape(experts * room, feature_dim) for s in range(split)]
    backs = [slot_back[:, s].reshape(experts * room, feature_dim) for s in range(split)]
    combined, prob_grad = 0.0, 0.0
    for one, gate, hot in zip(kept, gates, slots):
        picked = dot(one.astype(bf), result_shift, 1, 0)
        for part in results:
            picked = picked + dot(hot, part, 1, 0)
        combined = combined + gate * picked
        prob_grad = prob_grad + one * jnp.sum(upstream * picked, axis=1, keepdims=True)
    output = residual + combined
    logit_grad = (
        router_probs * (prob_grad - jnp.sum(router_probs * prob_grad, axis=-1, keepdims=True))
    ).astype(bf)
    router_w_grad = dot(normed_two, logit_grad, 0, 0)
    normed_two_grad = dot(logit_grad, router_weight, 1, 1)
    for part in backs:
        normed_two_grad = normed_two_grad + dot(any_slot, part, 1, 0)
    gain_two_grad = jnp.sum(normed_two_grad * unit_two, axis=0)
    bias_two_grad = jnp.sum(normed_two_grad, axis=0)
    residual_grad = upstream + normalize_back(normed_two_grad * gain_two, unit_two, scale_two)
    branch_grad = residual_grad.astype(bf)
    proj_w_grad = dot(mixed, branch_grad, 0, 0)
    proj_b_grad = jnp.sum(branch_grad, axis=0, dtype=f32)
    mixed_grad = dot(branch_grad, proj_weight, 1, 1).astype(bf)
    mixed_grad = mixed_grad.reshape(length, HEADS, head_dim)
    again_probs = jnp.exp(scores() - log_total)
    prob_grads = jnp.einsum("qhd,khd->hqk", mixed_grad, value_heads, preferred_element_type=f32)
    value_grad = jnp.einsum(
        "hqk,qhd->khd", again_probs.astype(bf), mixed_grad, preferred_element_type=f32
    )
    value_grad = value_grad.astype(bf).reshape(length, feature_dim)
    inner_sum = jnp.sum(again_probs * prob_grads, axis=-1, keepdims=True)
    score_grad = (again_probs * (prob_grads - inner_sum)).astype(bf)
    query_grad = jnp.einsum("hqk,khd->qhd", score_grad, key_heads, preferred_element_type=f32)
    query_grad = (query_grad * score_scale).astype(bf).reshape(length, feature_dim)
    key_grad = jnp.einsum("hqk,qhd->khd", score_grad, query_heads, preferred_element_type=f32)
    key_grad = (key_grad * score_scale).astype(bf).reshape(length, feature_dim)
    query_w_grad = dot(normed, query_grad, 0, 0)
    query_b_grad = jnp.sum(query_grad, axis=0, dtype=f32)
    key_w_grad = dot(normed, key_grad, 0, 0)
    value_w_grad = dot(normed, value_grad, 0, 0)
    value_b_grad = jnp.sum(value_grad, axis=0, dtype=f32)
    normed_grad = dot(query_grad, query_weight, 1, 1)
    normed_grad = normed_grad + dot(key_grad, key_weight, 1, 1)
    normed_grad = normed_grad + dot(value_grad, value_weight, 1, 1)
    gain_one_grad = jnp.sum(normed_grad * unit_one, axis=0)
    bias_one_grad = jnp.sum(normed_grad, axis=0)
    tokens_grad = residual_grad + normalize_back(normed_grad * gain_one, unit_one, scale_one)
    vector_sums, weight_sums, router_sum, shift_sum = scatter_all(
        [
            gain_one_grad,
            bias_one_grad,
            query_b_grad,
            value_b_grad,
            proj_b_grad,
            gain_two_grad,
            bias_two_grad,
        ],
        [query_w_grad, key_w_grad, value_w_grad, proj_w_grad],
        router_w_grad,
        shift_grad,
    )
    return (
        output.astype(jnp.bfloat16)[None],
        tokens_grad[None],
        vector_sums[0],
        vector_sums[1],
        weight_sums[0],
        vector_sums[2],
        weight_sums[1],
        weight_sums[2],
        vector_sums[3],
        weight_sums[3],
        vector_sums[4],
        vector_sums[5],
        vector_sums[6],
        router_sum,
        in_w_grad,
        in_b_grad[:, 0],
        out_w_grad,
        shift_sum,
    )


AHEAD = 1


def eye_of(n):
    same = lax.broadcasted_iota(jnp.int32, (n, n), 0) == lax.broadcasted_iota(jnp.int32, (n, n), 1)
    return same.astype(jnp.float32).astype(jnp.bfloat16)


def lanes_of(n=1):
    return lax.broadcasted_iota(jnp.int32, (n, 128), 1)


def mask_of(ints, cols):
    n = ints.shape[1]
    same = lax.broadcasted_iota(jnp.int32, (n, n), 0) == lax.broadcasted_iota(jnp.int32, (n, n), 1)
    near = cols[:, 0:1] == ints[0:1]
    open_key = jnp.where(same, 1.0, cols[:, 1:2]) > 0
    return jnp.where(near & open_key, 0.0, masked_score)


def side_masks(head_dim):
    lane = lanes_of()
    return [
        ((lane >= s * head_dim) & (lane < (s + 1) * head_dim)).astype(jnp.float32).astype(jnp.bfloat16)
        for s in range(128 // head_dim)
    ]


def vectors_of(small_ref):
    f32, bf = jnp.float32, jnp.bfloat16
    reps, groups, lines, _ = small_ref.shape
    count = reps * groups
    per = lines - 8
    tail = small_ref[...].astype(f32)[:, :, per:].reshape(count * 8, 128).astype(bf)
    wide = count * per
    spread = lax.broadcasted_iota(jnp.int32, (128, wide), 1) % per
    spread = (spread == lax.broadcasted_iota(jnp.int32, (128, wide), 0)).astype(f32).astype(bf)
    laid = dot(tail, spread, 1, 0)
    owner = lax.broadcasted_iota(jnp.int32, (count * 8, wide), 1) // per
    mine = owner == lax.broadcasted_iota(jnp.int32, (count * 8, wide), 0) // 8
    pick = lax.broadcasted_iota(jnp.int32, (8, count * 8), 1) % 8
    pick = (pick == lax.broadcasted_iota(jnp.int32, (8, count * 8), 0)).astype(f32).astype(bf)
    rows = dot(pick, jnp.where(mine, laid, 0.0).astype(bf), 1, 0)
    return [rows[i : i + 1] for i in range(7)]


def matrix_of(small_ref):
    reps, groups, lines, _ = small_ref.shape
    per = lines - 8
    part = small_ref[...].astype(jnp.float32)[:, :, :per]
    return part.reshape(reps * groups * per, 128).astype(jnp.bfloat16)


def weight_of(ref):
    wide = ref.shape[-1]
    return ref.astype(jnp.float32).reshape(-1, wide).astype(jnp.bfloat16)


def integer_rows(raw):
    raw = raw.astype(jnp.float32)
    line = lax.broadcasted_iota(jnp.int32, raw.shape, 0)
    order = raw[2:3]
    high = jnp.floor(order * (1.0 / 64.0))
    low = order - high * 64.0
    return jnp.where(line == 2, high, jnp.where(line == 5, low, raw)), order


def front_kernel(
    capacity,
    room,
    head_dim,
    tokens_ref,
    cot_ref,
    ints_ref,
    small_in,
    wq_in,
    wk_in,
    wv_in,
    wo_in,
    xs_ref,
    g_ref,
    gate_ref,
    resid_ref,
    q_ref,
    k_ref,
    v_ref,
    mixed_ref,
    lse_ref,
    info_ref,
    wa_ref,
    wo_ref,
    small_ref,
    mask_ref,
    a2_ref,
    gs_ref,
    own_sem,
    send_sem,
    recv_sem,
    g_send_sem,
    g_recv_sem,
    g_own_sem,
    side_send_sem,
    side_recv_sem,
):
    f32, bf = jnp.float32, jnp.bfloat16
    length, wide = tokens_ref.shape
    groups, blocks = xs_ref.shape[:2]
    me, rep = lax.axis_index("exp"), lax.axis_index("rep")
    level, core = me // 2, me % 2
    levels = groups // 2
    beside = (rep + 1 - 2 * (rep % 2), rep + 2 - 4 * ((rep // 2) % 2))
    bufs = (wa_ref, small_ref, wo_ref)
    mine = [
        pltpu.make_async_copy(wq_in, wa_ref.at[rep, me, 0], own_sem.at[0]),
        pltpu.make_async_copy(wk_in, wa_ref.at[rep, me, 1], own_sem.at[1]),
        pltpu.make_async_copy(wv_in, wa_ref.at[rep, me, 2], own_sem.at[2]),
        pltpu.make_async_copy(small_in, small_ref.at[rep, me], own_sem.at[3]),
        pltpu.make_async_copy(wo_in, wo_ref.at[rep, me], own_sem.at[4]),
    ]
    for c in mine:
        c.start()

    def flip(r):
        there = level
        for one in (1, 2):
            if r & one:
                there = there + one - 2 * one * ((there // one) % 2)
        return there

    def block(r):
        return flip(r) * 2 + core

    def send(src, a, r, n, device):
        return pltpu.make_async_remote_copy(
            src, src, send_sem.at[a, r, n], recv_sem.at[a, r, n], device_id=device, device_id_type=MESH
        )

    def up(a, r):
        far, here = (2, 1) if r == 3 else (r, 0)
        return send(bufs[a].at[rep, block(here)], a, r, 0, (rep, flip(far) * 2 + core))

    def aside(a, r, n):
        return send(bufs[a].at[rep, block(r)], a, r, 1 + n, (beside[n], me))

    def onward(a, r, n):
        ref = bufs[a].at[beside[n], block(r)]
        if a == 1:
            half = ref.shape[0] // 2
            ref = ref.at[pl.ds(n * half, half)]
        else:
            half = wide // 2
            ref = ref.at[(slice(None),) * (len(ref.shape) - 1) + (pl.ds(n * half, half),)]
        return send(ref, a, r, 3 + n, (beside[1 - n], me))

    def over(a, r):
        return send(bufs[a].at[:, block(r)], a, r, 5, (rep, me + 1 - 2 * core))

    barrier = pltpu.get_barrier_semaphore()
    peers = [lax.rem(me + s, groups) for s in range(1, groups)]
    for p in peers:
        pl.semaphore_signal(barrier, inc=1, device_id=(rep, p), device_id_type=MESH)
    for n in beside:
        pl.semaphore_signal(barrier, inc=1, device_id=(n, me), device_id_type=MESH)
    pl.semaphore_wait(barrier, groups + 1)
    for c in mine:
        c.wait()

    def step(sets, r):
        for a in sets:
            if 0 < r < levels:
                up(a, r).wait_recv()
            if r == 1 and levels > 2:
                up(a, 3).start()
            if r < levels:
                for n in range(2):
                    aside(a, r, n).start()
            if 0 < r <= levels:
                for n in range(2):
                    aside(a, r - 1, n).wait_recv()
                for n in range(2):
                    onward(a, r - 1, n).start()
            if 1 < r <= levels + 1:
                for n in range(2):
                    onward(a, r - 2, n).wait_recv()
                over(a, r - 2).start()

    early, late = (0, 1), (2,)
    near = range(1, min(levels, 3))
    for a in early + late:
        for r in near:
            up(a, r).start()
    step(early, 0)
    ints, priority_row = integer_rows(ints_ref[...])
    eye = eye_of(length)
    cols = dot(eye, ints.astype(bf), 1, 1)
    mask_ref[...] = mask_of(ints, cols)
    step(early, 1)
    token_row = lax.broadcasted_iota(jnp.int32, (length, length), 1).astype(f32)
    token_col = lax.broadcasted_iota(jnp.int32, (length, length), 0).astype(f32)
    priority_col = cols[:, 2:3] * 64.0 + cols[:, 5:6]
    rank_col = jnp.sum(jnp.where(priority_row == token_col, token_row, 0.0), axis=1, keepdims=True)
    rank_row = jnp.sum(jnp.where(priority_col == token_row, token_col, 0.0), axis=0, keepdims=True)
    earlier = (rank_row < rank_col).astype(f32).astype(bf)
    lane = lanes_of()
    expert_lane = (lane - 32).astype(f32)
    valid_col = cols[:, 1:2]
    before = jnp.zeros((1, 128), f32)
    keeps, places = [], []
    marks = jnp.zeros((length, 128), f32)
    for k in range(2):
        expert = cols[:, 3 + k : 4 + k]
        one = (expert == expert_lane).astype(f32)
        live = one * valid_col
        count = dot(earlier, live.astype(bf), 1, 0) + before
        before = before + jnp.sum(live, axis=0, keepdims=True)
        position = jnp.sum(count * one, axis=1, keepdims=True)
        keep = valid_col * (position < capacity).astype(f32)
        place = jnp.where(keep > 0, expert * room + position, -1.0)
        high = jnp.floor(place * (1.0 / 32.0))
        low = place - high * 32.0
        marks = jnp.where(lane == 2 * k, high, jnp.where(lane == 2 * k + 1, low, marks))
        keeps.append(keep)
        places.append(place)
    step(early, 2)
    for a in late:
        up(a, 1).wait_recv()
        if levels > 2:
            up(a, 3).start()
    turned = dot(marks.astype(bf), eye, 0, 0)
    place_rows = [turned[2 * k : 2 * k + 1] * 32.0 + turned[2 * k + 1 : 2 * k + 2] for k in range(2)]
    part = blocks * room
    slot = lax.broadcasted_iota(jnp.int32, (part, length), 0).astype(f32)

    def hots_of(d):
        first = (d * part).astype(f32)
        return [(slot == row - first).astype(f32).astype(bf) for row in place_rows]

    def fill_grads(d, _):
        hots = hots_of(d)
        grads = dot(hots[0] + hots[1], cot_ref[...], 1, 0)
        gs_ref[d] = grads.reshape(blocks, room, wide).astype(bf)
        return 0

    lax.fori_loop(0, groups, fill_grads, 0)

    def give(j, s):
        return pltpu.make_async_remote_copy(
            gs_ref.at[peers[s], j],
            g_ref.at[j, 0, me],
            g_send_sem.at[j, s],
            g_recv_sem.at[j, s],
            device_id=(rep, peers[s]),
            device_id_type=MESH,
        )

    def give_own(j):
        return pltpu.make_async_copy(gs_ref.at[me, j], g_ref.at[j, 0, me], g_own_sem.at[j])

    def spread(src, dst, j, n, device):
        return pltpu.make_async_remote_copy(
            src,
            dst,
            side_send_sem.at[j, n],
            side_recv_sem.at[j, n],
            device_id=(device, me),
            device_id_type=MESH,
        )

    def g_across(j, n):
        return spread(g_ref.at[j, 0], g_ref.at[j, 1 + n], j, n, beside[n])

    def g_onward(j, n):
        at = pl.ds(n * (groups // 2), groups // 2)
        return spread(g_ref.at[j, 1 + n, at], g_ref.at[j, 3, at], j, 2 + n, beside[1 - n])

    def begin_across(j):
        for n in range(2):
            g_across(j, n).start()

    def begin_onward(j):
        for n in range(2):
            g_across(j, n).wait_recv()
        for n in range(2):
            g_onward(j, n).start()

    ahead = AHEAD

    def begin_give(j):
        for s in range(groups - 1):
            give(j, s).start()
        give_own(j).start()

    def have(j):
        for s in range(groups - 1):
            give(j, s).wait_recv()
        give_own(j).wait()

    begin_give(0)
    inputs = tokens_ref[...].astype(f32)
    unit_one, _ = normalize(inputs)
    for r in range(3, levels):
        step(early, r)
    for a in late:
        for r in range(2, levels):
            up(a, r).wait_recv()
    begin_give(1)
    for a in late:
        for r in range(levels):
            for n in range(2):
                aside(a, r, n).start()
    for r in range(max(3, levels), levels + 2):
        step(early, r)
    for a in early:
        for r in range(levels):
            over(a, r).wait_recv()
    have(0)
    begin_across(0)
    for j in range(2, blocks - 1):
        begin_give(j)
    small_matrix = matrix_of(small_ref)
    gain_one, bias_one, query_shift, value_shift, proj_shift, gain_two, bias_two = vectors_of(small_ref)
    normed = (unit_one * gain_one + bias_one).astype(bf)
    q_ref[...] = (dot(normed, weight_of(wa_ref[:, :, 0]), 1, 0) + query_shift).astype(bf)
    k_ref[...] = dot(normed, weight_of(wa_ref[:, :, 1]), 1, 0).astype(bf)
    v_ref[...] = (dot(normed, weight_of(wa_ref[:, :, 2]), 1, 0) + value_shift).astype(bf)
    for a in late:
        for r in range(levels):
            for n in range(2):
                aside(a, r, n).wait_recv()
            for n in range(2):
                onward(a, r, n).start()
    sides = side_masks(head_dim)
    per = len(sides)
    scale = jnp.full((1, 128), head_dim**-0.5, f32).astype(bf)

    def heads(h, _):
        at = pl.ds(pl.multiple_of(h * 128, 128), 128)

        @pl.when(h == 1)
        def _():
            have(1)
            if ahead > 1:
                begin_across(1)
            if blocks > 2:
                begin_give(blocks - 1)

        query = q_ref[:, at] * scale
        total = jnp.zeros((128, length), f32)
        for s, side in enumerate(sides):
            score = dot(k_ref[:, at] * side, query, 1, 1) + mask_ref[...]
            top = jnp.max(score, axis=0, keepdims=True)
            expo = jnp.exp(score - top)
            norm = jnp.sum(expo, axis=0, keepdims=True)
            lse_ref[pl.ds(h * per + s, 1), :] = top + jnp.log(norm)
            probs = (expo * (1.0 / norm)).astype(bf)
            total = total + dot(v_ref[:, at] * side, probs, 0, 0)
        mixed_ref[at, :] = total.astype(bf)
        return 0

    half = wide // 256
    lax.fori_loop(0, half, heads, 0)
    for a in late:
        for r in range(levels):
            for n in range(2):
                onward(a, r, n).wait_recv()
            over(a, r).start()
    lax.fori_loop(half, wide // 128, heads, 0)
    begin_onward(0)
    for r in range(levels):
        over(2, r).wait_recv()
    residual = inputs + dot(mixed_ref[...], weight_of(wo_ref[...]), 0, 0) + proj_shift
    resid_ref[...] = residual
    unit_two, _ = normalize(residual)
    normed_two = (unit_two * gain_two + bias_two).astype(bf)
    a2_ref[...] = normed_two
    routed = (lane >= 32) & (lane < 64)
    logits = jnp.where(routed, dot(normed_two, small_matrix, 1, 0), masked_score)
    logit_exp = jnp.exp(logits - jnp.max(logits, axis=1, keepdims=True))
    probs = logit_exp / jnp.sum(logit_exp, axis=1, keepdims=True)
    info = probs
    gates = []
    for k in range(2):
        expert = cols[:, 3 + k : 4 + k]
        one = (expert == expert_lane).astype(f32)
        gate = jnp.sum(probs * one, axis=1, keepdims=True) * keeps[k]
        info = jnp.where(lane == k, places[k], jnp.where(lane == 2 + k, expert, info))
        high, _ = two_parts(gate)
        middle, low = two_parts(gate - high.astype(f32))
        split = jnp.where(lane == 1, middle.astype(f32), jnp.where(lane == 2, low.astype(f32), 0.0))
        gates.append(jnp.where(lane == 0, high.astype(f32), split).astype(bf))
    info_ref[...] = info

    def fill_inputs(d, _):
        hots = hots_of(d)
        inside = dot(hots[0] + hots[1], a2_ref[...], 1, 0)
        xs_ref[d] = inside.reshape(blocks, room, wide).astype(bf)
        gate = dot(gates[0], hots[0], 0, 1) + dot(gates[1], hots[1], 0, 1)
        gate_ref[d, 0:1, 0:part] = gate[0:1] + gate[1:2] + gate[2:3]
        return 0

    for j in range(1, ahead):
        begin_onward(j)
    gate_ref[...] = jnp.zeros(gate_ref.shape, f32)
    lax.fori_loop(0, groups, fill_inputs, 0)
    for j in range(blocks):
        for s in range(groups - 1):
            give(j, s).wait_send()
        if j > 1:
            have(j)
        if j < ahead:
            for n in range(2):
                g_onward(j, n).wait_recv()
            for n in range(2):
                g_across(j, n).wait_send()
                g_onward(j, n).wait_send()
    for a in early + late:
        for r in range(levels):
            if r > 0:
                up(a, r).wait_send()
            for n in range(2):
                aside(a, r, n).wait_send()
                onward(a, r, n).wait_send()
            over(a, r).wait_send()


def back_kernel(
    head_dim,
    tokens_ref,
    cot_ref,
    ints_ref,
    small_ref,
    wa_ref,
    wo_ref,
    res_ref,
    ig_ref,
    resid_ref,
    q_ref,
    k_ref,
    v_ref,
    mixed_ref,
    lse_ref,
    info_ref,
    gin_ref,
    gout_ref,
    out_ref,
    tokens_grad_ref,
    wq_grad_ref,
    wk_grad_ref,
    wv_grad_ref,
    wo_grad_ref,
    small_grad_ref,
    gin_out_ref,
    gout_out_ref,
    mask_ref,
    mixed_grad_ref,
    query_grad_ref,
    key_grad_ref,
    value_grad_ref,
    gin_buf,
    gout_buf,
    sem,
):
    f32, bf = jnp.float32, jnp.bfloat16
    length, wide = tokens_ref.shape
    slots = res_ref.shape[0]
    pieces = gin_ref.shape[0]
    carried = ((gin_ref, gin_buf, gin_out_ref), (gout_ref, gout_buf, gout_out_ref))

    def loads(j):
        return [
            pltpu.make_async_copy(src.at[j], buf, sem.at[0, i])
            for i, (src, buf, _) in enumerate(carried)
        ]

    def stores(j):
        return [
            pltpu.make_async_copy(buf, dst.at[j], sem.at[1, i])
            for i, (_, buf, dst) in enumerate(carried)
        ]

    for c in loads(0):
        c.start()
    ints, _ = integer_rows(ints_ref[...])
    cols = dot(eye_of(length), ints.astype(bf), 1, 1)
    mask_ref[...] = mask_of(ints, cols)
    small = matrix_of(small_ref)
    gain_one, bias_one, _, _, _, gain_two, bias_two = vectors_of(small_ref)
    lane = lanes_of()
    routed = ((lane >= 32) & (lane < 64)).astype(f32)
    info = info_ref[...]
    probs = info * routed
    upstream = cot_ref[...].astype(f32)
    slot_row = lax.broadcasted_iota(jnp.int32, (1, slots), 1).astype(f32)
    expert_lane = (lane - 32).astype(f32)
    residual = resid_ref[...]
    combined = residual
    prob_grad = jnp.zeros((length, 128), f32)
    gated = jnp.zeros((length, 128), f32)
    hots = []
    for k in range(2):
        place, expert = info[:, k : k + 1], info[:, 2 + k : 3 + k]
        kept = (expert == expert_lane).astype(f32) * (place >= 0).astype(f32)
        gate = jnp.sum(probs * kept, axis=1, keepdims=True)
        hot = (place == slot_row).astype(f32).astype(bf)
        hots.append(hot)
        picked = dot(hot, res_ref[...], 1, 0)
        picked = picked + dot(pltpu.roll(kept, 96, 1).astype(bf), small, 1, 1)
        combined = combined + gate * picked
        prob_grad = prob_grad + kept * jnp.sum(upstream * picked, axis=1, keepdims=True)
        gated = gated + kept * gate
    out_ref[...] = combined.astype(bf)
    inner = jnp.sum(probs * prob_grad, axis=1, keepdims=True)
    logit_grad = (probs * (prob_grad - inner)).astype(bf)
    unit_two, scale_two = normalize(residual)
    normed_two = (unit_two * gain_two + bias_two).astype(bf)
    high, low = two_parts(pltpu.roll(gated, 96, 1))
    small_grad = dot(normed_two, logit_grad, 0, 0)
    small_grad = small_grad + dot(cot_ref[...], high, 0, 0) + dot(cot_ref[...], low, 0, 0)
    normed_two_grad = dot(hots[0] + hots[1], ig_ref[...], 1, 0) + dot(logit_grad, small, 1, 1)
    vector_grads = {}
    vector_grads[5] = jnp.sum(normed_two_grad * unit_two, axis=0, keepdims=True)
    vector_grads[6] = jnp.sum(normed_two_grad, axis=0, keepdims=True)
    residual_grad = upstream + normalize_back(normed_two_grad * gain_two, unit_two, scale_two)
    tokens_grad_ref[...] = residual_grad
    branch_grad = residual_grad.astype(bf)
    wo_grad_ref[...] = dot(mixed_ref[...], branch_grad, 1, 0)
    vector_grads[4] = jnp.sum(branch_grad.astype(f32), axis=0, keepdims=True)
    mixed_grad_ref[...] = dot(branch_grad, weight_of(wo_ref[...]), 1, 1).astype(bf)
    sides = side_masks(head_dim)
    per = len(sides)
    scale = jnp.full((1, 128), head_dim**-0.5, f32).astype(bf)

    def heads(h, _):
        at = pl.ds(pl.multiple_of(h * 128, 128), 128)
        query = q_ref[:, at] * scale
        mixed_grad = mixed_grad_ref[:, at]

        @pl.when(h < pieces)
        def _():
            for c in loads(h):
                c.wait()
            for c in stores(h):
                c.start()

        query_total = jnp.zeros((128, length), f32)
        key_total = jnp.zeros((length, 128), f32)
        value_total = jnp.zeros((length, 128), f32)
        for s, side in enumerate(sides):
            key = k_ref[:, at] * side
            score = dot(key, query, 1, 1) + mask_ref[...]
            probs = jnp.exp(score - lse_ref[pl.ds(h * per + s, 1), :])
            prob_grads = dot(v_ref[:, at] * side, mixed_grad, 1, 1)
            inner = jnp.sum(probs * prob_grads, axis=0, keepdims=True)
            score_grad = (probs * (prob_grads - inner)).astype(bf)
            value_total = value_total + dot(probs.astype(bf), mixed_grad * side, 1, 0)
            key_total = key_total + dot(score_grad, query * side, 1, 0)
            query_total = query_total + dot(key * scale, score_grad, 0, 0)
        @pl.when(h < pieces)
        def _():
            for c in stores(h):
                c.wait()

        @pl.when(h + 1 < pieces)
        def _():
            for c in loads(h + 1):
                c.start()

        query_grad_ref[:, at] = jnp.transpose(query_total).astype(bf)
        key_grad_ref[:, at] = key_total.astype(bf)
        value_grad_ref[:, at] = value_total.astype(bf)
        return 0

    lax.fori_loop(0, wide // 128, heads, 0)
    inputs = tokens_ref[...].astype(f32)
    unit_one, scale_one = normalize(inputs)
    normed = (unit_one * gain_one + bias_one).astype(bf)
    wq_grad_ref[...] = dot(normed, query_grad_ref[...], 0, 0)
    wk_grad_ref[...] = dot(normed, key_grad_ref[...], 0, 0)
    wv_grad_ref[...] = dot(normed, value_grad_ref[...], 0, 0)
    vector_grads[2] = jnp.sum(query_grad_ref[...].astype(f32), axis=0, keepdims=True)
    vector_grads[3] = jnp.sum(value_grad_ref[...].astype(f32), axis=0, keepdims=True)
    normed_grad = dot(query_grad_ref[...], weight_of(wa_ref[:, :, 0]), 1, 1)
    normed_grad = normed_grad + dot(key_grad_ref[...], weight_of(wa_ref[:, :, 1]), 1, 1)
    normed_grad = normed_grad + dot(value_grad_ref[...], weight_of(wa_ref[:, :, 2]), 1, 1)
    vector_grads[0] = jnp.sum(normed_grad * unit_one, axis=0, keepdims=True)
    vector_grads[1] = jnp.sum(normed_grad, axis=0, keepdims=True)
    tokens_grad_ref[...] += normalize_back(normed_grad * gain_one, unit_one, scale_one)
    line = lax.broadcasted_iota(jnp.int32, (128, wide), 0)
    stacked = jnp.zeros((128, wide), f32)
    for i in range(7):
        stacked = jnp.where(line == 64 + i, vector_grads[i], stacked)
    small_grad_ref[...] = small_grad + jnp.transpose(stacked)


def front_call(capacity, room, groups, blocks, tokens, cot, ints, small, weights, reps):
    f32, bf = jnp.float32, jnp.bfloat16
    length, wide = tokens.shape
    shape = jax.ShapeDtypeStruct
    vm = pl.BlockSpec(memory_space=pltpu.VMEM)
    slots = shape((groups, blocks, room, wide), bf)
    line = shape((length, wide), bf)
    lanes = -(-blocks * room // 128) * 128
    outs = [slots, shape((blocks, reps, groups, room, wide), bf), shape((groups, 8, lanes), f32)]
    outs += [shape((length, wide), f32), line, line, line]
    outs += [shape((wide, length), bf), shape((16, length), f32), shape((length, 128), f32)]
    per = weights[0].shape[0]
    outs += [shape((reps, groups, 3, per, wide), bf), shape((reps, groups, per, wide), bf)]
    outs += [shape((reps, groups) + small.shape, bf)]
    sems = pltpu.SemaphoreType.DMA((3, groups // 2, 6))
    return pl.pallas_call(
        functools.partial(front_kernel, capacity, room, wide // HEADS),
        out_shape=outs,
        in_specs=[vm] * 8,
        out_specs=[vm] * len(outs),
        scratch_shapes=[
            pltpu.VMEM((length, length), f32),
            pltpu.VMEM((length, wide), bf),
            pltpu.VMEM(slots.shape, bf),
            pltpu.SemaphoreType.DMA((5,)),
            sems,
            sems,
            pltpu.SemaphoreType.DMA((blocks, groups - 1)),
            pltpu.SemaphoreType.DMA((blocks, groups - 1)),
            pltpu.SemaphoreType.DMA((blocks,)),
            pltpu.SemaphoreType.DMA((AHEAD, 4)),
            pltpu.SemaphoreType.DMA((AHEAD, 4)),
        ],
        compiler_params=pltpu.CompilerParams(
            collective_id=0, has_side_effects=True, vmem_limit_bytes=60 * MIB
        ),
    )(tokens, cot, ints, small, *weights)


def back_call(tokens, cot, ints, small, weights, res, ig, kept, gin, gout):
    f32, bf = jnp.float32, jnp.bfloat16
    length, wide = tokens.shape
    shape = jax.ShapeDtypeStruct
    vm = pl.BlockSpec(memory_space=pltpu.VMEM)
    hbm = pl.BlockSpec(memory_space=pl.ANY)
    square = shape((wide, wide), f32)
    outs = [shape((length, wide), bf), shape((length, wide), f32)] + [square] * 4
    outs += [shape((wide, 128), f32), shape(gin.shape, f32), shape(gout.shape, f32)]
    line = pltpu.VMEM((length, wide), bf)
    return pl.pallas_call(
        functools.partial(back_kernel, wide // HEADS),
        out_shape=outs,
        in_specs=[vm] * 15 + [hbm] * 2,
        out_specs=[vm] * 7 + [hbm] * 2,
        scratch_shapes=[
            pltpu.VMEM((length, length), f32),
            line,
            line,
            line,
            line,
            pltpu.VMEM(gin.shape[1:], f32),
            pltpu.VMEM(gout.shape[1:], f32),
            pltpu.SemaphoreType.DMA((2, 2)),
        ],
        compiler_params=pltpu.CompilerParams(vmem_limit_bytes=60 * MIB),
    )(tokens, cot, ints, small, *weights, res, ig, *kept, gin, gout)


def body_fast(
    tokens,
    segments,
    valid,
    routes,
    priority,
    ln1_gain,
    ln1_bias,
    w_query,
    query_bias,
    w_key,
    w_value,
    value_bias,
    w_attn_out,
    attn_out_bias,
    ln2_gain,
    ln2_bias,
    w_router,
    expert_in,
    expert_in_bias,
    expert_out,
    expert_out_bias,
    cotangent,
):
    reps, groups = lax.axis_size("rep"), lax.axis_size("exp")
    devices = reps * groups
    length, wide = tokens.shape[1:]
    per = w_query.shape[0]
    blocks = expert_in.shape[0]
    capacity, room = capacity_of(routes.shape[2], length)
    vectors = [ln1_gain, ln1_bias, query_bias, value_bias, attn_out_bias, ln2_gain, ln2_bias]
    small = jnp.concatenate([expert_out_bias.T, w_router], axis=1)
    small = jnp.pad(small, ((0, 0), (0, 128 - small.shape[1])))
    vectors = jnp.pad(jnp.stack(vectors), ((0, 1), (0, 128 - per)))
    small = jnp.concatenate([small, vectors], axis=0)
    ints = jnp.concatenate([segments, valid, priority, routes[0].T], axis=0)
    ints = jnp.pad(ints, ((0, 3), (0, 0)))
    weights = [w_query, w_key, w_value, w_attn_out]
    xs, g, gate, *kept, wa, wo, small = front_call(
        capacity, room, groups, blocks, tokens[0], cotangent[0], ints, small, weights, reps
    )
    weights = [wa, wo]
    res, ig, gin, gb, gout = experts_call(
        xs, g, gate, expert_in, expert_in_bias, expert_out, reps, groups
    )
    slots = groups * blocks * room
    output, tokens_grad, *grads, small_grad, gin, gout = back_call(
        tokens[0],
        cotangent[0],
        ints,
        small,
        weights,
        res.reshape(slots, wide),
        ig.reshape(slots, wide),
        kept,
        gin,
        gout,
    )
    sums, last = scatter_grads(grads, small_grad.reshape(devices, per, 128), reps, groups)
    columns = [last[:, 64 + i] for i in range(7)]
    return (
        output[None],
        tokens_grad[None],
        columns[0],
        columns[1],
        sums[0],
        columns[2],
        sums[1],
        sums[2],
        columns[3],
        sums[3],
        columns[4],
        columns[5],
        columns[6],
        last[:, 32:64],
        gin,
        gb[:, 0],
        gout,
        last[:, :32].T,
    )


def capacity_of(top_count, length):
    capacity = (105 * top_count * length + 100 * EXPERTS - 1) // (100 * EXPERTS)
    return capacity, -(-capacity // 8) * 8


def body(*args):
    routes, w_query, expert_in = args[3], args[7], args[17]
    reps, groups = lax.axis_size("rep"), lax.axis_size("exp")
    _, room = capacity_of(routes.shape[2], routes.shape[1])
    wide = w_query.shape[1]
    suits = (
        reps == 4
        and groups & (groups - 1) == 0
        and groups in (4, 8)
        and w_query.shape[0] % 8 == 0
        and w_query.shape[0] <= 128
        and groups * room <= 512
        and groups * expert_in.shape[0] == EXPERTS == 32
        and expert_in.shape[2] % (128 * reps) == 0
        and routes.shape[2] == 2
        and routes.shape[1] <= 64 * 256
        and 128 % (wide // HEADS) == 0
        and HEADS <= 16
        and 2 <= expert_in.shape[0] < wide // 128
    )
    return body_fast(*args) if suits else body_plain(*args)


def solution(mesh):
    in_specs = (
        P(("rep", "exp"), None, None),
        P(("rep", "exp"), None),
        P(("rep", "exp"), None),
        P(("rep", "exp"), None, None),
        P(("rep", "exp"), None),
        P(("rep", "exp")),
        P(("rep", "exp")),
        P(("rep", "exp"), None),
        P(("rep", "exp")),
        P(("rep", "exp"), None),
        P(("rep", "exp"), None),
        P(("rep", "exp")),
        P(("rep", "exp"), None),
        P(("rep", "exp")),
        P(("rep", "exp")),
        P(("rep", "exp")),
        P(("rep", "exp"), None),
        P("exp", None, None),
        P("exp", None),
        P("exp", None, None),
        P(None, ("rep", "exp")),
        P(("rep", "exp"), None, None),
    )
    out_specs = (
        P(("rep", "exp"), None, None),
        P(("rep", "exp"), None, None),
        P(("rep", "exp")),
        P(("rep", "exp")),
        P(("rep", "exp"), None),
        P(("rep", "exp")),
        P(("rep", "exp"), None),
        P(("rep", "exp"), None),
        P(("rep", "exp")),
        P(("rep", "exp"), None),
        P(("rep", "exp")),
        P(("rep", "exp")),
        P(("rep", "exp")),
        P(("rep", "exp"), None),
        P("exp", None, "rep"),
        P("exp", "rep"),
        P("exp", "rep", None),
        P(None, ("rep", "exp")),
    )
    return jax.shard_map(body, mesh=mesh, in_specs=in_specs, out_specs=out_specs, check_vma=False)
```

```python
import functools
import jax
import jax.numpy as jnp
from jax import lax
from jax.experimental import pallas as pl
from jax.experimental.pallas import tpu as pltpu
from jax.sharding import PartitionSpec as P

HEADS = 12
EXPERTS = 32
MESH = pl.DeviceIdType.MESH
MIB = 1 << 20

def bit_dims(reps, groups):
    rb, gb = reps.bit_length() - 1, groups.bit_length() - 1
    return [(0, 1 << k) for k in reversed(range(rb))] + [(1, 1 << k) for k in reversed(range(gb))]

def orders(dims):
    last = len(dims) - 1
    rep = [i for i, d in enumerate(dims) if d[0] == 0]
    exp = [i for i, d in enumerate(dims) if d[0] == 1 and i != last]
    exp = exp[::-1]
    return [[last] + rep + exp, [last] + rep[::-1] + exp, [last] + exp + rep]

def my_bits(dims):
    at = (lax.axis_index("rep"), lax.axis_index("exp"))
    return [(at[a] // s) % 2 for a, s in dims], at

def partner(dims, at, i):
    a, s = dims[i]
    bit = (at[a] // s) % 2
    there = at[a] + (1 - 2 * bit) * s
    return (there, at[1]) if a == 0 else (at[0], there)

def greet(dims, at):
    barrier = pltpu.get_barrier_semaphore()
    for i in range(len(dims)):
        pl.semaphore_signal(barrier, inc=1, device_id=partner(dims, at, i), device_id_type=MESH)
    pl.semaphore_wait(barrier, len(dims))

def scatter_kernel(dims, halves, count, *refs):
    f32 = jnp.float32
    ins, small_in, out_ref, small_out = refs[:count], refs[count], refs[count + 1], refs[count + 2]
    near_ref, far_ref, own_sem, core_send, core_recv, send_sem, recv_sem, small_send, small_recv = refs[count + 3 : count + 12]
    take = iter(refs[count + 12 :])
    n = len(dims)
    ways = orders(dims)
    parts = [(a, h) for a in range(count) for h in range(len(halves))]
    plan = [ways[p % 3] for p in range(len(parts))]
    bufs = {}
    for k in range(1, n):
        for p in range(len(parts)):
            bufs[k, p] = (next(take), next(take), next(take) if k < n - 1 else None)
    smalls = [(next(take), next(take) if k < n - 1 else None) for k in range(n)]
    bits, at = my_bits(dims)
    last = n - 1

    def lead(b):
        return (slice(None),) * (n - 1) + (b,)

    own = [pltpu.make_async_copy(ins[a].at[lead(bits[last])], near_ref.at[a], own_sem.at[a]) for a in range(count)]
    for c in own:
        c.start()
    greet(dims, at)
    core = []
    for a in range(count):
        core.append(pltpu.make_async_remote_copy(
            ins[a].at[lead(1 - bits[last])], far_ref.at[a], core_send.at[a], core_recv.at[a],
            device_id=partner(dims, at, last), device_id_type=MESH))
        core[a].start()
    left = [[j for j in range(n) if j != last] for _ in parts]
    small_left = list(range(n))

    def index(have, i, b):
        return tuple(b if j == i else slice(None) for j in have)

    def value(k, p, where):
        if k == 1:
            a, h = parts[p]
            where = (a,) + where + (slice(None), pl.ds(halves[h][0], halves[h][1]))
            return near_ref[where].astype(f32) + far_ref[where].astype(f32)
        return bufs[k - 1, p][2][where]

    def begin(k, p):
        i = plan[p][k]
        sb, rb, _ = bufs[k, p]
        sb[...] = value(k, p, index(left[p], i, 1 - bits[i])).astype(sb.dtype)
        c = pltpu.make_async_remote_copy(sb, rb, send_sem.at[k, p], recv_sem.at[k, p],
                                         device_id=partner(dims, at, i), device_id_type=MESH)
        c.start()
        return c

    def finish(k, p, c):
        i = plan[p][k]
        _, rb, acc = bufs[k, p]
        c.wait_recv()
        total = value(k, p, index(left[p], i, bits[i])) + rb[...].astype(f32)
        a, h = parts[p]
        if k < n - 1:
            acc[...] = total
        else:
            out_ref[a, :, halves[h][0] : halves[h][0] + halves[h][1]] = total
        left[p].remove(i)

    def small_begin(k):
        i = plan[0][k]
        src = (small_in if k == 0 else smalls[k - 1][1]).at[index(small_left, i, 1 - bits[i])]
        c = pltpu.make_async_remote_copy(src, smalls[k][0], small_send.at[k], small_recv.at[k],
                                         device_id=partner(dims, at, i), device_id_type=MESH)
        c.start()
        return c

    def small_finish(k, c):
        i = plan[0][k]
        c.wait_recv()
        total = (small_in if k == 0 else smalls[k - 1][1])[index(small_left, i, bits[i])] + smalls[k][0][...]
        if k < n - 1:
            smalls[k][1][...] = total
        else:
            small_out[...] = total
        small_left.remove(i)

    every = []
    small = small_begin(0)
    every.append(small)
    live = [None] * len(parts)
    for p, (a, h) in enumerate(parts):
        if h == 0:
            own[a].wait()
            core[a].wait_recv()
        live[p] = begin(1, p)
        every.append(live[p])
    for k in range(1, n):
        small_finish(k - 1, small)
        small = small_begin(k)
        every.append(small)
        for p in range(len(parts)):
            finish(k, p, live[p])
            if k < n - 1:
                live[p] = begin(k + 1, p)
                every.append(live[p])
    small_finish(n - 1, small)
    for c in core + every:
        c.wait_send()


def scatter_grads(grads, small, reps, groups):
    dims = bit_dims(reps, groups)
    n = len(dims)
    full, cols = grads[0].shape
    rows = full // (reps * groups)
    first = cols // 2 // 128 * 128
    halves = [(0, first), (first, cols - first)]
    count = len(grads)
    parts = count * len(halves)
    lead = (2,) * n
    link = grads[0].dtype
    f32 = jnp.float32
    grads = [g.reshape(lead + (rows, cols)) for g in grads]
    small = small.reshape(lead + small.shape[1:])
    sem = pltpu.SemaphoreType.DMA
    half = pltpu.VMEM((count,) + (2,) * (n - 1) + (rows, cols), link)
    scratch = [half, half, sem((count,)), sem((count,)), sem((count,)), sem((n, parts)), sem((n, parts)), sem((n,)), sem((n,))]
    for k in range(1, n):
        for p in range(parts):
            shape = (2,) * (n - 1 - k) + (rows, halves[p % 2][1])
            scratch += [pltpu.VMEM(shape, link), pltpu.VMEM(shape, link)]
            if k < n - 1:
                scratch.append(pltpu.VMEM(shape, f32))
    for k in range(n):
        shape = (2,) * (n - 1 - k) + small.shape[n:]
        scratch.append(pltpu.VMEM(shape, f32))
        if k < n - 1:
            scratch.append(pltpu.VMEM(shape, f32))
    vm = pl.BlockSpec(memory_space=pltpu.VMEM)
    hbm = pl.BlockSpec(memory_space=pl.ANY)
    return pl.pallas_call(
        functools.partial(scatter_kernel, dims, halves, count),
        out_shape=[jax.ShapeDtypeStruct((count, rows, cols), f32), jax.ShapeDtypeStruct(small.shape[n:], f32)],
        in_specs=[hbm] * count + [vm],
        out_specs=[vm] * 2,
        scratch_shapes=scratch,
        compiler_params=pltpu.CompilerParams(collective_id=1, has_side_effects=True, vmem_limit_bytes=60 * MIB),
    )(*grads, small)


def gather_all(vectors, weights, router, shift):
    axes = ("rep", "exp")
    return (
        [lax.all_gather(v, axes, axis=0, tiled=True) for v in vectors],
        [lax.all_gather(w, axes, axis=0, tiled=True) for w in weights],
        lax.all_gather(router, axes, axis=0, tiled=True),
        lax.all_gather(shift, axes, axis=1, tiled=True),
    )


def scatter_all(vectors, weights, router, shift):
    axes = ("rep", "exp")
    return (
        [lax.psum_scatter(v, axes, scatter_dimension=0, tiled=True) for v in vectors],
        [lax.psum_scatter(w, axes, scatter_dimension=0, tiled=True) for w in weights],
        lax.psum_scatter(router, axes, scatter_dimension=0, tiled=True),
        lax.psum_scatter(shift, axes, scatter_dimension=1, tiled=True),
    )


def normal_parts(v):
    e = jnp.exp(v * v * -0.5)
    t = 1.0 / (1.0 + (0.3275911 * 0.7071067811865476) * jnp.abs(v))
    poly = t * (0.127414796 + t * (-0.142248368 + t * (0.7107068705 + t * (-0.7265760135 + t * 0.5307027145))))
    q = poly * e
    return jnp.where(v < 0, q, 1.0 - q), e * 0.3989422804014327

def dot(a, b, ca, cb):
    return lax.dot_general(a, b, (((ca,), (cb,)), ((), ())), preferred_element_type=jnp.float32)

def experts_kernel(reps, groups, x_ref, g_ref, rest_ref, p_ref, win_ref, bias_in, wout_ref,
                   res_ref, ig_ref, gin_ref, gb_ref, gout_ref,
                   x_all, g_all, res_send, ig_send, wi, wo, wis, wos, act_all, pg_all, gin_buf, gout_buf, res_acc, ig_acc, bias_ref, p_all, p_turned, rg_all, p_rows,
                   own_sem, psem, prec, dsem, drec, rsem, rrec, bsem, brec, bown, wsem, ssem, osem):
    me, rep = lax.axis_index("exp"), lax.axis_index("rep")
    blocks = x_ref.shape[1]
    cap, wide = x_ref.shape[2:]
    rows = groups * cap
    chunks, part = wi.shape[0], wi.shape[2]
    half = groups // 2
    peers = [lax.rem(me + s, groups) for s in range(1, groups)]
    side = (rep + 1 - 2 * (rep % 2), rep + 2 - 4 * ((rep // 2) % 2))
    both = (x_all, g_all, p_all)
    back = ((res_send, res_ref), (ig_send, ig_ref))

    def load(j, f):
        return (pltpu.make_async_copy(win_ref.at[j, :, pl.ds(f * part, part)], wi.at[f], wsem.at[0, f]),
                pltpu.make_async_copy(wout_ref.at[j, pl.ds(f * part, part)], wo.at[f], wsem.at[1, f]))
    def load_slice(j):
        at = pl.ds(pl.multiple_of(rep * part, part), part)
        return (pltpu.make_async_copy(win_ref.at[j, :, at], wis, ssem.at[0]),
                pltpu.make_async_copy(wout_ref.at[j, at], wos, ssem.at[1]))
    def out_copies(j):
        return (pltpu.make_async_copy(gin_buf, gin_ref.at[j], osem.at[0]),
                pltpu.make_async_copy(gout_buf, gout_ref.at[j], osem.at[1]))
    ahead = AHEAD
    def dispatch(j, s):
        return pltpu.make_async_remote_copy(x_ref.at[peers[s], j], x_all.at[j, 0, me], dsem.at[j, s], drec.at[j, s],
                                            device_id=(rep, peers[s]), device_id_type=MESH)
    def dispatch_gates(s):
        return pltpu.make_async_remote_copy(p_ref.at[peers[s]], p_all.at[0, 0, me], psem.at[s], prec.at[s],
                                            device_id=(rep, peers[s]), device_id_type=MESH)
    def own(j, t):
        if t == 0:
            return pltpu.make_async_copy(x_ref.at[me, j], x_all.at[j, 0, me], own_sem.at[t, j])
        if t == 1:
            if j < ahead:
                return pltpu.make_async_copy(g_ref.at[j], g_all.at[j], own_sem.at[t, j])
            return pltpu.make_async_copy(rest_ref.at[j - ahead], g_all.at[j, 0], own_sem.at[t, j])
        return pltpu.make_async_copy(p_ref.at[me], p_all.at[0, 0, me], own_sem.at[t, 0])
    def across(j, t, n):
        dst = both[t]
        return pltpu.make_async_remote_copy(dst.at[j, 0], dst.at[j, 1 + n], rsem.at[t, j, n], rrec.at[t, j, n],
                                            device_id=(side[n], me), device_id_type=MESH)
    def onward(j, t, n):
        dst = both[t]
        at = pl.ds(n * half, half)
        return pltpu.make_async_remote_copy(dst.at[j, 1 + n, at], dst.at[j, 3, at], rsem.at[t, j, 2 + n], rrec.at[t, j, 2 + n],
                                            device_id=(side[1 - n], me), device_id_type=MESH)
    def give(j, t, s):
        src, dst = back[t]
        return pltpu.make_async_remote_copy(src.at[j, peers[s]], dst.at[me, j], bsem.at[t, j, s], brec.at[t, j, s],
                                            device_id=(rep, peers[s]), device_id_type=MESH)
    def give_own(j, t):
        src, dst = back[t]
        return pltpu.make_async_copy(src.at[j, me], dst.at[me, j], bown.at[t, j])
    def flat(v):
        return v.astype(jnp.float32).reshape(-1, wide).astype(jnp.bfloat16)

    barrier = pltpu.get_barrier_semaphore()
    for p in peers:
        pl.semaphore_signal(barrier, inc=1, device_id=(rep, p), device_id_type=MESH)
    for n in side:
        pl.semaphore_signal(barrier, inc=1, device_id=(n, me), device_id_type=MESH)
    pl.semaphore_wait(barrier, groups - 1 + 2)

    for s in range(groups - 1):
        dispatch_gates(s).start()
    own(0, 2).start()

    def send_inputs(j):
        for s in range(groups - 1):
            dispatch(j, s).start()
        own(j, 0).start()
    for j in range(min(2, blocks)):
        send_inputs(j)
    for j in range(blocks):
        own(j, 1).start()
    for j in range(blocks):
        for f in range(chunks):
            bias_ref[j, f] = bias_in[j : j + 1, f * part : (f + 1) * part].astype(jnp.float32)
    for f in range(chunks):
        for c in load(0, f): c.start()
    for c in load_slice(0): c.start()

    def turn_gates(r):
        for s in range(groups):
            p_rows[s : s + 1] = p_all[0, r, s, 0:1]
        p_turned[r] = jnp.transpose(p_rows[...])

    def gated(j, r):
        gates = p_turned[r, pl.ds(pl.multiple_of(j * cap, 8), cap)]
        parts = [g_all[j, r, s].astype(jnp.float32) * gates[:, s : s + 1] for s in range(groups)]
        return jnp.concatenate(parts, axis=0).astype(jnp.bfloat16)

    p_rows[...] = jnp.zeros(p_rows.shape, jnp.float32)
    for j in range(blocks):
        own(j, 1).wait()
        if j >= ahead:
            for n in range(2):
                across(j, 1, n).start()
    for s in range(groups - 1):
        dispatch_gates(s).wait_recv()
    own(0, 2).wait()
    for n in range(2):
        across(0, 2, n).start()
    turn_gates(0)

    def own_rows(j):
        x, g = flat(x_all[j, 0]), gated(j, 0)
        def chunk(f, _):
            for c in load(j, f): c.wait()
            pre = dot(x, wi[f], 1, 0) + bias_ref[j, f]
            cdf, pdf = normal_parts(pre)
            act = (pre * cdf).astype(jnp.bfloat16)
            ag = dot(g, wo[f], 1, 1)
            pg = (ag * (cdf + pre * pdf)).astype(jnp.bfloat16)
            more, less = dot(act, wo[f], 1, 0), dot(pg, wi[f], 1, 1)
            @pl.when(f == 0)
            def _():
                res_acc[...] = more
                ig_acc[...] = less
            @pl.when(f > 0)
            def _():
                res_acc[...] += more
                ig_acc[...] += less
            @pl.when(j + 1 < blocks)
            def _():
                for c in load(j + 1, f): c.start()
            return 0
        lax.fori_loop(0, chunks, chunk, 0)
        res_send[j] = res_acc[...].reshape(groups, cap, wide).astype(jnp.bfloat16)
        ig_send[j] = ig_acc[...].reshape(groups, cap, wide).astype(jnp.bfloat16)

    def weights(j):
        for c in load_slice(j): c.wait()
        def one(r, _):
            x, g = flat(x_all[j, r]), gated(j, r)
            rg_all[r] = g
            pre = dot(x, wis[...], 1, 0) + bias_ref[j, rep]
            cdf, pdf = normal_parts(pre)
            act_all[r] = (pre * cdf).astype(jnp.bfloat16)
            pg_all[r] = (dot(g, wos[...], 1, 1) * (cdf + pre * pdf)).astype(jnp.bfloat16)
            return 0
        lax.fori_loop(0, reps, one, 0)
        @pl.when(j + 1 < blocks)
        def _():
            for c in load_slice(j + 1): c.start()
        @pl.when(j > 0)
        def _():
            for c in out_copies(j - 1): c.wait()
        act, pg = act_all[...].reshape(reps * rows, part), pg_all[...].reshape(reps * rows, part)
        gout_buf[...] = dot(act, rg_all[...].reshape(reps * rows, wide), 0, 0)
        gin_buf[...] = dot(flat(x_all[j]), pg, 0, 0)
        gb_ref[j] = jnp.sum(pg.astype(jnp.float32), axis=0, keepdims=True)
        for c in out_copies(j): c.start()

    def step(k, _):
        @pl.when(k < blocks)
        def _():
            for s in range(groups - 1):
                dispatch(k, s).wait_recv()
            own(k, 0).wait()
            @pl.when(k + 2 < blocks)
            def _():
                send_inputs(k + 2)
            for n in range(2):
                across(k, 0, n).start()
            own_rows(k)
            for t in range(2):
                for s in range(groups - 1):
                    give(k, t, s).start()
                give_own(k, t).start()
        @pl.when((k > 0) & (k <= blocks))
        def _():
            for n in range(2):
                across(k - 1, 0, n).wait_recv()
            for n in range(2):
                onward(k - 1, 0, n).start()
        @pl.when((k > 0) & (k <= blocks - ahead))
        def _():
            for n in range(2):
                across(k - 1 + ahead, 1, n).wait_recv()
            for n in range(2):
                onward(k - 1 + ahead, 1, n).start()
        @pl.when(k == 1)
        def _():
            for n in range(2):
                across(0, 2, n).wait_recv()
            for n in range(2):
                onward(0, 2, n).start()
        @pl.when(k == 2)
        def _():
            for n in range(2):
                onward(0, 2, n).wait_recv()
            for r in range(1, reps):
                turn_gates(r)
        @pl.when(k > 1)
        def _():
            for n in range(2):
                onward(k - 2, 0, n).wait_recv()
            @pl.when(k - 2 >= ahead)
            def _():
                for n in range(2):
                    onward(k - 2, 1, n).wait_recv()
            weights(k - 2)
        return 0
    lax.fori_loop(0, blocks + 2, step, 0)

    for c in out_copies(blocks - 1): c.wait()
    def drain(j, _):
        for s in range(groups - 1):
            dispatch(j, s).wait_send()
        for t in range(2):
            for s in range(groups - 1):
                give(j, t, s).wait_recv()
                give(j, t, s).wait_send()
            give_own(j, t).wait()
        for n in range(2):
            across(j, 0, n).wait_send()
            onward(j, 0, n).wait_send()
        @pl.when(j >= ahead)
        def _():
            for n in range(2):
                across(j, 1, n).wait_send()
                onward(j, 1, n).wait_send()
        return 0
    lax.fori_loop(0, blocks, drain, 0)
    for s in range(groups - 1):
        dispatch_gates(s).wait_send()
    for n in range(2):
        across(0, 2, n).wait_send()
        onward(0, 2, n).wait_send()


def experts_call(x, g, rest, gate, w_in, b_in, w_out, reps, groups):
    _, blocks, cap, wide = x.shape
    hidden = w_in.shape[2]
    part = hidden // reps
    anyw = pl.BlockSpec(memory_space=pl.ANY)
    vm = pl.BlockSpec(memory_space=pltpu.VMEM)
    bf, f32 = jnp.bfloat16, jnp.float32
    sem = pltpu.SemaphoreType.DMA
    n = groups - 1
    rows = groups * cap
    lanes = gate.shape[-1]
    return pl.pallas_call(
        functools.partial(experts_kernel, reps, groups),
        out_shape=[jax.ShapeDtypeStruct(x.shape, bf), jax.ShapeDtypeStruct(x.shape, bf),
                   jax.ShapeDtypeStruct((blocks, wide, part), f32), jax.ShapeDtypeStruct((blocks, 1, part), f32),
                   jax.ShapeDtypeStruct((blocks, part, wide), f32)],
        in_specs=[anyw, anyw, anyw, vm, anyw, vm, anyw],
        out_specs=[anyw, anyw, anyw, vm, anyw],
        scratch_shapes=[
            pltpu.VMEM((blocks, reps, groups, cap, wide), bf), pltpu.VMEM((blocks, reps, groups, cap, wide), bf),
            pltpu.VMEM((blocks, groups, cap, wide), bf), pltpu.VMEM((blocks, groups, cap, wide), bf),
            pltpu.VMEM((reps, wide, part), bf), pltpu.VMEM((reps, part, wide), bf),
            pltpu.VMEM((wide, part), bf), pltpu.VMEM((part, wide), bf),
            pltpu.VMEM((reps, rows, part), bf), pltpu.VMEM((reps, rows, part), bf),
            pltpu.VMEM((wide, part), f32), pltpu.VMEM((part, wide), f32),
            pltpu.VMEM((rows, wide), f32), pltpu.VMEM((rows, wide), f32), pltpu.VMEM((blocks, reps, 1, part), f32),
            pltpu.VMEM((1, reps) + gate.shape, f32), pltpu.VMEM((reps, lanes, 128), f32), pltpu.VMEM((reps, rows, wide), bf), pltpu.VMEM((128, lanes), f32),
            sem((3, blocks)), sem((n,)), sem((n,)), sem((blocks, n)), sem((blocks, n)), sem((3, blocks, 4)), sem((3, blocks, 4)),
            sem((2, blocks, n)), sem((2, blocks, n)), sem((2, blocks)), sem((2, reps)), sem((2,)), sem((2,))],
        compiler_params=pltpu.CompilerParams(collective_id=2, has_side_effects=True, vmem_limit_bytes=60 * MIB),
    )(x, g, rest, gate, w_in, b_in, w_out)

def experts_plain(x, g, w_in, b_in, w_out):
    bf, f32 = jnp.bfloat16, jnp.float32
    rx = lax.all_to_all(x, "exp", split_axis=0, concat_axis=0, tiled=True)
    rg = lax.all_to_all(g, "exp", split_axis=0, concat_axis=0, tiled=True)
    pre = jnp.einsum("secd,edf->secf", rx, w_in, preferred_element_type=f32)
    pre = pre + b_in.astype(f32)[None, :, None, :]
    cdf, pdf = normal_parts(pre)
    act = (pre * cdf).astype(bf)
    res = jnp.einsum("secf,efd->secd", act, w_out, preferred_element_type=f32).astype(bf)
    pg = jnp.einsum("secd,efd->secf", rg, w_out, preferred_element_type=f32) * (cdf + pre * pdf)
    pg = pg.astype(bf)
    ig = jnp.einsum("secf,edf->secd", pg, w_in, preferred_element_type=f32).astype(bf)
    gout = jnp.einsum("secf,secd->efd", act, rg, preferred_element_type=f32).astype(bf)
    gin = jnp.einsum("secd,secf->edf", rx, pg, preferred_element_type=f32).astype(bf)
    gb = jnp.sum(pg, axis=(0, 2), dtype=f32).astype(bf)
    return (
        lax.all_to_all(res, "exp", split_axis=0, concat_axis=0, tiled=True),
        lax.all_to_all(ig, "exp", split_axis=0, concat_axis=0, tiled=True),
        lax.psum_scatter(gin, "rep", scatter_dimension=2, tiled=True).astype(f32),
        lax.psum_scatter(gb, "rep", scatter_dimension=1, tiled=True).astype(f32)[:, None],
        lax.psum_scatter(gout, "rep", scatter_dimension=1, tiled=True).astype(f32),
    )


epsilon = 1e-06
masked_score = -1e30


def normalize(values):
    center = values - jnp.mean(values, axis=-1, keepdims=True)
    spread = jnp.mean(center * center, axis=-1, keepdims=True)
    scale = lax.rsqrt(spread + epsilon)
    return center * scale, scale


def normalize_back(grad, unit, scale):
    mean = jnp.mean(grad, axis=-1, keepdims=True)
    along = jnp.mean(grad * unit, axis=-1, keepdims=True)
    return (grad - mean - unit * along) * scale


def two_parts(v):
    high = v.astype(jnp.bfloat16)
    return high, (v - high.astype(jnp.float32)).astype(jnp.bfloat16)


def positions_of(routes, valid_col, priority_col, priority_row, experts):
    length = routes.shape[0]
    f32, bf = jnp.float32, jnp.bfloat16
    token_row = lax.broadcasted_iota(jnp.int32, (length, length), 1)
    token_col = lax.broadcasted_iota(jnp.int32, (length, length), 0)
    rank_col = jnp.sum(
        jnp.where(priority_row == token_col, token_row, 0).astype(f32), axis=1, keepdims=True
    )
    rank_row = jnp.sum(
        jnp.where(priority_col == token_row, token_col, 0).astype(f32), axis=0, keepdims=True
    )
    earlier = (rank_row < rank_col).astype(f32).astype(bf)
    expert_row = lax.broadcasted_iota(jnp.int32, (length, experts), 1)
    ones = [(routes[:, k : k + 1] == expert_row).astype(f32) for k in range(routes.shape[1])]
    before = jnp.zeros((1, experts), f32)
    places = []
    for one in ones:
        live = one * valid_col
        count = dot(earlier, live.astype(bf), 1, 0) + before
        places.append(jnp.sum(count * one, axis=1, keepdims=True))
        before = before + jnp.sum(live, axis=0, keepdims=True)
    return ones, places


def body_plain(
    tokens,
    segments,
    valid,
    routes,
    priority,
    ln1_gain,
    ln1_bias,
    w_query,
    query_bias,
    w_key,
    w_value,
    value_bias,
    w_attn_out,
    attn_out_bias,
    ln2_gain,
    ln2_bias,
    w_router,
    expert_in,
    expert_in_bias,
    expert_out,
    expert_out_bias,
    cotangent,
):
    f32, bf = jnp.float32, jnp.bfloat16
    vectors, weights, router_weight, result_shift = gather_all(
        [ln1_gain, ln1_bias, query_bias, value_bias, attn_out_bias, ln2_gain, ln2_bias],
        [w_query, w_key, w_value, w_attn_out],
        w_router,
        expert_out_bias,
    )
    vectors = [v.astype(f32)[None] for v in vectors]
    gain_one, bias_one, query_shift, value_shift, proj_shift, gain_two, bias_two = vectors
    query_weight, key_weight, value_weight, proj_weight = weights
    length = tokens.shape[1]
    feature_dim = tokens.shape[2]
    head_dim = feature_dim // HEADS
    local_blocks = expert_in.shape[0]
    reps, groups = lax.axis_size("rep"), lax.axis_size("exp")
    experts = EXPERTS
    split = local_blocks * groups // experts
    top_count = routes.shape[2]
    capacity = (105 * top_count * length + 100 * experts - 1) // (100 * experts)
    room = -(-capacity // 8) * 8
    score_scale = head_dim ** (-0.5)
    inputs = tokens[0].astype(f32)
    row_segments = segments[0]
    row_valid = valid[0]
    places = jnp.arange(length, dtype=jnp.int32)
    allowed = (row_segments[:, None] == row_segments[None, :]) & (
        (row_valid[None, :] > 0) | (places[:, None] == places[None, :])
    )
    unit_one, scale_one = normalize(inputs)
    normed = (unit_one * gain_one + bias_one).astype(bf)
    query_rows = (dot(normed, query_weight, 1, 0) + query_shift).astype(bf)
    key_rows = dot(normed, key_weight, 1, 0).astype(bf)
    value_rows = (dot(normed, value_weight, 1, 0) + value_shift).astype(bf)
    query_heads = query_rows.reshape(length, HEADS, head_dim)
    key_heads = key_rows.reshape(length, HEADS, head_dim)
    value_heads = value_rows.reshape(length, HEADS, head_dim)

    def scores():
        return jnp.where(
            allowed[None],
            jnp.einsum("qhd,khd->hqk", query_heads, key_heads, preferred_element_type=f32)
            * score_scale,
            masked_score,
        )

    masked = scores()
    top_score = jnp.max(masked, axis=-1, keepdims=True)
    log_total = top_score + jnp.log(jnp.sum(jnp.exp(masked - top_score), axis=-1, keepdims=True))
    mixed = jnp.einsum(
        "hqk,khd->qhd",
        jnp.exp(masked - log_total).astype(bf),
        value_heads,
        preferred_element_type=f32,
    )
    mixed = mixed.reshape(length, feature_dim).astype(bf)
    residual = inputs + dot(mixed, proj_weight, 1, 0) + proj_shift
    unit_two, scale_two = normalize(residual)
    normed_two = (unit_two * gain_two + bias_two).astype(bf)
    logits = dot(normed_two, router_weight, 1, 0)
    logit_exp = jnp.exp(logits - jnp.max(logits, axis=-1, keepdims=True))
    router_probs = logit_exp / jnp.sum(logit_exp, axis=-1, keepdims=True)
    upstream = cotangent[0].astype(f32)
    ones, positions = positions_of(
        routes[0], row_valid[:, None].astype(f32), priority[0][:, None], priority[0][None], experts
    )
    expert_row = lax.broadcasted_iota(jnp.int32, (1, experts), 1).astype(f32)
    slot_row = lax.broadcasted_iota(jnp.int32, (1, experts * room), 1)
    kept, gates, slots, sent = [], [], [], jnp.zeros((experts * room, feature_dim), f32)
    for one, position in zip(ones, positions):
        keep = row_valid[:, None].astype(f32) * (position < capacity).astype(f32)
        gate = jnp.sum(router_probs * one, axis=1, keepdims=True) * keep
        place = jnp.sum(one * expert_row, axis=1, keepdims=True) * room + position
        place = jnp.where(keep > 0, place, -1.0).astype(jnp.int32)
        hot = (place == slot_row).astype(f32).astype(bf)
        kept.append(one * keep)
        gates.append(gate)
        slots.append(hot)
        sent = sent + dot(hot, (gate * upstream).astype(bf), 0, 0)
    any_slot = slots[0]
    for hot in slots[1:]:
        any_slot = any_slot + hot
    expert_slots = dot(any_slot, normed_two, 0, 0).astype(bf)
    gated = sum(one * gate for one, gate in zip(kept, gates))
    high, low = two_parts(gated)
    shift_grad = dot(high, cotangent[0], 0, 0) + dot(low, cotangent[0], 0, 0)

    def outgoing(v):
        v = v.astype(bf).reshape(experts, room, feature_dim)
        return jnp.repeat(v, split, axis=0).reshape(groups, local_blocks, room, feature_dim)

    moved = experts_plain(
        outgoing(expert_slots), outgoing(sent), expert_in, expert_in_bias, expert_out
    )
    result, slot_back, in_w_grad, in_b_grad, out_w_grad = moved
    result = result.reshape(experts, split, room, feature_dim)
    slot_back = slot_back.reshape(experts, split, room, feature_dim)
    results = [result[:, s].reshape(experts * room, feature_dim) for s in range(split)]
    backs = [slot_back[:, s].reshape(experts * room, feature_dim) for s in range(split)]
    combined, prob_grad = 0.0, 0.0
    for one, gate, hot in zip(kept, gates, slots):
        picked = dot(one.astype(bf), result_shift, 1, 0)
        for part in results:
            picked = picked + dot(hot, part, 1, 0)
        combined = combined + gate * picked
        prob_grad = prob_grad + one * jnp.sum(upstream * picked, axis=1, keepdims=True)
    output = residual + combined
    logit_grad = (
        router_probs * (prob_grad - jnp.sum(router_probs * prob_grad, axis=-1, keepdims=True))
    ).astype(bf)
    router_w_grad = dot(normed_two, logit_grad, 0, 0)
    normed_two_grad = dot(logit_grad, router_weight, 1, 1)
    for part in backs:
        normed_two_grad = normed_two_grad + dot(any_slot, part, 1, 0)
    gain_two_grad = jnp.sum(normed_two_grad * unit_two, axis=0)
    bias_two_grad = jnp.sum(normed_two_grad, axis=0)
    residual_grad = upstream + normalize_back(normed_two_grad * gain_two, unit_two, scale_two)
    branch_grad = residual_grad.astype(bf)
    proj_w_grad = dot(mixed, branch_grad, 0, 0)
    proj_b_grad = jnp.sum(branch_grad, axis=0, dtype=f32)
    mixed_grad = dot(branch_grad, proj_weight, 1, 1).astype(bf)
    mixed_grad = mixed_grad.reshape(length, HEADS, head_dim)
    again_probs = jnp.exp(scores() - log_total)
    prob_grads = jnp.einsum("qhd,khd->hqk", mixed_grad, value_heads, preferred_element_type=f32)
    value_grad = jnp.einsum(
        "hqk,qhd->khd", again_probs.astype(bf), mixed_grad, preferred_element_type=f32
    )
    value_grad = value_grad.astype(bf).reshape(length, feature_dim)
    inner_sum = jnp.sum(again_probs * prob_grads, axis=-1, keepdims=True)
    score_grad = (again_probs * (prob_grads - inner_sum)).astype(bf)
    query_grad = jnp.einsum("hqk,khd->qhd", score_grad, key_heads, preferred_element_type=f32)
    query_grad = (query_grad * score_scale).astype(bf).reshape(length, feature_dim)
    key_grad = jnp.einsum("hqk,qhd->khd", score_grad, query_heads, preferred_element_type=f32)
    key_grad = (key_grad * score_scale).astype(bf).reshape(length, feature_dim)
    query_w_grad = dot(normed, query_grad, 0, 0)
    query_b_grad = jnp.sum(query_grad, axis=0, dtype=f32)
    key_w_grad = dot(normed, key_grad, 0, 0)
    value_w_grad = dot(normed, value_grad, 0, 0)
    value_b_grad = jnp.sum(value_grad, axis=0, dtype=f32)
    normed_grad = dot(query_grad, query_weight, 1, 1)
    normed_grad = normed_grad + dot(key_grad, key_weight, 1, 1)
    normed_grad = normed_grad + dot(value_grad, value_weight, 1, 1)
    gain_one_grad = jnp.sum(normed_grad * unit_one, axis=0)
    bias_one_grad = jnp.sum(normed_grad, axis=0)
    tokens_grad = residual_grad + normalize_back(normed_grad * gain_one, unit_one, scale_one)
    vector_sums, weight_sums, router_sum, shift_sum = scatter_all(
        [
            gain_one_grad,
            bias_one_grad,
            query_b_grad,
            value_b_grad,
            proj_b_grad,
            gain_two_grad,
            bias_two_grad,
        ],
        [query_w_grad, key_w_grad, value_w_grad, proj_w_grad],
        router_w_grad,
        shift_grad,
    )
    return (
        output.astype(jnp.bfloat16)[None],
        tokens_grad[None],
        vector_sums[0],
        vector_sums[1],
        weight_sums[0],
        vector_sums[2],
        weight_sums[1],
        weight_sums[2],
        vector_sums[3],
        weight_sums[3],
        vector_sums[4],
        vector_sums[5],
        vector_sums[6],
        router_sum,
        in_w_grad,
        in_b_grad[:, 0],
        out_w_grad,
        shift_sum,
    )


AHEAD = 1


def eye_of(n):
    same = lax.broadcasted_iota(jnp.int32, (n, n), 0) == lax.broadcasted_iota(jnp.int32, (n, n), 1)
    return same.astype(jnp.float32).astype(jnp.bfloat16)


def lanes_of(n=1):
    return lax.broadcasted_iota(jnp.int32, (n, 128), 1)


def mask_of(ints, cols):
    n = ints.shape[1]
    same = lax.broadcasted_iota(jnp.int32, (n, n), 0) == lax.broadcasted_iota(jnp.int32, (n, n), 1)
    near = cols[:, 0:1] == ints[0:1]
    open_key = jnp.where(same, 1.0, cols[:, 1:2]) > 0
    return jnp.where(near & open_key, 0.0, masked_score)


def side_masks(head_dim):
    lane = lanes_of()
    return [
        ((lane >= s * head_dim) & (lane < (s + 1) * head_dim)).astype(jnp.float32).astype(jnp.bfloat16)
        for s in range(128 // head_dim)
    ]


def vectors_of(small_ref):
    f32, bf = jnp.float32, jnp.bfloat16
    reps, groups, lines, _ = small_ref.shape
    count = reps * groups
    per = lines - 8
    tail = small_ref[...].astype(f32)[:, :, per:].reshape(count * 8, 128).astype(bf)
    wide = count * per
    spread = lax.broadcasted_iota(jnp.int32, (128, wide), 1) % per
    spread = (spread == lax.broadcasted_iota(jnp.int32, (128, wide), 0)).astype(f32).astype(bf)
    laid = dot(tail, spread, 1, 0)
    owner = lax.broadcasted_iota(jnp.int32, (count * 8, wide), 1) // per
    mine = owner == lax.broadcasted_iota(jnp.int32, (count * 8, wide), 0) // 8
    pick = lax.broadcasted_iota(jnp.int32, (8, count * 8), 1) % 8
    pick = (pick == lax.broadcasted_iota(jnp.int32, (8, count * 8), 0)).astype(f32).astype(bf)
    rows = dot(pick, jnp.where(mine, laid, 0.0).astype(bf), 1, 0)
    return [rows[i : i + 1] for i in range(7)]


def matrix_of(small_ref):
    reps, groups, lines, _ = small_ref.shape
    per = lines - 8
    part = small_ref[...].astype(jnp.float32)[:, :, :per]
    return part.reshape(reps * groups * per, 128).astype(jnp.bfloat16)


def weight_of(ref):
    wide = ref.shape[-1]
    return ref.astype(jnp.float32).reshape(-1, wide).astype(jnp.bfloat16)


def integer_rows(raw):
    raw = raw.astype(jnp.float32)
    line = lax.broadcasted_iota(jnp.int32, raw.shape, 0)
    order = raw[2:3]
    high = jnp.floor(order * (1.0 / 64.0))
    low = order - high * 64.0
    return jnp.where(line == 2, high, jnp.where(line == 5, low, raw)), order


def front_kernel(
    capacity,
    room,
    head_dim,
    tokens_ref,
    cot_ref,
    ints_ref,
    small_in,
    wq_in,
    wk_in,
    wv_in,
    wo_in,
    xs_ref,
    g_first_out,
    g_rest_out,
    gate_ref,
    resid_out,
    q_out,
    k_out,
    v_out,
    mixed_out,
    lse_ref,
    info_ref,
    wa_out,
    wo_out,
    small_ref,
    g_ref,
    resid_ref,
    q_ref,
    k_ref,
    v_ref,
    mixed_ref,
    wa_ref,
    wo_ref,
    out_sem,
    mask_ref,
    a2_ref,
    gs_ref,
    own_sem,
    send_sem,
    recv_sem,
    g_send_sem,
    g_recv_sem,
    g_own_sem,
    side_send_sem,
    side_recv_sem,
):
    f32, bf = jnp.float32, jnp.bfloat16
    length, wide = tokens_ref.shape
    groups, blocks = xs_ref.shape[:2]
    me, rep = lax.axis_index("exp"), lax.axis_index("rep")
    level, core = me // 2, me % 2
    levels = groups // 2
    beside = (rep + 1 - 2 * (rep % 2), rep + 2 - 4 * ((rep // 2) % 2))
    bufs = (wa_ref, small_ref, wo_ref)
    mine = [
        pltpu.make_async_copy(wq_in, wa_ref.at[rep, me, 0], own_sem.at[0]),
        pltpu.make_async_copy(wk_in, wa_ref.at[rep, me, 1], own_sem.at[1]),
        pltpu.make_async_copy(wv_in, wa_ref.at[rep, me, 2], own_sem.at[2]),
        pltpu.make_async_copy(small_in, small_ref.at[rep, me], own_sem.at[3]),
        pltpu.make_async_copy(wo_in, wo_ref.at[rep, me], own_sem.at[4]),
    ]
    for c in mine:
        c.start()

    def flip(r):
        there = level
        for one in (1, 2):
            if r & one:
                there = there + one - 2 * one * ((there // one) % 2)
        return there

    def block(r):
        return flip(r) * 2 + core

    def send(src, a, r, n, device):
        return pltpu.make_async_remote_copy(
            src, src, send_sem.at[a, r, n], recv_sem.at[a, r, n], device_id=device, device_id_type=MESH
        )

    def up(a, r):
        far, here = (2, 1) if r == 3 else (r, 0)
        return send(bufs[a].at[rep, block(here)], a, r, 0, (rep, flip(far) * 2 + core))

    def aside(a, r, n):
        return send(bufs[a].at[rep, block(r)], a, r, 1 + n, (beside[n], me))

    def onward(a, r, n):
        ref = bufs[a].at[beside[n], block(r)]
        if a == 1:
            half = ref.shape[0] // 2
            ref = ref.at[pl.ds(n * half, half)]
        else:
            half = wide // 2
            ref = ref.at[(slice(None),) * (len(ref.shape) - 1) + (pl.ds(n * half, half),)]
        return send(ref, a, r, 3 + n, (beside[1 - n], me))

    def over(a, r):
        return send(bufs[a].at[:, block(r)], a, r, 5, (rep, me + 1 - 2 * core))

    barrier = pltpu.get_barrier_semaphore()
    peers = [lax.rem(me + s, groups) for s in range(1, groups)]
    for p in peers:
        pl.semaphore_signal(barrier, inc=1, device_id=(rep, p), device_id_type=MESH)
    for n in beside:
        pl.semaphore_signal(barrier, inc=1, device_id=(n, me), device_id_type=MESH)
    pl.semaphore_wait(barrier, groups + 1)
    for c in mine:
        c.wait()

    def step(sets, r):
        for a in sets:
            if 0 < r < levels:
                up(a, r).wait_recv()
            if r == 1 and levels > 2:
                up(a, 3).start()
            if r < levels:
                for n in range(2):
                    aside(a, r, n).start()
            if 0 < r <= levels:
                for n in range(2):
                    aside(a, r - 1, n).wait_recv()
                for n in range(2):
                    onward(a, r - 1, n).start()
            if 1 < r <= levels + 1:
                for n in range(2):
                    onward(a, r - 2, n).wait_recv()
                over(a, r - 2).start()

    early, late = (0, 1), (2,)
    near = range(1, min(levels, 3))
    for a in early + late:
        for r in near:
            up(a, r).start()
    step(early, 0)
    ints, priority_row = integer_rows(ints_ref[...])
    eye = eye_of(length)
    cols = dot(eye, ints.astype(bf), 1, 1)
    mask_ref[...] = mask_of(ints, cols)
    step(early, 1)
    token_row = lax.broadcasted_iota(jnp.int32, (length, length), 1).astype(f32)
    token_col = lax.broadcasted_iota(jnp.int32, (length, length), 0).astype(f32)
    priority_col = cols[:, 2:3] * 64.0 + cols[:, 5:6]
    rank_col = jnp.sum(jnp.where(priority_row == token_col, token_row, 0.0), axis=1, keepdims=True)
    rank_row = jnp.sum(jnp.where(priority_col == token_row, token_col, 0.0), axis=0, keepdims=True)
    earlier = (rank_row < rank_col).astype(f32).astype(bf)
    lane = lanes_of()
    expert_lane = (lane - 32).astype(f32)
    valid_col = cols[:, 1:2]
    before = jnp.zeros((1, 128), f32)
    keeps, places = [], []
    marks = jnp.zeros((length, 128), f32)
    for k in range(2):
        expert = cols[:, 3 + k : 4 + k]
        one = (expert == expert_lane).astype(f32)
        live = one * valid_col
        count = dot(earlier, live.astype(bf), 1, 0) + before
        before = before + jnp.sum(live, axis=0, keepdims=True)
        position = jnp.sum(count * one, axis=1, keepdims=True)
        keep = valid_col * (position < capacity).astype(f32)
        place = jnp.where(keep > 0, expert * room + position, -1.0)
        high = jnp.floor(place * (1.0 / 32.0))
        low = place - high * 32.0
        marks = jnp.where(lane == 2 * k, high, jnp.where(lane == 2 * k + 1, low, marks))
        keeps.append(keep)
        places.append(place)
    step(early, 2)
    for a in late:
        up(a, 1).wait_recv()
        if levels > 2:
            up(a, 3).start()
    turned = dot(marks.astype(bf), eye, 0, 0)
    place_rows = [turned[2 * k : 2 * k + 1] * 32.0 + turned[2 * k + 1 : 2 * k + 2] for k in range(2)]
    part = blocks * room
    slot = lax.broadcasted_iota(jnp.int32, (part, length), 0).astype(f32)

    def hots_of(d):
        first = (d * part).astype(f32)
        return [(slot == row - first).astype(f32).astype(bf) for row in place_rows]

    def fill_grads(d, _):
        hots = hots_of(d)
        grads = dot(hots[0] + hots[1], cot_ref[...], 1, 0)
        gs_ref[d] = grads.reshape(blocks, room, wide).astype(bf)
        return 0

    lax.fori_loop(0, groups, fill_grads, 0)

    def give(j, s):
        return pltpu.make_async_remote_copy(
            gs_ref.at[peers[s], j],
            g_ref.at[j, 0, me],
            g_send_sem.at[j, s],
            g_recv_sem.at[j, s],
            device_id=(rep, peers[s]),
            device_id_type=MESH,
        )

    def give_own(j):
        return pltpu.make_async_copy(gs_ref.at[me, j], g_ref.at[j, 0, me], g_own_sem.at[j])

    def spread(src, dst, j, n, device):
        return pltpu.make_async_remote_copy(
            src,
            dst,
            side_send_sem.at[j, n],
            side_recv_sem.at[j, n],
            device_id=(device, me),
            device_id_type=MESH,
        )

    def g_across(j, n):
        return spread(g_ref.at[j, 0], g_ref.at[j, 1 + n], j, n, beside[n])

    def g_onward(j, n):
        at = pl.ds(n * (groups // 2), groups // 2)
        return spread(g_ref.at[j, 1 + n, at], g_ref.at[j, 3, at], j, 2 + n, beside[1 - n])

    def begin_across(j):
        for n in range(2):
            g_across(j, n).start()

    def begin_onward(j):
        for n in range(2):
            g_across(j, n).wait_recv()
        for n in range(2):
            g_onward(j, n).start()

    ahead = AHEAD
    written = []

    def write(src, dst):
        c = pltpu.make_async_copy(src, dst, out_sem.at[len(written)])
        c.start()
        written.append(c)


    def begin_give(j):
        for s in range(groups - 1):
            give(j, s).start()
        give_own(j).start()

    def have(j):
        for s in range(groups - 1):
            give(j, s).wait_recv()
        give_own(j).wait()

    begin_give(0)
    inputs = tokens_ref[...].astype(f32)
    unit_one, _ = normalize(inputs)
    for r in range(3, levels):
        step(early, r)
    for a in late:
        for r in range(2, levels):
            up(a, r).wait_recv()
    begin_give(1)
    for a in late:
        for r in range(levels):
            for n in range(2):
                aside(a, r, n).start()
    for r in range(max(3, levels), levels + 2):
        step(early, r)
    for a in early:
        for r in range(levels):
            over(a, r).wait_recv()
    have(0)
    begin_across(0)
    for j in range(2, blocks - 1):
        begin_give(j)
    small_matrix = matrix_of(small_ref)
    gain_one, bias_one, query_shift, value_shift, proj_shift, gain_two, bias_two = vectors_of(small_ref)
    normed = (unit_one * gain_one + bias_one).astype(bf)
    q_ref[...] = (dot(normed, weight_of(wa_ref[:, :, 0]), 1, 0) + query_shift).astype(bf)
    k_ref[...] = dot(normed, weight_of(wa_ref[:, :, 1]), 1, 0).astype(bf)
    v_ref[...] = (dot(normed, weight_of(wa_ref[:, :, 2]), 1, 0) + value_shift).astype(bf)
    write(q_ref, q_out)
    write(k_ref, k_out)
    write(v_ref, v_out)
    write(wa_ref, wa_out)
    for a in late:
        for r in range(levels):
            for n in range(2):
                aside(a, r, n).wait_recv()
            for n in range(2):
                onward(a, r, n).start()
    sides = side_masks(head_dim)
    per = len(sides)
    scale = jnp.full((1, 128), head_dim**-0.5, f32).astype(bf)

    def heads(h, _):
        at = pl.ds(pl.multiple_of(h * 128, 128), 128)

        @pl.when(h == 1)
        def _():
            have(1)
            if ahead > 1:
                begin_across(1)
            if blocks > 2:
                begin_give(blocks - 1)

        query = q_ref[:, at] * scale
        total = jnp.zeros((128, length), f32)
        for s, side in enumerate(sides):
            score = dot(k_ref[:, at] * side, query, 1, 1) + mask_ref[...]
            top = jnp.max(score, axis=0, keepdims=True)
            expo = jnp.exp(score - top)
            norm = jnp.sum(expo, axis=0, keepdims=True)
            lse_ref[pl.ds(h * per + s, 1), :] = top + jnp.log(norm)
            probs = (expo * (1.0 / norm)).astype(bf)
            total = total + dot(v_ref[:, at] * side, probs, 0, 0)
        mixed_ref[at, :] = total.astype(bf)
        return 0

    half = wide // 256
    lax.fori_loop(0, half, heads, 0)
    for a in late:
        for r in range(levels):
            for n in range(2):
                onward(a, r, n).wait_recv()
            over(a, r).start()
    lax.fori_loop(half, wide // 128, heads, 0)
    begin_onward(0)
    write(mixed_ref, mixed_out)
    for r in range(levels):
        over(2, r).wait_recv()
    write(wo_ref, wo_out)
    residual = inputs + dot(mixed_ref[...], weight_of(wo_ref[...]), 0, 0) + proj_shift
    resid_ref[...] = residual
    write(resid_ref, resid_out)
    unit_two, _ = normalize(residual)
    normed_two = (unit_two * gain_two + bias_two).astype(bf)
    a2_ref[...] = normed_two
    routed = (lane >= 32) & (lane < 64)
    logits = jnp.where(routed, dot(normed_two, small_matrix, 1, 0), masked_score)
    logit_exp = jnp.exp(logits - jnp.max(logits, axis=1, keepdims=True))
    probs = logit_exp / jnp.sum(logit_exp, axis=1, keepdims=True)
    info = probs
    gates = []
    for k in range(2):
        expert = cols[:, 3 + k : 4 + k]
        one = (expert == expert_lane).astype(f32)
        gate = jnp.sum(probs * one, axis=1, keepdims=True) * keeps[k]
        info = jnp.where(lane == k, places[k], jnp.where(lane == 2 + k, expert, info))
        high, _ = two_parts(gate)
        middle, low = two_parts(gate - high.astype(f32))
        split = jnp.where(lane == 1, middle.astype(f32), jnp.where(lane == 2, low.astype(f32), 0.0))
        gates.append(jnp.where(lane == 0, high.astype(f32), split).astype(bf))
    info_ref[...] = info

    def fill_inputs(d, _):
        hots = hots_of(d)
        inside = dot(hots[0] + hots[1], a2_ref[...], 1, 0)
        xs_ref[d] = inside.reshape(blocks, room, wide).astype(bf)
        gate = dot(gates[0], hots[0], 0, 1) + dot(gates[1], hots[1], 0, 1)
        gate_ref[d, 0:1, 0:part] = gate[0:1] + gate[1:2] + gate[2:3]
        return 0

    for j in range(1, ahead):
        begin_onward(j)
    gate_ref[...] = jnp.zeros(gate_ref.shape, f32)
    lax.fori_loop(0, groups, fill_inputs, 0)
    for j in range(blocks):
        if j > 1:
            have(j)
        if j < ahead:
            for n in range(2):
                g_onward(j, n).wait_recv()
            write(g_ref.at[j], g_first_out.at[j])
        else:
            write(g_ref.at[j, 0], g_rest_out.at[j - ahead])
    for j in range(blocks):
        for s in range(groups - 1):
            give(j, s).wait_send()
    for j in range(ahead):
        for n in range(2):
            g_across(j, n).wait_send()
            g_onward(j, n).wait_send()
    for a in early + late:
        for r in range(levels):
            if r > 0:
                up(a, r).wait_send()
            for n in range(2):
                aside(a, r, n).wait_send()
                onward(a, r, n).wait_send()
            over(a, r).wait_send()
    for c in written:
        c.wait()


def back_kernel(
    head_dim,
    tokens_ref,
    cot_ref,
    ints_ref,
    small_ref,
    wa_in,
    wo_in,
    res_ref,
    ig_ref,
    resid_ref,
    q_in,
    k_in,
    v_in,
    mixed_in,
    lse_ref,
    info_ref,
    gin_ref,
    gout_ref,
    out_ref,
    tokens_grad_ref,
    wq_grad_ref,
    wk_grad_ref,
    wv_grad_ref,
    wo_grad_ref,
    small_grad_ref,
    gin_out_ref,
    gout_out_ref,
    mask_ref,
    mixed_grad_ref,
    query_grad_ref,
    key_grad_ref,
    value_grad_ref,
    gin_buf,
    gout_buf,
    sem,
    wa_ref,
    wo_ref,
    q_ref,
    k_ref,
    v_ref,
    mixed_ref,
    late_sem,
):
    f32, bf = jnp.float32, jnp.bfloat16
    length, wide = tokens_ref.shape
    slots = res_ref.shape[0]
    pieces = gin_ref.shape[0]
    carried = ((gin_ref, gin_buf, gin_out_ref), (gout_ref, gout_buf, gout_out_ref))

    def loads(j):
        return [
            pltpu.make_async_copy(src.at[j], buf, sem.at[0, i])
            for i, (src, buf, _) in enumerate(carried)
        ]

    def stores(j):
        return [
            pltpu.make_async_copy(buf, dst.at[j], sem.at[1, i])
            for i, (_, buf, dst) in enumerate(carried)
        ]

    for c in loads(0):
        c.start()
    late = [(mixed_in, mixed_ref), (wo_in, wo_ref), (q_in, q_ref), (k_in, k_ref), (v_in, v_ref), (wa_in, wa_ref)]
    late = [pltpu.make_async_copy(src, dst, late_sem.at[i]) for i, (src, dst) in enumerate(late)]
    for c in late:
        c.start()
    ints, _ = integer_rows(ints_ref[...])
    cols = dot(eye_of(length), ints.astype(bf), 1, 1)
    mask_ref[...] = mask_of(ints, cols)
    small = matrix_of(small_ref)
    gain_one, bias_one, _, _, _, gain_two, bias_two = vectors_of(small_ref)
    lane = lanes_of()
    routed = ((lane >= 32) & (lane < 64)).astype(f32)
    info = info_ref[...]
    probs = info * routed
    upstream = cot_ref[...].astype(f32)
    slot_row = lax.broadcasted_iota(jnp.int32, (1, slots), 1).astype(f32)
    expert_lane = (lane - 32).astype(f32)
    residual = resid_ref[...]
    combined = residual
    prob_grad = jnp.zeros((length, 128), f32)
    gated = jnp.zeros((length, 128), f32)
    hots = []
    for k in range(2):
        place, expert = info[:, k : k + 1], info[:, 2 + k : 3 + k]
        kept = (expert == expert_lane).astype(f32) * (place >= 0).astype(f32)
        gate = jnp.sum(probs * kept, axis=1, keepdims=True)
        hot = (place == slot_row).astype(f32).astype(bf)
        hots.append(hot)
        picked = dot(hot, res_ref[...], 1, 0)
        picked = picked + dot(pltpu.roll(kept, 96, 1).astype(bf), small, 1, 1)
        combined = combined + gate * picked
        prob_grad = prob_grad + kept * jnp.sum(upstream * picked, axis=1, keepdims=True)
        gated = gated + kept * gate
    out_ref[...] = combined.astype(bf)
    inner = jnp.sum(probs * prob_grad, axis=1, keepdims=True)
    logit_grad = (probs * (prob_grad - inner)).astype(bf)
    unit_two, scale_two = normalize(residual)
    normed_two = (unit_two * gain_two + bias_two).astype(bf)
    high, low = two_parts(pltpu.roll(gated, 96, 1))
    small_grad = dot(normed_two, logit_grad, 0, 0)
    small_grad = small_grad + dot(cot_ref[...], high, 0, 0) + dot(cot_ref[...], low, 0, 0)
    normed_two_grad = dot(hots[0] + hots[1], ig_ref[...], 1, 0) + dot(logit_grad, small, 1, 1)
    vector_grads = {}
    vector_grads[5] = jnp.sum(normed_two_grad * unit_two, axis=0, keepdims=True)
    vector_grads[6] = jnp.sum(normed_two_grad, axis=0, keepdims=True)
    residual_grad = upstream + normalize_back(normed_two_grad * gain_two, unit_two, scale_two)
    tokens_grad_ref[...] = residual_grad
    branch_grad = residual_grad.astype(bf)
    late[0].wait()
    late[1].wait()
    wo_grad_ref[...] = dot(mixed_ref[...], branch_grad, 1, 0).astype(bf)
    vector_grads[4] = jnp.sum(branch_grad.astype(f32), axis=0, keepdims=True)
    mixed_grad_ref[...] = dot(branch_grad, weight_of(wo_ref[...]), 1, 1).astype(bf)
    sides = side_masks(head_dim)
    per = len(sides)
    scale = jnp.full((1, 128), head_dim**-0.5, f32).astype(bf)

    def heads(h, _):
        at = pl.ds(pl.multiple_of(h * 128, 128), 128)
        query = q_ref[:, at] * scale
        mixed_grad = mixed_grad_ref[:, at]

        @pl.when(h < pieces)
        def _():
            for c in loads(h):
                c.wait()
            for c in stores(h):
                c.start()

        query_total = jnp.zeros((128, length), f32)
        key_total = jnp.zeros((length, 128), f32)
        value_total = jnp.zeros((length, 128), f32)
        for s, side in enumerate(sides):
            key = k_ref[:, at] * side
            score = dot(key, query, 1, 1) + mask_ref[...]
            probs = jnp.exp(score - lse_ref[pl.ds(h * per + s, 1), :])
            prob_grads = dot(v_ref[:, at] * side, mixed_grad, 1, 1)
            inner = jnp.sum(probs * prob_grads, axis=0, keepdims=True)
            score_grad = (probs * (prob_grads - inner)).astype(bf)
            value_total = value_total + dot(probs.astype(bf), mixed_grad * side, 1, 0)
            key_total = key_total + dot(score_grad, query * side, 1, 0)
            query_total = query_total + dot(key * scale, score_grad, 0, 0)
        @pl.when(h < pieces)
        def _():
            for c in stores(h):
                c.wait()

        @pl.when(h + 1 < pieces)
        def _():
            for c in loads(h + 1):
                c.start()

        query_grad_ref[:, at] = jnp.transpose(query_total).astype(bf)
        key_grad_ref[:, at] = key_total.astype(bf)
        value_grad_ref[:, at] = value_total.astype(bf)
        return 0

    for c in late[2:]:
        c.wait()
    lax.fori_loop(0, wide // 128, heads, 0)
    inputs = tokens_ref[...].astype(f32)
    unit_one, scale_one = normalize(inputs)
    normed = (unit_one * gain_one + bias_one).astype(bf)
    wq_grad_ref[...] = dot(normed, query_grad_ref[...], 0, 0).astype(bf)
    wk_grad_ref[...] = dot(normed, key_grad_ref[...], 0, 0).astype(bf)
    wv_grad_ref[...] = dot(normed, value_grad_ref[...], 0, 0).astype(bf)
    vector_grads[2] = jnp.sum(query_grad_ref[...].astype(f32), axis=0, keepdims=True)
    vector_grads[3] = jnp.sum(value_grad_ref[...].astype(f32), axis=0, keepdims=True)
    normed_grad = dot(query_grad_ref[...], weight_of(wa_ref[:, :, 0]), 1, 1)
    normed_grad = normed_grad + dot(key_grad_ref[...], weight_of(wa_ref[:, :, 1]), 1, 1)
    normed_grad = normed_grad + dot(value_grad_ref[...], weight_of(wa_ref[:, :, 2]), 1, 1)
    vector_grads[0] = jnp.sum(normed_grad * unit_one, axis=0, keepdims=True)
    vector_grads[1] = jnp.sum(normed_grad, axis=0, keepdims=True)
    tokens_grad_ref[...] += normalize_back(normed_grad * gain_one, unit_one, scale_one)
    line = lax.broadcasted_iota(jnp.int32, (128, wide), 0)
    stacked = jnp.zeros((128, wide), f32)
    for i in range(7):
        stacked = jnp.where(line == 64 + i, vector_grads[i], stacked)
    small_grad_ref[...] = small_grad + jnp.transpose(stacked)


def front_call(capacity, room, groups, blocks, tokens, cot, ints, small, weights, reps):
    f32, bf = jnp.float32, jnp.bfloat16
    length, wide = tokens.shape
    shape = jax.ShapeDtypeStruct
    vm = pl.BlockSpec(memory_space=pltpu.VMEM)
    hbm = pl.BlockSpec(memory_space=pl.ANY)
    slots = shape((groups, blocks, room, wide), bf)
    line = shape((length, wide), bf)
    lanes = -(-blocks * room // 128) * 128
    per = weights[0].shape[0]
    turned = shape((wide, length), bf)
    stacked, single = shape((reps, groups, 3, per, wide), bf), shape((reps, groups, per, wide), bf)
    full = shape((length, wide), f32)
    landed = (reps, groups, room, wide)
    outs = [(slots, vm), (shape((AHEAD,) + landed, bf), hbm)]
    outs += [(shape((blocks - AHEAD,) + landed[1:], bf), hbm), (shape((groups, 8, lanes), f32), vm)]
    outs += [(full, hbm), (line, hbm), (line, hbm), (line, hbm), (turned, hbm)]
    outs += [(shape((16, length), f32), vm), (shape((length, 128), f32), vm)]
    outs += [(stacked, hbm), (single, hbm), (shape((reps, groups) + small.shape, bf), vm)]
    kept = [shape((blocks,) + landed, bf), full, line, line, line, turned, stacked, single]
    sems = pltpu.SemaphoreType.DMA((3, groups // 2, 6))
    return pl.pallas_call(
        functools.partial(front_kernel, capacity, room, wide // HEADS),
        out_shape=[o for o, _ in outs],
        in_specs=[vm] * 8,
        out_specs=[place for _, place in outs],
        scratch_shapes=[pltpu.VMEM(o.shape, o.dtype) for o in kept]
        + [
            pltpu.SemaphoreType.DMA((7 + blocks,)),
            pltpu.VMEM((length, length), f32),
            pltpu.VMEM((length, wide), bf),
            pltpu.VMEM(slots.shape, bf),
            pltpu.SemaphoreType.DMA((5,)),
            sems,
            sems,
            pltpu.SemaphoreType.DMA((blocks, groups - 1)),
            pltpu.SemaphoreType.DMA((blocks, groups - 1)),
            pltpu.SemaphoreType.DMA((blocks,)),
            pltpu.SemaphoreType.DMA((AHEAD, 4)),
            pltpu.SemaphoreType.DMA((AHEAD, 4)),
        ],
        compiler_params=pltpu.CompilerParams(
            collective_id=0, has_side_effects=True, vmem_limit_bytes=60 * MIB
        ),
    )(tokens, cot, ints, small, *weights)


def back_call(tokens, cot, ints, small, weights, res, ig, kept, gin, gout):
    f32, bf = jnp.float32, jnp.bfloat16
    length, wide = tokens.shape
    shape = jax.ShapeDtypeStruct
    vm = pl.BlockSpec(memory_space=pltpu.VMEM)
    hbm = pl.BlockSpec(memory_space=pl.ANY)
    square = shape((wide, wide), bf)
    outs = [shape((length, wide), bf), shape((length, wide), f32)] + [square] * 4
    outs += [shape((wide, 128), f32), shape(gin.shape, f32), shape(gout.shape, f32)]
    line = pltpu.VMEM((length, wide), bf)
    return pl.pallas_call(
        functools.partial(back_kernel, wide // HEADS),
        out_shape=outs,
        in_specs=[vm] * 4 + [hbm] * 2 + [vm] * 3 + [hbm] * 4 + [vm] * 2 + [hbm] * 2,
        out_specs=[vm] * 7 + [hbm] * 2,
        scratch_shapes=[
            pltpu.VMEM((length, length), f32),
            line,
            line,
            line,
            line,
            pltpu.VMEM(gin.shape[1:], f32),
            pltpu.VMEM(gout.shape[1:], f32),
            pltpu.SemaphoreType.DMA((2, 2)),
            pltpu.VMEM(weights[0].shape, bf),
            pltpu.VMEM(weights[1].shape, bf),
            line,
            line,
            line,
            pltpu.VMEM((wide, length), bf),
            pltpu.SemaphoreType.DMA((6,)),
        ],
        compiler_params=pltpu.CompilerParams(vmem_limit_bytes=60 * MIB),
    )(tokens, cot, ints, small, *weights, res, ig, *kept, gin, gout)


def body_fast(
    tokens,
    segments,
    valid,
    routes,
    priority,
    ln1_gain,
    ln1_bias,
    w_query,
    query_bias,
    w_key,
    w_value,
    value_bias,
    w_attn_out,
    attn_out_bias,
    ln2_gain,
    ln2_bias,
    w_router,
    expert_in,
    expert_in_bias,
    expert_out,
    expert_out_bias,
    cotangent,
):
    reps, groups = lax.axis_size("rep"), lax.axis_size("exp")
    devices = reps * groups
    length, wide = tokens.shape[1:]
    per = w_query.shape[0]
    blocks = expert_in.shape[0]
    capacity, room = capacity_of(routes.shape[2], length)
    vectors = [ln1_gain, ln1_bias, query_bias, value_bias, attn_out_bias, ln2_gain, ln2_bias]
    small = jnp.concatenate([expert_out_bias.T, w_router], axis=1)
    small = jnp.pad(small, ((0, 0), (0, 128 - small.shape[1])))
    vectors = jnp.pad(jnp.stack(vectors), ((0, 1), (0, 128 - per)))
    small = jnp.concatenate([small, vectors], axis=0)
    ints = jnp.concatenate([segments, valid, priority, routes[0].T], axis=0)
    ints = jnp.pad(ints, ((0, 3), (0, 0)))
    weights = [w_query, w_key, w_value, w_attn_out]
    xs, g, g_rest, gate, *kept, wa, wo, small = front_call(
        capacity, room, groups, blocks, tokens[0], cotangent[0], ints, small, weights, reps
    )
    weights = [wa, wo]
    res, ig, gin, gb, gout = experts_call(
        xs, g, g_rest, gate, expert_in, expert_in_bias, expert_out, reps, groups
    )
    slots = groups * blocks * room
    output, tokens_grad, *grads, small_grad, gin, gout = back_call(
        tokens[0],
        cotangent[0],
        ints,
        small,
        weights,
        res.reshape(slots, wide),
        ig.reshape(slots, wide),
        kept,
        gin,
        gout,
    )
    sums, last = scatter_grads(grads, small_grad.reshape(devices, per, 128), reps, groups)
    columns = [last[:, 64 + i] for i in range(7)]
    return (
        output[None],
        tokens_grad[None],
        columns[0],
        columns[1],
        sums[0],
        columns[2],
        sums[1],
        sums[2],
        columns[3],
        sums[3],
        columns[4],
        columns[5],
        columns[6],
        last[:, 32:64],
        gin,
        gb[:, 0],
        gout,
        last[:, :32].T,
    )


def capacity_of(top_count, length):
    capacity = (105 * top_count * length + 100 * EXPERTS - 1) // (100 * EXPERTS)
    return capacity, -(-capacity // 8) * 8


def body(*args):
    routes, w_query, expert_in = args[3], args[7], args[17]
    reps, groups = lax.axis_size("rep"), lax.axis_size("exp")
    _, room = capacity_of(routes.shape[2], routes.shape[1])
    wide = w_query.shape[1]
    suits = (
        reps == 4
        and groups & (groups - 1) == 0
        and groups in (4, 8)
        and w_query.shape[0] % 8 == 0
        and w_query.shape[0] <= 128
        and groups * room <= 512
        and groups * expert_in.shape[0] == EXPERTS == 32
        and expert_in.shape[2] % (128 * reps) == 0
        and routes.shape[2] == 2
        and routes.shape[1] <= 64 * 256
        and 128 % (wide // HEADS) == 0
        and HEADS <= 16
        and 2 <= expert_in.shape[0] < wide // 128
    )
    return body_fast(*args) if suits else body_plain(*args)


def solution(mesh):
    in_specs = (
        P(("rep", "exp"), None, None),
        P(("rep", "exp"), None),
        P(("rep", "exp"), None),
        P(("rep", "exp"), None, None),
        P(("rep", "exp"), None),
        P(("rep", "exp")),
        P(("rep", "exp")),
        P(("rep", "exp"), None),
        P(("rep", "exp")),
        P(("rep", "exp"), None),
        P(("rep", "exp"), None),
        P(("rep", "exp")),
        P(("rep", "exp"), None),
        P(("rep", "exp")),
        P(("rep", "exp")),
        P(("rep", "exp")),
        P(("rep", "exp"), None),
        P("exp", None, None),
        P("exp", None),
        P("exp", None, None),
        P(None, ("rep", "exp")),
        P(("rep", "exp"), None, None),
    )
    out_specs = (
        P(("rep", "exp"), None, None),
        P(("rep", "exp"), None, None),
        P(("rep", "exp")),
        P(("rep", "exp")),
        P(("rep", "exp"), None),
        P(("rep", "exp")),
        P(("rep", "exp"), None),
        P(("rep", "exp"), None),
        P(("rep", "exp")),
        P(("rep", "exp"), None),
        P(("rep", "exp")),
        P(("rep", "exp")),
        P(("rep", "exp")),
        P(("rep", "exp"), None),
        P("exp", None, "rep"),
        P("exp", "rep"),
        P("exp", "rep", None),
        P(None, ("rep", "exp")),
    )
    return jax.shard_map(body, mesh=mesh, in_specs=in_specs, out_specs=out_specs, check_vma=False)
```

```python
import functools
import jax
import jax.numpy as jnp
from jax import lax
from jax.experimental import pallas as pl
from jax.experimental.pallas import tpu as pltpu
from jax.sharding import PartitionSpec as P

HEADS = 12
EXPERTS = 32
MESH = pl.DeviceIdType.MESH
MIB = 1 << 20

def bit_dims(reps, groups):
    rb, gb = reps.bit_length() - 1, groups.bit_length() - 1
    return [(0, 1 << k) for k in reversed(range(rb))] + [(1, 1 << k) for k in reversed(range(gb))]

def orders(dims):
    last = len(dims) - 1
    rep = [i for i, d in enumerate(dims) if d[0] == 0]
    exp = [i for i, d in enumerate(dims) if d[0] == 1 and i != last]
    exp = exp[::-1]
    return [[last] + rep + exp, [last] + rep[::-1] + exp, [last] + exp + rep]

def my_bits(dims):
    at = (lax.axis_index("rep"), lax.axis_index("exp"))
    return [(at[a] // s) % 2 for a, s in dims], at

def partner(dims, at, i):
    a, s = dims[i]
    bit = (at[a] // s) % 2
    there = at[a] + (1 - 2 * bit) * s
    return (there, at[1]) if a == 0 else (at[0], there)

def greet(dims, at):
    barrier = pltpu.get_barrier_semaphore()
    for i in range(len(dims)):
        pl.semaphore_signal(barrier, inc=1, device_id=partner(dims, at, i), device_id_type=MESH)
    pl.semaphore_wait(barrier, len(dims))

def scatter_kernel(dims, halves, count, *refs):
    f32 = jnp.float32
    ins, small_in, out_ref, small_out = refs[:count], refs[count], refs[count + 1], refs[count + 2]
    near_ref, far_ref, own_sem, core_send, core_recv, send_sem, recv_sem, small_send, small_recv = refs[count + 3 : count + 12]
    take = iter(refs[count + 12 :])
    n = len(dims)
    ways = orders(dims)
    parts = [(a, h) for a in range(count) for h in range(len(halves))]
    plan = [ways[p % 3] for p in range(len(parts))]
    bufs = {}
    for k in range(1, n):
        for p in range(len(parts)):
            bufs[k, p] = (next(take), next(take), next(take) if k < n - 1 else None)
    smalls = [(next(take), next(take) if k < n - 1 else None) for k in range(n)]
    bits, at = my_bits(dims)
    last = n - 1

    def lead(b):
        return (slice(None),) * (n - 1) + (b,)

    own = [pltpu.make_async_copy(ins[a].at[lead(bits[last])], near_ref.at[a], own_sem.at[a]) for a in range(count)]
    for c in own:
        c.start()
    greet(dims, at)
    core = []
    for a in range(count):
        core.append(pltpu.make_async_remote_copy(
            ins[a].at[lead(1 - bits[last])], far_ref.at[a], core_send.at[a], core_recv.at[a],
            device_id=partner(dims, at, last), device_id_type=MESH))
        core[a].start()
    left = [[j for j in range(n) if j != last] for _ in parts]
    small_left = list(range(n))

    def index(have, i, b):
        return tuple(b if j == i else slice(None) for j in have)

    def value(k, p, where):
        if k == 1:
            a, h = parts[p]
            where = (a,) + where + (slice(None), pl.ds(halves[h][0], halves[h][1]))
            return near_ref[where].astype(f32) + far_ref[where].astype(f32)
        return bufs[k - 1, p][2][where]

    def begin(k, p):
        i = plan[p][k]
        sb, rb, _ = bufs[k, p]
        sb[...] = value(k, p, index(left[p], i, 1 - bits[i])).astype(sb.dtype)
        c = pltpu.make_async_remote_copy(sb, rb, send_sem.at[k, p], recv_sem.at[k, p],
                                         device_id=partner(dims, at, i), device_id_type=MESH)
        c.start()
        return c

    def finish(k, p, c):
        i = plan[p][k]
        _, rb, acc = bufs[k, p]
        c.wait_recv()
        total = value(k, p, index(left[p], i, bits[i])) + rb[...].astype(f32)
        a, h = parts[p]
        if k < n - 1:
            acc[...] = total
        else:
            out_ref[a, :, halves[h][0] : halves[h][0] + halves[h][1]] = total
        left[p].remove(i)

    def small_begin(k):
        i = plan[0][k]
        src = (small_in if k == 0 else smalls[k - 1][1]).at[index(small_left, i, 1 - bits[i])]
        c = pltpu.make_async_remote_copy(src, smalls[k][0], small_send.at[k], small_recv.at[k],
                                         device_id=partner(dims, at, i), device_id_type=MESH)
        c.start()
        return c

    def small_finish(k, c):
        i = plan[0][k]
        c.wait_recv()
        total = (small_in if k == 0 else smalls[k - 1][1])[index(small_left, i, bits[i])] + smalls[k][0][...]
        if k < n - 1:
            smalls[k][1][...] = total
        else:
            small_out[...] = total
        small_left.remove(i)

    every = []
    small = small_begin(0)
    every.append(small)
    live = [None] * len(parts)
    for p, (a, h) in enumerate(parts):
        if h == 0:
            own[a].wait()
            core[a].wait_recv()
        live[p] = begin(1, p)
        every.append(live[p])
    for k in range(1, n):
        small_finish(k - 1, small)
        small = small_begin(k)
        every.append(small)
        for p in range(len(parts)):
            finish(k, p, live[p])
            if k < n - 1:
                live[p] = begin(k + 1, p)
                every.append(live[p])
    small_finish(n - 1, small)
    for c in core + every:
        c.wait_send()


def scatter_grads(grads, small, reps, groups):
    dims = bit_dims(reps, groups)
    n = len(dims)
    full, cols = grads[0].shape
    rows = full // (reps * groups)
    first = cols // 2 // 128 * 128
    halves = [(0, first), (first, cols - first)]
    count = len(grads)
    parts = count * len(halves)
    lead = (2,) * n
    link = grads[0].dtype
    f32 = jnp.float32
    grads = [g.reshape(lead + (rows, cols)) for g in grads]
    small = small.reshape(lead + small.shape[1:])
    sem = pltpu.SemaphoreType.DMA
    half = pltpu.VMEM((count,) + (2,) * (n - 1) + (rows, cols), link)
    scratch = [half, half, sem((count,)), sem((count,)), sem((count,)), sem((n, parts)), sem((n, parts)), sem((n,)), sem((n,))]
    for k in range(1, n):
        for p in range(parts):
            shape = (2,) * (n - 1 - k) + (rows, halves[p % 2][1])
            scratch += [pltpu.VMEM(shape, link), pltpu.VMEM(shape, link)]
            if k < n - 1:
                scratch.append(pltpu.VMEM(shape, f32))
    for k in range(n):
        shape = (2,) * (n - 1 - k) + small.shape[n:]
        scratch.append(pltpu.VMEM(shape, f32))
        if k < n - 1:
            scratch.append(pltpu.VMEM(shape, f32))
    vm = pl.BlockSpec(memory_space=pltpu.VMEM)
    hbm = pl.BlockSpec(memory_space=pl.ANY)
    return pl.pallas_call(
        functools.partial(scatter_kernel, dims, halves, count),
        out_shape=[jax.ShapeDtypeStruct((count, rows, cols), f32), jax.ShapeDtypeStruct(small.shape[n:], f32)],
        in_specs=[hbm] * count + [vm],
        out_specs=[vm] * 2,
        scratch_shapes=scratch,
        compiler_params=pltpu.CompilerParams(collective_id=1, has_side_effects=True, vmem_limit_bytes=60 * MIB),
    )(*grads, small)


def gather_all(vectors, weights, router, shift):
    axes = ("rep", "exp")
    return (
        [lax.all_gather(v, axes, axis=0, tiled=True) for v in vectors],
        [lax.all_gather(w, axes, axis=0, tiled=True) for w in weights],
        lax.all_gather(router, axes, axis=0, tiled=True),
        lax.all_gather(shift, axes, axis=1, tiled=True),
    )


def scatter_all(vectors, weights, router, shift):
    axes = ("rep", "exp")
    return (
        [lax.psum_scatter(v, axes, scatter_dimension=0, tiled=True) for v in vectors],
        [lax.psum_scatter(w, axes, scatter_dimension=0, tiled=True) for w in weights],
        lax.psum_scatter(router, axes, scatter_dimension=0, tiled=True),
        lax.psum_scatter(shift, axes, scatter_dimension=1, tiled=True),
    )


def normal_parts(v):
    e = jnp.exp(v * v * -0.5)
    t = 1.0 / (1.0 + (0.3275911 * 0.7071067811865476) * jnp.abs(v))
    poly = t * (0.127414796 + t * (-0.142248368 + t * (0.7107068705 + t * (-0.7265760135 + t * 0.5307027145))))
    q = poly * e
    return jnp.where(v < 0, q, 1.0 - q), e * 0.3989422804014327

def dot(a, b, ca, cb):
    return lax.dot_general(a, b, (((ca,), (cb,)), ((), ())), preferred_element_type=jnp.float32)

def experts_kernel(reps, groups, x_ref, g_ref, rest_ref, p_ref, win_ref, bias_in, wout_ref,
                   res_ref, ig_ref, gin_ref, gb_ref, gout_ref,
                   x_all, g_all, res_send, ig_send, wi, wo, wis, wos, act_all, pg_all, gin_buf, gout_buf, res_acc, ig_acc, bias_ref, p_all, p_turned, rg_all, p_rows,
                   own_sem, psem, prec, dsem, drec, rsem, rrec, bsem, brec, bown, wsem, ssem, osem):
    me, rep = lax.axis_index("exp"), lax.axis_index("rep")
    blocks = x_ref.shape[1]
    cap, wide = x_ref.shape[2:]
    rows = groups * cap
    chunks, part = wi.shape[0], wi.shape[2]
    half = groups // 2
    peers = [lax.rem(me + s, groups) for s in range(1, groups)]
    side = (rep + 1 - 2 * (rep % 2), rep + 2 - 4 * ((rep // 2) % 2))
    both = (x_all, g_all, p_all)
    back = ((res_send, res_ref), (ig_send, ig_ref))

    def load(j, f):
        return (pltpu.make_async_copy(win_ref.at[j, :, pl.ds(f * part, part)], wi.at[f], wsem.at[0, f]),
                pltpu.make_async_copy(wout_ref.at[j, pl.ds(f * part, part)], wo.at[f], wsem.at[1, f]))
    def load_slice(j):
        at = pl.ds(pl.multiple_of(rep * part, part), part)
        return (pltpu.make_async_copy(win_ref.at[j, :, at], wis, ssem.at[0]),
                pltpu.make_async_copy(wout_ref.at[j, at], wos, ssem.at[1]))
    def out_copies(j):
        return (pltpu.make_async_copy(gin_buf, gin_ref.at[j], osem.at[0]),
                pltpu.make_async_copy(gout_buf, gout_ref.at[j], osem.at[1]))
    ahead = AHEAD
    def dispatch(j, s):
        return pltpu.make_async_remote_copy(x_ref.at[peers[s], j], x_all.at[j, 0, me], dsem.at[j, s], drec.at[j, s],
                                            device_id=(rep, peers[s]), device_id_type=MESH)
    def dispatch_gates(s):
        return pltpu.make_async_remote_copy(p_ref.at[peers[s]], p_all.at[0, 0, me], psem.at[s], prec.at[s],
                                            device_id=(rep, peers[s]), device_id_type=MESH)
    def own(j, t):
        if t == 0:
            return pltpu.make_async_copy(x_ref.at[me, j], x_all.at[j, 0, me], own_sem.at[t, j])
        if t == 1:
            if j < ahead:
                return pltpu.make_async_copy(g_ref.at[j], g_all.at[j], own_sem.at[t, j])
            return pltpu.make_async_copy(rest_ref.at[j - ahead], g_all.at[j, 0], own_sem.at[t, j])
        return pltpu.make_async_copy(p_ref.at[me], p_all.at[0, 0, me], own_sem.at[t, 0])
    def across(j, t, n):
        dst = both[t]
        return pltpu.make_async_remote_copy(dst.at[j, 0], dst.at[j, 1 + n], rsem.at[t, j, n], rrec.at[t, j, n],
                                            device_id=(side[n], me), device_id_type=MESH)
    def onward(j, t, n):
        dst = both[t]
        at = pl.ds(n * half, half)
        return pltpu.make_async_remote_copy(dst.at[j, 1 + n, at], dst.at[j, 3, at], rsem.at[t, j, 2 + n], rrec.at[t, j, 2 + n],
                                            device_id=(side[1 - n], me), device_id_type=MESH)
    def give(j, t, s):
        src, dst = back[t]
        return pltpu.make_async_remote_copy(src.at[j, peers[s]], dst.at[me, j], bsem.at[t, j, s], brec.at[t, j, s],
                                            device_id=(rep, peers[s]), device_id_type=MESH)
    def give_own(j, t):
        src, dst = back[t]
        return pltpu.make_async_copy(src.at[j, me], dst.at[me, j], bown.at[t, j])
    def flat(v):
        return v.astype(jnp.float32).reshape(-1, wide).astype(jnp.bfloat16)

    barrier = pltpu.get_barrier_semaphore()
    for p in peers:
        pl.semaphore_signal(barrier, inc=1, device_id=(rep, p), device_id_type=MESH)
    for n in side:
        pl.semaphore_signal(barrier, inc=1, device_id=(n, me), device_id_type=MESH)
    pl.semaphore_wait(barrier, groups - 1 + 2)

    for s in range(groups - 1):
        dispatch_gates(s).start()
    own(0, 2).start()

    def send_inputs(j):
        for s in range(groups - 1):
            dispatch(j, s).start()
        own(j, 0).start()
    for j in range(min(2, blocks)):
        send_inputs(j)
    for j in range(blocks):
        own(j, 1).start()
    for j in range(blocks):
        for f in range(chunks):
            bias_ref[j, f] = bias_in[j : j + 1, f * part : (f + 1) * part].astype(jnp.float32)
    for f in range(chunks):
        for c in load(0, f): c.start()
    for c in load_slice(0): c.start()

    def turn_gates(r):
        for s in range(groups):
            p_rows[s : s + 1] = p_all[0, r, s, 0:1]
        p_turned[r] = jnp.transpose(p_rows[...])

    def gated(j, r):
        gates = p_turned[r, pl.ds(pl.multiple_of(j * cap, 8), cap)]
        parts = [g_all[j, r, s].astype(jnp.float32) * gates[:, s : s + 1] for s in range(groups)]
        return jnp.concatenate(parts, axis=0).astype(jnp.bfloat16)

    p_rows[...] = jnp.zeros(p_rows.shape, jnp.float32)
    for j in range(blocks):
        own(j, 1).wait()
        if j >= ahead:
            for n in range(2):
                across(j, 1, n).start()
    for s in range(groups - 1):
        dispatch_gates(s).wait_recv()
    own(0, 2).wait()
    for n in range(2):
        across(0, 2, n).start()
    turn_gates(0)

    def own_rows(j):
        x, g = flat(x_all[j, 0]), gated(j, 0)
        def chunk(f, _):
            for c in load(j, f): c.wait()
            pre = dot(x, wi[f], 1, 0) + bias_ref[j, f]
            cdf, pdf = normal_parts(pre)
            act = (pre * cdf).astype(jnp.bfloat16)
            ag = dot(g, wo[f], 1, 1)
            pg = (ag * (cdf + pre * pdf)).astype(jnp.bfloat16)
            more, less = dot(act, wo[f], 1, 0), dot(pg, wi[f], 1, 1)
            @pl.when(f == 0)
            def _():
                res_acc[...] = more
                ig_acc[...] = less
            @pl.when(f > 0)
            def _():
                res_acc[...] += more
                ig_acc[...] += less
            @pl.when(j + 1 < blocks)
            def _():
                for c in load(j + 1, f): c.start()
            return 0
        lax.fori_loop(0, chunks, chunk, 0)
        res_send[j] = res_acc[...].reshape(groups, cap, wide).astype(jnp.bfloat16)
        ig_send[j] = ig_acc[...].reshape(groups, cap, wide).astype(jnp.bfloat16)

    def weights(j):
        for c in load_slice(j): c.wait()
        def one(r, _):
            x, g = flat(x_all[j, r]), gated(j, r)
            rg_all[r] = g
            pre = dot(x, wis[...], 1, 0) + bias_ref[j, rep]
            cdf, pdf = normal_parts(pre)
            act_all[r] = (pre * cdf).astype(jnp.bfloat16)
            pg_all[r] = (dot(g, wos[...], 1, 1) * (cdf + pre * pdf)).astype(jnp.bfloat16)
            return 0
        lax.fori_loop(0, reps, one, 0)
        @pl.when(j + 1 < blocks)
        def _():
            for c in load_slice(j + 1): c.start()
        @pl.when(j > 0)
        def _():
            for c in out_copies(j - 1): c.wait()
        act, pg = act_all[...].reshape(reps * rows, part), pg_all[...].reshape(reps * rows, part)
        gout_buf[...] = dot(act, rg_all[...].reshape(reps * rows, wide), 0, 0)
        gin_buf[...] = dot(flat(x_all[j]), pg, 0, 0)
        gb_ref[j] = jnp.sum(pg.astype(jnp.float32), axis=0, keepdims=True)
        for c in out_copies(j): c.start()

    def step(k, _):
        @pl.when(k < blocks)
        def _():
            for s in range(groups - 1):
                dispatch(k, s).wait_recv()
            own(k, 0).wait()
            @pl.when(k + 2 < blocks)
            def _():
                send_inputs(k + 2)
            for n in range(2):
                across(k, 0, n).start()
            own_rows(k)
            for t in range(2):
                for s in range(groups - 1):
                    give(k, t, s).start()
                give_own(k, t).start()
        @pl.when((k > 0) & (k <= blocks))
        def _():
            for n in range(2):
                across(k - 1, 0, n).wait_recv()
            for n in range(2):
                onward(k - 1, 0, n).start()
        @pl.when((k > 0) & (k <= blocks - ahead))
        def _():
            for n in range(2):
                across(k - 1 + ahead, 1, n).wait_recv()
            for n in range(2):
                onward(k - 1 + ahead, 1, n).start()
        @pl.when(k == 1)
        def _():
            for n in range(2):
                across(0, 2, n).wait_recv()
            for n in range(2):
                onward(0, 2, n).start()
        @pl.when(k == 2)
        def _():
            for n in range(2):
                onward(0, 2, n).wait_recv()
            for r in range(1, reps):
                turn_gates(r)
        @pl.when(k > 1)
        def _():
            for n in range(2):
                onward(k - 2, 0, n).wait_recv()
            @pl.when(k - 2 >= ahead)
            def _():
                for n in range(2):
                    onward(k - 2, 1, n).wait_recv()
            weights(k - 2)
        return 0
    lax.fori_loop(0, blocks + 2, step, 0)

    for c in out_copies(blocks - 1): c.wait()
    def drain(j, _):
        for s in range(groups - 1):
            dispatch(j, s).wait_send()
        for t in range(2):
            for s in range(groups - 1):
                give(j, t, s).wait_recv()
                give(j, t, s).wait_send()
            give_own(j, t).wait()
        for n in range(2):
            across(j, 0, n).wait_send()
            onward(j, 0, n).wait_send()
        @pl.when(j >= ahead)
        def _():
            for n in range(2):
                across(j, 1, n).wait_send()
                onward(j, 1, n).wait_send()
        return 0
    lax.fori_loop(0, blocks, drain, 0)
    for s in range(groups - 1):
        dispatch_gates(s).wait_send()
    for n in range(2):
        across(0, 2, n).wait_send()
        onward(0, 2, n).wait_send()


def experts_call(x, g, rest, gate, w_in, b_in, w_out, reps, groups):
    _, blocks, cap, wide = x.shape
    hidden = w_in.shape[2]
    part = hidden // reps
    anyw = pl.BlockSpec(memory_space=pl.ANY)
    vm = pl.BlockSpec(memory_space=pltpu.VMEM)
    bf, f32 = jnp.bfloat16, jnp.float32
    sem = pltpu.SemaphoreType.DMA
    n = groups - 1
    rows = groups * cap
    lanes = gate.shape[-1]
    return pl.pallas_call(
        functools.partial(experts_kernel, reps, groups),
        out_shape=[jax.ShapeDtypeStruct(x.shape, bf), jax.ShapeDtypeStruct(x.shape, bf),
                   jax.ShapeDtypeStruct((blocks, wide, part), f32), jax.ShapeDtypeStruct((blocks, 1, part), f32),
                   jax.ShapeDtypeStruct((blocks, part, wide), f32)],
        in_specs=[anyw, anyw, anyw, vm, anyw, vm, anyw],
        out_specs=[anyw, anyw, anyw, vm, anyw],
        scratch_shapes=[
            pltpu.VMEM((blocks, reps, groups, cap, wide), bf), pltpu.VMEM((blocks, reps, groups, cap, wide), bf),
            pltpu.VMEM((blocks, groups, cap, wide), bf), pltpu.VMEM((blocks, groups, cap, wide), bf),
            pltpu.VMEM((reps, wide, part), bf), pltpu.VMEM((reps, part, wide), bf),
            pltpu.VMEM((wide, part), bf), pltpu.VMEM((part, wide), bf),
            pltpu.VMEM((reps, rows, part), bf), pltpu.VMEM((reps, rows, part), bf),
            pltpu.VMEM((wide, part), f32), pltpu.VMEM((part, wide), f32),
            pltpu.VMEM((rows, wide), f32), pltpu.VMEM((rows, wide), f32), pltpu.VMEM((blocks, reps, 1, part), f32),
            pltpu.VMEM((1, reps) + gate.shape, f32), pltpu.VMEM((reps, lanes, 128), f32), pltpu.VMEM((reps, rows, wide), bf), pltpu.VMEM((128, lanes), f32),
            sem((3, blocks)), sem((n,)), sem((n,)), sem((blocks, n)), sem((blocks, n)), sem((3, blocks, 4)), sem((3, blocks, 4)),
            sem((2, blocks, n)), sem((2, blocks, n)), sem((2, blocks)), sem((2, reps)), sem((2,)), sem((2,))],
        compiler_params=pltpu.CompilerParams(collective_id=2, has_side_effects=True, vmem_limit_bytes=60 * MIB),
    )(x, g, rest, gate, w_in, b_in, w_out)

def experts_plain(x, g, w_in, b_in, w_out):
    bf, f32 = jnp.bfloat16, jnp.float32
    rx = lax.all_to_all(x, "exp", split_axis=0, concat_axis=0, tiled=True)
    rg = lax.all_to_all(g, "exp", split_axis=0, concat_axis=0, tiled=True)
    pre = jnp.einsum("secd,edf->secf", rx, w_in, preferred_element_type=f32)
    pre = pre + b_in.astype(f32)[None, :, None, :]
    cdf, pdf = normal_parts(pre)
    act = (pre * cdf).astype(bf)
    res = jnp.einsum("secf,efd->secd", act, w_out, preferred_element_type=f32).astype(bf)
    pg = jnp.einsum("secd,efd->secf", rg, w_out, preferred_element_type=f32) * (cdf + pre * pdf)
    pg = pg.astype(bf)
    ig = jnp.einsum("secf,edf->secd", pg, w_in, preferred_element_type=f32).astype(bf)
    gout = jnp.einsum("secf,secd->efd", act, rg, preferred_element_type=f32).astype(bf)
    gin = jnp.einsum("secd,secf->edf", rx, pg, preferred_element_type=f32).astype(bf)
    gb = jnp.sum(pg, axis=(0, 2), dtype=f32).astype(bf)
    return (
        lax.all_to_all(res, "exp", split_axis=0, concat_axis=0, tiled=True),
        lax.all_to_all(ig, "exp", split_axis=0, concat_axis=0, tiled=True),
        lax.psum_scatter(gin, "rep", scatter_dimension=2, tiled=True).astype(f32),
        lax.psum_scatter(gb, "rep", scatter_dimension=1, tiled=True).astype(f32)[:, None],
        lax.psum_scatter(gout, "rep", scatter_dimension=1, tiled=True).astype(f32),
    )


epsilon = 1e-06
masked_score = -1e30


def normalize(values):
    center = values - jnp.mean(values, axis=-1, keepdims=True)
    spread = jnp.mean(center * center, axis=-1, keepdims=True)
    scale = lax.rsqrt(spread + epsilon)
    return center * scale, scale


def normalize_back(grad, unit, scale):
    mean = jnp.mean(grad, axis=-1, keepdims=True)
    along = jnp.mean(grad * unit, axis=-1, keepdims=True)
    return (grad - mean - unit * along) * scale


def two_parts(v):
    high = v.astype(jnp.bfloat16)
    return high, (v - high.astype(jnp.float32)).astype(jnp.bfloat16)


def positions_of(routes, valid_col, priority_col, priority_row, experts):
    length = routes.shape[0]
    f32, bf = jnp.float32, jnp.bfloat16
    token_row = lax.broadcasted_iota(jnp.int32, (length, length), 1)
    token_col = lax.broadcasted_iota(jnp.int32, (length, length), 0)
    rank_col = jnp.sum(
        jnp.where(priority_row == token_col, token_row, 0).astype(f32), axis=1, keepdims=True
    )
    rank_row = jnp.sum(
        jnp.where(priority_col == token_row, token_col, 0).astype(f32), axis=0, keepdims=True
    )
    earlier = (rank_row < rank_col).astype(f32).astype(bf)
    expert_row = lax.broadcasted_iota(jnp.int32, (length, experts), 1)
    ones = [(routes[:, k : k + 1] == expert_row).astype(f32) for k in range(routes.shape[1])]
    before = jnp.zeros((1, experts), f32)
    places = []
    for one in ones:
        live = one * valid_col
        count = dot(earlier, live.astype(bf), 1, 0) + before
        places.append(jnp.sum(count * one, axis=1, keepdims=True))
        before = before + jnp.sum(live, axis=0, keepdims=True)
    return ones, places


def body_plain(
    tokens,
    segments,
    valid,
    routes,
    priority,
    ln1_gain,
    ln1_bias,
    w_query,
    query_bias,
    w_key,
    w_value,
    value_bias,
    w_attn_out,
    attn_out_bias,
    ln2_gain,
    ln2_bias,
    w_router,
    expert_in,
    expert_in_bias,
    expert_out,
    expert_out_bias,
    cotangent,
):
    f32, bf = jnp.float32, jnp.bfloat16
    vectors, weights, router_weight, result_shift = gather_all(
        [ln1_gain, ln1_bias, query_bias, value_bias, attn_out_bias, ln2_gain, ln2_bias],
        [w_query, w_key, w_value, w_attn_out],
        w_router,
        expert_out_bias,
    )
    vectors = [v.astype(f32)[None] for v in vectors]
    gain_one, bias_one, query_shift, value_shift, proj_shift, gain_two, bias_two = vectors
    query_weight, key_weight, value_weight, proj_weight = weights
    length = tokens.shape[1]
    feature_dim = tokens.shape[2]
    head_dim = feature_dim // HEADS
    local_blocks = expert_in.shape[0]
    reps, groups = lax.axis_size("rep"), lax.axis_size("exp")
    experts = EXPERTS
    split = local_blocks * groups // experts
    top_count = routes.shape[2]
    capacity = (105 * top_count * length + 100 * experts - 1) // (100 * experts)
    room = -(-capacity // 8) * 8
    score_scale = head_dim ** (-0.5)
    inputs = tokens[0].astype(f32)
    row_segments = segments[0]
    row_valid = valid[0]
    places = jnp.arange(length, dtype=jnp.int32)
    allowed = (row_segments[:, None] == row_segments[None, :]) & (
        (row_valid[None, :] > 0) | (places[:, None] == places[None, :])
    )
    unit_one, scale_one = normalize(inputs)
    normed = (unit_one * gain_one + bias_one).astype(bf)
    query_rows = (dot(normed, query_weight, 1, 0) + query_shift).astype(bf)
    key_rows = dot(normed, key_weight, 1, 0).astype(bf)
    value_rows = (dot(normed, value_weight, 1, 0) + value_shift).astype(bf)
    query_heads = query_rows.reshape(length, HEADS, head_dim)
    key_heads = key_rows.reshape(length, HEADS, head_dim)
    value_heads = value_rows.reshape(length, HEADS, head_dim)

    def scores():
        return jnp.where(
            allowed[None],
            jnp.einsum("qhd,khd->hqk", query_heads, key_heads, preferred_element_type=f32)
            * score_scale,
            masked_score,
        )

    masked = scores()
    top_score = jnp.max(masked, axis=-1, keepdims=True)
    log_total = top_score + jnp.log(jnp.sum(jnp.exp(masked - top_score), axis=-1, keepdims=True))
    mixed = jnp.einsum(
        "hqk,khd->qhd",
        jnp.exp(masked - log_total).astype(bf),
        value_heads,
        preferred_element_type=f32,
    )
    mixed = mixed.reshape(length, feature_dim).astype(bf)
    residual = inputs + dot(mixed, proj_weight, 1, 0) + proj_shift
    unit_two, scale_two = normalize(residual)
    normed_two = (unit_two * gain_two + bias_two).astype(bf)
    logits = dot(normed_two, router_weight, 1, 0)
    logit_exp = jnp.exp(logits - jnp.max(logits, axis=-1, keepdims=True))
    router_probs = logit_exp / jnp.sum(logit_exp, axis=-1, keepdims=True)
    upstream = cotangent[0].astype(f32)
    ones, positions = positions_of(
        routes[0], row_valid[:, None].astype(f32), priority[0][:, None], priority[0][None], experts
    )
    expert_row = lax.broadcasted_iota(jnp.int32, (1, experts), 1).astype(f32)
    slot_row = lax.broadcasted_iota(jnp.int32, (1, experts * room), 1)
    kept, gates, slots, sent = [], [], [], jnp.zeros((experts * room, feature_dim), f32)
    for one, position in zip(ones, positions):
        keep = row_valid[:, None].astype(f32) * (position < capacity).astype(f32)
        gate = jnp.sum(router_probs * one, axis=1, keepdims=True) * keep
        place = jnp.sum(one * expert_row, axis=1, keepdims=True) * room + position
        place = jnp.where(keep > 0, place, -1.0).astype(jnp.int32)
        hot = (place == slot_row).astype(f32).astype(bf)
        kept.append(one * keep)
        gates.append(gate)
        slots.append(hot)
        sent = sent + dot(hot, (gate * upstream).astype(bf), 0, 0)
    any_slot = slots[0]
    for hot in slots[1:]:
        any_slot = any_slot + hot
    expert_slots = dot(any_slot, normed_two, 0, 0).astype(bf)
    gated = sum(one * gate for one, gate in zip(kept, gates))
    high, low = two_parts(gated)
    shift_grad = dot(high, cotangent[0], 0, 0) + dot(low, cotangent[0], 0, 0)

    def outgoing(v):
        v = v.astype(bf).reshape(experts, room, feature_dim)
        return jnp.repeat(v, split, axis=0).reshape(groups, local_blocks, room, feature_dim)

    moved = experts_plain(
        outgoing(expert_slots), outgoing(sent), expert_in, expert_in_bias, expert_out
    )
    result, slot_back, in_w_grad, in_b_grad, out_w_grad = moved
    result = result.reshape(experts, split, room, feature_dim)
    slot_back = slot_back.reshape(experts, split, room, feature_dim)
    results = [result[:, s].reshape(experts * room, feature_dim) for s in range(split)]
    backs = [slot_back[:, s].reshape(experts * room, feature_dim) for s in range(split)]
    combined, prob_grad = 0.0, 0.0
    for one, gate, hot in zip(kept, gates, slots):
        picked = dot(one.astype(bf), result_shift, 1, 0)
        for part in results:
            picked = picked + dot(hot, part, 1, 0)
        combined = combined + gate * picked
        prob_grad = prob_grad + one * jnp.sum(upstream * picked, axis=1, keepdims=True)
    output = residual + combined
    logit_grad = (
        router_probs * (prob_grad - jnp.sum(router_probs * prob_grad, axis=-1, keepdims=True))
    ).astype(bf)
    router_w_grad = dot(normed_two, logit_grad, 0, 0)
    normed_two_grad = dot(logit_grad, router_weight, 1, 1)
    for part in backs:
        normed_two_grad = normed_two_grad + dot(any_slot, part, 1, 0)
    gain_two_grad = jnp.sum(normed_two_grad * unit_two, axis=0)
    bias_two_grad = jnp.sum(normed_two_grad, axis=0)
    residual_grad = upstream + normalize_back(normed_two_grad * gain_two, unit_two, scale_two)
    branch_grad = residual_grad.astype(bf)
    proj_w_grad = dot(mixed, branch_grad, 0, 0)
    proj_b_grad = jnp.sum(branch_grad, axis=0, dtype=f32)
    mixed_grad = dot(branch_grad, proj_weight, 1, 1).astype(bf)
    mixed_grad = mixed_grad.reshape(length, HEADS, head_dim)
    again_probs = jnp.exp(scores() - log_total)
    prob_grads = jnp.einsum("qhd,khd->hqk", mixed_grad, value_heads, preferred_element_type=f32)
    value_grad = jnp.einsum(
        "hqk,qhd->khd", again_probs.astype(bf), mixed_grad, preferred_element_type=f32
    )
    value_grad = value_grad.astype(bf).reshape(length, feature_dim)
    inner_sum = jnp.sum(again_probs * prob_grads, axis=-1, keepdims=True)
    score_grad = (again_probs * (prob_grads - inner_sum)).astype(bf)
    query_grad = jnp.einsum("hqk,khd->qhd", score_grad, key_heads, preferred_element_type=f32)
    query_grad = (query_grad * score_scale).astype(bf).reshape(length, feature_dim)
    key_grad = jnp.einsum("hqk,qhd->khd", score_grad, query_heads, preferred_element_type=f32)
    key_grad = (key_grad * score_scale).astype(bf).reshape(length, feature_dim)
    query_w_grad = dot(normed, query_grad, 0, 0)
    query_b_grad = jnp.sum(query_grad, axis=0, dtype=f32)
    key_w_grad = dot(normed, key_grad, 0, 0)
    value_w_grad = dot(normed, value_grad, 0, 0)
    value_b_grad = jnp.sum(value_grad, axis=0, dtype=f32)
    normed_grad = dot(query_grad, query_weight, 1, 1)
    normed_grad = normed_grad + dot(key_grad, key_weight, 1, 1)
    normed_grad = normed_grad + dot(value_grad, value_weight, 1, 1)
    gain_one_grad = jnp.sum(normed_grad * unit_one, axis=0)
    bias_one_grad = jnp.sum(normed_grad, axis=0)
    tokens_grad = residual_grad + normalize_back(normed_grad * gain_one, unit_one, scale_one)
    vector_sums, weight_sums, router_sum, shift_sum = scatter_all(
        [
            gain_one_grad,
            bias_one_grad,
            query_b_grad,
            value_b_grad,
            proj_b_grad,
            gain_two_grad,
            bias_two_grad,
        ],
        [query_w_grad, key_w_grad, value_w_grad, proj_w_grad],
        router_w_grad,
        shift_grad,
    )
    return (
        output.astype(jnp.bfloat16)[None],
        tokens_grad[None],
        vector_sums[0],
        vector_sums[1],
        weight_sums[0],
        vector_sums[2],
        weight_sums[1],
        weight_sums[2],
        vector_sums[3],
        weight_sums[3],
        vector_sums[4],
        vector_sums[5],
        vector_sums[6],
        router_sum,
        in_w_grad,
        in_b_grad[:, 0],
        out_w_grad,
        shift_sum,
    )


AHEAD = 1


def eye_of(n):
    same = lax.broadcasted_iota(jnp.int32, (n, n), 0) == lax.broadcasted_iota(jnp.int32, (n, n), 1)
    return same.astype(jnp.float32).astype(jnp.bfloat16)


def lanes_of(n=1):
    return lax.broadcasted_iota(jnp.int32, (n, 128), 1)


def mask_of(ints, cols):
    n = ints.shape[1]
    same = lax.broadcasted_iota(jnp.int32, (n, n), 0) == lax.broadcasted_iota(jnp.int32, (n, n), 1)
    near = cols[:, 0:1] == ints[0:1]
    open_key = jnp.where(same, 1.0, cols[:, 1:2]) > 0
    return jnp.where(near & open_key, 0.0, masked_score)


def side_masks(head_dim):
    lane = lanes_of()
    return [
        ((lane >= s * head_dim) & (lane < (s + 1) * head_dim)).astype(jnp.float32).astype(jnp.bfloat16)
        for s in range(128 // head_dim)
    ]


def vectors_of(small_ref):
    f32, bf = jnp.float32, jnp.bfloat16
    reps, groups, lines, _ = small_ref.shape
    count = reps * groups
    per = lines - 8
    tail = small_ref[...].astype(f32)[:, :, per:].reshape(count * 8, 128).astype(bf)
    wide = count * per
    spread = lax.broadcasted_iota(jnp.int32, (128, wide), 1) % per
    spread = (spread == lax.broadcasted_iota(jnp.int32, (128, wide), 0)).astype(f32).astype(bf)
    laid = dot(tail, spread, 1, 0)
    owner = lax.broadcasted_iota(jnp.int32, (count * 8, wide), 1) // per
    mine = owner == lax.broadcasted_iota(jnp.int32, (count * 8, wide), 0) // 8
    pick = lax.broadcasted_iota(jnp.int32, (8, count * 8), 1) % 8
    pick = (pick == lax.broadcasted_iota(jnp.int32, (8, count * 8), 0)).astype(f32).astype(bf)
    rows = dot(pick, jnp.where(mine, laid, 0.0).astype(bf), 1, 0)
    return [rows[i : i + 1] for i in range(7)]


def matrix_of(small_ref):
    reps, groups, lines, _ = small_ref.shape
    per = lines - 8
    part = small_ref[...].astype(jnp.float32)[:, :, :per]
    return part.reshape(reps * groups * per, 128).astype(jnp.bfloat16)


def weight_of(ref):
    wide = ref.shape[-1]
    return ref.astype(jnp.float32).reshape(-1, wide).astype(jnp.bfloat16)


def integer_rows(raw):
    raw = raw.astype(jnp.float32)
    line = lax.broadcasted_iota(jnp.int32, raw.shape, 0)
    order = raw[2:3]
    high = jnp.floor(order * (1.0 / 64.0))
    low = order - high * 64.0
    return jnp.where(line == 2, high, jnp.where(line == 5, low, raw)), order


def front_kernel(
    capacity,
    room,
    head_dim,
    tokens_ref,
    cot_ref,
    ints_ref,
    small_in,
    wq_in,
    wk_in,
    wv_in,
    wo_in,
    xs_ref,
    g_first_out,
    g_rest_out,
    gate_ref,
    resid_out,
    q_out,
    k_out,
    v_out,
    mixed_out,
    lse_ref,
    info_ref,
    wa_out,
    wo_out,
    small_ref,
    g_ref,
    resid_ref,
    q_ref,
    k_ref,
    v_ref,
    mixed_ref,
    wa_ref,
    wo_ref,
    out_sem,
    mask_ref,
    a2_ref,
    gs_ref,
    own_sem,
    send_sem,
    recv_sem,
    g_send_sem,
    g_recv_sem,
    g_own_sem,
    side_send_sem,
    side_recv_sem,
):
    f32, bf = jnp.float32, jnp.bfloat16
    length, wide = tokens_ref.shape
    groups, blocks = xs_ref.shape[:2]
    me, rep = lax.axis_index("exp"), lax.axis_index("rep")
    level, core = me // 2, me % 2
    levels = groups // 2
    beside = (rep + 1 - 2 * (rep % 2), rep + 2 - 4 * ((rep // 2) % 2))
    bufs = (wa_ref, small_ref, wo_ref)
    mine = [
        pltpu.make_async_copy(wq_in, wa_ref.at[rep, me, 0], own_sem.at[0]),
        pltpu.make_async_copy(wk_in, wa_ref.at[rep, me, 1], own_sem.at[1]),
        pltpu.make_async_copy(wv_in, wa_ref.at[rep, me, 2], own_sem.at[2]),
        pltpu.make_async_copy(small_in, small_ref.at[rep, me], own_sem.at[3]),
        pltpu.make_async_copy(wo_in, wo_ref.at[rep, me], own_sem.at[4]),
    ]
    for c in mine:
        c.start()

    def flip(r):
        there = level
        for one in (1, 2):
            if r & one:
                there = there + one - 2 * one * ((there // one) % 2)
        return there

    def block(r):
        return flip(r) * 2 + core

    def send(src, a, r, n, device):
        return pltpu.make_async_remote_copy(
            src, src, send_sem.at[a, r, n], recv_sem.at[a, r, n], device_id=device, device_id_type=MESH
        )

    between = (level == 1) | (level == 2)

    def up(a, held, to, r, n=0):
        src = bufs[a].at[rep, block(held)]
        return pltpu.make_async_remote_copy(
            src,
            src,
            send_sem.at[a, r, n],
            recv_sem.at[a, r, 0],
            device_id=(rep, flip(to) * 2 + core),
            device_id_type=MESH,
        )

    def up_first(a):
        up(a, 0, 1, 1).start()

        @pl.when(between)
        def _():
            up(a, 0, 3, 3).start()

    def up_step(a, r):
        if r == 1:
            up(a, 0, 1, 1).wait_recv()

            @pl.when(between)
            def _():
                up(a, 1, 3, 2).start()

        elif r == 2:

            @pl.when(between)
            def _():
                up(a, 0, 3, 3).wait_recv()
                up(a, 3, 1, 2, 6).start()
                up(a, 1, 3, 2).wait_recv()
                up(a, 2, 1, 3, 6).start()

            @pl.when(jnp.logical_not(between))
            def _():
                up(a, 1, 3, 2).wait_recv()

        else:

            @pl.when(jnp.logical_not(between))
            def _():
                up(a, 0, 3, 3).wait_recv()

    def up_end(a):
        up(a, 0, 1, 1).wait_send()

        @pl.when(between)
        def _():
            up(a, 0, 3, 3).wait_send()
            up(a, 1, 3, 2).wait_send()
            up(a, 3, 1, 2, 6).wait_send()
            up(a, 2, 1, 3, 6).wait_send()

    def aside(a, r, n):
        return send(bufs[a].at[rep, block(r)], a, r, 1 + n, (beside[n], me))

    def onward(a, r, n):
        ref = bufs[a].at[beside[n], block(r)]
        if a == 1:
            half = ref.shape[0] // 2
            ref = ref.at[pl.ds(n * half, half)]
        else:
            half = wide // 2
            ref = ref.at[(slice(None),) * (len(ref.shape) - 1) + (pl.ds(n * half, half),)]
        return send(ref, a, r, 3 + n, (beside[1 - n], me))

    def over(a, r):
        return send(bufs[a].at[:, block(r)], a, r, 5, (rep, me + 1 - 2 * core))

    barrier = pltpu.get_barrier_semaphore()
    peers = [lax.rem(me + s, groups) for s in range(1, groups)]
    for p in peers:
        pl.semaphore_signal(barrier, inc=1, device_id=(rep, p), device_id_type=MESH)
    for n in beside:
        pl.semaphore_signal(barrier, inc=1, device_id=(n, me), device_id_type=MESH)
    pl.semaphore_wait(barrier, groups + 1)
    for c in mine:
        c.wait()

    def step(sets, r):
        for a in sets:
            if 0 < r < levels:
                up_step(a, r)
            if r < levels:
                for n in range(2):
                    aside(a, r, n).start()
            if 0 < r <= levels:
                for n in range(2):
                    aside(a, r - 1, n).wait_recv()
                for n in range(2):
                    onward(a, r - 1, n).start()
            if 1 < r <= levels + 1:
                for n in range(2):
                    onward(a, r - 2, n).wait_recv()
                over(a, r - 2).start()

    early, late = (0, 1), (2,)
    for a in early + late:
        up_first(a)
    step(early, 0)
    ints, priority_row = integer_rows(ints_ref[...])
    eye = eye_of(length)
    cols = dot(eye, ints.astype(bf), 1, 1)
    mask_ref[...] = mask_of(ints, cols)
    step(early, 1)
    token_row = lax.broadcasted_iota(jnp.int32, (length, length), 1).astype(f32)
    token_col = lax.broadcasted_iota(jnp.int32, (length, length), 0).astype(f32)
    priority_col = cols[:, 2:3] * 64.0 + cols[:, 5:6]
    rank_col = jnp.sum(jnp.where(priority_row == token_col, token_row, 0.0), axis=1, keepdims=True)
    rank_row = jnp.sum(jnp.where(priority_col == token_row, token_col, 0.0), axis=0, keepdims=True)
    earlier = (rank_row < rank_col).astype(f32).astype(bf)
    lane = lanes_of()
    expert_lane = (lane - 32).astype(f32)
    valid_col = cols[:, 1:2]
    before = jnp.zeros((1, 128), f32)
    keeps, places = [], []
    marks = jnp.zeros((length, 128), f32)
    for k in range(2):
        expert = cols[:, 3 + k : 4 + k]
        one = (expert == expert_lane).astype(f32)
        live = one * valid_col
        count = dot(earlier, live.astype(bf), 1, 0) + before
        before = before + jnp.sum(live, axis=0, keepdims=True)
        position = jnp.sum(count * one, axis=1, keepdims=True)
        keep = valid_col * (position < capacity).astype(f32)
        place = jnp.where(keep > 0, expert * room + position, -1.0)
        high = jnp.floor(place * (1.0 / 32.0))
        low = place - high * 32.0
        marks = jnp.where(lane == 2 * k, high, jnp.where(lane == 2 * k + 1, low, marks))
        keeps.append(keep)
        places.append(place)
    step(early, 2)
    for a in late:
        up_step(a, 1)
    turned = dot(marks.astype(bf), eye, 0, 0)
    place_rows = [turned[2 * k : 2 * k + 1] * 32.0 + turned[2 * k + 1 : 2 * k + 2] for k in range(2)]
    part = blocks * room
    slot = lax.broadcasted_iota(jnp.int32, (part, length), 0).astype(f32)

    def hots_of(d):
        first = (d * part).astype(f32)
        return [(slot == row - first).astype(f32).astype(bf) for row in place_rows]

    def fill_grads(d, _):
        hots = hots_of(d)
        grads = dot(hots[0] + hots[1], cot_ref[...], 1, 0)
        gs_ref[d] = grads.reshape(blocks, room, wide).astype(bf)
        return 0

    lax.fori_loop(0, groups, fill_grads, 0)

    def give(j, s):
        return pltpu.make_async_remote_copy(
            gs_ref.at[peers[s], j],
            g_ref.at[j, 0, me],
            g_send_sem.at[j, s],
            g_recv_sem.at[j, s],
            device_id=(rep, peers[s]),
            device_id_type=MESH,
        )

    def give_own(j):
        return pltpu.make_async_copy(gs_ref.at[me, j], g_ref.at[j, 0, me], g_own_sem.at[j])

    def spread(src, dst, j, n, device):
        return pltpu.make_async_remote_copy(
            src,
            dst,
            side_send_sem.at[j, n],
            side_recv_sem.at[j, n],
            device_id=(device, me),
            device_id_type=MESH,
        )

    def g_across(j, n):
        return spread(g_ref.at[j, 0], g_ref.at[j, 1 + n], j, n, beside[n])

    def g_onward(j, n):
        at = pl.ds(n * (groups // 2), groups // 2)
        return spread(g_ref.at[j, 1 + n, at], g_ref.at[j, 3, at], j, 2 + n, beside[1 - n])

    def begin_across(j):
        for n in range(2):
            g_across(j, n).start()

    def begin_onward(j):
        for n in range(2):
            g_across(j, n).wait_recv()
        for n in range(2):
            g_onward(j, n).start()

    ahead = AHEAD
    written = []

    def write(src, dst):
        c = pltpu.make_async_copy(src, dst, out_sem.at[len(written)])
        c.start()
        written.append(c)


    def begin_give(j):
        for s in range(groups - 1):
            give(j, s).start()
        give_own(j).start()

    def have(j):
        for s in range(groups - 1):
            give(j, s).wait_recv()
        give_own(j).wait()

    begin_give(0)
    inputs = tokens_ref[...].astype(f32)
    unit_one, _ = normalize(inputs)
    for r in range(3, levels):
        step(early, r)
    for a in late:
        for r in range(2, levels):
            up_step(a, r)
    begin_give(1)
    for a in late:
        for r in range(levels):
            for n in range(2):
                aside(a, r, n).start()
    for r in range(max(3, levels), levels + 2):
        step(early, r)
    for a in early:
        for r in range(levels):
            over(a, r).wait_recv()
    have(0)
    begin_across(0)
    for j in range(2, blocks - 1):
        begin_give(j)
    small_matrix = matrix_of(small_ref)
    gain_one, bias_one, query_shift, value_shift, proj_shift, gain_two, bias_two = vectors_of(small_ref)
    normed = (unit_one * gain_one + bias_one).astype(bf)
    q_ref[...] = (dot(normed, weight_of(wa_ref[:, :, 0]), 1, 0) + query_shift).astype(bf)
    k_ref[...] = dot(normed, weight_of(wa_ref[:, :, 1]), 1, 0).astype(bf)
    v_ref[...] = (dot(normed, weight_of(wa_ref[:, :, 2]), 1, 0) + value_shift).astype(bf)
    write(q_ref, q_out)
    write(k_ref, k_out)
    write(v_ref, v_out)
    write(wa_ref, wa_out)
    for a in late:
        for r in range(levels):
            for n in range(2):
                aside(a, r, n).wait_recv()
            for n in range(2):
                onward(a, r, n).start()
    sides = side_masks(head_dim)
    per = len(sides)
    scale = jnp.full((1, 128), head_dim**-0.5, f32).astype(bf)

    def heads(h, _):
        at = pl.ds(pl.multiple_of(h * 128, 128), 128)

        @pl.when(h == 1)
        def _():
            have(1)
            if ahead > 1:
                begin_across(1)
            if blocks > 2:
                begin_give(blocks - 1)

        query = q_ref[:, at] * scale
        total = jnp.zeros((128, length), f32)
        for s, side in enumerate(sides):
            score = dot(k_ref[:, at] * side, query, 1, 1) + mask_ref[...]
            top = jnp.max(score, axis=0, keepdims=True)
            expo = jnp.exp(score - top)
            norm = jnp.sum(expo, axis=0, keepdims=True)
            lse_ref[pl.ds(h * per + s, 1), :] = top + jnp.log(norm)
            probs = (expo * (1.0 / norm)).astype(bf)
            total = total + dot(v_ref[:, at] * side, probs, 0, 0)
        mixed_ref[at, :] = total.astype(bf)
        return 0

    half = wide // 256
    lax.fori_loop(0, half, heads, 0)
    for a in late:
        for r in range(levels):
            for n in range(2):
                onward(a, r, n).wait_recv()
            over(a, r).start()
    lax.fori_loop(half, wide // 128, heads, 0)
    begin_onward(0)
    write(mixed_ref, mixed_out)
    for r in range(levels):
        over(2, r).wait_recv()
    write(wo_ref, wo_out)
    residual = inputs + dot(mixed_ref[...], weight_of(wo_ref[...]), 0, 0) + proj_shift
    resid_ref[...] = residual
    write(resid_ref, resid_out)
    unit_two, _ = normalize(residual)
    normed_two = (unit_two * gain_two + bias_two).astype(bf)
    a2_ref[...] = normed_two
    routed = (lane >= 32) & (lane < 64)
    logits = jnp.where(routed, dot(normed_two, small_matrix, 1, 0), masked_score)
    logit_exp = jnp.exp(logits - jnp.max(logits, axis=1, keepdims=True))
    probs = logit_exp / jnp.sum(logit_exp, axis=1, keepdims=True)
    info = probs
    gates = []
    for k in range(2):
        expert = cols[:, 3 + k : 4 + k]
        one = (expert == expert_lane).astype(f32)
        gate = jnp.sum(probs * one, axis=1, keepdims=True) * keeps[k]
        info = jnp.where(lane == k, places[k], jnp.where(lane == 2 + k, expert, info))
        high, _ = two_parts(gate)
        middle, low = two_parts(gate - high.astype(f32))
        split = jnp.where(lane == 1, middle.astype(f32), jnp.where(lane == 2, low.astype(f32), 0.0))
        gates.append(jnp.where(lane == 0, high.astype(f32), split).astype(bf))
    info_ref[...] = info

    def fill_inputs(d, _):
        hots = hots_of(d)
        inside = dot(hots[0] + hots[1], a2_ref[...], 1, 0)
        xs_ref[d] = inside.reshape(blocks, room, wide).astype(bf)
        gate = dot(gates[0], hots[0], 0, 1) + dot(gates[1], hots[1], 0, 1)
        gate_ref[d, 0:1, 0:part] = gate[0:1] + gate[1:2] + gate[2:3]
        return 0

    for j in range(1, ahead):
        begin_onward(j)
    gate_ref[...] = jnp.zeros(gate_ref.shape, f32)
    lax.fori_loop(0, groups, fill_inputs, 0)
    for j in range(blocks):
        if j > 1:
            have(j)
        if j < ahead:
            for n in range(2):
                g_onward(j, n).wait_recv()
            write(g_ref.at[j], g_first_out.at[j])
        else:
            write(g_ref.at[j, 0], g_rest_out.at[j - ahead])
    for j in range(blocks):
        for s in range(groups - 1):
            give(j, s).wait_send()
    for j in range(ahead):
        for n in range(2):
            g_across(j, n).wait_send()
            g_onward(j, n).wait_send()
    for a in early + late:
        up_end(a)
        for r in range(levels):
            for n in range(2):
                aside(a, r, n).wait_send()
                onward(a, r, n).wait_send()
            over(a, r).wait_send()
    for c in written:
        c.wait()


def back_kernel(
    head_dim,
    tokens_in,
    cot_ref,
    ints_ref,
    small_ref,
    wa_in,
    wo_in,
    res_ref,
    ig_in,
    resid_ref,
    q_in,
    k_in,
    v_in,
    mixed_in,
    lse_ref,
    info_ref,
    gin_ref,
    gout_ref,
    out_ref,
    tokens_grad_ref,
    wq_grad_out,
    wk_grad_out,
    wv_grad_out,
    wo_grad_out,
    small_grad_ref,
    gin_out_ref,
    gout_out_ref,
    mixed_grad_ref,
    grads_ref,
    qkv_grad_ref,
    wo_grad_ref,
    mask_ref,
    gin_buf,
    gout_buf,
    sem,
    wa_ref,
    wo_ref,
    q_ref,
    k_ref,
    v_ref,
    mixed_ref,
    tokens_ref,
    ig_ref,
    late_sem,
    out_sem,
):
    f32, bf = jnp.float32, jnp.bfloat16
    length, wide = cot_ref.shape
    slots = res_ref.shape[0]
    pieces = gin_ref.shape[0]
    carried = ((gin_ref, gin_buf, gin_out_ref), (gout_ref, gout_buf, gout_out_ref))

    def loads(j):
        return [
            pltpu.make_async_copy(src.at[j], buf, sem.at[0, i])
            for i, (src, buf, _) in enumerate(carried)
        ]

    def stores(j):
        return [
            pltpu.make_async_copy(buf, dst.at[j], sem.at[1, i])
            for i, (_, buf, dst) in enumerate(carried)
        ]

    for c in loads(0):
        c.start()
    late = [(ig_in, ig_ref), (tokens_in, tokens_ref), (mixed_in, mixed_ref), (wo_in, wo_ref), (q_in, q_ref), (k_in, k_ref), (v_in, v_ref), (wa_in, wa_ref)]
    late = [pltpu.make_async_copy(src, dst, late_sem.at[i]) for i, (src, dst) in enumerate(late)]
    for c in late:
        c.start()
    per = 128 // head_dim

    ints, _ = integer_rows(ints_ref[...])
    cols = dot(eye_of(length), ints.astype(bf), 1, 1)
    mask_ref[...] = mask_of(ints, cols)
    small = matrix_of(small_ref)
    gain_one, bias_one, _, _, _, gain_two, bias_two = vectors_of(small_ref)
    lane = lanes_of()
    routed = ((lane >= 32) & (lane < 64)).astype(f32)
    info = info_ref[...]
    probs = info * routed
    upstream = cot_ref[...].astype(f32)
    slot_row = lax.broadcasted_iota(jnp.int32, (1, slots), 1).astype(f32)
    expert_lane = (lane - 32).astype(f32)
    residual = resid_ref[...]
    combined = residual
    prob_grad = jnp.zeros((length, 128), f32)
    gated = jnp.zeros((length, 128), f32)
    hots = []
    for k in range(2):
        place, expert = info[:, k : k + 1], info[:, 2 + k : 3 + k]
        kept = (expert == expert_lane).astype(f32) * (place >= 0).astype(f32)
        gate = jnp.sum(probs * kept, axis=1, keepdims=True)
        hot = (place == slot_row).astype(f32).astype(bf)
        hots.append(hot)
        picked = dot(hot, res_ref[...], 1, 0)
        picked = picked + dot(pltpu.roll(kept, 96, 1).astype(bf), small, 1, 1)
        combined = combined + gate * picked
        prob_grad = prob_grad + kept * jnp.sum(upstream * picked, axis=1, keepdims=True)
        gated = gated + kept * gate
    out_ref[...] = combined.astype(bf)
    inner = jnp.sum(probs * prob_grad, axis=1, keepdims=True)
    logit_grad = (probs * (prob_grad - inner)).astype(bf)
    unit_two, scale_two = normalize(residual)
    normed_two = (unit_two * gain_two + bias_two).astype(bf)
    high, low = two_parts(pltpu.roll(gated, 96, 1))
    small_grad = dot(normed_two, logit_grad, 0, 0)
    both = dot(cot_ref[...], high + pltpu.roll(low.astype(f32), 96, 1).astype(bf), 0, 0)
    small_grad = small_grad + jnp.where(lane < 32, both + pltpu.roll(both, 32, 1), 0.0)
    late[0].wait()
    normed_two_grad = dot(hots[0] + hots[1], ig_ref[...], 1, 0) + dot(logit_grad, small, 1, 1)
    vector_grads = {}
    vector_grads[5] = jnp.sum(normed_two_grad * unit_two, axis=0, keepdims=True)
    vector_grads[6] = jnp.sum(normed_two_grad, axis=0, keepdims=True)
    residual_grad = upstream + normalize_back(normed_two_grad * gain_two, unit_two, scale_two)
    tokens_grad_ref[...] = residual_grad
    branch_grad = residual_grad.astype(bf)
    late[2].wait()
    late[3].wait()
    wo_grad_ref[...] = dot(mixed_ref[...], branch_grad, 1, 0).astype(bf)
    out_copies = [pltpu.make_async_copy(wo_grad_ref, wo_grad_out, out_sem.at[3])]
    out_copies[0].start()
    vector_grads[4] = jnp.sum(branch_grad.astype(f32), axis=0, keepdims=True)
    mixed_grad_ref[...] = dot(branch_grad, weight_of(wo_ref[...]), 1, 1).astype(bf)
    sides = side_masks(head_dim)
    scale = jnp.full((1, 128), head_dim**-0.5, f32).astype(bf)

    def heads(h, _):
        at = pl.ds(pl.multiple_of(h * 128, 128), 128)
        query = q_ref[:, at] * scale
        mixed_grad = mixed_grad_ref[:, at]

        @pl.when(h < pieces)
        def _():
            for c in loads(h):
                c.wait()
            for c in stores(h):
                c.start()

        query_total = jnp.zeros((128, length), f32)
        key_total = jnp.zeros((length, 128), f32)
        value_total = jnp.zeros((length, 128), f32)
        for s, side in enumerate(sides):
            key = k_ref[:, at] * side
            score = dot(key, query, 1, 1) + mask_ref[...]
            probs = jnp.exp(score - lse_ref[pl.ds(h * per + s, 1), :])
            prob_grads = dot(v_ref[:, at] * side, mixed_grad, 1, 1)
            inner = jnp.sum(probs * prob_grads, axis=0, keepdims=True)
            score_grad = (probs * (prob_grads - inner)).astype(bf)
            value_total = value_total + dot(probs.astype(bf), mixed_grad * side, 1, 0)
            key_total = key_total + dot(score_grad, query * side, 1, 0)
            query_total = query_total + dot(key * scale, score_grad, 0, 0)
        @pl.when(h < pieces)
        def _():
            for c in stores(h):
                c.wait()

        @pl.when(h + 1 < pieces)
        def _():
            for c in loads(h + 1):
                c.start()

        totals = (jnp.transpose(query_total), key_total, value_total)
        for i, total in enumerate(totals):
            there = pl.ds(pl.multiple_of(i * wide + h * 128, 128), 128)
            grads_ref[:, there] = total.astype(bf)
        return 0

    for c in late[4:]:
        c.wait()
    lax.fori_loop(0, wide // 128, heads, 0)
    late[1].wait()
    inputs = tokens_ref[...].astype(f32)
    unit_one, scale_one = normalize(inputs)
    normed = (unit_one * gain_one + bias_one).astype(bf)
    qkv_grad_ref[...] = dot(normed, grads_ref[...], 0, 0).astype(bf)
    for i, out in enumerate((wq_grad_out, wk_grad_out, wv_grad_out)):
        src = qkv_grad_ref.at[:, pl.ds(i * wide, wide)]
        out_copies.append(pltpu.make_async_copy(src, out, out_sem.at[i]))
        out_copies[-1].start()
    vector_grads[2] = jnp.sum(grads_ref[:, :wide].astype(f32), axis=0, keepdims=True)
    vector_grads[3] = jnp.sum(grads_ref[:, 2 * wide :].astype(f32), axis=0, keepdims=True)
    normed_grad = jnp.zeros((length, wide), f32)
    for i in range(3):
        part = grads_ref[:, i * wide : (i + 1) * wide]
        normed_grad = normed_grad + dot(part, weight_of(wa_ref[:, :, i]), 1, 1)
    vector_grads[0] = jnp.sum(normed_grad * unit_one, axis=0, keepdims=True)
    vector_grads[1] = jnp.sum(normed_grad, axis=0, keepdims=True)
    tokens_grad_ref[...] += normalize_back(normed_grad * gain_one, unit_one, scale_one)
    line = lax.broadcasted_iota(jnp.int32, (128, wide), 0)
    stacked = jnp.zeros((128, wide), f32)
    for i in range(7):
        stacked = jnp.where(line == 64 + i, vector_grads[i], stacked)
    small_grad_ref[...] = small_grad + jnp.transpose(stacked)
    for c in out_copies:
        c.wait()


def front_call(capacity, room, groups, blocks, tokens, cot, ints, small, weights, reps):
    f32, bf = jnp.float32, jnp.bfloat16
    length, wide = tokens.shape
    shape = jax.ShapeDtypeStruct
    vm = pl.BlockSpec(memory_space=pltpu.VMEM)
    hbm = pl.BlockSpec(memory_space=pl.ANY)
    slots = shape((groups, blocks, room, wide), bf)
    line = shape((length, wide), bf)
    lanes = -(-blocks * room // 128) * 128
    per = weights[0].shape[0]
    turned = shape((wide, length), bf)
    stacked, single = shape((reps, groups, 3, per, wide), bf), shape((reps, groups, per, wide), bf)
    full = shape((length, wide), f32)
    landed = (reps, groups, room, wide)
    outs = [(slots, vm), (shape((AHEAD,) + landed, bf), hbm)]
    outs += [(shape((blocks - AHEAD,) + landed[1:], bf), hbm), (shape((groups, 8, lanes), f32), vm)]
    outs += [(full, hbm), (line, hbm), (line, hbm), (line, hbm), (turned, hbm)]
    outs += [(shape((16, length), f32), vm), (shape((length, 128), f32), vm)]
    outs += [(stacked, hbm), (single, hbm), (shape((reps, groups) + small.shape, bf), vm)]
    kept = [shape((blocks,) + landed, bf), full, line, line, line, turned, stacked, single]
    sems = pltpu.SemaphoreType.DMA((3, groups // 2, 7))
    return pl.pallas_call(
        functools.partial(front_kernel, capacity, room, wide // HEADS),
        out_shape=[o for o, _ in outs],
        in_specs=[vm] * 8,
        out_specs=[place for _, place in outs],
        scratch_shapes=[pltpu.VMEM(o.shape, o.dtype) for o in kept]
        + [
            pltpu.SemaphoreType.DMA((7 + blocks,)),
            pltpu.VMEM((length, length), f32),
            pltpu.VMEM((length, wide), bf),
            pltpu.VMEM(slots.shape, bf),
            pltpu.SemaphoreType.DMA((5,)),
            sems,
            sems,
            pltpu.SemaphoreType.DMA((blocks, groups - 1)),
            pltpu.SemaphoreType.DMA((blocks, groups - 1)),
            pltpu.SemaphoreType.DMA((blocks,)),
            pltpu.SemaphoreType.DMA((AHEAD, 4)),
            pltpu.SemaphoreType.DMA((AHEAD, 4)),
        ],
        compiler_params=pltpu.CompilerParams(
            collective_id=0, has_side_effects=True, vmem_limit_bytes=60 * MIB
        ),
    )(tokens, cot, ints, small, *weights)


def back_call(tokens, cot, ints, small, weights, res, ig, kept, gin, gout):
    f32, bf = jnp.float32, jnp.bfloat16
    length, wide = tokens.shape
    shape = jax.ShapeDtypeStruct
    vm = pl.BlockSpec(memory_space=pltpu.VMEM)
    hbm = pl.BlockSpec(memory_space=pl.ANY)
    square = shape((wide, wide), bf)
    outs = [shape((length, wide), bf), shape((length, wide), f32)] + [square] * 4
    outs += [shape((wide, 128), f32), shape(gin.shape, f32), shape(gout.shape, f32)]
    line = pltpu.VMEM((length, wide), bf)
    return pl.pallas_call(
        functools.partial(back_kernel, wide // HEADS),
        out_shape=outs,
        in_specs=[hbm, vm, vm, vm, hbm, hbm, vm, hbm, vm] + [hbm] * 4 + [vm] * 2 + [hbm] * 2,
        out_specs=[vm] * 2 + [hbm] * 4 + [vm] + [hbm] * 2,
        scratch_shapes=[
            line,
            pltpu.VMEM((length, 3 * wide), bf),
            pltpu.VMEM((wide, 3 * wide), bf),
            pltpu.VMEM((wide, wide), bf),
            pltpu.VMEM((length, length), f32),
            pltpu.VMEM(gin.shape[1:], f32),
            pltpu.VMEM(gout.shape[1:], f32),
            pltpu.SemaphoreType.DMA((2, 2)),
            pltpu.VMEM(weights[0].shape, bf),
            pltpu.VMEM(weights[1].shape, bf),
            line,
            line,
            line,
            pltpu.VMEM((wide, length), bf),
            line,
            pltpu.VMEM(ig.shape, bf),
            pltpu.SemaphoreType.DMA((8,)),
            pltpu.SemaphoreType.DMA((4,)),
        ],
        compiler_params=pltpu.CompilerParams(vmem_limit_bytes=60 * MIB),
    )(tokens, cot, ints, small, *weights, res, ig, *kept, gin, gout)


def body_fast(
    tokens,
    segments,
    valid,
    routes,
    priority,
    ln1_gain,
    ln1_bias,
    w_query,
    query_bias,
    w_key,
    w_value,
    value_bias,
    w_attn_out,
    attn_out_bias,
    ln2_gain,
    ln2_bias,
    w_router,
    expert_in,
    expert_in_bias,
    expert_out,
    expert_out_bias,
    cotangent,
):
    reps, groups = lax.axis_size("rep"), lax.axis_size("exp")
    devices = reps * groups
    length, wide = tokens.shape[1:]
    per = w_query.shape[0]
    blocks = expert_in.shape[0]
    capacity, room = capacity_of(routes.shape[2], length)
    vectors = [ln1_gain, ln1_bias, query_bias, value_bias, attn_out_bias, ln2_gain, ln2_bias]
    small = jnp.concatenate([expert_out_bias.T, w_router], axis=1)
    small = jnp.pad(small, ((0, 0), (0, 128 - small.shape[1])))
    vectors = jnp.pad(jnp.stack(vectors), ((0, 1), (0, 128 - per)))
    small = jnp.concatenate([small, vectors], axis=0)
    ints = jnp.concatenate([segments, valid, priority, routes[0].T], axis=0)
    ints = jnp.pad(ints, ((0, 3), (0, 0)))
    weights = [w_query, w_key, w_value, w_attn_out]
    xs, g, g_rest, gate, *kept, wa, wo, small = front_call(
        capacity, room, groups, blocks, tokens[0], cotangent[0], ints, small, weights, reps
    )
    weights = [wa, wo]
    res, ig, gin, gb, gout = experts_call(
        xs, g, g_rest, gate, expert_in, expert_in_bias, expert_out, reps, groups
    )
    slots = groups * blocks * room
    output, tokens_grad, *grads, small_grad, gin, gout = back_call(
        tokens[0],
        cotangent[0],
        ints,
        small,
        weights,
        res.reshape(slots, wide),
        ig.reshape(slots, wide),
        kept,
        gin,
        gout,
    )
    sums, last = scatter_grads(grads, small_grad.reshape(devices, per, 128), reps, groups)
    columns = [last[:, 64 + i] for i in range(7)]
    return (
        output[None],
        tokens_grad[None],
        columns[0],
        columns[1],
        sums[0],
        columns[2],
        sums[1],
        sums[2],
        columns[3],
        sums[3],
        columns[4],
        columns[5],
        columns[6],
        last[:, 32:64],
        gin,
        gb[:, 0],
        gout,
        last[:, :32].T,
    )


def capacity_of(top_count, length):
    capacity = (105 * top_count * length + 100 * EXPERTS - 1) // (100 * EXPERTS)
    return capacity, -(-capacity // 8) * 8


def body(*args):
    routes, w_query, expert_in = args[3], args[7], args[17]
    reps, groups = lax.axis_size("rep"), lax.axis_size("exp")
    _, room = capacity_of(routes.shape[2], routes.shape[1])
    wide = w_query.shape[1]
    suits = (
        reps == 4
        and groups & (groups - 1) == 0
        and groups == 8
        and w_query.shape[0] % 8 == 0
        and w_query.shape[0] <= 128
        and groups * room <= 512
        and groups * expert_in.shape[0] == EXPERTS == 32
        and expert_in.shape[2] % (128 * reps) == 0
        and routes.shape[2] == 2
        and routes.shape[1] <= 64 * 256
        and 128 % (wide // HEADS) == 0
        and HEADS <= 16
        and 2 <= expert_in.shape[0] < wide // 128
    )
    return body_fast(*args) if suits else body_plain(*args)


def solution(mesh):
    in_specs = (
        P(("rep", "exp"), None, None),
        P(("rep", "exp"), None),
        P(("rep", "exp"), None),
        P(("rep", "exp"), None, None),
        P(("rep", "exp"), None),
        P(("rep", "exp")),
        P(("rep", "exp")),
        P(("rep", "exp"), None),
        P(("rep", "exp")),
        P(("rep", "exp"), None),
        P(("rep", "exp"), None),
        P(("rep", "exp")),
        P(("rep", "exp"), None),
        P(("rep", "exp")),
        P(("rep", "exp")),
        P(("rep", "exp")),
        P(("rep", "exp"), None),
        P("exp", None, None),
        P("exp", None),
        P("exp", None, None),
        P(None, ("rep", "exp")),
        P(("rep", "exp"), None, None),
    )
    out_specs = (
        P(("rep", "exp"), None, None),
        P(("rep", "exp"), None, None),
        P(("rep", "exp")),
        P(("rep", "exp")),
        P(("rep", "exp"), None),
        P(("rep", "exp")),
        P(("rep", "exp"), None),
        P(("rep", "exp"), None),
        P(("rep", "exp")),
        P(("rep", "exp"), None),
        P(("rep", "exp")),
        P(("rep", "exp")),
        P(("rep", "exp")),
        P(("rep", "exp"), None),
        P("exp", None, "rep"),
        P("exp", "rep"),
        P("exp", "rep", None),
        P(None, ("rep", "exp")),
    )
    return jax.shard_map(body, mesh=mesh, in_specs=in_specs, out_specs=out_specs, check_vma=False)
```

```python
import functools
import jax
import jax.numpy as jnp
from jax import lax
from jax.experimental import pallas as pl
from jax.experimental.pallas import tpu as pltpu
from jax.sharding import PartitionSpec as P

HEADS = 12
EXPERTS = 32
MESH = pl.DeviceIdType.MESH
MIB = 1 << 20

def bit_dims(reps, groups):
    rb, gb = reps.bit_length() - 1, groups.bit_length() - 1
    return [(0, 1 << k) for k in reversed(range(rb))] + [(1, 1 << k) for k in reversed(range(gb))]

def orders(dims):
    last = len(dims) - 1
    rep = [i for i, d in enumerate(dims) if d[0] == 0]
    exp = [i for i, d in enumerate(dims) if d[0] == 1 and i != last]
    exp = exp[::-1]
    return [[last] + rep + exp, [last] + rep[::-1] + exp, [last] + exp + rep]

def my_bits(dims):
    at = (lax.axis_index("rep"), lax.axis_index("exp"))
    return [(at[a] // s) % 2 for a, s in dims], at

def partner(dims, at, i):
    a, s = dims[i]
    bit = (at[a] // s) % 2
    there = at[a] + (1 - 2 * bit) * s
    return (there, at[1]) if a == 0 else (at[0], there)

def greet(dims, at):
    barrier = pltpu.get_barrier_semaphore()
    for i in range(len(dims)):
        pl.semaphore_signal(barrier, inc=1, device_id=partner(dims, at, i), device_id_type=MESH)
    pl.semaphore_wait(barrier, len(dims))

def scatter_kernel(dims, halves, count, *refs):
    f32 = jnp.float32
    ins, small_in, out_ref, small_out = refs[:count], refs[count], refs[count + 1], refs[count + 2]
    near_ref, far_ref, own_sem, core_send, core_recv, send_sem, recv_sem, small_send, small_recv = refs[count + 3 : count + 12]
    take = iter(refs[count + 12 :])
    n = len(dims)
    ways = orders(dims)
    parts = [(a, h) for a in range(count) for h in range(len(halves))]
    plan = [ways[p % 3] for p in range(len(parts))]
    bufs = {}
    for k in range(1, n):
        for p in range(len(parts)):
            bufs[k, p] = (next(take), next(take), next(take) if k < n - 1 else None)
    smalls = [(next(take), next(take) if k < n - 1 else None) for k in range(n)]
    bits, at = my_bits(dims)
    last = n - 1

    def lead(b):
        return (slice(None),) * (n - 1) + (b,)

    own = [pltpu.make_async_copy(ins[a].at[lead(bits[last])], near_ref.at[a], own_sem.at[a]) for a in range(count)]
    for c in own:
        c.start()
    greet(dims, at)
    core = []
    for a in range(count):
        core.append(pltpu.make_async_remote_copy(
            ins[a].at[lead(1 - bits[last])], far_ref.at[a], core_send.at[a], core_recv.at[a],
            device_id=partner(dims, at, last), device_id_type=MESH))
        core[a].start()
    left = [[j for j in range(n) if j != last] for _ in parts]
    small_left = list(range(n))

    def index(have, i, b):
        return tuple(b if j == i else slice(None) for j in have)

    def value(k, p, where):
        if k == 1:
            a, h = parts[p]
            where = (a,) + where + (slice(None), pl.ds(halves[h][0], halves[h][1]))
            return near_ref[where].astype(f32) + far_ref[where].astype(f32)
        return bufs[k - 1, p][2][where]

    def begin(k, p):
        i = plan[p][k]
        sb, rb, _ = bufs[k, p]
        sb[...] = value(k, p, index(left[p], i, 1 - bits[i])).astype(sb.dtype)
        c = pltpu.make_async_remote_copy(sb, rb, send_sem.at[k, p], recv_sem.at[k, p],
                                         device_id=partner(dims, at, i), device_id_type=MESH)
        c.start()
        return c

    def finish(k, p, c):
        i = plan[p][k]
        _, rb, acc = bufs[k, p]
        c.wait_recv()
        total = value(k, p, index(left[p], i, bits[i])) + rb[...].astype(f32)
        a, h = parts[p]
        if k < n - 1:
            acc[...] = total
        else:
            out_ref[a, :, halves[h][0] : halves[h][0] + halves[h][1]] = total
        left[p].remove(i)

    def small_begin(k):
        i = plan[0][k]
        src = (small_in if k == 0 else smalls[k - 1][1]).at[index(small_left, i, 1 - bits[i])]
        c = pltpu.make_async_remote_copy(src, smalls[k][0], small_send.at[k], small_recv.at[k],
                                         device_id=partner(dims, at, i), device_id_type=MESH)
        c.start()
        return c

    def small_finish(k, c):
        i = plan[0][k]
        c.wait_recv()
        total = (small_in if k == 0 else smalls[k - 1][1])[index(small_left, i, bits[i])] + smalls[k][0][...]
        if k < n - 1:
            smalls[k][1][...] = total
        else:
            small_out[...] = total
        small_left.remove(i)

    every = []
    small = small_begin(0)
    every.append(small)
    live = [None] * len(parts)
    for p, (a, h) in enumerate(parts):
        if h == 0:
            own[a].wait()
            core[a].wait_recv()
        live[p] = begin(1, p)
        every.append(live[p])
    for k in range(1, n):
        small_finish(k - 1, small)
        small = small_begin(k)
        every.append(small)
        for p in range(len(parts)):
            finish(k, p, live[p])
            if k < n - 1:
                live[p] = begin(k + 1, p)
                every.append(live[p])
    small_finish(n - 1, small)
    for c in core + every:
        c.wait_send()


def scatter_grads(grads, small, reps, groups):
    dims = bit_dims(reps, groups)
    n = len(dims)
    full, cols = grads[0].shape
    rows = full // (reps * groups)
    first = cols // 3 // 128 * 128
    halves = [(0, first), (first, first), (2 * first, cols - 2 * first)]
    count = len(grads)
    parts = count * len(halves)
    lead = (2,) * n
    link = grads[0].dtype
    f32 = jnp.float32
    grads = [g.reshape(lead + (rows, cols)) for g in grads]
    small = small.reshape(lead + small.shape[1:])
    sem = pltpu.SemaphoreType.DMA
    half = pltpu.VMEM((count,) + (2,) * (n - 1) + (rows, cols), link)
    scratch = [half, half, sem((count,)), sem((count,)), sem((count,)), sem((n, parts)), sem((n, parts)), sem((n,)), sem((n,))]
    for k in range(1, n):
        for p in range(parts):
            shape = (2,) * (n - 1 - k) + (rows, halves[p % len(halves)][1])
            scratch += [pltpu.VMEM(shape, link), pltpu.VMEM(shape, link)]
            if k < n - 1:
                scratch.append(pltpu.VMEM(shape, f32))
    for k in range(n):
        shape = (2,) * (n - 1 - k) + small.shape[n:]
        scratch.append(pltpu.VMEM(shape, f32))
        if k < n - 1:
            scratch.append(pltpu.VMEM(shape, f32))
    vm = pl.BlockSpec(memory_space=pltpu.VMEM)
    hbm = pl.BlockSpec(memory_space=pl.ANY)
    return pl.pallas_call(
        functools.partial(scatter_kernel, dims, halves, count),
        out_shape=[jax.ShapeDtypeStruct((count, rows, cols), f32), jax.ShapeDtypeStruct(small.shape[n:], f32)],
        in_specs=[hbm] * count + [vm],
        out_specs=[vm] * 2,
        scratch_shapes=scratch,
        compiler_params=pltpu.CompilerParams(collective_id=1, has_side_effects=True, vmem_limit_bytes=60 * MIB),
    )(*grads, small)


def gather_all(vectors, weights, router, shift):
    axes = ("rep", "exp")
    return (
        [lax.all_gather(v, axes, axis=0, tiled=True) for v in vectors],
        [lax.all_gather(w, axes, axis=0, tiled=True) for w in weights],
        lax.all_gather(router, axes, axis=0, tiled=True),
        lax.all_gather(shift, axes, axis=1, tiled=True),
    )


def scatter_all(vectors, weights, router, shift):
    axes = ("rep", "exp")
    return (
        [lax.psum_scatter(v, axes, scatter_dimension=0, tiled=True) for v in vectors],
        [lax.psum_scatter(w, axes, scatter_dimension=0, tiled=True) for w in weights],
        lax.psum_scatter(router, axes, scatter_dimension=0, tiled=True),
        lax.psum_scatter(shift, axes, scatter_dimension=1, tiled=True),
    )


def normal_parts(v):
    e = jnp.exp(v * v * -0.5)
    t = 1.0 / (1.0 + (0.3275911 * 0.7071067811865476) * jnp.abs(v))
    poly = t * (0.127414796 + t * (-0.142248368 + t * (0.7107068705 + t * (-0.7265760135 + t * 0.5307027145))))
    q = poly * e
    return jnp.where(v < 0, q, 1.0 - q), e * 0.3989422804014327

def dot(a, b, ca, cb):
    return lax.dot_general(a, b, (((ca,), (cb,)), ((), ())), preferred_element_type=jnp.float32)

def experts_kernel(reps, groups, x_ref, g_ref, rest_ref, p_ref, win_ref, bias_in, wout_ref,
                   res_ref, ig_ref, gin_ref, gb_ref, gout_ref,
                   x_all, g_all, res_send, ig_send, wi, wo, wis, wos, act_all, pg_all, gin_buf, gout_buf, res_acc, ig_acc, bias_ref, p_all, p_turned, rg_all, p_rows,
                   own_sem, psem, prec, dsem, drec, rsem, rrec, bsem, brec, bown, wsem, ssem, osem):
    me, rep = lax.axis_index("exp"), lax.axis_index("rep")
    blocks = x_ref.shape[1]
    cap, wide = x_ref.shape[2:]
    rows = groups * cap
    chunks, part = wi.shape[0], wi.shape[2]
    half = groups // 2
    peers = [lax.rem(me + s, groups) for s in range(1, groups)]
    side = (rep + 1 - 2 * (rep % 2), rep + 2 - 4 * ((rep // 2) % 2))
    both = (x_all, g_all, p_all)
    back = ((res_send, res_ref), (ig_send, ig_ref))

    def load(j, f):
        return (pltpu.make_async_copy(win_ref.at[j, :, pl.ds(f * part, part)], wi.at[f], wsem.at[0, f]),
                pltpu.make_async_copy(wout_ref.at[j, pl.ds(f * part, part)], wo.at[f], wsem.at[1, f]))
    def load_slice(j):
        at = pl.ds(pl.multiple_of(rep * part, part), part)
        return (pltpu.make_async_copy(win_ref.at[j, :, at], wis, ssem.at[0]),
                pltpu.make_async_copy(wout_ref.at[j, at], wos, ssem.at[1]))
    def out_copies(j):
        return (pltpu.make_async_copy(gin_buf, gin_ref.at[j], osem.at[0]),
                pltpu.make_async_copy(gout_buf, gout_ref.at[j], osem.at[1]))
    ahead = AHEAD
    def dispatch(j, s):
        return pltpu.make_async_remote_copy(x_ref.at[peers[s], j], x_all.at[j, 0, me], dsem.at[j, s], drec.at[j, s],
                                            device_id=(rep, peers[s]), device_id_type=MESH)
    def dispatch_gates(s):
        return pltpu.make_async_remote_copy(p_ref.at[peers[s]], p_all.at[0, 0, me], psem.at[s], prec.at[s],
                                            device_id=(rep, peers[s]), device_id_type=MESH)
    def own(j, t):
        if t == 0:
            return pltpu.make_async_copy(x_ref.at[me, j], x_all.at[j, 0, me], own_sem.at[t, j])
        if t == 1:
            if j < ahead:
                return pltpu.make_async_copy(g_ref.at[j], g_all.at[j], own_sem.at[t, j])
            return pltpu.make_async_copy(rest_ref.at[j - ahead], g_all.at[j, 0], own_sem.at[t, j])
        return pltpu.make_async_copy(p_ref.at[me], p_all.at[0, 0, me], own_sem.at[t, 0])
    def across(j, t, n):
        dst = both[t]
        return pltpu.make_async_remote_copy(dst.at[j, 0], dst.at[j, 1 + n], rsem.at[t, j, n], rrec.at[t, j, n],
                                            device_id=(side[n], me), device_id_type=MESH)
    def onward(j, t, n):
        dst = both[t]
        at = pl.ds(n * half, half)
        return pltpu.make_async_remote_copy(dst.at[j, 1 + n, at], dst.at[j, 3, at], rsem.at[t, j, 2 + n], rrec.at[t, j, 2 + n],
                                            device_id=(side[1 - n], me), device_id_type=MESH)
    def give(j, t, s):
        src, dst = back[t]
        return pltpu.make_async_remote_copy(src.at[j, peers[s]], dst.at[me, j], bsem.at[t, j, s], brec.at[t, j, s],
                                            device_id=(rep, peers[s]), device_id_type=MESH)
    def give_own(j, t):
        src, dst = back[t]
        return pltpu.make_async_copy(src.at[j, me], dst.at[me, j], bown.at[t, j])
    def flat(v):
        return v.astype(jnp.float32).reshape(-1, wide).astype(jnp.bfloat16)

    barrier = pltpu.get_barrier_semaphore()
    for p in peers:
        pl.semaphore_signal(barrier, inc=1, device_id=(rep, p), device_id_type=MESH)
    for n in side:
        pl.semaphore_signal(barrier, inc=1, device_id=(n, me), device_id_type=MESH)
    pl.semaphore_wait(barrier, groups - 1 + 2)

    for s in range(groups - 1):
        dispatch_gates(s).start()
    own(0, 2).start()

    def send_inputs(j):
        for s in range(groups - 1):
            dispatch(j, s).start()
        own(j, 0).start()
    for j in range(min(2, blocks)):
        send_inputs(j)
    for j in range(blocks):
        own(j, 1).start()
    for j in range(blocks):
        for f in range(chunks):
            bias_ref[j, f] = bias_in[j : j + 1, f * part : (f + 1) * part].astype(jnp.float32)
    for f in range(chunks):
        for c in load(0, f): c.start()
    for c in load_slice(0): c.start()

    def turn_gates(r):
        for s in range(groups):
            p_rows[s : s + 1] = p_all[0, r, s, 0:1]
        p_turned[r] = jnp.transpose(p_rows[...])

    def gated(j, r):
        gates = p_turned[r, pl.ds(pl.multiple_of(j * cap, 8), cap)]
        parts = [g_all[j, r, s].astype(jnp.float32) * gates[:, s : s + 1] for s in range(groups)]
        return jnp.concatenate(parts, axis=0).astype(jnp.bfloat16)

    p_rows[...] = jnp.zeros(p_rows.shape, jnp.float32)
    for j in range(blocks):
        own(j, 1).wait()
        if j >= ahead:
            for n in range(2):
                across(j, 1, n).start()
    for s in range(groups - 1):
        dispatch_gates(s).wait_recv()
    own(0, 2).wait()
    for n in range(2):
        across(0, 2, n).start()
    turn_gates(0)

    def own_rows(j):
        x, g = flat(x_all[j, 0]), gated(j, 0)
        def chunk(f, _):
            for c in load(j, f): c.wait()
            pre = dot(x, wi[f], 1, 0) + bias_ref[j, f]
            cdf, pdf = normal_parts(pre)
            act = (pre * cdf).astype(jnp.bfloat16)
            ag = dot(g, wo[f], 1, 1)
            pg = (ag * (cdf + pre * pdf)).astype(jnp.bfloat16)
            more, less = dot(act, wo[f], 1, 0), dot(pg, wi[f], 1, 1)
            @pl.when(f == 0)
            def _():
                res_acc[...] = more
                ig_acc[...] = less
            @pl.when(f > 0)
            def _():
                res_acc[...] += more
                ig_acc[...] += less
            @pl.when(j + 1 < blocks)
            def _():
                for c in load(j + 1, f): c.start()
            return 0
        lax.fori_loop(0, chunks, chunk, 0)
        res_send[j] = res_acc[...].reshape(groups, cap, wide).astype(jnp.bfloat16)
        ig_send[j] = ig_acc[...].reshape(groups, cap, wide).astype(jnp.bfloat16)

    def weights(j):
        for c in load_slice(j): c.wait()
        def one(r, _):
            x, g = flat(x_all[j, r]), gated(j, r)
            rg_all[r] = g
            pre = dot(x, wis[...], 1, 0) + bias_ref[j, rep]
            cdf, pdf = normal_parts(pre)
            act_all[r] = (pre * cdf).astype(jnp.bfloat16)
            pg_all[r] = (dot(g, wos[...], 1, 1) * (cdf + pre * pdf)).astype(jnp.bfloat16)
            return 0
        lax.fori_loop(0, reps, one, 0)
        @pl.when(j + 1 < blocks)
        def _():
            for c in load_slice(j + 1): c.start()
        @pl.when(j > 0)
        def _():
            for c in out_copies(j - 1): c.wait()
        act, pg = act_all[...].reshape(reps * rows, part), pg_all[...].reshape(reps * rows, part)
        gout_buf[...] = dot(act, rg_all[...].reshape(reps * rows, wide), 0, 0)
        gin_buf[...] = dot(flat(x_all[j]), pg, 0, 0)
        gb_ref[j] = jnp.sum(pg.astype(jnp.float32), axis=0, keepdims=True)
        for c in out_copies(j): c.start()

    def step(k, _):
        @pl.when(k < blocks)
        def _():
            for s in range(groups - 1):
                dispatch(k, s).wait_recv()
            own(k, 0).wait()
            @pl.when(k + 2 < blocks)
            def _():
                send_inputs(k + 2)
            for n in range(2):
                across(k, 0, n).start()
            own_rows(k)
            for t in range(2):
                for s in range(groups - 1):
                    give(k, t, s).start()
                give_own(k, t).start()
        @pl.when((k > 0) & (k <= blocks))
        def _():
            for n in range(2):
                across(k - 1, 0, n).wait_recv()
            for n in range(2):
                onward(k - 1, 0, n).start()
        @pl.when((k > 0) & (k <= blocks - ahead))
        def _():
            for n in range(2):
                across(k - 1 + ahead, 1, n).wait_recv()
            for n in range(2):
                onward(k - 1 + ahead, 1, n).start()
        @pl.when(k == 1)
        def _():
            for n in range(2):
                across(0, 2, n).wait_recv()
            for n in range(2):
                onward(0, 2, n).start()
        @pl.when(k == 2)
        def _():
            for n in range(2):
                onward(0, 2, n).wait_recv()
            for r in range(1, reps):
                turn_gates(r)
        @pl.when(k > 1)
        def _():
            for n in range(2):
                onward(k - 2, 0, n).wait_recv()
            @pl.when(k - 2 >= ahead)
            def _():
                for n in range(2):
                    onward(k - 2, 1, n).wait_recv()
            weights(k - 2)
        return 0
    lax.fori_loop(0, blocks + 2, step, 0)

    for c in out_copies(blocks - 1): c.wait()
    def drain(j, _):
        for s in range(groups - 1):
            dispatch(j, s).wait_send()
        for t in range(2):
            for s in range(groups - 1):
                give(j, t, s).wait_recv()
                give(j, t, s).wait_send()
            give_own(j, t).wait()
        for n in range(2):
            across(j, 0, n).wait_send()
            onward(j, 0, n).wait_send()
        @pl.when(j >= ahead)
        def _():
            for n in range(2):
                across(j, 1, n).wait_send()
                onward(j, 1, n).wait_send()
        return 0
    lax.fori_loop(0, blocks, drain, 0)
    for s in range(groups - 1):
        dispatch_gates(s).wait_send()
    for n in range(2):
        across(0, 2, n).wait_send()
        onward(0, 2, n).wait_send()


def experts_call(x, g, rest, gate, w_in, b_in, w_out, reps, groups):
    _, blocks, cap, wide = x.shape
    hidden = w_in.shape[2]
    part = hidden // reps
    anyw = pl.BlockSpec(memory_space=pl.ANY)
    vm = pl.BlockSpec(memory_space=pltpu.VMEM)
    bf, f32 = jnp.bfloat16, jnp.float32
    sem = pltpu.SemaphoreType.DMA
    n = groups - 1
    rows = groups * cap
    lanes = gate.shape[-1]
    return pl.pallas_call(
        functools.partial(experts_kernel, reps, groups),
        out_shape=[jax.ShapeDtypeStruct(x.shape, bf), jax.ShapeDtypeStruct(x.shape, bf),
                   jax.ShapeDtypeStruct((blocks, wide, part), f32), jax.ShapeDtypeStruct((blocks, 1, part), f32),
                   jax.ShapeDtypeStruct((blocks, part, wide), f32)],
        in_specs=[anyw, anyw, anyw, vm, anyw, vm, anyw],
        out_specs=[anyw, anyw, anyw, vm, anyw],
        scratch_shapes=[
            pltpu.VMEM((blocks, reps, groups, cap, wide), bf), pltpu.VMEM((blocks, reps, groups, cap, wide), bf),
            pltpu.VMEM((blocks, groups, cap, wide), bf), pltpu.VMEM((blocks, groups, cap, wide), bf),
            pltpu.VMEM((reps, wide, part), bf), pltpu.VMEM((reps, part, wide), bf),
            pltpu.VMEM((wide, part), bf), pltpu.VMEM((part, wide), bf),
            pltpu.VMEM((reps, rows, part), bf), pltpu.VMEM((reps, rows, part), bf),
            pltpu.VMEM((wide, part), f32), pltpu.VMEM((part, wide), f32),
            pltpu.VMEM((rows, wide), f32), pltpu.VMEM((rows, wide), f32), pltpu.VMEM((blocks, reps, 1, part), f32),
            pltpu.VMEM((1, reps) + gate.shape, f32), pltpu.VMEM((reps, lanes, 128), f32), pltpu.VMEM((reps, rows, wide), bf), pltpu.VMEM((128, lanes), f32),
            sem((3, blocks)), sem((n,)), sem((n,)), sem((blocks, n)), sem((blocks, n)), sem((3, blocks, 4)), sem((3, blocks, 4)),
            sem((2, blocks, n)), sem((2, blocks, n)), sem((2, blocks)), sem((2, reps)), sem((2,)), sem((2,))],
        compiler_params=pltpu.CompilerParams(collective_id=2, has_side_effects=True, vmem_limit_bytes=60 * MIB),
    )(x, g, rest, gate, w_in, b_in, w_out)

def experts_plain(x, g, w_in, b_in, w_out):
    bf, f32 = jnp.bfloat16, jnp.float32
    rx = lax.all_to_all(x, "exp", split_axis=0, concat_axis=0, tiled=True)
    rg = lax.all_to_all(g, "exp", split_axis=0, concat_axis=0, tiled=True)
    pre = jnp.einsum("secd,edf->secf", rx, w_in, preferred_element_type=f32)
    pre = pre + b_in.astype(f32)[None, :, None, :]
    cdf, pdf = normal_parts(pre)
    act = (pre * cdf).astype(bf)
    res = jnp.einsum("secf,efd->secd", act, w_out, preferred_element_type=f32).astype(bf)
    pg = jnp.einsum("secd,efd->secf", rg, w_out, preferred_element_type=f32) * (cdf + pre * pdf)
    pg = pg.astype(bf)
    ig = jnp.einsum("secf,edf->secd", pg, w_in, preferred_element_type=f32).astype(bf)
    gout = jnp.einsum("secf,secd->efd", act, rg, preferred_element_type=f32).astype(bf)
    gin = jnp.einsum("secd,secf->edf", rx, pg, preferred_element_type=f32).astype(bf)
    gb = jnp.sum(pg, axis=(0, 2), dtype=f32).astype(bf)
    return (
        lax.all_to_all(res, "exp", split_axis=0, concat_axis=0, tiled=True),
        lax.all_to_all(ig, "exp", split_axis=0, concat_axis=0, tiled=True),
        lax.psum_scatter(gin, "rep", scatter_dimension=2, tiled=True).astype(f32),
        lax.psum_scatter(gb, "rep", scatter_dimension=1, tiled=True).astype(f32)[:, None],
        lax.psum_scatter(gout, "rep", scatter_dimension=1, tiled=True).astype(f32),
    )


epsilon = 1e-06
masked_score = -1e30


def normalize(values):
    center = values - jnp.mean(values, axis=-1, keepdims=True)
    spread = jnp.mean(center * center, axis=-1, keepdims=True)
    scale = lax.rsqrt(spread + epsilon)
    return center * scale, scale


def normalize_back(grad, unit, scale):
    mean = jnp.mean(grad, axis=-1, keepdims=True)
    along = jnp.mean(grad * unit, axis=-1, keepdims=True)
    return (grad - mean - unit * along) * scale


def two_parts(v):
    high = v.astype(jnp.bfloat16)
    return high, (v - high.astype(jnp.float32)).astype(jnp.bfloat16)


def positions_of(routes, valid_col, priority_col, priority_row, experts):
    length = routes.shape[0]
    f32, bf = jnp.float32, jnp.bfloat16
    token_row = lax.broadcasted_iota(jnp.int32, (length, length), 1)
    token_col = lax.broadcasted_iota(jnp.int32, (length, length), 0)
    rank_col = jnp.sum(
        jnp.where(priority_row == token_col, token_row, 0).astype(f32), axis=1, keepdims=True
    )
    rank_row = jnp.sum(
        jnp.where(priority_col == token_row, token_col, 0).astype(f32), axis=0, keepdims=True
    )
    earlier = (rank_row < rank_col).astype(f32).astype(bf)
    expert_row = lax.broadcasted_iota(jnp.int32, (length, experts), 1)
    ones = [(routes[:, k : k + 1] == expert_row).astype(f32) for k in range(routes.shape[1])]
    before = jnp.zeros((1, experts), f32)
    places = []
    for one in ones:
        live = one * valid_col
        count = dot(earlier, live.astype(bf), 1, 0) + before
        places.append(jnp.sum(count * one, axis=1, keepdims=True))
        before = before + jnp.sum(live, axis=0, keepdims=True)
    return ones, places


def body_plain(
    tokens,
    segments,
    valid,
    routes,
    priority,
    ln1_gain,
    ln1_bias,
    w_query,
    query_bias,
    w_key,
    w_value,
    value_bias,
    w_attn_out,
    attn_out_bias,
    ln2_gain,
    ln2_bias,
    w_router,
    expert_in,
    expert_in_bias,
    expert_out,
    expert_out_bias,
    cotangent,
):
    f32, bf = jnp.float32, jnp.bfloat16
    vectors, weights, router_weight, result_shift = gather_all(
        [ln1_gain, ln1_bias, query_bias, value_bias, attn_out_bias, ln2_gain, ln2_bias],
        [w_query, w_key, w_value, w_attn_out],
        w_router,
        expert_out_bias,
    )
    vectors = [v.astype(f32)[None] for v in vectors]
    gain_one, bias_one, query_shift, value_shift, proj_shift, gain_two, bias_two = vectors
    query_weight, key_weight, value_weight, proj_weight = weights
    length = tokens.shape[1]
    feature_dim = tokens.shape[2]
    head_dim = feature_dim // HEADS
    local_blocks = expert_in.shape[0]
    reps, groups = lax.axis_size("rep"), lax.axis_size("exp")
    experts = EXPERTS
    split = local_blocks * groups // experts
    top_count = routes.shape[2]
    capacity = (105 * top_count * length + 100 * experts - 1) // (100 * experts)
    room = -(-capacity // 8) * 8
    score_scale = head_dim ** (-0.5)
    inputs = tokens[0].astype(f32)
    row_segments = segments[0]
    row_valid = valid[0]
    places = jnp.arange(length, dtype=jnp.int32)
    allowed = (row_segments[:, None] == row_segments[None, :]) & (
        (row_valid[None, :] > 0) | (places[:, None] == places[None, :])
    )
    unit_one, scale_one = normalize(inputs)
    normed = (unit_one * gain_one + bias_one).astype(bf)
    query_rows = (dot(normed, query_weight, 1, 0) + query_shift).astype(bf)
    key_rows = dot(normed, key_weight, 1, 0).astype(bf)
    value_rows = (dot(normed, value_weight, 1, 0) + value_shift).astype(bf)
    query_heads = query_rows.reshape(length, HEADS, head_dim)
    key_heads = key_rows.reshape(length, HEADS, head_dim)
    value_heads = value_rows.reshape(length, HEADS, head_dim)

    def scores():
        return jnp.where(
            allowed[None],
            jnp.einsum("qhd,khd->hqk", query_heads, key_heads, preferred_element_type=f32)
            * score_scale,
            masked_score,
        )

    masked = scores()
    top_score = jnp.max(masked, axis=-1, keepdims=True)
    log_total = top_score + jnp.log(jnp.sum(jnp.exp(masked - top_score), axis=-1, keepdims=True))
    mixed = jnp.einsum(
        "hqk,khd->qhd",
        jnp.exp(masked - log_total).astype(bf),
        value_heads,
        preferred_element_type=f32,
    )
    mixed = mixed.reshape(length, feature_dim).astype(bf)
    residual = inputs + dot(mixed, proj_weight, 1, 0) + proj_shift
    unit_two, scale_two = normalize(residual)
    normed_two = (unit_two * gain_two + bias_two).astype(bf)
    logits = dot(normed_two, router_weight, 1, 0)
    logit_exp = jnp.exp(logits - jnp.max(logits, axis=-1, keepdims=True))
    router_probs = logit_exp / jnp.sum(logit_exp, axis=-1, keepdims=True)
    upstream = cotangent[0].astype(f32)
    ones, positions = positions_of(
        routes[0], row_valid[:, None].astype(f32), priority[0][:, None], priority[0][None], experts
    )
    expert_row = lax.broadcasted_iota(jnp.int32, (1, experts), 1).astype(f32)
    slot_row = lax.broadcasted_iota(jnp.int32, (1, experts * room), 1)
    kept, gates, slots, sent = [], [], [], jnp.zeros((experts * room, feature_dim), f32)
    for one, position in zip(ones, positions):
        keep = row_valid[:, None].astype(f32) * (position < capacity).astype(f32)
        gate = jnp.sum(router_probs * one, axis=1, keepdims=True) * keep
        place = jnp.sum(one * expert_row, axis=1, keepdims=True) * room + position
        place = jnp.where(keep > 0, place, -1.0).astype(jnp.int32)
        hot = (place == slot_row).astype(f32).astype(bf)
        kept.append(one * keep)
        gates.append(gate)
        slots.append(hot)
        sent = sent + dot(hot, (gate * upstream).astype(bf), 0, 0)
    any_slot = slots[0]
    for hot in slots[1:]:
        any_slot = any_slot + hot
    expert_slots = dot(any_slot, normed_two, 0, 0).astype(bf)
    gated = sum(one * gate for one, gate in zip(kept, gates))
    high, low = two_parts(gated)
    shift_grad = dot(high, cotangent[0], 0, 0) + dot(low, cotangent[0], 0, 0)

    def outgoing(v):
        v = v.astype(bf).reshape(experts, room, feature_dim)
        return jnp.repeat(v, split, axis=0).reshape(groups, local_blocks, room, feature_dim)

    moved = experts_plain(
        outgoing(expert_slots), outgoing(sent), expert_in, expert_in_bias, expert_out
    )
    result, slot_back, in_w_grad, in_b_grad, out_w_grad = moved
    result = result.reshape(experts, split, room, feature_dim)
    slot_back = slot_back.reshape(experts, split, room, feature_dim)
    results = [result[:, s].reshape(experts * room, feature_dim) for s in range(split)]
    backs = [slot_back[:, s].reshape(experts * room, feature_dim) for s in range(split)]
    combined, prob_grad = 0.0, 0.0
    for one, gate, hot in zip(kept, gates, slots):
        picked = dot(one.astype(bf), result_shift, 1, 0)
        for part in results:
            picked = picked + dot(hot, part, 1, 0)
        combined = combined + gate * picked
        prob_grad = prob_grad + one * jnp.sum(upstream * picked, axis=1, keepdims=True)
    output = residual + combined
    logit_grad = (
        router_probs * (prob_grad - jnp.sum(router_probs * prob_grad, axis=-1, keepdims=True))
    ).astype(bf)
    router_w_grad = dot(normed_two, logit_grad, 0, 0)
    normed_two_grad = dot(logit_grad, router_weight, 1, 1)
    for part in backs:
        normed_two_grad = normed_two_grad + dot(any_slot, part, 1, 0)
    gain_two_grad = jnp.sum(normed_two_grad * unit_two, axis=0)
    bias_two_grad = jnp.sum(normed_two_grad, axis=0)
    residual_grad = upstream + normalize_back(normed_two_grad * gain_two, unit_two, scale_two)
    branch_grad = residual_grad.astype(bf)
    proj_w_grad = dot(mixed, branch_grad, 0, 0)
    proj_b_grad = jnp.sum(branch_grad, axis=0, dtype=f32)
    mixed_grad = dot(branch_grad, proj_weight, 1, 1).astype(bf)
    mixed_grad = mixed_grad.reshape(length, HEADS, head_dim)
    again_probs = jnp.exp(scores() - log_total)
    prob_grads = jnp.einsum("qhd,khd->hqk", mixed_grad, value_heads, preferred_element_type=f32)
    value_grad = jnp.einsum(
        "hqk,qhd->khd", again_probs.astype(bf), mixed_grad, preferred_element_type=f32
    )
    value_grad = value_grad.astype(bf).reshape(length, feature_dim)
    inner_sum = jnp.sum(again_probs * prob_grads, axis=-1, keepdims=True)
    score_grad = (again_probs * (prob_grads - inner_sum)).astype(bf)
    query_grad = jnp.einsum("hqk,khd->qhd", score_grad, key_heads, preferred_element_type=f32)
    query_grad = (query_grad * score_scale).astype(bf).reshape(length, feature_dim)
    key_grad = jnp.einsum("hqk,qhd->khd", score_grad, query_heads, preferred_element_type=f32)
    key_grad = (key_grad * score_scale).astype(bf).reshape(length, feature_dim)
    query_w_grad = dot(normed, query_grad, 0, 0)
    query_b_grad = jnp.sum(query_grad, axis=0, dtype=f32)
    key_w_grad = dot(normed, key_grad, 0, 0)
    value_w_grad = dot(normed, value_grad, 0, 0)
    value_b_grad = jnp.sum(value_grad, axis=0, dtype=f32)
    normed_grad = dot(query_grad, query_weight, 1, 1)
    normed_grad = normed_grad + dot(key_grad, key_weight, 1, 1)
    normed_grad = normed_grad + dot(value_grad, value_weight, 1, 1)
    gain_one_grad = jnp.sum(normed_grad * unit_one, axis=0)
    bias_one_grad = jnp.sum(normed_grad, axis=0)
    tokens_grad = residual_grad + normalize_back(normed_grad * gain_one, unit_one, scale_one)
    vector_sums, weight_sums, router_sum, shift_sum = scatter_all(
        [
            gain_one_grad,
            bias_one_grad,
            query_b_grad,
            value_b_grad,
            proj_b_grad,
            gain_two_grad,
            bias_two_grad,
        ],
        [query_w_grad, key_w_grad, value_w_grad, proj_w_grad],
        router_w_grad,
        shift_grad,
    )
    return (
        output.astype(jnp.bfloat16)[None],
        tokens_grad[None],
        vector_sums[0],
        vector_sums[1],
        weight_sums[0],
        vector_sums[2],
        weight_sums[1],
        weight_sums[2],
        vector_sums[3],
        weight_sums[3],
        vector_sums[4],
        vector_sums[5],
        vector_sums[6],
        router_sum,
        in_w_grad,
        in_b_grad[:, 0],
        out_w_grad,
        shift_sum,
    )


AHEAD = 1


def eye_of(n):
    same = lax.broadcasted_iota(jnp.int32, (n, n), 0) == lax.broadcasted_iota(jnp.int32, (n, n), 1)
    return same.astype(jnp.float32).astype(jnp.bfloat16)


def lanes_of(n=1):
    return lax.broadcasted_iota(jnp.int32, (n, 128), 1)


def mask_of(ints, cols):
    n = ints.shape[1]
    same = lax.broadcasted_iota(jnp.int32, (n, n), 0) == lax.broadcasted_iota(jnp.int32, (n, n), 1)
    near = cols[:, 0:1] == ints[0:1]
    open_key = jnp.where(same, 1.0, cols[:, 1:2]) > 0
    return jnp.where(near & open_key, 0.0, masked_score)


def side_masks(head_dim):
    lane = lanes_of()
    return [
        ((lane >= s * head_dim) & (lane < (s + 1) * head_dim)).astype(jnp.float32).astype(jnp.bfloat16)
        for s in range(128 // head_dim)
    ]


def vectors_of(small_ref):
    f32, bf = jnp.float32, jnp.bfloat16
    reps, groups, lines, _ = small_ref.shape
    count = reps * groups
    per = lines - 8
    tail = small_ref[...].astype(f32)[:, :, per:].reshape(count * 8, 128).astype(bf)
    wide = count * per
    spread = lax.broadcasted_iota(jnp.int32, (128, wide), 1) % per
    spread = (spread == lax.broadcasted_iota(jnp.int32, (128, wide), 0)).astype(f32).astype(bf)
    laid = dot(tail, spread, 1, 0)
    owner = lax.broadcasted_iota(jnp.int32, (count * 8, wide), 1) // per
    mine = owner == lax.broadcasted_iota(jnp.int32, (count * 8, wide), 0) // 8
    pick = lax.broadcasted_iota(jnp.int32, (8, count * 8), 1) % 8
    pick = (pick == lax.broadcasted_iota(jnp.int32, (8, count * 8), 0)).astype(f32).astype(bf)
    rows = dot(pick, jnp.where(mine, laid, 0.0).astype(bf), 1, 0)
    return [rows[i : i + 1] for i in range(7)]


def matrix_of(small_ref):
    reps, groups, lines, _ = small_ref.shape
    per = lines - 8
    part = small_ref[...].astype(jnp.float32)[:, :, :per]
    return part.reshape(reps * groups * per, 128).astype(jnp.bfloat16)


def weight_of(ref):
    wide = ref.shape[-1]
    return ref.astype(jnp.float32).reshape(-1, wide).astype(jnp.bfloat16)


def integer_rows(raw):
    raw = raw.astype(jnp.float32)
    line = lax.broadcasted_iota(jnp.int32, raw.shape, 0)
    order = raw[2:3]
    high = jnp.floor(order * (1.0 / 64.0))
    low = order - high * 64.0
    return jnp.where(line == 2, high, jnp.where(line == 5, low, raw)), order


def front_kernel(
    capacity,
    room,
    head_dim,
    tokens_ref,
    cot_ref,
    ints_ref,
    small_in,
    wq_in,
    wk_in,
    wv_in,
    wo_in,
    xs_ref,
    g_first_out,
    g_rest_out,
    gate_ref,
    resid_out,
    q_out,
    k_out,
    v_out,
    mixed_out,
    lse_ref,
    info_ref,
    wa_out,
    wo_out,
    small_ref,
    g_ref,
    resid_ref,
    q_ref,
    k_ref,
    v_ref,
    mixed_ref,
    wa_ref,
    wo_ref,
    out_sem,
    mask_ref,
    a2_ref,
    gs_ref,
    own_sem,
    send_sem,
    recv_sem,
    g_send_sem,
    g_recv_sem,
    g_own_sem,
    side_send_sem,
    side_recv_sem,
):
    f32, bf = jnp.float32, jnp.bfloat16
    length, wide = tokens_ref.shape
    groups, blocks = xs_ref.shape[:2]
    me, rep = lax.axis_index("exp"), lax.axis_index("rep")
    level, core = me // 2, me % 2
    levels = groups // 2
    beside = (rep + 1 - 2 * (rep % 2), rep + 2 - 4 * ((rep // 2) % 2))
    bufs = (wa_ref, small_ref, wo_ref)
    mine = [
        pltpu.make_async_copy(wq_in, wa_ref.at[rep, me, 0], own_sem.at[0]),
        pltpu.make_async_copy(wk_in, wa_ref.at[rep, me, 1], own_sem.at[1]),
        pltpu.make_async_copy(wv_in, wa_ref.at[rep, me, 2], own_sem.at[2]),
        pltpu.make_async_copy(small_in, small_ref.at[rep, me], own_sem.at[3]),
        pltpu.make_async_copy(wo_in, wo_ref.at[rep, me], own_sem.at[4]),
    ]
    for c in mine:
        c.start()

    def flip(r):
        there = level
        for one in (1, 2):
            if r & one:
                there = there + one - 2 * one * ((there // one) % 2)
        return there

    def block(r):
        return flip(r) * 2 + core

    def send(src, a, r, n, device):
        return pltpu.make_async_remote_copy(
            src, src, send_sem.at[a, r, n], recv_sem.at[a, r, n], device_id=device, device_id_type=MESH
        )

    between = (level == 1) | (level == 2)

    def up(a, held, to, r, n=0):
        src = bufs[a].at[rep, block(held)]
        return pltpu.make_async_remote_copy(
            src,
            src,
            send_sem.at[a, r, n],
            recv_sem.at[a, r, 0],
            device_id=(rep, flip(to) * 2 + core),
            device_id_type=MESH,
        )

    def up_first(a):
        up(a, 0, 1, 1).start()

        @pl.when(between)
        def _():
            up(a, 0, 3, 3).start()

    def up_step(a, r):
        if r == 1:
            up(a, 0, 1, 1).wait_recv()

            @pl.when(between)
            def _():
                up(a, 1, 3, 2).start()

        elif r == 2:

            @pl.when(between)
            def _():
                up(a, 0, 3, 3).wait_recv()
                up(a, 3, 1, 2, 6).start()
                up(a, 1, 3, 2).wait_recv()
                up(a, 2, 1, 3, 6).start()

            @pl.when(jnp.logical_not(between))
            def _():
                up(a, 1, 3, 2).wait_recv()

        else:

            @pl.when(jnp.logical_not(between))
            def _():
                up(a, 0, 3, 3).wait_recv()

    def up_end(a):
        up(a, 0, 1, 1).wait_send()

        @pl.when(between)
        def _():
            up(a, 0, 3, 3).wait_send()
            up(a, 1, 3, 2).wait_send()
            up(a, 3, 1, 2, 6).wait_send()
            up(a, 2, 1, 3, 6).wait_send()

    def aside(a, r, n):
        return send(bufs[a].at[rep, block(r)], a, r, 1 + n, (beside[n], me))

    def onward(a, r, n):
        ref = bufs[a].at[beside[n], block(r)]
        if a == 1:
            half = ref.shape[0] // 2
            ref = ref.at[pl.ds(n * half, half)]
        else:
            half = wide // 2
            ref = ref.at[(slice(None),) * (len(ref.shape) - 1) + (pl.ds(n * half, half),)]
        return send(ref, a, r, 3 + n, (beside[1 - n], me))

    def over(a, r):
        return send(bufs[a].at[:, block(r)], a, r, 5, (rep, me + 1 - 2 * core))

    barrier = pltpu.get_barrier_semaphore()
    peers = [lax.rem(me + s, groups) for s in range(1, groups)]
    for p in peers:
        pl.semaphore_signal(barrier, inc=1, device_id=(rep, p), device_id_type=MESH)
    for n in beside:
        pl.semaphore_signal(barrier, inc=1, device_id=(n, me), device_id_type=MESH)
    pl.semaphore_wait(barrier, groups + 1)
    for c in mine:
        c.wait()

    def step(sets, r):
        for a in sets:
            if 0 < r < levels:
                up_step(a, r)
            if r < levels:
                for n in range(2):
                    aside(a, r, n).start()
            if 0 < r <= levels:
                for n in range(2):
                    aside(a, r - 1, n).wait_recv()
                for n in range(2):
                    onward(a, r - 1, n).start()
            if 1 < r <= levels + 1:
                for n in range(2):
                    onward(a, r - 2, n).wait_recv()
                over(a, r - 2).start()

    early, late = (0, 1), (2,)
    for a in early + late:
        up_first(a)
    step(early, 0)
    ints, priority_row = integer_rows(ints_ref[...])
    eye = eye_of(length)
    cols = dot(eye, ints.astype(bf), 1, 1)
    mask_ref[...] = mask_of(ints, cols)
    step(early, 1)
    token_row = lax.broadcasted_iota(jnp.int32, (length, length), 1).astype(f32)
    token_col = lax.broadcasted_iota(jnp.int32, (length, length), 0).astype(f32)
    priority_col = cols[:, 2:3] * 64.0 + cols[:, 5:6]
    rank_col = jnp.sum(jnp.where(priority_row == token_col, token_row, 0.0), axis=1, keepdims=True)
    rank_row = jnp.sum(jnp.where(priority_col == token_row, token_col, 0.0), axis=0, keepdims=True)
    earlier = (rank_row < rank_col).astype(f32).astype(bf)
    lane = lanes_of()
    expert_lane = (lane - 32).astype(f32)
    valid_col = cols[:, 1:2]
    before = jnp.zeros((1, 128), f32)
    keeps, places = [], []
    marks = jnp.zeros((length, 128), f32)
    for k in range(2):
        expert = cols[:, 3 + k : 4 + k]
        one = (expert == expert_lane).astype(f32)
        live = one * valid_col
        count = dot(earlier, live.astype(bf), 1, 0) + before
        before = before + jnp.sum(live, axis=0, keepdims=True)
        position = jnp.sum(count * one, axis=1, keepdims=True)
        keep = valid_col * (position < capacity).astype(f32)
        place = jnp.where(keep > 0, expert * room + position, -1.0)
        high = jnp.floor(place * (1.0 / 32.0))
        low = place - high * 32.0
        marks = jnp.where(lane == 2 * k, high, jnp.where(lane == 2 * k + 1, low, marks))
        keeps.append(keep)
        places.append(place)
    step(early, 2)
    for a in late:
        up_step(a, 1)
    turned = dot(marks.astype(bf), eye, 0, 0)
    place_rows = [turned[2 * k : 2 * k + 1] * 32.0 + turned[2 * k + 1 : 2 * k + 2] for k in range(2)]
    part = blocks * room
    slot = lax.broadcasted_iota(jnp.int32, (part, length), 0).astype(f32)

    def hots_of(d):
        first = (d * part).astype(f32)
        return [(slot == row - first).astype(f32).astype(bf) for row in place_rows]

    def fill_grads(d, _):
        hots = hots_of(d)
        grads = dot(hots[0] + hots[1], cot_ref[...], 1, 0)
        gs_ref[d] = grads.reshape(blocks, room, wide).astype(bf)
        return 0

    lax.fori_loop(0, groups, fill_grads, 0)

    def give(j, s):
        return pltpu.make_async_remote_copy(
            gs_ref.at[peers[s], j],
            g_ref.at[j, 0, me],
            g_send_sem.at[j, s],
            g_recv_sem.at[j, s],
            device_id=(rep, peers[s]),
            device_id_type=MESH,
        )

    def give_own(j):
        return pltpu.make_async_copy(gs_ref.at[me, j], g_ref.at[j, 0, me], g_own_sem.at[j])

    def spread(src, dst, j, n, device):
        return pltpu.make_async_remote_copy(
            src,
            dst,
            side_send_sem.at[j, n],
            side_recv_sem.at[j, n],
            device_id=(device, me),
            device_id_type=MESH,
        )

    def g_across(j, n):
        return spread(g_ref.at[j, 0], g_ref.at[j, 1 + n], j, n, beside[n])

    def g_onward(j, n):
        at = pl.ds(n * (groups // 2), groups // 2)
        return spread(g_ref.at[j, 1 + n, at], g_ref.at[j, 3, at], j, 2 + n, beside[1 - n])

    def begin_across(j):
        for n in range(2):
            g_across(j, n).start()

    def begin_onward(j):
        for n in range(2):
            g_across(j, n).wait_recv()
        for n in range(2):
            g_onward(j, n).start()

    ahead = AHEAD
    written = []

    def write(src, dst):
        c = pltpu.make_async_copy(src, dst, out_sem.at[len(written)])
        c.start()
        written.append(c)


    def begin_give(j):
        for s in range(groups - 1):
            give(j, s).start()
        give_own(j).start()

    def have(j):
        for s in range(groups - 1):
            give(j, s).wait_recv()
        give_own(j).wait()

    begin_give(0)
    inputs = tokens_ref[...].astype(f32)
    unit_one, _ = normalize(inputs)
    for r in range(3, levels):
        step(early, r)
    for a in late:
        for r in range(2, levels):
            up_step(a, r)
    begin_give(1)
    for a in late:
        for r in range(levels):
            for n in range(2):
                aside(a, r, n).start()
    for r in range(max(3, levels), levels + 2):
        step(early, r)
    for a in early:
        for r in range(levels):
            over(a, r).wait_recv()
    have(0)
    begin_across(0)
    for j in range(2, blocks - 1):
        begin_give(j)
    small_matrix = matrix_of(small_ref)
    gain_one, bias_one, query_shift, value_shift, proj_shift, gain_two, bias_two = vectors_of(small_ref)
    normed = (unit_one * gain_one + bias_one).astype(bf)
    q_ref[...] = (dot(normed, weight_of(wa_ref[:, :, 0]), 1, 0) + query_shift).astype(bf)
    k_ref[...] = dot(normed, weight_of(wa_ref[:, :, 1]), 1, 0).astype(bf)
    v_ref[...] = (dot(normed, weight_of(wa_ref[:, :, 2]), 1, 0) + value_shift).astype(bf)
    write(q_ref, q_out)
    write(k_ref, k_out)
    write(v_ref, v_out)
    write(wa_ref, wa_out)
    for a in late:
        for r in range(levels):
            for n in range(2):
                aside(a, r, n).wait_recv()
            for n in range(2):
                onward(a, r, n).start()
    sides = side_masks(head_dim)
    per = len(sides)
    scale = jnp.full((1, 128), head_dim**-0.5, f32).astype(bf)

    def heads(h, _):
        at = pl.ds(pl.multiple_of(h * 128, 128), 128)

        @pl.when(h == 1)
        def _():
            have(1)
            if ahead > 1:
                begin_across(1)
            if blocks > 2:
                begin_give(blocks - 1)

        query = q_ref[:, at] * scale
        total = jnp.zeros((128, length), f32)
        for s, side in enumerate(sides):
            score = dot(k_ref[:, at] * side, query, 1, 1) + mask_ref[...]
            top = jnp.max(score, axis=0, keepdims=True)
            expo = jnp.exp(score - top)
            norm = jnp.sum(expo, axis=0, keepdims=True)
            lse_ref[pl.ds(h * per + s, 1), :] = top + jnp.log(norm)
            probs = (expo * (1.0 / norm)).astype(bf)
            total = total + dot(v_ref[:, at] * side, probs, 0, 0)
        mixed_ref[at, :] = total.astype(bf)
        return 0

    half = wide // 256
    lax.fori_loop(0, half, heads, 0)
    for a in late:
        for r in range(levels):
            for n in range(2):
                onward(a, r, n).wait_recv()
            over(a, r).start()
    lax.fori_loop(half, wide // 128, heads, 0)
    begin_onward(0)
    write(mixed_ref, mixed_out)
    for r in range(levels):
        over(2, r).wait_recv()
    write(wo_ref, wo_out)
    residual = inputs + dot(mixed_ref[...], weight_of(wo_ref[...]), 0, 0) + proj_shift
    resid_ref[...] = residual
    write(resid_ref, resid_out)
    unit_two, _ = normalize(residual)
    normed_two = (unit_two * gain_two + bias_two).astype(bf)
    a2_ref[...] = normed_two
    routed = (lane >= 32) & (lane < 64)
    logits = jnp.where(routed, dot(normed_two, small_matrix, 1, 0), masked_score)
    logit_exp = jnp.exp(logits - jnp.max(logits, axis=1, keepdims=True))
    probs = logit_exp / jnp.sum(logit_exp, axis=1, keepdims=True)
    info = probs
    gates = []
    for k in range(2):
        expert = cols[:, 3 + k : 4 + k]
        one = (expert == expert_lane).astype(f32)
        gate = jnp.sum(probs * one, axis=1, keepdims=True) * keeps[k]
        info = jnp.where(lane == k, places[k], jnp.where(lane == 2 + k, expert, info))
        high, _ = two_parts(gate)
        middle, low = two_parts(gate - high.astype(f32))
        split = jnp.where(lane == 1, middle.astype(f32), jnp.where(lane == 2, low.astype(f32), 0.0))
        gates.append(jnp.where(lane == 0, high.astype(f32), split).astype(bf))
    info_ref[...] = info

    def fill_inputs(d, _):
        hots = hots_of(d)
        inside = dot(hots[0] + hots[1], a2_ref[...], 1, 0)
        xs_ref[d] = inside.reshape(blocks, room, wide).astype(bf)
        gate = dot(gates[0], hots[0], 0, 1) + dot(gates[1], hots[1], 0, 1)
        gate_ref[d, 0:1, 0:part] = gate[0:1] + gate[1:2] + gate[2:3]
        return 0

    for j in range(1, ahead):
        begin_onward(j)
    gate_ref[...] = jnp.zeros(gate_ref.shape, f32)
    lax.fori_loop(0, groups, fill_inputs, 0)
    for j in range(blocks):
        if j > 1:
            have(j)
        if j < ahead:
            for n in range(2):
                g_onward(j, n).wait_recv()
            write(g_ref.at[j], g_first_out.at[j])
        else:
            write(g_ref.at[j, 0], g_rest_out.at[j - ahead])
    for j in range(blocks):
        for s in range(groups - 1):
            give(j, s).wait_send()
    for j in range(ahead):
        for n in range(2):
            g_across(j, n).wait_send()
            g_onward(j, n).wait_send()
    for a in early + late:
        up_end(a)
        for r in range(levels):
            for n in range(2):
                aside(a, r, n).wait_send()
                onward(a, r, n).wait_send()
            over(a, r).wait_send()
    for c in written:
        c.wait()


def back_kernel(
    head_dim,
    tokens_in,
    cot_ref,
    ints_ref,
    small_ref,
    wa_in,
    wo_in,
    res_ref,
    ig_in,
    resid_ref,
    q_in,
    k_in,
    v_in,
    mixed_in,
    lse_ref,
    info_ref,
    gin_ref,
    gout_ref,
    out_ref,
    tokens_grad_ref,
    wq_grad_out,
    wk_grad_out,
    wv_grad_out,
    wo_grad_out,
    small_grad_ref,
    gin_out_ref,
    gout_out_ref,
    mixed_grad_ref,
    grads_ref,
    qkv_grad_ref,
    wo_grad_ref,
    mask_ref,
    gin_buf,
    gout_buf,
    sem,
    wa_ref,
    wo_ref,
    q_ref,
    k_ref,
    v_ref,
    mixed_ref,
    tokens_ref,
    ig_ref,
    late_sem,
    out_sem,
):
    f32, bf = jnp.float32, jnp.bfloat16
    length, wide = cot_ref.shape
    slots = res_ref.shape[0]
    pieces = gin_ref.shape[0]
    carried = ((gin_ref, gin_buf, gin_out_ref), (gout_ref, gout_buf, gout_out_ref))

    def loads(j):
        return [
            pltpu.make_async_copy(src.at[j], buf, sem.at[0, i])
            for i, (src, buf, _) in enumerate(carried)
        ]

    def stores(j):
        return [
            pltpu.make_async_copy(buf, dst.at[j], sem.at[1, i])
            for i, (_, buf, dst) in enumerate(carried)
        ]

    for c in loads(0):
        c.start()
    late = [(ig_in, ig_ref), (tokens_in, tokens_ref), (mixed_in, mixed_ref), (wo_in, wo_ref), (q_in, q_ref), (k_in, k_ref), (v_in, v_ref), (wa_in, wa_ref)]
    late = [pltpu.make_async_copy(src, dst, late_sem.at[i]) for i, (src, dst) in enumerate(late)]
    for c in late:
        c.start()
    per = 128 // head_dim

    ints, _ = integer_rows(ints_ref[...])
    cols = dot(eye_of(length), ints.astype(bf), 1, 1)
    mask_ref[...] = mask_of(ints, cols)
    small = matrix_of(small_ref)
    gain_one, bias_one, _, _, _, gain_two, bias_two = vectors_of(small_ref)
    lane = lanes_of()
    routed = ((lane >= 32) & (lane < 64)).astype(f32)
    info = info_ref[...]
    probs = info * routed
    upstream = cot_ref[...].astype(f32)
    slot_row = lax.broadcasted_iota(jnp.int32, (1, slots), 1).astype(f32)
    expert_lane = (lane - 32).astype(f32)
    residual = resid_ref[...]
    combined = residual
    prob_grad = jnp.zeros((length, 128), f32)
    gated = jnp.zeros((length, 128), f32)
    hots = []
    for k in range(2):
        place, expert = info[:, k : k + 1], info[:, 2 + k : 3 + k]
        kept = (expert == expert_lane).astype(f32) * (place >= 0).astype(f32)
        gate = jnp.sum(probs * kept, axis=1, keepdims=True)
        hot = (place == slot_row).astype(f32).astype(bf)
        hots.append(hot)
        picked = dot(hot, res_ref[...], 1, 0)
        picked = picked + dot(pltpu.roll(kept, 96, 1).astype(bf), small, 1, 1)
        combined = combined + gate * picked
        prob_grad = prob_grad + kept * jnp.sum(upstream * picked, axis=1, keepdims=True)
        gated = gated + kept * gate
    out_ref[...] = combined.astype(bf)
    inner = jnp.sum(probs * prob_grad, axis=1, keepdims=True)
    logit_grad = (probs * (prob_grad - inner)).astype(bf)
    unit_two, scale_two = normalize(residual)
    normed_two = (unit_two * gain_two + bias_two).astype(bf)
    high, low = two_parts(pltpu.roll(gated, 96, 1))
    small_grad = dot(normed_two, logit_grad, 0, 0)
    both = dot(cot_ref[...], high + pltpu.roll(low.astype(f32), 96, 1).astype(bf), 0, 0)
    small_grad = small_grad + jnp.where(lane < 32, both + pltpu.roll(both, 32, 1), 0.0)
    late[0].wait()
    normed_two_grad = dot(hots[0] + hots[1], ig_ref[...], 1, 0) + dot(logit_grad, small, 1, 1)
    vector_grads = {}
    vector_grads[5] = jnp.sum(normed_two_grad * unit_two, axis=0, keepdims=True)
    vector_grads[6] = jnp.sum(normed_two_grad, axis=0, keepdims=True)
    residual_grad = upstream + normalize_back(normed_two_grad * gain_two, unit_two, scale_two)
    tokens_grad_ref[...] = residual_grad
    branch_grad = residual_grad.astype(bf)
    late[2].wait()
    late[3].wait()
    wo_grad_ref[...] = dot(mixed_ref[...], branch_grad, 1, 0).astype(bf)
    out_copies = [pltpu.make_async_copy(wo_grad_ref, wo_grad_out, out_sem.at[3])]
    out_copies[0].start()
    vector_grads[4] = jnp.sum(branch_grad.astype(f32), axis=0, keepdims=True)
    mixed_grad_ref[...] = dot(branch_grad, weight_of(wo_ref[...]), 1, 1).astype(bf)
    sides = side_masks(head_dim)
    scale = jnp.full((1, 128), head_dim**-0.5, f32).astype(bf)

    def heads(h, _):
        at = pl.ds(pl.multiple_of(h * 128, 128), 128)
        query = q_ref[:, at] * scale
        mixed_grad = mixed_grad_ref[:, at]

        @pl.when(h < pieces)
        def _():
            for c in loads(h):
                c.wait()
            for c in stores(h):
                c.start()

        query_total = jnp.zeros((128, length), f32)
        key_total = jnp.zeros((length, 128), f32)
        value_total = jnp.zeros((length, 128), f32)
        for s, side in enumerate(sides):
            key = k_ref[:, at] * side
            score = dot(key, query, 1, 1) + mask_ref[...]
            probs = jnp.exp(score - lse_ref[pl.ds(h * per + s, 1), :])
            prob_grads = dot(v_ref[:, at] * side, mixed_grad, 1, 1)
            inner = jnp.sum(probs * prob_grads, axis=0, keepdims=True)
            score_grad = (probs * (prob_grads - inner)).astype(bf)
            value_total = value_total + dot(probs.astype(bf), mixed_grad * side, 1, 0)
            key_total = key_total + dot(score_grad, query * side, 1, 0)
            query_total = query_total + dot(key * scale, score_grad, 0, 0)
        @pl.when(h < pieces)
        def _():
            for c in stores(h):
                c.wait()

        @pl.when(h + 1 < pieces)
        def _():
            for c in loads(h + 1):
                c.start()

        totals = (jnp.transpose(query_total), key_total, value_total)
        for i, total in enumerate(totals):
            there = pl.ds(pl.multiple_of(i * wide + h * 128, 128), 128)
            grads_ref[:, there] = total.astype(bf)
        return 0

    for c in late[4:]:
        c.wait()
    lax.fori_loop(0, wide // 128, heads, 0)
    late[1].wait()
    inputs = tokens_ref[...].astype(f32)
    unit_one, scale_one = normalize(inputs)
    normed = (unit_one * gain_one + bias_one).astype(bf)
    qkv_grad_ref[...] = dot(normed, grads_ref[...], 0, 0).astype(bf)
    for i, out in enumerate((wq_grad_out, wk_grad_out, wv_grad_out)):
        src = qkv_grad_ref.at[:, pl.ds(i * wide, wide)]
        out_copies.append(pltpu.make_async_copy(src, out, out_sem.at[i]))
        out_copies[-1].start()
    vector_grads[2] = jnp.sum(grads_ref[:, :wide].astype(f32), axis=0, keepdims=True)
    vector_grads[3] = jnp.sum(grads_ref[:, 2 * wide :].astype(f32), axis=0, keepdims=True)
    normed_grad = jnp.zeros((length, wide), f32)
    for i in range(3):
        part = grads_ref[:, i * wide : (i + 1) * wide]
        normed_grad = normed_grad + dot(part, weight_of(wa_ref[:, :, i]), 1, 1)
    vector_grads[0] = jnp.sum(normed_grad * unit_one, axis=0, keepdims=True)
    vector_grads[1] = jnp.sum(normed_grad, axis=0, keepdims=True)
    tokens_grad_ref[...] += normalize_back(normed_grad * gain_one, unit_one, scale_one)
    line = lax.broadcasted_iota(jnp.int32, (128, wide), 0)
    stacked = jnp.zeros((128, wide), f32)
    for i in range(7):
        stacked = jnp.where(line == 64 + i, vector_grads[i], stacked)
    small_grad_ref[...] = small_grad + jnp.transpose(stacked)
    for c in out_copies:
        c.wait()


def front_call(capacity, room, groups, blocks, tokens, cot, ints, small, weights, reps):
    f32, bf = jnp.float32, jnp.bfloat16
    length, wide = tokens.shape
    shape = jax.ShapeDtypeStruct
    vm = pl.BlockSpec(memory_space=pltpu.VMEM)
    hbm = pl.BlockSpec(memory_space=pl.ANY)
    slots = shape((groups, blocks, room, wide), bf)
    line = shape((length, wide), bf)
    lanes = -(-blocks * room // 128) * 128
    per = weights[0].shape[0]
    turned = shape((wide, length), bf)
    stacked, single = shape((reps, groups, 3, per, wide), bf), shape((reps, groups, per, wide), bf)
    full = shape((length, wide), f32)
    landed = (reps, groups, room, wide)
    outs = [(slots, vm), (shape((AHEAD,) + landed, bf), hbm)]
    outs += [(shape((blocks - AHEAD,) + landed[1:], bf), hbm), (shape((groups, 8, lanes), f32), vm)]
    outs += [(full, hbm), (line, hbm), (line, hbm), (line, hbm), (turned, hbm)]
    outs += [(shape((16, length), f32), vm), (shape((length, 128), f32), vm)]
    outs += [(stacked, hbm), (single, hbm), (shape((reps, groups) + small.shape, bf), vm)]
    kept = [shape((blocks,) + landed, bf), full, line, line, line, turned, stacked, single]
    sems = pltpu.SemaphoreType.DMA((3, groups // 2, 7))
    return pl.pallas_call(
        functools.partial(front_kernel, capacity, room, wide // HEADS),
        out_shape=[o for o, _ in outs],
        in_specs=[vm] * 8,
        out_specs=[place for _, place in outs],
        scratch_shapes=[pltpu.VMEM(o.shape, o.dtype) for o in kept]
        + [
            pltpu.SemaphoreType.DMA((7 + blocks,)),
            pltpu.VMEM((length, length), f32),
            pltpu.VMEM((length, wide), bf),
            pltpu.VMEM(slots.shape, bf),
            pltpu.SemaphoreType.DMA((5,)),
            sems,
            sems,
            pltpu.SemaphoreType.DMA((blocks, groups - 1)),
            pltpu.SemaphoreType.DMA((blocks, groups - 1)),
            pltpu.SemaphoreType.DMA((blocks,)),
            pltpu.SemaphoreType.DMA((AHEAD, 4)),
            pltpu.SemaphoreType.DMA((AHEAD, 4)),
        ],
        compiler_params=pltpu.CompilerParams(
            collective_id=0, has_side_effects=True, vmem_limit_bytes=60 * MIB
        ),
    )(tokens, cot, ints, small, *weights)


def back_call(tokens, cot, ints, small, weights, res, ig, kept, gin, gout):
    f32, bf = jnp.float32, jnp.bfloat16
    length, wide = tokens.shape
    shape = jax.ShapeDtypeStruct
    vm = pl.BlockSpec(memory_space=pltpu.VMEM)
    hbm = pl.BlockSpec(memory_space=pl.ANY)
    square = shape((wide, wide), bf)
    outs = [shape((length, wide), bf), shape((length, wide), f32)] + [square] * 4
    outs += [shape((wide, 128), f32), shape(gin.shape, f32), shape(gout.shape, f32)]
    line = pltpu.VMEM((length, wide), bf)
    return pl.pallas_call(
        functools.partial(back_kernel, wide // HEADS),
        out_shape=outs,
        in_specs=[hbm, vm, vm, vm, hbm, hbm, vm, hbm, vm] + [hbm] * 4 + [vm] * 2 + [hbm] * 2,
        out_specs=[vm] * 2 + [hbm] * 4 + [vm] + [hbm] * 2,
        scratch_shapes=[
            line,
            pltpu.VMEM((length, 3 * wide), bf),
            pltpu.VMEM((wide, 3 * wide), bf),
            pltpu.VMEM((wide, wide), bf),
            pltpu.VMEM((length, length), f32),
            pltpu.VMEM(gin.shape[1:], f32),
            pltpu.VMEM(gout.shape[1:], f32),
            pltpu.SemaphoreType.DMA((2, 2)),
            pltpu.VMEM(weights[0].shape, bf),
            pltpu.VMEM(weights[1].shape, bf),
            line,
            line,
            line,
            pltpu.VMEM((wide, length), bf),
            line,
            pltpu.VMEM(ig.shape, bf),
            pltpu.SemaphoreType.DMA((8,)),
            pltpu.SemaphoreType.DMA((4,)),
        ],
        compiler_params=pltpu.CompilerParams(vmem_limit_bytes=60 * MIB),
    )(tokens, cot, ints, small, *weights, res, ig, *kept, gin, gout)


def body_fast(
    tokens,
    segments,
    valid,
    routes,
    priority,
    ln1_gain,
    ln1_bias,
    w_query,
    query_bias,
    w_key,
    w_value,
    value_bias,
    w_attn_out,
    attn_out_bias,
    ln2_gain,
    ln2_bias,
    w_router,
    expert_in,
    expert_in_bias,
    expert_out,
    expert_out_bias,
    cotangent,
):
    reps, groups = lax.axis_size("rep"), lax.axis_size("exp")
    devices = reps * groups
    length, wide = tokens.shape[1:]
    per = w_query.shape[0]
    blocks = expert_in.shape[0]
    capacity, room = capacity_of(routes.shape[2], length)
    vectors = [ln1_gain, ln1_bias, query_bias, value_bias, attn_out_bias, ln2_gain, ln2_bias]
    small = jnp.concatenate([expert_out_bias.T, w_router], axis=1)
    small = jnp.pad(small, ((0, 0), (0, 128 - small.shape[1])))
    vectors = jnp.pad(jnp.stack(vectors), ((0, 1), (0, 128 - per)))
    small = jnp.concatenate([small, vectors], axis=0)
    ints = jnp.concatenate([segments, valid, priority, routes[0].T], axis=0)
    ints = jnp.pad(ints, ((0, 3), (0, 0)))
    weights = [w_query, w_key, w_value, w_attn_out]
    xs, g, g_rest, gate, *kept, wa, wo, small = front_call(
        capacity, room, groups, blocks, tokens[0], cotangent[0], ints, small, weights, reps
    )
    weights = [wa, wo]
    res, ig, gin, gb, gout = experts_call(
        xs, g, g_rest, gate, expert_in, expert_in_bias, expert_out, reps, groups
    )
    slots = groups * blocks * room
    output, tokens_grad, *grads, small_grad, gin, gout = back_call(
        tokens[0],
        cotangent[0],
        ints,
        small,
        weights,
        res.reshape(slots, wide),
        ig.reshape(slots, wide),
        kept,
        gin,
        gout,
    )
    sums, last = scatter_grads(grads, small_grad.reshape(devices, per, 128), reps, groups)
    columns = [last[:, 64 + i] for i in range(7)]
    return (
        output[None],
        tokens_grad[None],
        columns[0],
        columns[1],
        sums[0],
        columns[2],
        sums[1],
        sums[2],
        columns[3],
        sums[3],
        columns[4],
        columns[5],
        columns[6],
        last[:, 32:64],
        gin,
        gb[:, 0],
        gout,
        last[:, :32].T,
    )


def capacity_of(top_count, length):
    capacity = (105 * top_count * length + 100 * EXPERTS - 1) // (100 * EXPERTS)
    return capacity, -(-capacity // 8) * 8


def body(*args):
    routes, w_query, expert_in = args[3], args[7], args[17]
    reps, groups = lax.axis_size("rep"), lax.axis_size("exp")
    _, room = capacity_of(routes.shape[2], routes.shape[1])
    wide = w_query.shape[1]
    suits = (
        reps == 4
        and groups & (groups - 1) == 0
        and groups == 8
        and w_query.shape[0] % 8 == 0
        and w_query.shape[0] <= 128
        and groups * room <= 512
        and groups * expert_in.shape[0] == EXPERTS == 32
        and expert_in.shape[2] % (128 * reps) == 0
        and routes.shape[2] == 2
        and routes.shape[1] <= 64 * 256
        and 128 % (wide // HEADS) == 0
        and HEADS <= 16
        and 2 <= expert_in.shape[0] < wide // 128
    )
    return body_fast(*args) if suits else body_plain(*args)


def solution(mesh):
    in_specs = (
        P(("rep", "exp"), None, None),
        P(("rep", "exp"), None),
        P(("rep", "exp"), None),
        P(("rep", "exp"), None, None),
        P(("rep", "exp"), None),
        P(("rep", "exp")),
        P(("rep", "exp")),
        P(("rep", "exp"), None),
        P(("rep", "exp")),
        P(("rep", "exp"), None),
        P(("rep", "exp"), None),
        P(("rep", "exp")),
        P(("rep", "exp"), None),
        P(("rep", "exp")),
        P(("rep", "exp")),
        P(("rep", "exp")),
        P(("rep", "exp"), None),
        P("exp", None, None),
        P("exp", None),
        P("exp", None, None),
        P(None, ("rep", "exp")),
        P(("rep", "exp"), None, None),
    )
    out_specs = (
        P(("rep", "exp"), None, None),
        P(("rep", "exp"), None, None),
        P(("rep", "exp")),
        P(("rep", "exp")),
        P(("rep", "exp"), None),
        P(("rep", "exp")),
        P(("rep", "exp"), None),
        P(("rep", "exp"), None),
        P(("rep", "exp")),
        P(("rep", "exp"), None),
        P(("rep", "exp")),
        P(("rep", "exp")),
        P(("rep", "exp")),
        P(("rep", "exp"), None),
        P("exp", None, "rep"),
        P("exp", "rep"),
        P("exp", "rep", None),
        P(None, ("rep", "exp")),
    )
    return jax.shard_map(body, mesh=mesh, in_specs=in_specs, out_specs=out_specs, check_vma=False)
```
